32 devices in a mesh: dp: 4 (over x, core), fsdp: 8 (over z, y).
Axes of the slice: x: 2, y: 2, z: 4, core: 2. Of those that a mesh axis runs over, the one named last changes fastest.
Arguments:
- layer_in: bfloat16 [4096, 2048], P(('dp', 'fsdp')), may hold values from -12 to 12
- cotangent: bfloat16 [4096, 2048], P(('dp', 'fsdp')), may hold values from -6 to 6
- w_qkv: bfloat16 [2048, 6144], P(('dp', 'fsdp')), may hold values from -1 to 1
- w_out: bfloat16 [2048, 2048], P(('dp', 'fsdp')), may hold values from -0.5 to 0.5
- w_up: bfloat16 [2048, 8192], P(('dp', 'fsdp')), may hold values from -0.125 to 0.125
- w_down: bfloat16 [8192, 2048], P(('dp', 'fsdp')), may hold values from -0.0625 to 0.0625
- gain_attn: bfloat16 [2048], P(('dp', 'fsdp')), may hold values from 0.5 to 1.5
- shift_attn: bfloat16 [2048], P(('dp', 'fsdp')), may hold values from -1.5 to 1.5
- bias_query: bfloat16 [2048], P(('dp', 'fsdp')), may hold values from -1.5 to 1.5
- bias_value: bfloat16 [2048], P(('dp', 'fsdp')), may hold values from -1.5 to 1.5
- bias_out: bfloat16 [2048], P(('dp', 'fsdp')), may hold values from -1.5 to 1.5
- gain_mlp: bfloat16 [2048], P(('dp', 'fsdp')), may hold values from 0.5 to 1.5
- shift_mlp: bfloat16 [2048], P(('dp', 'fsdp')), may hold values from -1.5 to 1.5
- bias_up: bfloat16 [8192], P(('dp', 'fsdp')), may hold values from -1.5 to 1.5
- bias_down: bfloat16 [2048], P(('dp', 'fsdp')), may hold values from -1.5 to 1.5
- parents: int32 [4, 13], P('dp'), may hold values from 0 to 4, as said below
- seg_blocks: int32 [4, 32], P('dp'), may hold values from 0 to 12, as said below
- token_valid: int32 [4, 1024], P('dp'), may hold values from 0 to 1, as said below
Outputs:
- layer_out: bfloat16 [4096, 2048], P(('dp', 'fsdp'))
- grad_x: bfloat16 [4096, 2048], P(('dp', 'fsdp'))
- grad_w_qkv: float32 [2048, 6144], P(('dp', 'fsdp'))
- grad_w_out: float32 [2048, 2048], P(('dp', 'fsdp'))
- grad_w_up: float32 [2048, 8192], P(('dp', 'fsdp'))
- grad_w_down: float32 [8192, 2048], P(('dp', 'fsdp'))
- grad_gain_attn: float32 [2048], P(('dp', 'fsdp'))
- grad_shift_attn: float32 [2048], P(('dp', 'fsdp'))
- grad_bias_query: float32 [2048], P(('dp', 'fsdp'))
- grad_bias_value: float32 [2048], P(('dp', 'fsdp'))
- grad_bias_out: float32 [2048], P(('dp', 'fsdp'))
- grad_gain_mlp: float32 [2048], P(('dp', 'fsdp'))
- grad_shift_mlp: float32 [2048], P(('dp', 'fsdp'))
- grad_bias_up: float32 [8192], P(('dp', 'fsdp'))
- grad_bias_down: float32 [2048], P(('dp', 'fsdp'))
- root_squares: float32 [2], replicated
The draws below stay inside these ranges and needn't reach their ends.
Inputs may be any that keep to these rules, and one draw needn't show every extreme that they name: `parents`: segment 0 of each tree is its trunk and has parent 0; segments 1 to 4 are branches with parent 0; the other segments are leaves, two under each branch. `seg_blocks`: each segment holds one run of whole consecutive blocks, one or more; the trunk holds 16 blocks. `token_valid`: padding lies only at the end of the last block of a segment, which keeps one valid token or more and loses one or more.
All inputs are finite; a program needn't handle non-finite values.
Results may differ from the reference program's by a relative error of at most 0.014.
Values may be sent and summed in bfloat16 or wider, within the bound.
A program may use at most 704 MiB of HBM per device.

```python
import math
import jax
import jax.numpy as jnp
from jax import lax

D = 2048
H = 32
HD = 64
FF = 8192
BLK = 32
BRANCHES = 4
SEGS = 13
TREE = 1024
NB = 32
TOKENS = 4096
N_DP = 4


def tree_shape(key):

    def one_tree(number):
        tree_key = jax.random.fold_in(key, number)
        leaf_key, cut_key, order_key, keep_key = jax.random.split(tree_key, 4)
        leaf_order = jax.random.permutation(leaf_key, 2 * BRANCHES).astype(jnp.int32)
        parent_row = jnp.concatenate([jnp.zeros((1 + BRANCHES,), jnp.int32), 1 + leaf_order // 2])
        remaining = NB - NB // 2
        cuts = jnp.sort(jax.random.permutation(cut_key, remaining - 1).astype(jnp.int32)[:3 * BRANCHES - 1] + 1)
        bounds = jnp.concatenate([jnp.zeros((1,), jnp.int32), cuts, jnp.full((1,), remaining, jnp.int32)])
        lengths = jnp.concatenate([jnp.full((1,), NB // 2, jnp.int32), bounds[1:] - bounds[:-1]])
        order = jax.random.permutation(order_key, SEGS).astype(jnp.int32)
        placed = lengths[order]
        ends = jnp.cumsum(placed).astype(jnp.int32)
        blocks = jnp.arange(NB, dtype=jnp.int32)
        slot = jnp.sum((blocks[:, None] >= ends[None, :]).astype(jnp.int32), axis=1)
        block_row = order[slot]
        keep = jax.random.randint(keep_key, (SEGS,), 1, BLK, dtype=jnp.int32)
        return (parent_row, block_row, keep)
    return jax.vmap(one_tree)(jnp.arange(N_DP, dtype=jnp.int32))


def draw_parents(key, part):
    return tree_shape(key)[0]


def draw_seg_blocks(key, part):
    return tree_shape(key)[1]


def draw_token_valid(key, part):
    parent_rows, block_rows, keep_rows = tree_shape(key)

    def one_tree(block_row, keep_row):
        following = jnp.concatenate([block_row[1:], jnp.full((1,), -1, jnp.int32)])
        closing = block_row != following
        tokens = jnp.arange(TREE, dtype=jnp.int32)
        block = tokens // BLK
        within = tokens % BLK
        keep_token = keep_row[block_row[block]]
        live = jnp.where(closing[block], within < keep_token, True)
        return live.astype(jnp.int32)
    return jax.vmap(one_tree)(block_rows, keep_rows)


def draw_layer_in(key, part):
    key = jax.random.fold_in(key, 7)
    ramp = jnp.exp(jnp.log(3.0) * jnp.arange(TOKENS, dtype=jnp.float32) / TOKENS)[:, None]
    base = jnp.clip(jax.random.normal(key, (TOKENS, D), jnp.float32), -4.0, 4.0)
    return (base * ramp).astype(jnp.bfloat16)


def draw_w_qkv(key, part):
    key = jax.random.fold_in(key, 11)
    base = jnp.clip(jax.random.normal(key, (D, 3 * D), jnp.float32), -5.0, 5.0)
    shared = jnp.clip(jax.random.normal(jax.random.fold_in(key, 1), (1, 3 * D), jnp.float32), -4.0, 4.0)
    return ((base + 0.5 * shared) / jnp.sqrt(jnp.float32(D))).astype(jnp.bfloat16)


def block_levels(own_key, dims, cuts, low, top_value):
    level, own = 1.0, jax.random.fold_in(own_key, 6)
    for dim, blocks in cuts:
        draws = jnp.exp(jax.random.uniform(jax.random.fold_in(own, dim), (blocks,), jnp.float32, low / len(cuts), top_value / len(cuts)))
        level = level * jnp.repeat(draws, dims[dim] // blocks).reshape([-1 if axis == dim else 1 for axis in range(len(dims))])
    return level


def gaussian(key, extent, width, bound, shards=(), kind=jnp.bfloat16):
    drawn = jax.random.normal(key, extent, jnp.float32) * width
    if len(shards) > 0:
        drawn = block_levels(key, extent, shards, -0.22, 0.18) * drawn
    return jnp.clip(drawn, min=-bound, max=bound).astype(kind)


def setup_inputs(seed: int = 0) -> dict:
    key_list = jax.random.split(jax.random.key(seed), 19)
    layer_in = draw_layer_in(jax.random.fold_in(key_list[18], 71), 0)
    cotangent = gaussian(key_list[1], (TOKENS, D), 1.0, 6.0, ((0, 32),))
    w_qkv = draw_w_qkv(jax.random.fold_in(key_list[18], 71), 0)
    w_out = gaussian(key_list[3], (D, D), (D // 16) ** -0.5, 0.5, ((0, 32),))
    w_up = gaussian(key_list[4], (D, FF), D ** -0.5, 0.125, ((0, 32),))
    w_down = gaussian(key_list[5], (FF, D), FF ** -0.5, 0.0625, ((0, 32),))
    gain_attn = jnp.clip(1.0 + 0.1 * jax.random.normal(key_list[6], (D,), jnp.float32), 0.5, 1.5).astype(jnp.bfloat16)
    shift_attn = gaussian(key_list[7], (D,), 0.3, 1.5, ((0, 32),))
    bias_query = gaussian(key_list[8], (D,), 0.3, 1.5, ((0, 32),))
    bias_value = gaussian(key_list[9], (D,), 0.3, 1.5, ((0, 32),))
    bias_out = gaussian(key_list[10], (D,), 0.3, 1.5, ((0, 32),))
    gain_mlp = jnp.clip(1.0 + 0.1 * jax.random.normal(key_list[11], (D,), jnp.float32), 0.5, 1.5).astype(jnp.bfloat16)
    shift_mlp = gaussian(key_list[12], (D,), 0.3, 1.5, ((0, 32),))
    bias_up = gaussian(key_list[13], (FF,), 0.3, 1.5, ((0, 32),))
    bias_down = gaussian(key_list[14], (D,), 0.3, 1.5, ((0, 32),))
    parents = draw_parents(jax.random.fold_in(key_list[18], 71), 0)
    seg_blocks = draw_seg_blocks(jax.random.fold_in(key_list[18], 71), 0)
    token_valid = draw_token_valid(jax.random.fold_in(key_list[18], 71), 0)
    return {"layer_in": layer_in, "cotangent": cotangent, "w_qkv": w_qkv, "w_out": w_out, "w_up": w_up, "w_down": w_down, "gain_attn": gain_attn, "shift_attn": shift_attn, "bias_query": bias_query, "bias_value": bias_value, "bias_out": bias_out, "gain_mlp": gain_mlp, "shift_mlp": shift_mlp, "bias_up": bias_up, "bias_down": bias_down, "parents": parents, "seg_blocks": seg_blocks, "token_valid": token_valid}


@jax.custom_vjp
def low(v):
    return lax.optimization_barrier(v.astype(jnp.bfloat16)).astype(jnp.float32)

@jax.custom_vjp
def low_back(v):
    return v

def low_keep(v):
    return (low(v), None)

def low_pass(kept, grad):
    return (grad,)

def back_keep(v):
    return (v, None)

def back_low(kept, grad):
    return (low(grad),)
low.defvjp(low_keep, low_pass)
low_back.defvjp(back_keep, back_low)
EPSILON = 1e-05
MASKED = -1e+30
PRECISE = lax.Precision.HIGHEST

def matmul(left, right):
    return jnp.dot(left, right, precision=PRECISE, preferred_element_type=jnp.float32)

def layer_norm(values, gain, shift):
    center = values - lax.optimization_barrier(jnp.mean(values, axis=-1, keepdims=True))
    scaled = center * lax.rsqrt(lax.optimization_barrier(jnp.mean(center * center, axis=-1, keepdims=True)) + EPSILON)
    return scaled * gain + shift

def tree_tables(parents, seg_blocks, valid):
    segments = parents.shape[0]
    seg_tokens = jnp.broadcast_to(seg_blocks[:, None], (seg_blocks.shape[0], BLK)).reshape(-1).astype(jnp.int32)
    labels = jnp.arange(segments, dtype=jnp.int32)
    member = (seg_tokens[:, None] == labels[None, :]).astype(jnp.int32)
    counted = member * valid[:, None]
    before = (jnp.cumsum(counted, axis=0) - counted).astype(jnp.int32)
    rank = lax.optimization_barrier(jnp.sum(before * member, axis=1)).astype(jnp.int32)
    seg_len = lax.optimization_barrier(jnp.sum(counted, axis=0)).astype(jnp.int32)
    grand = parents[parents]
    ancestor = ((labels[None, :] == parents[:, None]) | (labels[None, :] == grand[:, None])) & (labels[None, :] != labels[:, None])
    offset = lax.optimization_barrier(jnp.sum(ancestor.astype(jnp.int32) * seg_len[None, :], axis=1)).astype(jnp.int32)
    position = (lax.optimization_barrier(jnp.sum(member * offset[None, :], axis=1)) + rank).astype(jnp.int32)
    return (seg_tokens, position, ancestor.astype(jnp.float32))

def allowed_pairs(seg_query, pos_query, index_query, seg_key, pos_key, index_key, valid_key, ancestor):
    labels = jnp.arange(ancestor.shape[0], dtype=jnp.int32)
    member_query = (seg_query[:, None] == labels[None, :]).astype(jnp.float32)
    member_key = (seg_key[:, None] == labels[None, :]).astype(jnp.float32)
    reach = jnp.dot(jnp.dot(member_query, ancestor), member_key.T) > 0.5
    causal = (seg_query[:, None] == seg_key[None, :]) & (index_key[None, :] <= index_query[:, None])
    visible = (valid_key[None, :] == 1) | (index_key[None, :] == index_query[:, None])
    distance = (pos_query[:, None] - pos_key[None, :]).astype(jnp.float32)
    return ((reach | causal) & visible, distance)

def attention(queries, keys, values, seg_tokens, position, ancestor, valid):
    tree = queries.shape[0]
    block = math.gcd(tree, 512)
    key_heads = keys.reshape(tree, H, HD)
    value_heads = values.reshape(tree, H, HD)
    slopes = jnp.exp2(-8.0 * (jnp.arange(H, dtype=jnp.float32) + 1.0) / H)
    index_all = jnp.arange(tree, dtype=jnp.int32)

    def one_block(start):
        query_heads = lax.dynamic_slice_in_dim(queries, start, block, 0).reshape(block, H, HD)
        index_query = start + jnp.arange(block, dtype=jnp.int32)
        seg_query = lax.dynamic_slice_in_dim(seg_tokens, start, block, 0)
        pos_query = lax.dynamic_slice_in_dim(position, start, block, 0)
        mask, distance = allowed_pairs(seg_query, pos_query, index_query, seg_tokens, position, index_all, valid, ancestor)
        raw = low_back(jnp.einsum('qhd,khd->hqk', query_heads, key_heads, precision=PRECISE))
        logits = jnp.where(mask[None], raw * HD ** (-0.5) - slopes[:, None, None] * distance[None], MASKED)
        weights = low(jax.nn.softmax(logits, axis=-1))
        mixed = jnp.einsum('hqk,khd->qhd', weights, value_heads, precision=PRECISE)
        return mixed.reshape(block, H * HD)
    starts = jnp.arange(tree // block, dtype=jnp.int32) * block
    return lax.map(jax.checkpoint(one_block), starts).reshape(tree, H * HD)

def tree_forward(inputs, tables, params):
    w_qkv, w_out, w_up, w_down, gain_attn, shift_attn, bias_query, bias_value, bias_out, gain_mlp, shift_mlp, bias_up, bias_down = params
    seg_tokens, position, ancestor, valid = tables
    first_in = low(layer_norm(inputs, gain_attn, shift_attn))
    joined = matmul(first_in, w_qkv) + jnp.concatenate([bias_query, jnp.zeros_like(bias_query), bias_value])
    joined = low(low_back(joined))
    queries, keys, values = jnp.split(joined, 3, axis=1)
    mixed = low(low_back(attention(queries, keys, values, seg_tokens, position, ancestor, valid)))
    branch = low_back(matmul(mixed, w_out) + bias_out)
    middle = inputs + branch
    second_in = low(layer_norm(middle, gain_mlp, shift_mlp))
    hidden = low_back(matmul(second_in, w_up) + bias_up)
    active = low(jax.nn.gelu(hidden, approximate=False))
    update = low_back(matmul(active, w_down) + bias_down)
    return (middle + update, branch)

def reference(layer_in, cotangent, w_qkv, w_out, w_up, w_down, gain_attn, shift_attn, bias_query, bias_value, bias_out, gain_mlp, shift_mlp, bias_up, bias_down, parents, seg_blocks, token_valid):
    floats = [arr.astype(jnp.float32) for arr in (layer_in, w_qkv, w_out, w_up, w_down, gain_attn, shift_attn, bias_query, bias_value, bias_out, gain_mlp, shift_mlp, bias_up, bias_down)]
    trees = parents.shape[0]

    def forward(inputs, *params):

        def per_tree(carry, item):
            tree_in, tree_parents, tree_blocks, tree_valid = item
            seg_tokens, position, ancestor = tree_tables(tree_parents, tree_blocks, tree_valid)
            result, branch = tree_forward(tree_in, (seg_tokens, position, ancestor, tree_valid), params)
            return (carry, (result, jnp.sum(branch * branch)))
        start = jnp.zeros((), jnp.float32)
        _, (results, branch_sq) = lax.scan(per_tree, start, (inputs.reshape(trees, -1, D), parents, seg_blocks, token_valid))
        return (results.reshape(-1, D), jnp.sum(branch_sq))
    result, pull, branch_sq = jax.vjp(forward, *floats, has_aux=True)
    grads = pull(cotangent.astype(jnp.float32))
    entries = result.shape[0] * result.shape[1]
    root_squares = jnp.sqrt(jnp.stack([jnp.sum(result * result), branch_sq]) / entries)
    return (result.astype(jnp.bfloat16), grads[0].astype(jnp.bfloat16), grads[1], grads[2], grads[3], grads[4], grads[5], grads[6], grads[7], grads[8], grads[9], grads[10], grads[11], grads[12], grads[13], root_squares)
```

```python
import jax
import jax.numpy as jnp
from jax import lax
from jax.sharding import PartitionSpec as P

H = 32
HD = 64
BLK = 32

EPSILON = 1e-05
MASKED = -1e30
BF = jnp.bfloat16
F32 = jnp.float32
BOTH = ("dp", "fsdp")


def norm_parts(values):
    center = values - jnp.mean(values, axis=-1, keepdims=True)
    inverse = lax.rsqrt(jnp.mean(center * center, axis=-1, keepdims=True) + EPSILON)
    return (center * inverse, inverse)


def norm_back(grad_normed, normed, inverse):
    mean_grad = jnp.mean(grad_normed, axis=-1, keepdims=True)
    mean_cross = jnp.mean(grad_normed * normed, axis=-1, keepdims=True)
    return inverse * (grad_normed - mean_grad - normed * mean_cross)


def tree_tables(parents, seg_blocks, valid):
    segments = parents.shape[0]
    seg_tokens = jnp.broadcast_to(seg_blocks[:, None], (seg_blocks.shape[0], BLK)).reshape(-1)
    labels = jnp.arange(segments, dtype=jnp.int32)
    member = (seg_tokens[:, None] == labels[None, :]).astype(jnp.int32)
    counted = member * valid[:, None]
    before = jnp.cumsum(counted, axis=0) - counted
    rank = jnp.sum(before * member, axis=1)
    seg_len = jnp.sum(counted, axis=0)
    picked = (parents[:, None] == labels[None, :]).astype(jnp.int32)
    grand = jnp.sum(picked * parents[None, :], axis=1)
    ancestor = ((labels[None, :] == parents[:, None]) | (labels[None, :] == grand[:, None])) & (
        labels[None, :] != labels[:, None]
    )
    offset = jnp.sum(ancestor.astype(jnp.int32) * seg_len[None, :], axis=1)
    position = jnp.sum(member * offset[None, :], axis=1) + rank
    return (seg_tokens, position, ancestor.astype(jnp.float32))


def allowed_mask(seg, index, valid, ancestor):
    labels = jnp.arange(ancestor.shape[0], dtype=jnp.int32)
    member = (seg[:, None] == labels[None, :]).astype(jnp.float32)
    reach = jnp.dot(jnp.dot(member, ancestor), member.T) > 0.5
    causal = (seg[:, None] == seg[None, :]) & (index[None, :] <= index[:, None])
    visible = (valid[None, :] == 1) | (index[None, :] == index[:, None])
    return (reach | causal) & visible


def gelu_exact(value):
    return jax.nn.gelu(value, approximate=False)


def mm(spec, a, b):
    return jnp.einsum(spec, a, b, preferred_element_type=F32)


def gather_tokens(x):
    return lax.all_gather(x, "fsdp", axis=0, tiled=True)


def scatter_tokens(x):
    return lax.psum_scatter(x.astype(BF), "fsdp", scatter_dimension=0, tiled=True).astype(F32)


def scatter_dp(x):
    return lax.psum_scatter(x, "dp", scatter_dimension=0, tiled=True)


def gather_dp(x):
    return lax.all_gather(x, "dp", axis=0, tiled=True)


def per_device(
    layer_in,
    cotangent,
    w_qkv,
    w_out,
    w_up,
    w_down,
    gain_attn,
    shift_attn,
    bias_query,
    bias_value,
    bias_out,
    gain_mlp,
    shift_mlp,
    bias_up,
    bias_down,
    parents,
    seg_blocks,
    token_valid,
):
    rows, width = layer_in.shape
    dp, fsdp = lax.axis_size("dp"), lax.axis_size("fsdp")
    devices = dp * fsdp
    rank = lax.axis_index("fsdp")
    heads = H // fsdp
    cols = heads * HD
    tree = token_valid.shape[1]
    part = w_qkv.shape[0]
    unit = w_down.shape[0]

    vec = jnp.concatenate(
        [gain_attn, shift_attn, bias_query, bias_value, bias_out, gain_mlp, shift_mlp, bias_down, bias_up]
    )
    vec = lax.all_gather(vec, BOTH, axis=0, tiled=False).astype(F32)
    (gain_one, shift_one, query_bias, value_bias, out_bias, gain_two, shift_two, down_bias) = [
        vec[:, i * part : (i + 1) * part].reshape(-1) for i in range(8)
    ]
    up_bias = vec[:, 8 * part :].reshape(dp, fsdp, unit)
    up_bias = lax.dynamic_index_in_dim(up_bias, rank, 1, keepdims=False).reshape(-1)

    inputs = layer_in.astype(F32)
    normed_one, inverse_one = norm_parts(inputs)
    attn_in = gather_tokens((normed_one * gain_one + shift_one).astype(BF))

    def to_rank(w):
        return gather_dp(lax.all_to_all(w, "fsdp", split_axis=2, concat_axis=0, tiled=True))

    qkv_w = to_rank(w_qkv.reshape(part, 3, fsdp, cols)).reshape(width, 3 * cols)
    out_w = lax.all_gather(w_out, BOTH, axis=0, tiled=True)
    up_w = to_rank(w_up.reshape(part, dp, fsdp, unit)).reshape(width, dp * unit)
    down_w = gather_dp(w_down)
    cot = gather_tokens(cotangent)

    def own_cols(v):
        return lax.dynamic_slice_in_dim(v, rank * cols, cols, 0)

    joined_bias = jnp.concatenate([own_cols(query_bias), jnp.zeros((cols,), F32), own_cols(value_bias)])
    joined = (jnp.dot(attn_in, qkv_w, preferred_element_type=F32) + joined_bias).astype(BF)
    joined = joined.reshape(tree, 3, heads, HD)
    queries, keys, values = joined[:, 0], joined[:, 1], joined[:, 2]

    valid = token_valid[0]
    seg, position, ancestor = tree_tables(parents[0], seg_blocks[0], valid)
    index = jnp.arange(tree, dtype=jnp.int32)
    mask = allowed_mask(seg, index, valid, ancestor)
    distance = (position[:, None] - position[None, :]).astype(F32)
    numbers = (rank * heads + jnp.arange(heads)).astype(F32)
    slopes = jnp.exp2(-8.0 * (numbers + 1.0) / H)
    raw = mm("qhd,khd->hqk", queries, keys)
    logits = jnp.where(mask[None], raw * HD ** (-0.5) - slopes[:, None, None] * distance[None], MASKED)
    peak = jnp.max(logits, axis=-1, keepdims=True)
    weights = jnp.exp(logits - peak)
    probs = weights / jnp.sum(weights, axis=-1, keepdims=True)
    probs_low = probs.astype(BF)
    mixed = mm("hqk,khd->qhd", probs_low, values).reshape(tree, cols).astype(BF)

    mixed_own = lax.all_to_all(mixed, "fsdp", split_axis=0, concat_axis=1, tiled=True)
    branch = jnp.dot(mixed_own, out_w, preferred_element_type=F32) + out_bias
    middle = inputs + branch
    normed_two, inverse_two = norm_parts(middle)
    mlp_in = gather_tokens((normed_two * gain_two + shift_two).astype(BF))
    hidden = jnp.dot(mlp_in, up_w, preferred_element_type=F32) + up_bias
    active_float, gelu_pull = jax.vjp(gelu_exact, hidden)
    active = active_float.astype(BF)
    grad_active = mm("td,fd->tf", cot, down_w)
    grad_hidden = gelu_pull(grad_active)[0].astype(BF)
    grad_mlp_in = scatter_tokens(mm("tf,df->td", grad_hidden, up_w))
    update = scatter_tokens(jnp.dot(active, down_w, preferred_element_type=F32)) + down_bias
    result = middle + update

    cot_own = cotangent.astype(F32)
    grad_middle = cot_own + norm_back(grad_mlp_in * gain_two, normed_two, inverse_two)
    grad_branch = grad_middle.astype(BF)
    grad_mixed = mm("te,de->td", grad_branch, out_w).astype(BF)
    grad_heads = lax.all_to_all(grad_mixed, "fsdp", split_axis=1, concat_axis=0, tiled=True)
    grad_heads = grad_heads.reshape(tree, heads, HD)
    grad_probs = mm("qhd,khd->hqk", grad_heads, values)
    delta = jnp.sum(probs * grad_probs, axis=-1, keepdims=True)
    grad_raw = (probs * (grad_probs - delta) * HD ** (-0.5)).astype(BF)
    grad_q = mm("hqk,khd->qhd", grad_raw, keys)
    grad_k = mm("hqk,qhd->khd", grad_raw, queries)
    grad_v = mm("hqk,qhd->khd", probs_low, grad_heads)
    grad_joined = jnp.stack([grad_q, grad_k, grad_v], axis=1).reshape(tree, 3 * cols).astype(BF)
    grad_attn_in = scatter_tokens(mm("te,de->td", grad_joined, qkv_w))
    grad_inputs = grad_middle + norm_back(grad_attn_in * gain_one, normed_one, inverse_one)

    def to_owner(g, outer, inner):
        g = scatter_dp(g.astype(BF)).reshape(fsdp, part, outer * inner)
        g = lax.all_to_all(g, "fsdp", split_axis=0, concat_axis=0, tiled=True)
        g = g.reshape(fsdp, part, outer, inner).transpose(1, 2, 0, 3)
        return g.reshape(part, outer * fsdp * inner).astype(F32)

    grad_down_w = scatter_dp(mm("tf,td->fd", active, cot).astype(BF)).astype(F32)
    grad_up_w = to_owner(mm("td,tf->df", mlp_in, grad_hidden), dp, unit)
    grad_out_w = scatter_dp(mm("td,te->de", mixed_own, grad_branch).astype(BF))
    grad_out_w = lax.psum_scatter(grad_out_w, "fsdp", scatter_dimension=0, tiled=True).astype(F32)
    grad_qkv_w = to_owner(mm("td,te->de", attn_in, grad_joined), 3, cols)

    col = jnp.sum(grad_joined.astype(F32), axis=0)

    def spread(v):
        return lax.dynamic_update_slice_in_dim(jnp.zeros((width,), F32), v, rank * cols, 0)

    smalls = [
        jnp.sum(grad_attn_in * normed_one, axis=0),
        jnp.sum(grad_attn_in, axis=0),
        spread(col[:cols]),
        spread(col[2 * cols :]),
        jnp.sum(grad_branch.astype(F32), axis=0),
        jnp.sum(grad_mlp_in * normed_two, axis=0),
        jnp.sum(grad_mlp_in, axis=0),
        jnp.sum(cot_own, axis=0),
    ]
    grad_bias_up = jnp.sum(grad_hidden.astype(F32), axis=0)
    grad_bias_up = lax.dynamic_update_slice_in_dim(
        jnp.zeros((dp, fsdp, unit), F32), grad_bias_up.reshape(dp, 1, unit), rank, 1
    )
    packed = jnp.concatenate(
        [v.reshape(devices, part) for v in smalls] + [grad_bias_up.reshape(devices, unit)], axis=1
    )
    packed = lax.psum_scatter(packed, BOTH, scatter_dimension=0, tiled=True)[0]
    small = [packed[i * part : (i + 1) * part] for i in range(8)]
    squares = lax.psum(jnp.stack([jnp.sum(result * result), jnp.sum(branch * branch)]), BOTH)
    root_squares = jnp.sqrt(squares / (devices * rows * width))
    return (
        result.astype(BF),
        grad_inputs.astype(BF),
        grad_qkv_w,
        grad_out_w,
        grad_up_w,
        grad_down_w,
        small[0],
        small[1],
        small[2],
        small[3],
        small[4],
        small[5],
        small[6],
        packed[8 * part :],
        small[7],
        root_squares,
    )


def solution(mesh):
    matrix, vector, table = P(BOTH, None), P(BOTH), P("dp", None)
    return jax.shard_map(
        per_device,
        mesh=mesh,
        in_specs=(matrix,) * 6 + (vector,) * 9 + (table,) * 3,
        out_specs=(matrix,) * 6 + (vector,) * 9 + (P(),),
        check_vma=False,
    )
```

```python
import functools

import jax
import jax.numpy as jnp
from jax import lax
from jax.experimental import pallas as pl
from jax.experimental.pallas import tpu as pltpu
from jax.sharding import PartitionSpec as P

H = 32
HD = 64
BLK = 32

EPSILON = 1e-05
MASKED = -1e30
BF = jnp.bfloat16
F32 = jnp.float32
BOTH = ("dp", "fsdp")
MESH = pl.DeviceIdType.MESH
HBM = pl.BlockSpec(memory_space=pl.ANY)
VM = pl.BlockSpec(memory_space=pltpu.VMEM)
MIB = 2**20


def place():
    d, f = lax.axis_index("dp"), lax.axis_index("fsdp")
    return d // 2, d % 2, f // 2, f % 2


def at(x, c, z, y):
    return (x * 2 + c, z * 2 + y)


def remote(src, dst, send, recv, target):
    return pltpu.make_async_remote_copy(
        src_ref=src, dst_ref=dst, send_sem=send, recv_sem=recv, device_id=target, device_id_type=MESH
    )


def greet(partners):
    barrier = pltpu.get_barrier_semaphore()
    count = 0
    for condition, device in partners:

        @pl.when(condition)
        def _():
            pl.semaphore_signal(barrier, inc=1, device_id=device, device_id_type=MESH)

        count = count + jnp.asarray(condition).astype(jnp.int32)
    pl.semaphore_wait(barrier, count)


def greet_all(devices, fsdp, me):
    barrier = pltpu.get_barrier_semaphore()

    def one(k, _):
        other = (me + k) % devices
        pl.semaphore_signal(barrier, inc=1, device_id=(other // fsdp, other % fsdp), device_id_type=MESH)
        return 0

    lax.fori_loop(1, devices, one, 0)
    pl.semaphore_wait(barrier, devices - 1)


def line_partners(nz, pos):
    x, c, z, y = pos
    return [(z >= 0, at(x, 1 - c, z, y)), (z > 0, at(x, c, z - 1, y)), (z < nz - 1, at(x, c, z + 1, y))]


def rank_partners(nz, pos):
    x, c, z, y = pos
    n = 2 * nz
    others = [(z * 2 + c + k) % n for k in range(1, n)]
    return [(z >= 0, at(x, p % 2, p // 2, y)) for p in others]


def group_partners(pos):
    x, c, z, y = pos
    return [(z >= 0, at(x ^ (m // 2), c, z, y ^ (m % 2))) for m in (1, 2, 3)]


def line_gather(src, dst, send, recv, nz, swap, pos):
    x, c, z, y = pos
    own = z * 2 + c
    sib = at(x, 1 - c, z, y)
    up_dev, dn_dev = at(x, c, z + 1, y), at(x, c, z - 1, y)
    UP, DN, SU, SD = 0, nz, 2 * nz, 3 * nz
    OWN = 4 * nz

    def block(b, moved):
        return dst.at[b] if moved else src

    def up(k):
        b = (z - k) * 2 + c
        return remote(block(b, k or swap), dst.at[b], send.at[UP + k], recv.at[UP + k], up_dev)

    def dn(k):
        b = (z + k) * 2 + c
        return remote(block(b, k or swap), dst.at[b], send.at[DN + k], recv.at[DN + k], dn_dev)

    def side(k, base, sign):
        b = (z + sign * k) * 2 + c
        return remote(block(b, k or swap), dst.at[b], send.at[base + k], recv.at[base + k], sib)

    def got(b, sem):
        return remote(dst.at[b], dst.at[b], send.at[OWN], recv.at[sem], sib)

    local = pltpu.make_async_copy(src, dst.at[own], recv.at[OWN])
    trade = remote(src, dst.at[z * 2 + y], send.at[OWN], recv.at[OWN], at(x, y, z, c))

    def first():
        if swap:
            pl.when(c == y)(local.start)
            pl.when(c != y)(trade.start)
        else:
            local.start()

    def spread():
        if swap:
            local.wait()
        pl.when(z < nz - 1)(up(0).start)
        pl.when(z > 0)(dn(0).start)
        side(0, SU, 1).start()

    def step(k):
        @pl.when(z >= k)
        def _():
            got((z - k) * 2 + c, UP + k - 1).wait_recv()
            pl.when(z < nz - 1)(up(k).start)
            side(k, SU, -1).start()

        @pl.when(z + k < nz)
        def _():
            got((z + k) * 2 + c, DN + k - 1).wait_recv()
            pl.when(z > 0)(dn(k).start)
            side(k, SD, 1).start()

    def last():
        if swap:
            pl.when(c != y)(trade.wait_send)
        else:
            local.wait()
        got(z * 2 + 1 - c, SU).wait_recv()
        pl.when(z < nz - 1)(up(0).wait_send)
        pl.when(z > 0)(dn(0).wait_send)
        side(0, SU, 1).wait_send()
        for k in range(1, nz):

            @pl.when(z >= k)
            def _():
                got((z - k) * 2 + 1 - c, SU + k).wait_recv()
                pl.when(z < nz - 1)(up(k).wait_send)
                side(k, SU, -1).wait_send()

            @pl.when(z + k < nz)
            def _():
                got((z + k) * 2 + 1 - c, SD + k).wait_recv()
                pl.when(z > 0)(dn(k).wait_send)
                side(k, SD, 1).wait_send()

    return [first, spread] + [functools.partial(step, k) for k in range(1, nz)] + [last]


def gather_sems(nz):
    return [pltpu.SemaphoreType.DMA((4 * nz + 1,))] * 2


def gather_kernel(nz, src, dst, send, recv):
    pos = place()
    greet(line_partners(nz, pos))
    for stage in line_gather(src, dst, send, recv, nz, False, pos):
        stage()


def params(cid, vmem=None):
    return pltpu.CompilerParams(collective_id=cid, has_side_effects=True, vmem_limit_bytes=vmem)


def gather_tokens(a, nz, cid):
    return pl.pallas_call(
        functools.partial(gather_kernel, nz),
        out_shape=jax.ShapeDtypeStruct((2 * nz,) + a.shape, a.dtype),
        in_specs=[HBM],
        out_specs=HBM,
        scratch_shapes=gather_sems(nz),
        compiler_params=params(cid),
        name="gather_tokens",
    )(a)


def scatter_kernel(nz, p, out, acc, ups, dns, send, recv):
    pos = place()
    x, c, z, y = pos
    greet(line_partners(nz, pos))
    sib = at(x, 1 - c, z, y)
    S, U, D = 0, nz, 2 * nz

    def f(v):
        return v.astype(F32)

    def swap(t):
        return remote(p.at[t * 2 + 1 - c], acc.at[t], send.at[S + t], recv.at[S + t], sib)

    def up(t):
        return remote(acc.at[t], ups.at[t], send.at[U + t], recv.at[U + t], at(x, c, z + 1, y))

    def dn(t):
        return remote(acc.at[t], dns.at[t], send.at[D + t], recv.at[D + t], at(x, c, z - 1, y))

    order = []
    for i in range(nz - 1):
        order += [(True, nz - 1 - i), (False, i)]
    for upward, t in order:
        pl.when(z < t if upward else z > t)(swap(t).start)
    swap(z).start()
    for upward, t in order:

        @pl.when(z < t if upward else z > t)
        def _():
            swap(t).wait_recv()
            acc[t] = (f(acc[t]) + f(p[t * 2 + c])).astype(BF)
            move, came = (up, ups) if upward else (dn, dns)

            @pl.when(z > 0 if upward else z < nz - 1)
            def _():
                move(t).wait_recv()
                acc[t] = (f(acc[t]) + f(came[t])).astype(BF)

            move(t).start()

    swap(z).wait_recv()
    out[...] = f(acc[z]) + f(p[z * 2 + c])

    @pl.when(z > 0)
    def _():
        up(z).wait_recv()
        out[...] += f(ups[z])

    @pl.when(z < nz - 1)
    def _():
        dn(z).wait_recv()
        out[...] += f(dns[z])

    for t in range(nz):
        swap(t).wait_send()
        pl.when(z < t)(up(t).wait_send)
        pl.when(z > t)(dn(t).wait_send)


def scatter_tokens(p, nz, cid):
    blocks, rows, width = p.shape
    return pl.pallas_call(
        functools.partial(scatter_kernel, nz),
        out_shape=jax.ShapeDtypeStruct((rows, width), F32),
        in_specs=[VM],
        out_specs=VM,
        scratch_shapes=[pltpu.VMEM((nz, rows, width), BF)] * 3 + [pltpu.SemaphoreType.DMA((3 * nz,))] * 2,
        compiler_params=params(cid, 60 * MIB),
        name="scatter_tokens",
    )(p)


def block_of(x, c, z, y, nz):
    return (x * 2 + c) * 2 * nz + z * 2 + y


def sliced_gather(src, dst, cuts, sems, nz, pos):
    x, c, z, y = pos
    n = 2 * nz
    me = z * 2 + c
    send1, recv1, send2, recv2 = sems

    def pieces(p):
        if cuts is None:
            return [(src.at[p], slice(None))]
        return [(src.at[:, a], b) for a, b in cuts(p)]

    def row(p, gx, gy):
        return block_of(gx, p % 2, p // 2, gy, nz)

    mine = row(me, x, y)

    def out(k):
        p = (me + k) % n
        return [
            remote(a, dst.at[mine, :, b], send1.at[p], recv1.at[me], at(x, p % 2, p // 2, y))
            for a, b in pieces(p)
        ]

    def whole(p, gx, gy, sem):
        b = dst.at[row(p, gx, gy)]
        return remote(b, b, send1.at[me], sem, at(x, 1 - c, z, y))

    local = [pltpu.make_async_copy(a, dst.at[mine, :, b], recv1.at[me]) for a, b in pieces(me)]

    def forward(k, m):
        p = (me - k + n) % n
        b = dst.at[row(p, x, y)]
        slot = (m - 1) * n + p
        return remote(b, b, send2.at[slot], recv2.at[slot], at(x ^ (m // 2), c, z, y ^ (m % 2)))

    def first():
        for copy in local:
            copy.start()
        for k in range(1, n):
            for copy in out(k):
                copy.start()

    def step(k):
        p = (me - k + n) % n
        whole(p, x, y, recv1.at[p]).wait_recv()
        for m in (3, 1, 2):
            forward(k, m).start()

    def last():
        for k in range(n):
            p = (me - k + n) % n
            for m in (1, 2, 3):
                slot = (m - 1) * n + p
                whole(p, x ^ (m // 2), y ^ (m % 2), recv2.at[slot]).wait_recv()
        for k in range(n):
            if k:
                p = (me + k) % n
                whole_send = remote(
                    dst.at[mine], dst.at[mine], send1.at[p], recv1.at[me], at(x, p % 2, p // 2, y)
                )
                whole_send.wait_send()
            for m in (1, 2, 3):
                forward(k, m).wait_send()

    return [first] + [functools.partial(step, k) for k in range(n)] + [last]


def sliced_sems(nz):
    n = 2 * nz
    return [pltpu.SemaphoreType.DMA((n,))] * 2 + [pltpu.SemaphoreType.DMA((3 * n,))] * 2


def group_gather(src, dst, send, recv, pos):
    x, c, z, y = pos
    g = x * 2 + y
    local = pltpu.make_async_copy(src, dst.at[g], recv.at[0])

    def out(m):
        return remote(src, dst.at[g], send.at[m], recv.at[m], at(x ^ (m // 2), c, z, y ^ (m % 2)))

    def first():
        local.start()
        for m in (3, 1, 2):
            out(m).start()

    def last():
        local.wait()
        for m in (1, 2, 3):
            there = dst.at[(x ^ (m // 2)) * 2 + (y ^ (m % 2))]
            remote(there, there, send.at[m], recv.at[m], at(x, 1 - c, z, y)).wait_recv()
            out(m).wait_send()

    return [first, last]


def head_runs(nz, cols):
    return lambda p: [
        (block_of(x, p % 2, p // 2, 0, nz) * HD, x * cols // 2, cols // 2) for x in range(2)
    ]


def qkv_cuts(nz, width, cols):
    runs = head_runs(nz, cols)
    return lambda p: [
        (pl.ds(j * width + there, size), pl.ds(j * cols + here, size)) for j in range(3) for there, here, size in runs(p)
    ]


def up_cuts(nz, unit):
    def cuts(p):
        z, c = p // 2, p % 2
        return [
            (pl.ds(((x * 2 + c) * 2 * nz + z * 2) * unit, 2 * unit), pl.ds(x * 2 * unit, 2 * unit))
            for x in range(2)
        ]

    return cuts


def fetch_kernel(
    nz, width, cols, unit, x_in, cot, w_qkv, w_up, w_down, vec, tab,
    x_all, cot_all, qkv_w, up_w, down_w, vecs, tab_out, *sems,
):
    pos = place()
    x, c, z, y = pos
    fsdp = 2 * nz
    devices = 4 * fsdp
    me = (x * 2 + c) * fsdp + z * 2 + y
    sems = list(sems)
    x_sems, cot_sems, qkv_sems, up_sems = sems[:2], sems[2:4], sems[4:8], sems[8:12]
    down_sems, vec_sems, tab_sems = sems[12:14], sems[14:16], sems[16:18]
    greet_all(devices, fsdp, me)

    def vec_copy(other):
        return remote(vec, vecs.at[me], vec_sems[0].at[other], vec_sems[1].at[me], (other // fsdp, other % fsdp))

    def each(fn):
        def body(k, _):
            fn((me + k) % devices)
            return 0

        lax.fori_loop(1, devices, body, 0)

    vec_local = pltpu.make_async_copy(vec, vecs.at[me], vec_sems[1].at[me])
    tab_local = pltpu.make_async_copy(tab, tab_out, tab_sems[1].at[0])
    tab_trade = remote(tab, tab_out, tab_sems[0].at[0], tab_sems[1].at[0], at(x, y, z, c))

    gx = line_gather(x_in, x_all, *x_sems, nz, True, pos)
    gc = line_gather(cot, cot_all, *cot_sems, nz, True, pos)
    cuts = qkv_cuts(nz, width, cols) if len(w_qkv.shape) == 2 else None
    gq = sliced_gather(w_qkv, qkv_w, cuts, qkv_sems, nz, pos)
    gu = sliced_gather(w_up, up_w, up_cuts(nz, unit), up_sems, nz, pos)
    gd = group_gather(w_down, down_w, *down_sems, pos)
    gx[0]()
    gq[0]()
    gx[1]()
    vec_local.start()
    each(lambda other: vec_copy(other).start())
    pl.when(c == y)(tab_local.start)
    pl.when(c != y)(tab_trade.start)
    gd[0]()
    gc[0]()
    gu[0]()
    for k in range(1, fsdp + 1):
        gq[k]()
    for stage in gx[2:]:
        stage()
    gc[1]()
    for k in range(1, fsdp + 1):
        gu[k]()
    for stage in gc[2:]:
        stage()
    gq[-1]()
    gu[-1]()
    gd[-1]()

    def vec_done(other):
        remote(vec, vecs.at[other], vec_sems[0].at[other], vec_sems[1].at[other], at(x, 1 - c, z, y)).wait_recv()
        vec_copy(other).wait_send()

    vec_local.wait()
    each(vec_done)
    tab_local.wait()
    pl.when(c != y)(tab_trade.wait_send)


def fetch(nz, x_in, cot, w_qkv, w_up, w_down, vec, tab, cid):
    rows, width = x_in.shape
    n = 2 * nz
    devices = 4 * n
    part, unit = w_up.shape[0], w_down.shape[0]
    cols = width // n
    shapes = [
        ((n, rows, width), BF),
        ((n, rows, width), BF),
        ((devices, part, 3 * cols), BF),
        ((devices, part, 4 * unit), BF),
        ((4, unit, width), BF),
        ((devices,) + vec.shape, F32),
        (tab.shape, jnp.int32),
    ]
    return pl.pallas_call(
        functools.partial(fetch_kernel, nz, width, cols, unit),
        out_shape=[jax.ShapeDtypeStruct(s, t) for s, t in shapes],
        in_specs=[HBM] * 7,
        out_specs=[HBM] * 7,
        scratch_shapes=gather_sems(nz) * 2
        + sliced_sems(nz) * 2
        + [pltpu.SemaphoreType.DMA((4,))] * 2
        + [pltpu.SemaphoreType.DMA((devices,))] * 2
        + [pltpu.SemaphoreType.DMA((1,))] * 2,
        compiler_params=params(cid),
        name="fetch",
    )(x_in, cot, w_qkv, w_up, w_down, vec, tab)


def exchange_kernel(nz, count, *refs):
    srcs, dsts, (send, recv) = refs[:count], refs[count : 2 * count], refs[2 * count :]
    pos = place()
    x, c, z, y = pos
    n = 2 * nz
    me = z * 2 + c
    greet(rank_partners(nz, pos))

    def move(i, p):
        return remote(srcs[i].at[p], dsts[i].at[me], send.at[i * n + p], recv.at[i * n + me], at(x, p % 2, p // 2, y))

    def come(i, p):
        there = dsts[i].at[p]
        return remote(there, there, send.at[i * n + me], recv.at[i * n + p], at(x, 1 - c, z, y))

    local = [pltpu.make_async_copy(s.at[me], d.at[me], recv.at[i * n + me]) for i, (s, d) in enumerate(zip(srcs, dsts))]
    for i in range(count):
        local[i].start()
        for k in range(1, n):
            move(i, (me + k) % n).start()
    for i in range(count):
        local[i].wait()
        for k in range(1, n):
            come(i, (me - k + n) % n).wait_recv()
            move(i, (me + k) % n).wait_send()


def exchange(arrays, nz, cid, name):
    n = 2 * nz
    return pl.pallas_call(
        functools.partial(exchange_kernel, nz, len(arrays)),
        out_shape=[jax.ShapeDtypeStruct(a.shape, a.dtype) for a in arrays],
        in_specs=[HBM] * len(arrays),
        out_specs=[HBM] * len(arrays),
        scratch_shapes=[pltpu.SemaphoreType.DMA((len(arrays) * n,))] * 2,
        compiler_params=params(cid),
        name=name,
    )(*arrays)


def hand_kernel(nz, kinds, *refs):
    count = len(kinds)
    srcs, dsts, (send, recv) = refs[:count], refs[count : 2 * count], refs[2 * count :]
    pos = place()
    x, c, z, y = pos
    n = 2 * nz
    greet(group_partners(pos))

    def copies(i, m):
        gx, gy = x ^ (m // 2), y ^ (m % 2)
        sem = i * 3 + m - 1
        target = at(gx, c, z, gy)
        if not kinds[i]:
            return [remote(srcs[i].at[gx * 2 + gy], dsts[i].at[m - 1], send.at[sem], recv.at[sem], target)]
        return [
            remote(
                srcs[i].at[block_of(gx, p % 2, p // 2, gy, nz)],
                dsts[i].at[m - 1, p],
                send.at[sem],
                recv.at[sem],
                target,
            )
            for p in range(n)
        ]

    for i in range(count):
        for m in (3, 1, 2):
            for copy in copies(i, m):
                copy.start()
    for i in range(count):
        for m in (1, 2, 3):
            sem = i * 3 + m - 1
            there = dsts[i].at[m - 1]
            whole = remote(there, there, send.at[sem], recv.at[sem], at(x, 1 - c, z, y))
            whole.wait_recv()
            whole.wait_send()


def hand(arrays, kinds, nz, cid):
    n = 2 * nz
    shapes = [(3, n) + a.shape[1:] if k else (3,) + a.shape[1:] for a, k in zip(arrays, kinds)]
    return pl.pallas_call(
        functools.partial(hand_kernel, nz, kinds),
        out_shape=[jax.ShapeDtypeStruct(s, a.dtype) for s, a in zip(shapes, arrays)],
        in_specs=[HBM] * len(arrays),
        out_specs=[HBM] * len(arrays),
        scratch_shapes=[pltpu.SemaphoreType.DMA((3 * len(arrays),))] * 2,
        compiler_params=params(cid),
        name="hand",
    )(*arrays)


def finish_kernel(nz, res, grad, small, res_out, grad_out, small_out, came, send, recv):
    pos = place()
    x, c, z, y = pos
    fsdp = 2 * nz
    devices = 4 * fsdp
    me = (x * 2 + c) * fsdp + z * 2 + y
    greet_all(devices, fsdp, me)

    def each(fn):
        def body(k, _):
            fn((me + k) % devices)
            return 0

        lax.fori_loop(1, devices, body, 0)

    def share(other):
        return remote(small.at[other], came.at[me], send.at[other], recv.at[me], (other // fsdp, other % fsdp))

    each(lambda other: share(other).start())
    homes = [(res, res_out, devices), (grad, grad_out, devices + 1)]
    for src, dst, sem in homes:
        pl.when(c == y)(pltpu.make_async_copy(src, dst, recv.at[sem]).start)
        pl.when(c != y)(remote(src, dst, send.at[sem], recv.at[sem], at(x, y, z, c)).start)

    def done(other):
        remote(small.at[me], came.at[other], send.at[other], recv.at[other], at(x, 1 - c, z, y)).wait_recv()
        share(other).wait_send()

    each(done)
    came[me] = small[me]
    small_out[...] = jnp.sum(came[...], axis=0)
    for src, dst, sem in homes:
        pltpu.make_async_copy(src, dst, recv.at[sem]).wait()
        pl.when(c != y)(remote(src, dst, send.at[sem], recv.at[sem], at(x, y, z, c)).wait_send)


def finish(res, grad, small, nz, cid):
    devices = small.shape[0]
    return pl.pallas_call(
        functools.partial(finish_kernel, nz),
        out_shape=[
            jax.ShapeDtypeStruct(res.shape, res.dtype),
            jax.ShapeDtypeStruct(grad.shape, grad.dtype),
            jax.ShapeDtypeStruct(small.shape[1:], F32),
        ],
        in_specs=[HBM, HBM, VM],
        out_specs=[HBM, HBM, VM],
        scratch_shapes=[pltpu.VMEM(small.shape, F32)] + [pltpu.SemaphoreType.DMA((devices + 2,))] * 2,
        compiler_params=params(cid, 32 * MIB),
        name="finish",
    )(res, grad, small)


def dot(a, b, dims):
    return lax.dot_general(a, b, (dims, ((), ())), preferred_element_type=F32)


NN = ((1,), (0,))
NT = ((1,), (1,))
TN = ((0,), (0,))


def attend_kernel(heads, slopes, far, joined_q, joined, out):
    cols = heads * HD
    gap = far[...]
    for h in range(heads):
        q = joined_q[:, h * HD : (h + 1) * HD]
        k = joined[:, cols + h * HD : cols + (h + 1) * HD]
        v = joined[:, 2 * cols + h * HD : 2 * cols + (h + 1) * HD]
        logits = dot(q, k, NT) * HD ** (-0.5) + slopes[h] * gap
        weights = jnp.exp(logits - jnp.max(logits, axis=1, keepdims=True))
        probs = weights * (1.0 / jnp.sum(weights, axis=1, keepdims=True))
        out[:, h * HD : (h + 1) * HD] = dot(probs.astype(BF), v, NN).astype(BF)


def attend(slopes, far, joined, heads):
    tree = far.shape[0]
    cols = heads * HD
    rows = min(256, tree)
    return pl.pallas_call(
        functools.partial(attend_kernel, heads),
        out_shape=jax.ShapeDtypeStruct((tree, cols), BF),
        grid=(tree // rows,),
        in_specs=[
            pl.BlockSpec(memory_space=pltpu.SMEM),
            pl.BlockSpec((rows, tree), lambda i: (i, 0)),
            pl.BlockSpec((rows, 3 * cols), lambda i: (i, 0)),
            pl.BlockSpec((tree, 3 * cols), lambda i: (0, 0)),
        ],
        out_specs=pl.BlockSpec((rows, cols), lambda i: (i, 0)),
        compiler_params=pltpu.CompilerParams(vmem_limit_bytes=56 * MIB),
        cost_estimate=pl.CostEstimate(
            flops=4 * heads * tree * tree * HD, bytes_accessed=4 * tree * tree, transcendentals=heads * tree * tree
        ),
        name="attend",
    )(slopes, far, joined, joined)


def attend_back_kernel(heads, slopes, far, joined_q, joined, grad, out_q, out_k, out_v, acc_k, acc_v):
    cols = heads * HD
    step = pl.program_id(0)

    @pl.when(step == 0)
    def _():
        acc_k[...] = jnp.zeros_like(acc_k)
        acc_v[...] = jnp.zeros_like(acc_v)

    gap = far[...]
    for h in range(heads):
        here = slice(h * HD, (h + 1) * HD)
        q = joined_q[:, here]
        k = joined[:, cols + h * HD : cols + (h + 1) * HD]
        v = joined[:, 2 * cols + h * HD : 2 * cols + (h + 1) * HD]
        g = grad[:, here]
        logits = dot(k, q, NT) * HD ** (-0.5) + slopes[h] * gap
        weights = jnp.exp(logits - jnp.max(logits, axis=0, keepdims=True))
        probs = weights * (1.0 / jnp.sum(weights, axis=0, keepdims=True))
        grad_probs = dot(v, g, NT)
        delta = jnp.sum(probs * grad_probs, axis=0, keepdims=True)
        grad_raw = (probs * (grad_probs - delta) * HD ** (-0.5)).astype(BF)
        acc_v[:, here] += dot(probs.astype(BF), g, NN)
        acc_k[:, here] += dot(grad_raw, q, NN)
        out_q[:, here] = dot(grad_raw, k, TN).astype(BF)

    @pl.when(step == pl.num_programs(0) - 1)
    def _():
        out_k[...] = acc_k[...].astype(BF)
        out_v[...] = acc_v[...].astype(BF)


def attend_back(slopes, far_t, joined, grad, heads):
    tree = far_t.shape[0]
    cols = heads * HD
    rows = min(256, tree)
    full = pl.BlockSpec((tree, cols), lambda i: (0, 0))
    part = pl.BlockSpec((rows, cols), lambda i: (i, 0))
    return pl.pallas_call(
        functools.partial(attend_back_kernel, heads),
        out_shape=[jax.ShapeDtypeStruct((tree, cols), BF)] * 3,
        grid=(tree // rows,),
        in_specs=[
            pl.BlockSpec(memory_space=pltpu.SMEM),
            pl.BlockSpec((tree, rows), lambda i: (0, i)),
            pl.BlockSpec((rows, 3 * cols), lambda i: (i, 0)),
            pl.BlockSpec((tree, 3 * cols), lambda i: (0, 0)),
            part,
        ],
        out_specs=[part, full, full],
        scratch_shapes=[pltpu.VMEM((tree, cols), F32)] * 2,
        compiler_params=pltpu.CompilerParams(vmem_limit_bytes=56 * MIB),
        cost_estimate=pl.CostEstimate(
            flops=10 * heads * tree * tree * HD, bytes_accessed=4 * tree * tree, transcendentals=heads * tree * tree
        ),
        name="attend_back",
    )(slopes, far_t, joined, joined, grad)


def norm_parts(values):
    center = values - jnp.mean(values, axis=-1, keepdims=True)
    inverse = lax.rsqrt(jnp.mean(center * center, axis=-1, keepdims=True) + EPSILON)
    return (center * inverse, inverse)


def norm_back(grad_normed, normed, inverse):
    mean_grad = jnp.mean(grad_normed, axis=-1, keepdims=True)
    mean_cross = jnp.mean(grad_normed * normed, axis=-1, keepdims=True)
    return inverse * (grad_normed - mean_grad - normed * mean_cross)


def tree_tables(parents, seg_blocks, valid):
    segments = parents.shape[0]
    seg_tokens = jnp.broadcast_to(seg_blocks[:, None], (seg_blocks.shape[0], BLK)).reshape(-1)
    labels = jnp.arange(segments, dtype=jnp.int32)
    member = (seg_tokens[:, None] == labels[None, :]).astype(jnp.int32)
    counted = member * valid[:, None]
    before = jnp.cumsum(counted, axis=0) - counted
    rank = jnp.sum(before * member, axis=1)
    seg_len = jnp.sum(counted, axis=0)
    picked = (parents[:, None] == labels[None, :]).astype(jnp.int32)
    grand = jnp.sum(picked * parents[None, :], axis=1)
    ancestor = ((labels[None, :] == parents[:, None]) | (labels[None, :] == grand[:, None])) & (
        labels[None, :] != labels[:, None]
    )
    offset = jnp.sum(ancestor.astype(jnp.int32) * seg_len[None, :], axis=1)
    position = jnp.sum(member * offset[None, :], axis=1) + rank
    return (seg_tokens, position, ancestor.astype(jnp.float32))


def allowed_mask(seg, index, valid, ancestor):
    labels = jnp.arange(ancestor.shape[0], dtype=jnp.int32)
    member = (seg[:, None] == labels[None, :]).astype(jnp.float32)
    reach = jnp.dot(jnp.dot(member, ancestor), member.T) > 0.5
    causal = (seg[:, None] == seg[None, :]) & (index[None, :] <= index[:, None])
    visible = (valid[None, :] == 1) | (index[None, :] == index[:, None])
    return (reach | causal) & visible


def gelu_exact(value):
    return jax.nn.gelu(value, approximate=False)


def mm(spec, a, b):
    return jnp.einsum(spec, a, b, preferred_element_type=F32)


def padded(flat, lanes):
    return jnp.pad(flat, [(0, 0)] * (flat.ndim - 1) + [(0, -flat.shape[-1] % lanes)])


def per_device(
    layer_in,
    cotangent,
    w_qkv,
    w_out,
    w_up,
    w_down,
    gain_attn,
    shift_attn,
    bias_query,
    bias_value,
    bias_out,
    gain_mlp,
    shift_mlp,
    bias_up,
    bias_down,
    parents,
    seg_blocks,
    token_valid,
):
    rows, width = layer_in.shape
    fsdp = lax.axis_size("fsdp")
    nz = fsdp // 2
    devices = 4 * fsdp
    x, c, z, y = place()
    rank = z * 2 + c
    heads = H // fsdp
    cols = heads * HD
    tree = token_valid.shape[1]
    part = w_qkv.shape[0]
    unit = w_down.shape[0]

    vec = jnp.concatenate(
        [gain_attn, shift_attn, bias_query, bias_value, bias_out, gain_mlp, shift_mlp, bias_down, bias_up]
    ).astype(F32)
    vec = padded(vec, 1024).reshape(-1, 128)
    tab = jnp.concatenate([token_valid[0], seg_blocks[0], parents[0]])
    tab = padded(tab, 1024).reshape(-1, 128)
    out_w = lax.all_gather(w_out, BOTH, axis=0, tiled=True)
    aligned = part == HD and cols % 256 == 0
    if not aligned:
        w_qkv = w_qkv.reshape(part, 3, fsdp, cols).transpose(2, 0, 1, 3).reshape(fsdp, part, 3 * cols)
    x_all, cot, qkv_w, up_w, down_w, vecs, tab = fetch(nz, layer_in, cotangent, w_qkv, w_up, w_down, vec, tab, 1)
    x_all, cot = x_all.reshape(tree, width), cot.reshape(tree, width)
    qkv_w = qkv_w.reshape(width, 3 * cols)
    up_w = up_w.reshape(width, 4 * unit)
    down_w = down_w.reshape(4 * unit, width)
    vecs = vecs.reshape(devices, -1)
    (gain_one, shift_one, query_bias, value_bias, out_bias, gain_two, shift_two, down_bias) = [
        vecs[:, i * part : (i + 1) * part].reshape(-1) for i in range(8)
    ]
    up_bias = vecs[:, 8 * part : 8 * part + unit].reshape(2, 2, nz, 2, unit)
    up_bias = lax.dynamic_slice(up_bias, (0, c, z, 0, 0), (2, 1, 1, 2, unit)).reshape(-1)

    def own_rows(v):
        return lax.dynamic_slice_in_dim(v, rank * rows, rows, 0)

    normed_all, _ = norm_parts(x_all.astype(F32))
    attn_in = (normed_all * gain_one + shift_one).astype(BF)
    inputs = own_rows(x_all).astype(F32)
    normed_one, inverse_one = norm_parts(inputs)

    if aligned:

        def own_cols(v):
            v = v.reshape(2, 2, nz, 2, HD)
            return lax.dynamic_slice(v, (0, c, z, 0, 0), (2, 1, 1, 2, HD)).reshape(-1)

        def spread(v):
            v = v.reshape(2, 1, 1, 2, HD)
            return lax.dynamic_update_slice(jnp.zeros((2, 2, nz, 2, HD), F32), v, (0, c, z, 0, 0))

        numbers = block_of(jnp.arange(2)[:, None], c, z, jnp.arange(2)[None, :], nz).reshape(-1)
    else:

        def own_cols(v):
            return lax.dynamic_slice_in_dim(v, rank * cols, cols, 0)

        def spread(v):
            return lax.dynamic_update_slice_in_dim(jnp.zeros((width,), F32), v, rank * cols, 0)

        numbers = rank * heads + jnp.arange(heads)

    joined_bias = jnp.concatenate([own_cols(query_bias), jnp.zeros((cols,), F32), own_cols(value_bias)])
    joined = (jnp.dot(attn_in, qkv_w, preferred_element_type=F32) + joined_bias).astype(BF)

    tab = tab.reshape(-1)
    blocks = seg_blocks.shape[1]
    valid = tab[:tree]
    seg, position, ancestor = tree_tables(
        tab[tree + blocks : tree + blocks + parents.shape[1]], tab[tree : tree + blocks], valid
    )
    index = jnp.arange(tree, dtype=jnp.int32)
    mask = allowed_mask(seg, index, valid, ancestor)
    far = jnp.where(mask, (position[None, :] - position[:, None]).astype(F32), MASKED)
    slopes = jnp.exp2(-8.0 * (numbers.astype(F32) + 1.0) / H)
    mixed = attend(slopes, far, joined, heads)

    (mixed_own,) = exchange([mixed.reshape(fsdp, rows, cols)], nz, 2, "mixed_to_tokens")
    if aligned:
        mixed_own = mixed_own.reshape(nz, 2, rows, 2, 2 * HD).transpose(2, 3, 1, 0, 4).reshape(rows, width)
    else:
        mixed_own = mixed_own.transpose(1, 0, 2).reshape(rows, width)
    branch = jnp.dot(mixed_own, out_w, preferred_element_type=F32) + out_bias
    middle = inputs + branch
    normed_two, inverse_two = norm_parts(middle)
    mlp_in = gather_tokens((normed_two * gain_two + shift_two).astype(BF), nz, 3).reshape(tree, width)
    hidden = jnp.dot(mlp_in, up_w, preferred_element_type=F32) + up_bias
    active_float, gelu_pull = jax.vjp(gelu_exact, hidden)
    active = active_float.astype(BF)
    grad_active = mm("td,fd->tf", cot, down_w)
    grad_hidden = gelu_pull(grad_active)[0].astype(BF)

    def scatter(v):
        return scatter_tokens(v.astype(BF).reshape(fsdp, rows, width), nz, 4)

    grad_mlp_in = scatter(mm("tf,df->td", grad_hidden, up_w))
    update = scatter(jnp.dot(active, down_w, preferred_element_type=F32)) + down_bias
    result = middle + update

    cot_own = own_rows(cot).astype(F32)
    grad_middle = cot_own + norm_back(grad_mlp_in * gain_two, normed_two, inverse_two)
    grad_branch = grad_middle.astype(BF)
    grad_mixed = mm("te,de->td", grad_branch, out_w).astype(BF)
    if aligned:
        branch_all = gather_tokens(grad_branch, nz, 3).reshape(tree, width)
        out_g = mm("td,te->de", mixed, branch_all).astype(BF).reshape(4, part, width)
    else:
        grad_out_w = lax.psum_scatter(
            mm("td,te->de", mixed_own, grad_branch).astype(BF), BOTH, scatter_dimension=0, tiled=True
        ).astype(F32)
    if aligned:
        grad_mixed = grad_mixed.reshape(rows, 2, 2, nz, 2 * HD).transpose(3, 2, 0, 1, 4).reshape(fsdp, rows, cols)
    else:
        grad_mixed = grad_mixed.reshape(rows, fsdp, cols).transpose(1, 0, 2)
    (grad_heads,) = exchange([grad_mixed], nz, 5, "grad_to_heads")
    grad_heads = grad_heads.reshape(tree, cols)
    grad_q, grad_k, grad_v = attend_back(slopes, far.T, joined, grad_heads, heads)
    grad_joined = jnp.concatenate([grad_q, grad_k, grad_v], axis=1)
    grad_attn_in = scatter(mm("te,de->td", grad_joined, qkv_w))
    grad_inputs = grad_middle + norm_back(grad_attn_in * gain_one, normed_one, inverse_one)

    down_g = mm("tf,td->fd", active, cot).astype(BF).reshape(4, unit, width)
    up_g = mm("td,tf->df", mlp_in, grad_hidden).astype(BF).reshape(devices, part, 4 * unit)
    qkv_g = mm("td,te->de", attn_in, grad_joined).astype(BF).reshape(devices, part, 3 * cols)
    flat = [down_g, out_g] if aligned else [down_g]
    *flat_c, up_c, qkv_c = hand(flat + [up_g, qkv_g], (False,) * len(flat) + (True, True), nz, 6)

    def mine(g, came):
        g = g.reshape((2, 2, nz, 2) + g.shape[1:])
        g = lax.dynamic_slice(g, (x, 0, 0, y, 0, 0), (1, 2, nz, 1) + g.shape[4:])
        g = g.reshape((2, nz) + g.shape[4:]).swapaxes(0, 1)
        return (g.reshape(came.shape[1:]).astype(F32) + jnp.sum(came.astype(F32), axis=0)).astype(BF)

    def mine_flat(g, came):
        return lax.dynamic_index_in_dim(g, x * 2 + y, 0, keepdims=False).astype(F32) + jnp.sum(came.astype(F32), axis=0)

    grad_down_w = mine_flat(down_g, flat_c[0])
    if aligned:
        grad_out_w = mine_flat(out_g, flat_c[1])
    up_s, qkv_s = mine(up_g, up_c), mine(qkv_g, qkv_c)

    up_s, qkv_s = exchange([up_s, qkv_s], nz, 7, "grads_to_owners")
    grad_up_w = up_s.reshape(nz, 2, part, 2, 2, unit).transpose(2, 3, 1, 0, 4, 5).reshape(part, -1).astype(F32)
    if aligned:
        grad_qkv_w = qkv_s.reshape(nz, 2, part, 3, 2, 2 * HD).transpose(2, 3, 4, 1, 0, 5)
    else:
        grad_qkv_w = qkv_s.reshape(fsdp, part, 3, cols).transpose(1, 2, 0, 3)
    grad_qkv_w = grad_qkv_w.reshape(part, -1).astype(F32)

    col = jnp.sum(grad_joined.astype(F32), axis=0)

    smalls = [
        jnp.sum(grad_attn_in * normed_one, axis=0),
        jnp.sum(grad_attn_in, axis=0),
        spread(col[:cols]),
        spread(col[2 * cols :]),
        jnp.sum(grad_branch.astype(F32), axis=0),
        jnp.sum(grad_mlp_in * normed_two, axis=0),
        jnp.sum(grad_mlp_in, axis=0),
        jnp.sum(cot_own, axis=0),
    ]
    grad_bias_up = jnp.sum(grad_hidden.astype(F32), axis=0).reshape(2, 1, 1, 2, unit)
    grad_bias_up = lax.dynamic_update_slice(jnp.zeros((2, 2, nz, 2, unit), F32), grad_bias_up, (0, c, z, 0, 0))
    squares = jnp.stack([jnp.sum(result * result), jnp.sum(branch * branch)])
    packed = jnp.concatenate(
        [v.reshape(devices, part) for v in smalls]
        + [grad_bias_up.reshape(devices, unit), jnp.broadcast_to(squares, (devices, 2))],
        axis=1,
    )
    packed = padded(packed, 1024).reshape(devices, -1, 128)
    layer_out, grad_x, packed = finish(result.astype(BF), grad_inputs.astype(BF), packed, nz, 8)
    packed = packed.reshape(-1)
    small = [packed[i * part : (i + 1) * part] for i in range(8)]
    up_at = 8 * part
    root_squares = jnp.sqrt(packed[up_at + unit : up_at + unit + 2] / (devices * rows * width))
    return (
        layer_out,
        grad_x,
        grad_qkv_w,
        grad_out_w,
        grad_up_w,
        grad_down_w,
        small[0],
        small[1],
        small[2],
        small[3],
        small[4],
        small[5],
        small[6],
        packed[up_at : up_at + unit],
        small[7],
        root_squares,
    )


def solution(mesh):
    matrix, vector, table = P(BOTH, None), P(BOTH), P("dp", None)
    return jax.shard_map(
        per_device,
        mesh=mesh,
        in_specs=(matrix,) * 6 + (vector,) * 9 + (table,) * 3,
        out_specs=(matrix,) * 6 + (vector,) * 9 + (P(),),
        check_vma=False,
    )
```

```python
import functools

import jax
import jax.numpy as jnp
from jax import lax
from jax.experimental import pallas as pl
from jax.experimental.pallas import tpu as pltpu
from jax.sharding import PartitionSpec as P

H = 32
HD = 64
BLK = 32

EPSILON = 1e-05
MASKED = -1e30
BF = jnp.bfloat16
F32 = jnp.float32
BOTH = ("dp", "fsdp")
MESH = pl.DeviceIdType.MESH
HBM = pl.BlockSpec(memory_space=pl.ANY)
VM = pl.BlockSpec(memory_space=pltpu.VMEM)
MIB = 2**20


def place():
    d, f = lax.axis_index("dp"), lax.axis_index("fsdp")
    return d // 2, d % 2, f // 2, f % 2


def at(x, c, z, y):
    return (x * 2 + c, z * 2 + y)


def remote(src, dst, send, recv, target):
    return pltpu.make_async_remote_copy(
        src_ref=src, dst_ref=dst, send_sem=send, recv_sem=recv, device_id=target, device_id_type=MESH
    )


def greet(partners):
    barrier = pltpu.get_barrier_semaphore()
    count = 0
    for condition, device in partners:

        @pl.when(condition)
        def _():
            pl.semaphore_signal(barrier, inc=1, device_id=device, device_id_type=MESH)

        count = count + jnp.asarray(condition).astype(jnp.int32)
    pl.semaphore_wait(barrier, count)


def greet_all(devices, fsdp, me):
    barrier = pltpu.get_barrier_semaphore()

    def one(k, _):
        other = (me + k) % devices
        pl.semaphore_signal(barrier, inc=1, device_id=(other // fsdp, other % fsdp), device_id_type=MESH)
        return 0

    lax.fori_loop(1, devices, one, 0)
    pl.semaphore_wait(barrier, devices - 1)


def line_partners(nz, pos):
    x, c, z, y = pos
    return [(z >= 0, at(x, 1 - c, z, y)), (z > 0, at(x, c, z - 1, y)), (z < nz - 1, at(x, c, z + 1, y))]


def rank_partners(nz, pos):
    x, c, z, y = pos
    n = 2 * nz
    others = [(z * 2 + c + k) % n for k in range(1, n)]
    return [(z >= 0, at(x, p % 2, p // 2, y)) for p in others]


def group_partners(pos):
    x, c, z, y = pos
    return [(z >= 0, at(x ^ (m // 2), c, z, y ^ (m % 2))) for m in (1, 2, 3)]


def line_gather(src, dst, send, recv, nz, swap, pos):
    x, c, z, y = pos
    own = z * 2 + c
    sib = at(x, 1 - c, z, y)
    up_dev, dn_dev = at(x, c, z + 1, y), at(x, c, z - 1, y)
    UP, DN, SU, SD = 0, nz, 2 * nz, 3 * nz
    OWN = 4 * nz

    def block(b, moved):
        return dst.at[b] if moved else src

    def up(k):
        b = (z - k) * 2 + c
        return remote(block(b, k or swap), dst.at[b], send.at[UP + k], recv.at[UP + k], up_dev)

    def dn(k):
        b = (z + k) * 2 + c
        return remote(block(b, k or swap), dst.at[b], send.at[DN + k], recv.at[DN + k], dn_dev)

    def side(k, base, sign):
        b = (z + sign * k) * 2 + c
        return remote(block(b, k or swap), dst.at[b], send.at[base + k], recv.at[base + k], sib)

    def got(b, sem):
        return remote(dst.at[b], dst.at[b], send.at[OWN], recv.at[sem], sib)

    local = pltpu.make_async_copy(src, dst.at[own], recv.at[OWN])
    trade = remote(src, dst.at[z * 2 + y], send.at[OWN], recv.at[OWN], at(x, y, z, c))

    def first():
        if swap:
            pl.when(c == y)(local.start)
            pl.when(c != y)(trade.start)
        else:
            local.start()

    def spread():
        if swap:
            local.wait()
        pl.when(z < nz - 1)(up(0).start)
        pl.when(z > 0)(dn(0).start)
        side(0, SU, 1).start()

    def step(k):
        @pl.when(z >= k)
        def _():
            got((z - k) * 2 + c, UP + k - 1).wait_recv()
            pl.when(z < nz - 1)(up(k).start)
            side(k, SU, -1).start()

        @pl.when(z + k < nz)
        def _():
            got((z + k) * 2 + c, DN + k - 1).wait_recv()
            pl.when(z > 0)(dn(k).start)
            side(k, SD, 1).start()

    def last():
        if swap:
            pl.when(c != y)(trade.wait_send)
        else:
            local.wait()
        got(z * 2 + 1 - c, SU).wait_recv()
        pl.when(z < nz - 1)(up(0).wait_send)
        pl.when(z > 0)(dn(0).wait_send)
        side(0, SU, 1).wait_send()
        for k in range(1, nz):

            @pl.when(z >= k)
            def _():
                got((z - k) * 2 + 1 - c, SU + k).wait_recv()
                pl.when(z < nz - 1)(up(k).wait_send)
                side(k, SU, -1).wait_send()

            @pl.when(z + k < nz)
            def _():
                got((z + k) * 2 + 1 - c, SD + k).wait_recv()
                pl.when(z > 0)(dn(k).wait_send)
                side(k, SD, 1).wait_send()

    return [first, spread] + [functools.partial(step, k) for k in range(1, nz)] + [last]


def gather_sems(nz):
    return [pltpu.SemaphoreType.DMA((4 * nz + 1,))] * 2


def gather_kernel(nz, src, dst, send, recv):
    pos = place()
    greet(line_partners(nz, pos))
    for stage in line_gather(src, dst, send, recv, nz, False, pos):
        stage()


def params(cid, vmem=None):
    return pltpu.CompilerParams(collective_id=cid, has_side_effects=True, vmem_limit_bytes=vmem)


def gather_tokens(a, nz, cid):
    return pl.pallas_call(
        functools.partial(gather_kernel, nz),
        out_shape=jax.ShapeDtypeStruct((2 * nz,) + a.shape, a.dtype),
        in_specs=[HBM],
        out_specs=HBM,
        scratch_shapes=gather_sems(nz),
        compiler_params=params(cid),
        name="gather_tokens",
    )(a)


def scatter_blocks(nz, pos, p, out, acc, ups, dns, send, recv):
    x, c, z, y = pos
    sib = at(x, 1 - c, z, y)
    S, U, D = 0, nz, 2 * nz

    def f(v):
        return v.astype(F32)

    def swap(t):
        return remote(p.at[t * 2 + 1 - c], acc.at[t], send.at[S + t], recv.at[S + t], sib)

    def up(t):
        return remote(acc.at[t], ups.at[t], send.at[U + t], recv.at[U + t], at(x, c, z + 1, y))

    def dn(t):
        return remote(acc.at[t], dns.at[t], send.at[D + t], recv.at[D + t], at(x, c, z - 1, y))

    order = []
    for i in range(nz - 1):
        order += [(True, nz - 1 - i), (False, i)]
    for upward, t in order:
        pl.when(z < t if upward else z > t)(swap(t).start)
    swap(z).start()
    for upward, t in order:

        @pl.when(z < t if upward else z > t)
        def _():
            swap(t).wait_recv()
            acc[t] = (f(acc[t]) + f(p[t * 2 + c])).astype(BF)
            move, came = (up, ups) if upward else (dn, dns)

            @pl.when(z > 0 if upward else z < nz - 1)
            def _():
                move(t).wait_recv()
                acc[t] = (f(acc[t]) + f(came[t])).astype(BF)

            move(t).start()

    swap(z).wait_recv()
    out[...] = f(acc[z]) + f(p[z * 2 + c])

    @pl.when(z > 0)
    def _():
        up(z).wait_recv()
        out[...] += f(ups[z])

    @pl.when(z < nz - 1)
    def _():
        dn(z).wait_recv()
        out[...] += f(dns[z])

    for t in range(nz):
        swap(t).wait_send()
        pl.when(z < t)(up(t).wait_send)
        pl.when(z > t)(dn(t).wait_send)


def scatter_scratch(nz, rows, width):
    return [pltpu.VMEM((nz, rows, width), BF)] * 3 + [pltpu.SemaphoreType.DMA((3 * nz,))] * 2


def scatter_kernel(nz, p, out, *scratch):
    pos = place()
    greet(line_partners(nz, pos))
    scatter_blocks(nz, pos, p, out, *scratch)


def scatter_tokens(p, nz, cid):
    blocks, rows, width = p.shape
    return pl.pallas_call(
        functools.partial(scatter_kernel, nz),
        out_shape=jax.ShapeDtypeStruct((rows, width), F32),
        in_specs=[VM],
        out_specs=VM,
        scratch_shapes=scatter_scratch(nz, rows, width),
        compiler_params=params(cid, 60 * MIB),
        name="scatter_tokens",
    )(p)


def scatter_and_hand_kernel(nz, kinds, runs, p, up_s, res, *refs):
    count = len(kinds)
    srcs, refs = refs[:count], refs[count:]
    out, up_o, res_o, refs = *refs[:3], refs[3:]
    dsts, refs = refs[:count], refs[count:]
    scratch, hsems, esems, tsems = refs[:5], refs[5:7], refs[7:9], refs[9:11]
    pos = place()
    x, c, z, y = pos
    greet(rank_partners(nz, pos) + group_partners(pos) + [(c != y, at(x, y, z, c))])
    hs = hand_stages(srcs, dsts, kinds, *hsems, nz, pos)
    es = exchange_stages(up_s, up_o, runs, *esems, nz, pos)
    ts = trade_stages(res, res_o, *tsems, pos)
    hs[0]()
    es[0]()
    ts[0]()
    scatter_blocks(nz, pos, p, out, *scratch)
    hs[1]()
    es[1]()
    ts[1]()


def scatter_and_hand(p, up_s, runs, res, arrays, kinds, nz, cid):
    blocks, rows, width = p.shape
    n, part, share = up_s.shape
    return pl.pallas_call(
        functools.partial(scatter_and_hand_kernel, nz, kinds, runs),
        out_shape=[
            jax.ShapeDtypeStruct((rows, width), F32),
            jax.ShapeDtypeStruct((part, n * share), BF),
            jax.ShapeDtypeStruct(res.shape, BF),
        ]
        + hand_shapes(arrays, kinds, nz),
        in_specs=[VM] + [HBM] * (2 + len(arrays)),
        out_specs=[VM] + [HBM] * (2 + len(arrays)),
        scratch_shapes=scatter_scratch(nz, rows, width) + hand_sems(kinds) + exchange_sems(runs, nz) + trade_sems(),
        compiler_params=params(cid, 60 * MIB),
        name="scatter_and_hand",
    )(p, up_s, res, *arrays)


def block_of(x, c, z, y, nz):
    return (x * 2 + c) * 2 * nz + z * 2 + y


def halves(ref, rows):
    half = rows // 2
    if half % 16:
        return {1: None, 2: ref}
    return {1: ref.at[pl.ds(half, half)], 2: ref.at[pl.ds(0, half)]}


def sliced_gather(src, dst, runs, sems, nz, pos):
    x, c, z, y = pos
    n = 2 * nz
    me = z * 2 + c
    part = dst.shape[1]
    send1, recv1, send2, recv2 = sems

    def pieces(p):
        if runs is None:
            return [(src.at[p], slice(None))]
        return [(src.at[:, pl.ds(there, size)], pl.ds(here, size)) for there, here, size in runs(p)]

    def row(p, gx, gy):
        return dst.at[block_of(gx, p % 2, p // 2, gy, nz)]

    mine = block_of(x, c, z, y, nz)

    def out(k):
        p = (me + k) % n
        return [
            remote(a, dst.at[mine, :, b], send1.at[p], recv1.at[me], at(x, p % 2, p // 2, y))
            for a, b in pieces(p)
        ]

    local = [pltpu.make_async_copy(a, dst.at[mine, :, b], recv1.at[me]) for a, b in pieces(me)]

    def came(k):
        return (me - k + n) % n

    def arrival(b, sem):
        return remote(b, b, send1.at[me], sem, at(x, 1 - c, z, y))

    def neighbour(m):
        return at(x ^ (m // 2), c, z, y ^ (m % 2))

    def forward(k, m):
        p = came(k)
        b = row(p, x, y)
        slot = (m - 1) * n + p
        return remote(b, b, send2.at[slot], recv2.at[slot], neighbour(m))

    def relay(k, m):
        p = came(k)
        b = halves(row(p, x ^ (m // 2), y ^ (m % 2)), part)[m]
        slot = (1 + m) * n + p
        return b is not None and remote(b, b, send2.at[slot], recv2.at[slot], neighbour(3 - m))

    def first():
        for copy in local:
            copy.start()
        for k in range(1, n):
            for copy in out(k):
                copy.start()

    def step(k):
        p = came(k)
        arrival(row(p, x, y), recv1.at[p]).wait_recv()
        for m in (1, 2):
            forward(k, m).start()

    def pass_on(k):
        p = came(k)
        for m in (1, 2):
            arrival(row(p, x ^ (m // 2), y ^ (m % 2)), recv2.at[(m - 1) * n + p]).wait_recv()
            if relay(k, m):
                relay(k, m).start()

    def last():
        for k in range(n):
            p = came(k)
            parts = halves(row(p, 1 - x, 1 - y), part)
            for m in (1, 2):
                if parts[m] is not None:
                    arrival(parts[m], recv2.at[(1 + m) * n + p]).wait_recv()
        for k in range(n):
            if k:
                p = (me + k) % n
                b = dst.at[mine]
                remote(b, b, send1.at[p], recv1.at[me], at(x, p % 2, p // 2, y)).wait_send()
            for m in (1, 2):
                forward(k, m).wait_send()
                if relay(k, m):
                    relay(k, m).wait_send()

    stages = [functools.partial(step, k) for k in range(n)] + [functools.partial(pass_on, k) for k in range(n)]
    return [first] + stages + [last]


def sliced_sems(nz):
    n = 2 * nz
    return [pltpu.SemaphoreType.DMA((n,))] * 2 + [pltpu.SemaphoreType.DMA((4 * n,))] * 2


def group_gather(src, dst, send, recv, pos):
    x, c, z, y = pos
    rows = src.shape[0]
    local = pltpu.make_async_copy(src, dst.at[x * 2 + y], recv.at[0])

    def there(m):
        return dst.at[(x ^ (m // 2)) * 2 + (y ^ (m % 2))]

    def neighbour(m):
        return at(x ^ (m // 2), c, z, y ^ (m % 2))

    def out(m):
        return remote(src, dst.at[x * 2 + y], send.at[m], recv.at[m], neighbour(m))

    def relay(m):
        b = halves(there(m), rows)[m]
        return b is not None and remote(b, b, send.at[2 + m], recv.at[2 + m], neighbour(3 - m))

    def arrival(b, sem):
        return remote(b, b, send.at[0], sem, at(x, 1 - c, z, y))

    def first():
        local.start()
        for m in (1, 2):
            out(m).start()

    def pass_on():
        for m in (1, 2):
            arrival(there(m), recv.at[m]).wait_recv()
            if relay(m):
                relay(m).start()

    def last():
        local.wait()
        parts = halves(there(3), rows)
        for m in (1, 2):
            if parts[m] is not None:
                arrival(parts[m], recv.at[2 + m]).wait_recv()
            out(m).wait_send()
            if relay(m):
                relay(m).wait_send()

    return [first, pass_on, last]


def full_gather(src, dst, send, recv, nz, pos):
    x, c, z, y = pos
    rows = src.shape[0]
    sib = at(x, 1 - c, z, y)
    mine = dst.at[block_of(x, c, z, y, nz)]

    def row(core, k, m):
        return dst.at[block_of(x ^ (m // 2), core, z + k, y ^ (m % 2), nz)]

    def neighbour(m):
        return at(x ^ (m // 2), c, z, y ^ (m % 2))

    def arrival(b, sem):
        return remote(b, b, send.at[0], recv.at[sem], sib)

    def along(k, sign):
        b = row(c, k, 0)
        return remote(
            b if k else src, b, send.at[(0 if sign > 0 else nz) + z + k], recv.at[z + k], at(x, c, z + sign, y)
        )

    def forward(k, m):
        b = row(c, k, 0)
        return remote(b if k else src, b, send.at[(1 + m) * nz + z + k], recv.at[m * nz + z + k], neighbour(m))

    def relay(k, m):
        b = halves(row(c, k, m), rows)[m]
        if b is None:
            return None
        return remote(b, b, send.at[(3 + m) * nz + z + k], recv.at[(2 + m) * nz + z + k], neighbour(3 - m))

    def side(k, m):
        b = row(c, k, m)
        return remote(b if k or m else src, b, send.at[(6 + m) * nz + z + k], recv.at[(5 + m) * nz + z + k], sib)

    local = pltpu.make_async_copy(src, mine, recv.at[z])

    def first():
        local.start()
        pl.when(z < nz - 1)(along(0, 1).start)
        pl.when(z > 0)(along(0, -1).start)
        for m in (1, 2):
            forward(0, m).start()
        side(0, 0).start()

    def both(k, fn):
        @pl.when(z >= k)
        def _():
            fn(-k)

        if k:

            @pl.when(z + k < nz)
            def _():
                fn(k)

    def step(k):
        def one(k):
            arrival(row(c, k, 0), z + k).wait_recv()
            if k > 0:
                pl.when(z > 0)(along(k, -1).start)
            else:
                pl.when(z < nz - 1)(along(k, 1).start)
            for m in (1, 2):
                forward(k, m).start()
            side(k, 0).start()

        both(k, one)

    def pass_on(k):
        def one(k):
            for m in (1, 2):
                arrival(row(c, k, m), m * nz + z + k).wait_recv()
                if relay(k, m) is not None:
                    relay(k, m).start()
                side(k, m).start()

        both(k, one)

    def diagonal(k):
        def one(k):
            parts = halves(row(c, k, 3), rows)
            for m in (1, 2):
                if parts[m] is not None:
                    arrival(parts[m], (2 + m) * nz + z + k).wait_recv()
            side(k, 3).start()

        both(k, one)

    def last():
        local.wait()

        def one(k):
            for m in range(4):
                arrival(row(1 - c, k, m), (5 + m) * nz + z + k).wait_recv()
                side(k, m).wait_send()
            if k >= 0:
                pl.when(z > 0)(along(k, -1).wait_send)
            if k <= 0:
                pl.when(z < nz - 1)(along(k, 1).wait_send)
            for m in (1, 2):
                forward(k, m).wait_send()
                if relay(k, m) is not None:
                    relay(k, m).wait_send()

        for k in range(nz):
            both(k, one)

    return (
        [first]
        + [functools.partial(step, k) for k in range(1, nz)]
        + [functools.partial(pass_on, k) for k in range(nz)]
        + [functools.partial(diagonal, k) for k in range(nz)]
        + [last]
    )


def full_sems(nz):
    return [pltpu.SemaphoreType.DMA((10 * nz,)), pltpu.SemaphoreType.DMA((9 * nz,))]


def head_runs(nz, cols):
    return lambda p: [
        (block_of(x, p % 2, p // 2, 0, nz) * HD, x * cols // 2, cols // 2) for x in range(2)
    ]


def up_runs(nz, unit):
    return lambda p: [(block_of(x, p % 2, p // 2, 0, nz) * unit, x * 2 * unit, 2 * unit) for x in range(2)]


def qkv_runs(nz, width, cols):
    runs = head_runs(nz, cols)
    return lambda p: [(j * width + there, j * cols + here, size) for j in range(3) for there, here, size in runs(p)]


def fetch_kernel(
    nz, width, cols, x_in, w_qkv, w_down, vec, tab, x_all, qkv_w, down_w, vecs, tab_out, *sems
):
    pos = place()
    x, c, z, y = pos
    fsdp = 2 * nz
    devices = 4 * fsdp
    me = (x * 2 + c) * fsdp + z * 2 + y
    x_sems, qkv_sems, vec_sems, tab_sems, down_sems = sems[:2], sems[2:6], sems[6:8], sems[8:10], sems[10:]
    greet_all(devices, fsdp, me)

    def vec_copy(other):
        return remote(vec, vecs.at[me], vec_sems[0].at[other], vec_sems[1].at[me], (other // fsdp, other % fsdp))

    def each(fn):
        def body(k, _):
            fn((me + k) % devices)
            return 0

        lax.fori_loop(1, devices, body, 0)

    vec_local = pltpu.make_async_copy(vec, vecs.at[me], vec_sems[1].at[me])
    tab_local = pltpu.make_async_copy(tab, tab_out, tab_sems[1].at[0])
    tab_trade = remote(tab, tab_out, tab_sems[0].at[0], tab_sems[1].at[0], at(x, y, z, c))

    gx = line_gather(x_in, x_all, *x_sems, nz, True, pos)
    runs = qkv_runs(nz, width, cols) if len(w_qkv.shape) == 2 else None
    gq = sliced_gather(w_qkv, qkv_w, runs, qkv_sems, nz, pos)
    gx[0]()
    gq[0]()
    gx[1]()
    vec_local.start()
    each(lambda other: vec_copy(other).start())
    pl.when(c == y)(tab_local.start)
    pl.when(c != y)(tab_trade.start)
    gd = group_gather(w_down, down_w, *down_sems, pos)
    for stage in gq[1 : fsdp + 1]:
        stage()
    gx[2]()
    gd[0]()
    for stage in gx[3:-1]:
        stage()
    for stage in gq[fsdp + 1 :]:
        stage()
    gx[-1]()
    for stage in gd[1:]:
        stage()

    def vec_done(other):
        remote(vec, vecs.at[other], vec_sems[0].at[other], vec_sems[1].at[other], at(x, 1 - c, z, y)).wait_recv()
        vec_copy(other).wait_send()

    vec_local.wait()
    each(vec_done)
    tab_local.wait()
    pl.when(c != y)(tab_trade.wait_send)


def fetch(nz, x_in, w_qkv, w_down, part, vec, tab, cid):
    rows, width = x_in.shape
    n = 2 * nz
    devices = 4 * n
    cols = width // n
    shapes = [
        ((n, rows, width), BF),
        ((devices, part, 3 * cols), BF),
        ((4,) + w_down.shape, BF),
        ((devices,) + vec.shape, F32),
        (tab.shape, jnp.int32),
    ]
    return pl.pallas_call(
        functools.partial(fetch_kernel, nz, width, cols),
        out_shape=[jax.ShapeDtypeStruct(s, t) for s, t in shapes],
        in_specs=[HBM] * 5,
        out_specs=[HBM] * 5,
        scratch_shapes=gather_sems(nz)
        + sliced_sems(nz)
        + [pltpu.SemaphoreType.DMA((devices,))] * 2
        + [pltpu.SemaphoreType.DMA((1,))] * 2
        + [pltpu.SemaphoreType.DMA((5,))] * 2,
        compiler_params=params(cid),
        name="fetch",
    )(x_in, w_qkv, w_down, vec, tab)


def hand_stages(srcs, dsts, kinds, send, recv, nz, pos):
    x, c, z, y = pos
    n = 2 * nz
    count = len(kinds)

    def copies(i, m):
        gx, gy = x ^ (m // 2), y ^ (m % 2)
        sem = i * 3 + m - 1
        target = at(gx, c, z, gy)
        if not kinds[i]:
            return [remote(srcs[i].at[gx * 2 + gy], dsts[i].at[m - 1], send.at[sem], recv.at[sem], target)]
        return [
            remote(
                srcs[i].at[block_of(gx, p % 2, p // 2, gy, nz)],
                dsts[i].at[m - 1, p],
                send.at[sem],
                recv.at[sem],
                target,
            )
            for p in range(n)
        ]

    def first():
        for i in range(count):
            for m in (3, 1, 2):
                for copy in copies(i, m):
                    copy.start()

    def last():
        for i in range(count):
            for m in (1, 2, 3):
                sem = i * 3 + m - 1
                there = dsts[i].at[m - 1]
                whole = remote(there, there, send.at[sem], recv.at[sem], at(x, 1 - c, z, y))
                whole.wait_recv()
                whole.wait_send()

    return [first, last]


def hand_shapes(arrays, kinds, nz):
    return [
        jax.ShapeDtypeStruct((3, 2 * nz) + a.shape[1:] if k else (3,) + a.shape[1:], a.dtype)
        for a, k in zip(arrays, kinds)
    ]


def hand_sems(kinds):
    return [pltpu.SemaphoreType.DMA((3 * len(kinds),))] * 2


def exchange_stages(src, dst, runs, send, recv, nz, pos):
    x, c, z, y = pos
    n = 2 * nz
    me = z * 2 + c

    def give(to, p):
        if runs is None:
            return [(src.at[to], dst.at[p])]
        return [(src.at[to, :, pl.ds(here, size)], dst.at[:, pl.ds(there, size)]) for there, here, size in runs(p)]

    width = len(give(0, 0))

    def move(p):
        return [
            remote(a, b, send.at[p * width + i], recv.at[me * width + i], at(x, p % 2, p // 2, y))
            for i, (a, b) in enumerate(give(p, me))
        ]

    def come(p):
        return [
            remote(b, b, send.at[me * width + i], recv.at[p * width + i], at(x, 1 - c, z, y))
            for i, (_, b) in enumerate(give(me, p))
        ]

    local = [pltpu.make_async_copy(a, b, recv.at[me * width + i]) for i, (a, b) in enumerate(give(me, me))]

    def first():
        for copy in local:
            copy.start()
        for k in range(1, n):
            for copy in move((me + k) % n):
                copy.start()

    def last():
        for copy in local:
            copy.wait()
        for k in range(1, n):
            for copy in come((me - k + n) % n):
                copy.wait_recv()
            for copy in move((me + k) % n):
                copy.wait_send()

    return [first, last]


def exchange_sems(runs, nz):
    width = 1 if runs is None else len(runs(0))
    return [pltpu.SemaphoreType.DMA((width * 2 * nz,))] * 2


def exchange_kernel(nz, src, dst, send, recv):
    pos = place()
    greet(rank_partners(nz, pos))
    for stage in exchange_stages(src, dst, None, send, recv, nz, pos):
        stage()


def exchange(a, nz, cid, name):
    return pl.pallas_call(
        functools.partial(exchange_kernel, nz),
        out_shape=jax.ShapeDtypeStruct(a.shape, a.dtype),
        in_specs=[HBM],
        out_specs=HBM,
        scratch_shapes=exchange_sems(None, nz),
        compiler_params=params(cid),
        name=name,
    )(a)


def trade_stages(src, dst, send, recv, pos):
    x, c, z, y = pos
    local = pltpu.make_async_copy(src, dst, recv.at[0])
    trade = remote(src, dst, send.at[0], recv.at[0], at(x, y, z, c))

    def first():
        pl.when(c == y)(local.start)
        pl.when(c != y)(trade.start)

    def last():
        local.wait()
        pl.when(c != y)(trade.wait_send)

    return [first, last]


def trade_sems():
    return [pltpu.SemaphoreType.DMA((1,))] * 2


def finish_kernel(nz, runs, grad, small, qkv_s, grad_out, small_out, qkv_o, came, send, recv, *sems):
    pos = place()
    x, c, z, y = pos
    fsdp = 2 * nz
    devices = 4 * fsdp
    me = (x * 2 + c) * fsdp + z * 2 + y
    es = exchange_stages(qkv_s, qkv_o, runs, *sems[:2], nz, pos)
    ts = trade_stages(grad, grad_out, *sems[2:], pos)
    greet_all(devices, fsdp, me)

    def each(fn):
        def body(k, _):
            fn((me + k) % devices)
            return 0

        lax.fori_loop(1, devices, body, 0)

    def share(other):
        return remote(small.at[other], came.at[me], send.at[other], recv.at[me], (other // fsdp, other % fsdp))

    es[0]()
    ts[0]()
    each(lambda other: share(other).start())

    def done(other):
        remote(small.at[me], came.at[other], send.at[other], recv.at[other], at(x, 1 - c, z, y)).wait_recv()
        share(other).wait_send()

    each(done)
    came[me] = small[me]
    small_out[...] = jnp.sum(came[...], axis=0)
    ts[1]()
    es[1]()


def finish(grad, small, qkv_s, runs, nz, cid):
    devices = small.shape[0]
    out_shape = qkv_s.shape if runs is None else (qkv_s.shape[1], qkv_s.shape[0] * qkv_s.shape[2])
    return pl.pallas_call(
        functools.partial(finish_kernel, nz, runs),
        out_shape=[
            jax.ShapeDtypeStruct(grad.shape, grad.dtype),
            jax.ShapeDtypeStruct(small.shape[1:], F32),
            jax.ShapeDtypeStruct(out_shape, BF),
        ],
        in_specs=[HBM, VM, HBM],
        out_specs=[HBM, VM, HBM],
        scratch_shapes=[pltpu.VMEM(small.shape, F32)]
        + [pltpu.SemaphoreType.DMA((devices,))] * 2
        + exchange_sems(runs, nz)
        + trade_sems(),
        compiler_params=params(cid, 32 * MIB),
        name="finish",
    )(grad, small, qkv_s)


def dot(a, b, dims):
    return lax.dot_general(a, b, (dims, ((), ())), preferred_element_type=F32)


NN = ((1,), (0,))
NT = ((1,), (1,))
TN = ((0,), (0,))


def attend_kernel(
    heads, nz, unit, slopes, far, joined_q, joined, cot, w_up, w_out, out, cot_all, up_w, out_w, *sems
):
    cols = heads * HD
    step, steps = pl.program_id(0), pl.num_programs(0)
    pos = place()
    n = 2 * nz
    gc = line_gather(cot, cot_all, *sems[:2], nz, True, pos)
    gu = sliced_gather(w_up, up_w, up_runs(nz, unit), sems[2:6], nz, pos)
    go = full_gather(w_out, out_w, *sems[6:8], nz, pos)

    @pl.when(step == 0)
    def _():
        x, c, z, y = pos
        greet(rank_partners(nz, pos) + group_partners(pos) + [(c != y, at(x, y, z, c))])
        gc[0]()
        gu[0]()
        go[0]()

    @pl.when(step == 1)
    def _():
        for stage in go[1:nz]:
            stage()

    @pl.when(step == 2)
    def _():
        for stage in gu[1 : n + 1]:
            stage()
        gc[1]()

    gap = far[...]
    for h in range(heads):
        q = joined_q[:, h * HD : (h + 1) * HD]
        k = joined[:, cols + h * HD : cols + (h + 1) * HD]
        v = joined[:, 2 * cols + h * HD : 2 * cols + (h + 1) * HD]
        logits = dot(q, k, NT) * HD ** (-0.5) + slopes[h] * gap
        weights = jnp.exp(logits - jnp.max(logits, axis=1, keepdims=True))
        probs = weights * (1.0 / jnp.sum(weights, axis=1, keepdims=True))
        out[:, h * HD : (h + 1) * HD] = dot(probs.astype(BF), v, NN).astype(BF)

    @pl.when(step == steps - 1)
    def _():
        for stage in go[nz : 2 * nz]:
            stage()
        ahead, later = gc[2:-1], gu[n + 1 : -1]
        for i, stage in enumerate(ahead):
            stage()
            for other in later[i * n // len(ahead) : (i + 1) * n // len(ahead)]:
                other()
        for stage in go[2 * nz :]:
            stage()
        gc[-1]()
        gu[-1]()


def attend(slopes, far, joined, cot, w_up, w_out, unit, heads, nz, cid):
    tree = far.shape[0]
    cols = heads * HD
    rows = min(256, max(128, 2**18 // tree))
    block, width = cot.shape
    part = w_up.shape[0]
    n = 2 * nz
    shapes = [(tree, cols), (n, block, width), (4 * n, part, 4 * unit), (4 * n, part, width)]
    return pl.pallas_call(
        functools.partial(attend_kernel, heads, nz, unit),
        out_shape=[jax.ShapeDtypeStruct(s, BF) for s in shapes],
        grid=(tree // rows,),
        in_specs=[
            pl.BlockSpec(memory_space=pltpu.SMEM),
            pl.BlockSpec((rows, tree), lambda i: (i, 0)),
            pl.BlockSpec((rows, 3 * cols), lambda i: (i, 0)),
            pl.BlockSpec((tree, 3 * cols), lambda i: (0, 0)),
            HBM,
            HBM,
            HBM,
        ],
        out_specs=[pl.BlockSpec((rows, cols), lambda i: (i, 0)), HBM, HBM, HBM],
        scratch_shapes=gather_sems(nz) + sliced_sems(nz) + full_sems(nz),
        compiler_params=params(cid, 56 * MIB),
        name="attend",
    )(slopes, far, joined, joined, cot, w_up, w_out)


def attend_back_kernel(heads, nz, kinds, slopes, far, joined_q, joined, grad, branch, part_sums, *refs):
    count = len(kinds)
    srcs, refs = refs[:count], refs[count:]
    out_q, out_k, out_v, branch_all, update, refs = *refs[:5], refs[5:]
    dsts, refs = refs[:count], refs[count:]
    acc_k, acc_v, p, refs = *refs[:3], refs[3:]
    scratch, gsems, hsems, psem = refs[:5], refs[5:7], refs[7:9], refs[9]
    cols = heads * HD
    step = pl.program_id(0)
    pos = place()
    gb = line_gather(branch, branch_all, *gsems, nz, False, pos)
    hs = hand_stages(srcs, dsts, kinds, *hsems, nz, pos)
    load = pltpu.make_async_copy(part_sums, p, psem.at[0])

    @pl.when(step == 0)
    def _():
        acc_k[...] = jnp.zeros_like(acc_k)
        acc_v[...] = jnp.zeros_like(acc_v)
        greet(line_partners(nz, pos) + group_partners(pos))
        hs[0]()
        gb[0]()
        gb[1]()
        load.start()

    @pl.when(step == 3)
    def _():
        gb[2]()

    gap = far[...]
    for h in range(heads):
        here = slice(h * HD, (h + 1) * HD)
        q = joined_q[:, here]
        k = joined[:, cols + h * HD : cols + (h + 1) * HD]
        v = joined[:, 2 * cols + h * HD : 2 * cols + (h + 1) * HD]
        g = grad[:, here]
        logits = dot(k, q, NT) * HD ** (-0.5) + slopes[h] * gap
        weights = jnp.exp(logits - jnp.max(logits, axis=0, keepdims=True))
        probs = weights * (1.0 / jnp.sum(weights, axis=0, keepdims=True))
        grad_probs = dot(v, g, NT)
        delta = jnp.sum(probs * grad_probs, axis=0, keepdims=True)
        grad_raw = (probs * (grad_probs - delta) * HD ** (-0.5)).astype(BF)
        acc_v[:, here] += dot(probs.astype(BF), g, NN)
        acc_k[:, here] += dot(grad_raw, q, NN)
        out_q[:, here] = dot(grad_raw, k, TN).astype(BF)

    @pl.when(step == pl.num_programs(0) - 1)
    def _():
        out_k[...] = acc_k[...].astype(BF)
        out_v[...] = acc_v[...].astype(BF)
        for stage in gb[3:]:
            stage()
        load.wait()
        scatter_blocks(nz, pos, p, update, *scratch)
        hs[1]()


def attend_back(slopes, far_t, joined, grad, branch, part_sums, arrays, kinds, heads, nz, cid):
    tree = far_t.shape[0]
    cols = heads * HD
    rows = min(256, max(128, 2**18 // tree))
    block, width = branch.shape
    full = pl.BlockSpec((tree, cols), lambda i: (0, 0))
    part = pl.BlockSpec((rows, cols), lambda i: (i, 0))
    return pl.pallas_call(
        functools.partial(attend_back_kernel, heads, nz, kinds),
        out_shape=[jax.ShapeDtypeStruct((tree, cols), BF)] * 3
        + [jax.ShapeDtypeStruct((2 * nz, block, width), BF), jax.ShapeDtypeStruct((block, width), F32)]
        + hand_shapes(arrays, kinds, nz),
        grid=(tree // rows,),
        in_specs=[
            pl.BlockSpec(memory_space=pltpu.SMEM),
            pl.BlockSpec((tree, rows), lambda i: (0, i)),
            pl.BlockSpec((rows, 3 * cols), lambda i: (i, 0)),
            pl.BlockSpec((tree, 3 * cols), lambda i: (0, 0)),
            part,
            HBM,
            HBM,
        ]
        + [HBM] * len(arrays),
        out_specs=[part, full, full, HBM, pl.BlockSpec((block, width), lambda i: (0, 0))] + [HBM] * len(arrays),
        scratch_shapes=[pltpu.VMEM((tree, cols), F32)] * 2
        + [pltpu.VMEM((2 * nz, block, width), BF)]
        + scatter_scratch(nz, block, width)
        + gather_sems(nz)
        + hand_sems(kinds)
        + [pltpu.SemaphoreType.DMA((1,))],
        compiler_params=params(cid, 62 * MIB),
        name="attend_back",
    )(slopes, far_t, joined, joined, grad, branch, part_sums, *arrays)


def norm_parts(values):
    center = values - jnp.mean(values, axis=-1, keepdims=True)
    inverse = lax.rsqrt(jnp.mean(center * center, axis=-1, keepdims=True) + EPSILON)
    return (center * inverse, inverse)


def norm_back(grad_normed, normed, inverse):
    mean_grad = jnp.mean(grad_normed, axis=-1, keepdims=True)
    mean_cross = jnp.mean(grad_normed * normed, axis=-1, keepdims=True)
    return inverse * (grad_normed - mean_grad - normed * mean_cross)


def tree_tables(parents, seg_blocks, valid):
    segments = parents.shape[0]
    seg_tokens = jnp.broadcast_to(seg_blocks[:, None], (seg_blocks.shape[0], BLK)).reshape(-1)
    labels = jnp.arange(segments, dtype=jnp.int32)
    member = (seg_tokens[:, None] == labels[None, :]).astype(jnp.int32)
    counted = member * valid[:, None]
    before = jnp.cumsum(counted, axis=0) - counted
    rank = jnp.sum(before * member, axis=1)
    seg_len = jnp.sum(counted, axis=0)
    picked = (parents[:, None] == labels[None, :]).astype(jnp.int32)
    grand = jnp.sum(picked * parents[None, :], axis=1)
    ancestor = ((labels[None, :] == parents[:, None]) | (labels[None, :] == grand[:, None])) & (
        labels[None, :] != labels[:, None]
    )
    offset = jnp.sum(ancestor.astype(jnp.int32) * seg_len[None, :], axis=1)
    position = jnp.sum(member * offset[None, :], axis=1) + rank
    return (seg_tokens, position, ancestor.astype(jnp.float32))


def allowed_mask(seg, index, valid, ancestor):
    labels = jnp.arange(ancestor.shape[0], dtype=jnp.int32)
    member = (seg[:, None] == labels[None, :]).astype(jnp.float32)
    reach = jnp.dot(jnp.dot(member, ancestor), member.T) > 0.5
    causal = (seg[:, None] == seg[None, :]) & (index[None, :] <= index[:, None])
    visible = (valid[None, :] == 1) | (index[None, :] == index[:, None])
    return (reach | causal) & visible


def gelu_exact(value):
    return jax.nn.gelu(value, approximate=False)


def mm(spec, a, b):
    return jnp.einsum(spec, a, b, preferred_element_type=F32)


def padded(flat, lanes):
    return jnp.pad(flat, [(0, 0)] * (flat.ndim - 1) + [(0, -flat.shape[-1] % lanes)])


def per_device(
    layer_in,
    cotangent,
    w_qkv,
    w_out,
    w_up,
    w_down,
    gain_attn,
    shift_attn,
    bias_query,
    bias_value,
    bias_out,
    gain_mlp,
    shift_mlp,
    bias_up,
    bias_down,
    parents,
    seg_blocks,
    token_valid,
):
    rows, width = layer_in.shape
    fsdp = lax.axis_size("fsdp")
    nz = fsdp // 2
    devices = 4 * fsdp
    x, c, z, y = place()
    rank = z * 2 + c
    heads = H // fsdp
    cols = heads * HD
    tree = token_valid.shape[1]
    part = w_up.shape[0]
    unit = w_down.shape[0]

    vec = jnp.concatenate(
        [gain_attn, shift_attn, bias_query, bias_value, bias_out, gain_mlp, shift_mlp, bias_down, bias_up]
    ).astype(F32)
    vec = padded(vec, 1024).reshape(-1, 128)
    tab = jnp.concatenate([token_valid[0], seg_blocks[0], parents[0]])
    tab = padded(tab, 1024).reshape(-1, 128)
    aligned = part == HD and cols % 256 == 0
    if not aligned:
        w_qkv = w_qkv.reshape(part, 3, fsdp, cols).transpose(2, 0, 1, 3).reshape(fsdp, part, 3 * cols)
    x_all, qkv_w, down_w, vecs, tab = fetch(nz, layer_in, w_qkv, w_down, part, vec, tab, 1)
    down_w = down_w.reshape(4 * unit, width)
    x_all = x_all.reshape(tree, width)
    qkv_w = qkv_w.reshape(width, 3 * cols)
    vecs = vecs.reshape(devices, -1)
    (gain_one, shift_one, query_bias, value_bias, out_bias, gain_two, shift_two, down_bias) = [
        vecs[:, i * part : (i + 1) * part].reshape(-1) for i in range(8)
    ]
    up_bias = vecs[:, 8 * part : 8 * part + unit].reshape(2, 2, nz, 2, unit)
    up_bias = lax.dynamic_slice(up_bias, (0, c, z, 0, 0), (2, 1, 1, 2, unit)).reshape(-1)

    def own_rows(v):
        return lax.dynamic_slice_in_dim(v, rank * rows, rows, 0)

    normed_all, _ = norm_parts(x_all.astype(F32))
    attn_in = (normed_all * gain_one + shift_one).astype(BF)
    inputs = own_rows(x_all).astype(F32)
    normed_one, inverse_one = norm_parts(inputs)

    if aligned:

        def own_cols(v):
            v = v.reshape(2, 2, nz, 2, HD)
            return lax.dynamic_slice(v, (0, c, z, 0, 0), (2, 1, 1, 2, HD)).reshape(-1)

        def spread(v):
            v = v.reshape(2, 1, 1, 2, HD)
            return lax.dynamic_update_slice(jnp.zeros((2, 2, nz, 2, HD), F32), v, (0, c, z, 0, 0))

        numbers = block_of(jnp.arange(2)[:, None], c, z, jnp.arange(2)[None, :], nz).reshape(-1)
    else:

        def own_cols(v):
            return lax.dynamic_slice_in_dim(v, rank * cols, cols, 0)

        def spread(v):
            return lax.dynamic_update_slice_in_dim(jnp.zeros((width,), F32), v, rank * cols, 0)

        numbers = rank * heads + jnp.arange(heads)

    joined_bias = jnp.concatenate([own_cols(query_bias), jnp.zeros((cols,), F32), own_cols(value_bias)])
    joined = (jnp.dot(attn_in, qkv_w, preferred_element_type=F32) + joined_bias).astype(BF)

    tab = tab.reshape(-1)
    blocks = seg_blocks.shape[1]
    valid = tab[:tree]
    seg, position, ancestor = tree_tables(
        tab[tree + blocks : tree + blocks + parents.shape[1]], tab[tree : tree + blocks], valid
    )
    index = jnp.arange(tree, dtype=jnp.int32)
    mask = allowed_mask(seg, index, valid, ancestor)
    far = jnp.where(mask, (position[None, :] - position[:, None]).astype(F32), MASKED)
    slopes = jnp.exp2(-8.0 * (numbers.astype(F32) + 1.0) / H)
    mixed, cot, up_w, out_w = attend(slopes, far, joined, cotangent, w_up, w_out, unit, heads, nz, 9)
    out_w = out_w.reshape(width, width)
    cot = cot.reshape(tree, width)
    up_w = up_w.reshape(width, 4 * unit)

    mixed_own = exchange(mixed.reshape(fsdp, rows, cols), nz, 2, "mixed_to_tokens")
    if aligned:
        mixed_own = mixed_own.reshape(nz, 2, rows, 2, 2 * HD).transpose(2, 3, 1, 0, 4).reshape(rows, width)
    else:
        mixed_own = mixed_own.transpose(1, 0, 2).reshape(rows, width)
    branch = jnp.dot(mixed_own, out_w, preferred_element_type=F32) + out_bias
    middle = inputs + branch
    normed_two, inverse_two = norm_parts(middle)
    mlp_in = gather_tokens((normed_two * gain_two + shift_two).astype(BF), nz, 3).reshape(tree, width)
    hidden = jnp.dot(mlp_in, up_w, preferred_element_type=F32) + up_bias
    active_float, gelu_pull = jax.vjp(gelu_exact, hidden)
    active = active_float.astype(BF)
    grad_active = mm("td,fd->tf", cot, down_w)
    grad_hidden = gelu_pull(grad_active)[0].astype(BF)

    def scatter(v):
        return scatter_tokens(v.astype(BF).reshape(fsdp, rows, width), nz, 4)

    grad_mlp_in = scatter(mm("tf,df->td", grad_hidden, up_w))
    update = jnp.dot(active, down_w, preferred_element_type=F32).astype(BF).reshape(fsdp, rows, width)
    down_g = mm("tf,td->fd", active, cot).astype(BF).reshape(4, unit, width)
    up_g = mm("td,tf->df", mlp_in, grad_hidden).astype(BF).reshape(devices, part, 4 * unit)

    cot_own = own_rows(cot).astype(F32)
    grad_middle = cot_own + norm_back(grad_mlp_in * gain_two, normed_two, inverse_two)
    grad_branch = grad_middle.astype(BF)
    grad_mixed = mm("te,de->td", grad_branch, out_w).astype(BF)
    if not aligned:
        grad_out_w = lax.psum_scatter(
            mm("td,te->de", mixed_own, grad_branch).astype(BF), BOTH, scatter_dimension=0, tiled=True
        ).astype(F32)
    if aligned:
        grad_mixed = grad_mixed.reshape(rows, 2, 2, nz, 2 * HD).transpose(3, 2, 0, 1, 4).reshape(fsdp, rows, cols)
    else:
        grad_mixed = grad_mixed.reshape(rows, fsdp, cols).transpose(1, 0, 2)
    grad_heads = exchange(grad_mixed, nz, 5, "grad_to_heads")
    grad_heads = grad_heads.reshape(tree, cols)
    grad_q, grad_k, grad_v, branch_all, update, down_c, up_c = attend_back(
        slopes, far.T, joined, grad_heads, grad_branch, update, [down_g, up_g], (False, True), heads, nz, 6
    )
    result = middle + update + down_bias
    grad_joined = jnp.concatenate([grad_q, grad_k, grad_v], axis=1)

    def mine(g, came):
        g = g.reshape((2, 2, nz, 2) + g.shape[1:])
        g = lax.dynamic_slice(g, (x, 0, 0, y, 0, 0), (1, 2, nz, 1) + g.shape[4:])
        g = g.reshape((2, nz) + g.shape[4:]).swapaxes(0, 1)
        return (g.reshape(came.shape[1:]).astype(F32) + jnp.sum(came.astype(F32), axis=0)).astype(BF)

    def mine_flat(g, came):
        return lax.dynamic_index_in_dim(g, x * 2 + y, 0, keepdims=False).astype(F32) + jnp.sum(came.astype(F32), axis=0)

    grad_down_w = mine_flat(down_g, down_c)
    qkv_g = mm("td,te->de", attn_in, grad_joined).astype(BF).reshape(devices, part, 3 * cols)
    flat = []
    if aligned:
        flat = [mm("td,te->de", mixed, branch_all.reshape(tree, width)).astype(BF).reshape(4, part, width)]
    kinds = (True,) + (False,) * len(flat)
    grad_attn_in = mm("te,de->td", grad_joined, qkv_w).astype(BF).reshape(fsdp, rows, width)
    grad_attn_in, grad_up_w, layer_out, qkv_c, *out_c = scatter_and_hand(
        grad_attn_in, mine(up_g, up_c), up_runs(nz, unit), result.astype(BF), [qkv_g] + flat, kinds, nz, 10
    )
    grad_up_w = grad_up_w.astype(F32)
    if aligned:
        grad_out_w = mine_flat(flat[0], out_c[0])
    grad_inputs = grad_middle + norm_back(grad_attn_in * gain_one, normed_one, inverse_one)

    col = jnp.sum(grad_joined.astype(F32), axis=0)

    smalls = [
        jnp.sum(grad_attn_in * normed_one, axis=0),
        jnp.sum(grad_attn_in, axis=0),
        spread(col[:cols]),
        spread(col[2 * cols :]),
        jnp.sum(grad_branch.astype(F32), axis=0),
        jnp.sum(grad_mlp_in * normed_two, axis=0),
        jnp.sum(grad_mlp_in, axis=0),
        jnp.sum(cot_own, axis=0),
    ]
    grad_bias_up = jnp.sum(grad_hidden.astype(F32), axis=0).reshape(2, 1, 1, 2, unit)
    grad_bias_up = lax.dynamic_update_slice(jnp.zeros((2, 2, nz, 2, unit), F32), grad_bias_up, (0, c, z, 0, 0))
    squares = jnp.stack([jnp.sum(result * result), jnp.sum(branch * branch)])
    packed = jnp.concatenate(
        [v.reshape(devices, part) for v in smalls]
        + [grad_bias_up.reshape(devices, unit), jnp.broadcast_to(squares, (devices, 2))],
        axis=1,
    )
    packed = padded(packed, 1024).reshape(devices, -1, 128)
    runs = qkv_runs(nz, width, cols) if aligned else None
    grad_x, packed, grad_qkv_w = finish(grad_inputs.astype(BF), packed, mine(qkv_g, qkv_c), runs, nz, 8)
    if not aligned:
        grad_qkv_w = grad_qkv_w.reshape(fsdp, part, 3, cols).transpose(1, 2, 0, 3).reshape(part, -1)
    grad_qkv_w = grad_qkv_w.astype(F32)
    packed = packed.reshape(-1)
    small = [packed[i * part : (i + 1) * part] for i in range(8)]
    up_at = 8 * part
    root_squares = jnp.sqrt(packed[up_at + unit : up_at + unit + 2] / (devices * rows * width))
    return (
        layer_out,
        grad_x,
        grad_qkv_w,
        grad_out_w,
        grad_up_w,
        grad_down_w,
        small[0],
        small[1],
        small[2],
        small[3],
        small[4],
        small[5],
        small[6],
        packed[up_at : up_at + unit],
        small[7],
        root_squares,
    )


def solution(mesh):
    matrix, vector, table = P(BOTH, None), P(BOTH), P("dp", None)
    return jax.shard_map(
        per_device,
        mesh=mesh,
        in_specs=(matrix,) * 6 + (vector,) * 9 + (table,) * 3,
        out_specs=(matrix,) * 6 + (vector,) * 9 + (P(),),
        check_vma=False,
    )
```

```python
import functools
import math

import jax
import jax.numpy as jnp
from jax import lax
from jax.experimental import pallas as pl
from jax.experimental.pallas import tpu as pltpu
from jax.sharding import PartitionSpec as P

H = 32
HD = 64
BLK = 32

EPSILON = 1e-05
MASKED = -1e30
BF = jnp.bfloat16
F32 = jnp.float32
BOTH = ("dp", "fsdp")
MESH = pl.DeviceIdType.MESH
HBM = pl.BlockSpec(memory_space=pl.ANY)
VM = pl.BlockSpec(memory_space=pltpu.VMEM)
MIB = 2**20


def place():
    d, f = lax.axis_index("dp"), lax.axis_index("fsdp")
    return d // 2, d % 2, f // 2, f % 2


def at(x, c, z, y):
    return (x * 2 + c, z * 2 + y)


def remote(src, dst, send, recv, target):
    return pltpu.make_async_remote_copy(
        src_ref=src, dst_ref=dst, send_sem=send, recv_sem=recv, device_id=target, device_id_type=MESH
    )


def greet(partners):
    barrier = pltpu.get_barrier_semaphore()
    count = 0
    for condition, device in partners:

        @pl.when(condition)
        def _():
            pl.semaphore_signal(barrier, inc=1, device_id=device, device_id_type=MESH)

        count = count + jnp.asarray(condition).astype(jnp.int32)
    pl.semaphore_wait(barrier, count)


def greet_all(devices, fsdp, me):
    barrier = pltpu.get_barrier_semaphore()

    def one(k, _):
        other = (me + k) % devices
        pl.semaphore_signal(barrier, inc=1, device_id=(other // fsdp, other % fsdp), device_id_type=MESH)
        return 0

    lax.fori_loop(1, devices, one, 0)
    pl.semaphore_wait(barrier, devices - 1)


def line_partners(nz, pos):
    x, c, z, y = pos
    return [(z >= 0, at(x, 1 - c, z, y)), (z > 0, at(x, c, z - 1, y)), (z < nz - 1, at(x, c, z + 1, y))]


def rank_partners(nz, pos):
    x, c, z, y = pos
    n = 2 * nz
    others = [(z * 2 + c + k) % n for k in range(1, n)]
    return [(z >= 0, at(x, p % 2, p // 2, y)) for p in others]


def group_partners(pos):
    x, c, z, y = pos
    return [(z >= 0, at(x ^ (m // 2), c, z, y ^ (m % 2))) for m in (1, 2, 3)]


def line_gather(src, dst, send, recv, nz, swap, pos):
    x, c, z, y = pos
    own = z * 2 + c
    sib = at(x, 1 - c, z, y)
    up_dev, dn_dev = at(x, c, z + 1, y), at(x, c, z - 1, y)
    UP, DN, SU, SD = 0, nz, 2 * nz, 3 * nz
    OWN = 4 * nz

    def block(b, moved):
        return dst.at[b] if moved else src

    def up(k):
        b = (z - k) * 2 + c
        return remote(block(b, k or swap), dst.at[b], send.at[UP + k], recv.at[UP + k], up_dev)

    def dn(k):
        b = (z + k) * 2 + c
        return remote(block(b, k or swap), dst.at[b], send.at[DN + k], recv.at[DN + k], dn_dev)

    def side(k, base, sign):
        b = (z + sign * k) * 2 + c
        return remote(block(b, k or swap), dst.at[b], send.at[base + k], recv.at[base + k], sib)

    def got(b, sem):
        return remote(dst.at[b], dst.at[b], send.at[OWN], recv.at[sem], sib)

    local = pltpu.make_async_copy(src, dst.at[own], recv.at[OWN])
    trade = remote(src, dst.at[z * 2 + y], send.at[OWN], recv.at[OWN], at(x, y, z, c))

    def first():
        if swap:
            pl.when(c == y)(local.start)
            pl.when(c != y)(trade.start)
        else:
            local.start()

    def spread():
        if swap:
            local.wait()
        pl.when(z < nz - 1)(up(0).start)
        pl.when(z > 0)(dn(0).start)
        side(0, SU, 1).start()

    def step(k):
        @pl.when(z >= k)
        def _():
            got((z - k) * 2 + c, UP + k - 1).wait_recv()
            pl.when(z < nz - 1)(up(k).start)
            side(k, SU, -1).start()

        @pl.when(z + k < nz)
        def _():
            got((z + k) * 2 + c, DN + k - 1).wait_recv()
            pl.when(z > 0)(dn(k).start)
            side(k, SD, 1).start()

    def last():
        if swap:
            pl.when(c != y)(trade.wait_send)
        else:
            local.wait()
        got(z * 2 + 1 - c, SU).wait_recv()
        pl.when(z < nz - 1)(up(0).wait_send)
        pl.when(z > 0)(dn(0).wait_send)
        side(0, SU, 1).wait_send()
        for k in range(1, nz):

            @pl.when(z >= k)
            def _():
                got((z - k) * 2 + 1 - c, SU + k).wait_recv()
                pl.when(z < nz - 1)(up(k).wait_send)
                side(k, SU, -1).wait_send()

            @pl.when(z + k < nz)
            def _():
                got((z + k) * 2 + 1 - c, SD + k).wait_recv()
                pl.when(z > 0)(dn(k).wait_send)
                side(k, SD, 1).wait_send()

    return [first, spread] + [functools.partial(step, k) for k in range(1, nz)] + [last]


def gather_sems(nz):
    return [pltpu.SemaphoreType.DMA((4 * nz + 1,))] * 2


def gather_kernel(nz, src, dst, send, recv):
    pos = place()
    greet(line_partners(nz, pos))
    for stage in line_gather(src, dst, send, recv, nz, False, pos):
        stage()


def params(cid, vmem=None):
    return pltpu.CompilerParams(collective_id=cid, has_side_effects=True, vmem_limit_bytes=vmem)


def gather_tokens(a, nz, cid):
    return pl.pallas_call(
        functools.partial(gather_kernel, nz),
        out_shape=jax.ShapeDtypeStruct((2 * nz,) + a.shape, a.dtype),
        in_specs=[HBM],
        out_specs=HBM,
        scratch_shapes=gather_sems(nz),
        compiler_params=params(cid),
        name="gather_tokens",
    )(a)


def scatter_blocks(nz, pos, p, out, acc, ups, dns, send, recv):
    x, c, z, y = pos
    sib = at(x, 1 - c, z, y)
    S, U, D = 0, nz, 2 * nz

    def f(v):
        return v.astype(F32)

    def swap(t):
        return remote(p.at[t * 2 + 1 - c], acc.at[t], send.at[S + t], recv.at[S + t], sib)

    def up(t):
        return remote(acc.at[t], ups.at[t], send.at[U + t], recv.at[U + t], at(x, c, z + 1, y))

    def dn(t):
        return remote(acc.at[t], dns.at[t], send.at[D + t], recv.at[D + t], at(x, c, z - 1, y))

    order = []
    for i in range(nz - 1):
        order += [(True, nz - 1 - i), (False, i)]
    for upward, t in order:
        pl.when(z < t if upward else z > t)(swap(t).start)
    swap(z).start()
    for upward, t in order:

        @pl.when(z < t if upward else z > t)
        def _():
            swap(t).wait_recv()
            acc[t] = (f(acc[t]) + f(p[t * 2 + c])).astype(BF)
            move, came = (up, ups) if upward else (dn, dns)

            @pl.when(z > 0 if upward else z < nz - 1)
            def _():
                move(t).wait_recv()
                acc[t] = (f(acc[t]) + f(came[t])).astype(BF)

            move(t).start()

    swap(z).wait_recv()
    out[...] = f(acc[z]) + f(p[z * 2 + c])

    @pl.when(z > 0)
    def _():
        up(z).wait_recv()
        out[...] += f(ups[z])

    @pl.when(z < nz - 1)
    def _():
        dn(z).wait_recv()
        out[...] += f(dns[z])

    for t in range(nz):
        swap(t).wait_send()
        pl.when(z < t)(up(t).wait_send)
        pl.when(z > t)(dn(t).wait_send)


def scatter_scratch(nz, rows, width):
    return [pltpu.VMEM((nz, rows, width), BF)] * 3 + [pltpu.SemaphoreType.DMA((3 * nz,))] * 2


def scatter_kernel(nz, p, out, *scratch):
    pos = place()
    greet(line_partners(nz, pos))
    scatter_blocks(nz, pos, p, out, *scratch)


def scatter_tokens(p, nz, cid):
    blocks, rows, width = p.shape
    return pl.pallas_call(
        functools.partial(scatter_kernel, nz),
        out_shape=jax.ShapeDtypeStruct((rows, width), F32),
        in_specs=[VM],
        out_specs=VM,
        scratch_shapes=scatter_scratch(nz, rows, width),
        compiler_params=params(cid, 60 * MIB),
        name="scatter_tokens",
    )(p)


def scatter_and_hand_kernel(nz, kinds, runs, p, up_s, res, *refs):
    count = len(kinds)
    srcs, refs = refs[:count], refs[count:]
    out, up_o, res_o, refs = *refs[:3], refs[3:]
    dsts, refs = refs[:count], refs[count:]
    scratch, hsems, esems, tsems = refs[:5], refs[5:7], refs[7:9], refs[9:11]
    pos = place()
    x, c, z, y = pos
    greet(rank_partners(nz, pos) + group_partners(pos) + [(c != y, at(x, y, z, c))])
    hs = hand_stages(srcs, dsts, kinds, *hsems, nz, pos)
    es = exchange_stages(up_s, up_o, runs, *esems, nz, pos)
    ts = trade_stages(res, res_o, *tsems, pos)
    hs[0]()
    es[0]()
    ts[0]()
    scatter_blocks(nz, pos, p, out, *scratch)
    hs[1]()
    es[1]()
    ts[1]()


def scatter_and_hand(p, up_s, runs, res, arrays, kinds, nz, cid):
    blocks, rows, width = p.shape
    n, part, share = up_s.shape
    return pl.pallas_call(
        functools.partial(scatter_and_hand_kernel, nz, kinds, runs),
        out_shape=[
            jax.ShapeDtypeStruct((rows, width), F32),
            jax.ShapeDtypeStruct((part, n * share), BF),
            jax.ShapeDtypeStruct(res.shape, BF),
        ]
        + hand_shapes(arrays, kinds, nz),
        in_specs=[VM] + [HBM] * (2 + len(arrays)),
        out_specs=[VM] + [HBM] * (2 + len(arrays)),
        scratch_shapes=scatter_scratch(nz, rows, width) + hand_sems(kinds) + exchange_sems(runs, nz) + trade_sems(),
        compiler_params=params(cid, 60 * MIB),
        name="scatter_and_hand",
    )(p, up_s, res, *arrays)


def block_of(x, c, z, y, nz):
    return (x * 2 + c) * 2 * nz + z * 2 + y


def halves(ref, rows):
    half = rows // 2
    if half % 16:
        return {1: None, 2: ref}
    return {1: ref.at[pl.ds(half, half)], 2: ref.at[pl.ds(0, half)]}


def sliced_gather(src, dst, runs, sems, nz, pos):
    x, c, z, y = pos
    n = 2 * nz
    me = z * 2 + c
    part = dst.shape[1]
    send1, recv1, send2, recv2 = sems

    def pieces(p):
        if runs is None:
            return [(src.at[p], slice(None))]
        return [(src.at[:, pl.ds(there, size)], pl.ds(here, size)) for there, here, size in runs(p)]

    def row(p, gx, gy):
        return dst.at[block_of(gx, p % 2, p // 2, gy, nz)]

    mine = block_of(x, c, z, y, nz)

    def out(k):
        p = (me + k) % n
        return [
            remote(a, dst.at[mine, :, b], send1.at[p], recv1.at[me], at(x, p % 2, p // 2, y))
            for a, b in pieces(p)
        ]

    local = [pltpu.make_async_copy(a, dst.at[mine, :, b], recv1.at[me]) for a, b in pieces(me)]

    def came(k):
        return (me - k + n) % n

    def arrival(b, sem):
        return remote(b, b, send1.at[me], sem, at(x, 1 - c, z, y))

    def neighbour(m):
        return at(x ^ (m // 2), c, z, y ^ (m % 2))

    def forward(k, m):
        p = came(k)
        b = row(p, x, y)
        slot = (m - 1) * n + p
        return remote(b, b, send2.at[slot], recv2.at[slot], neighbour(m))

    def relay(k, m):
        p = came(k)
        b = halves(row(p, x ^ (m // 2), y ^ (m % 2)), part)[m]
        slot = (1 + m) * n + p
        return b is not None and remote(b, b, send2.at[slot], recv2.at[slot], neighbour(3 - m))

    def first():
        for copy in local:
            copy.start()
        for k in range(1, n):
            for copy in out(k):
                copy.start()

    def step(k):
        p = came(k)
        arrival(row(p, x, y), recv1.at[p]).wait_recv()
        for m in (1, 2):
            forward(k, m).start()

    def pass_on(k):
        p = came(k)
        for m in (1, 2):
            arrival(row(p, x ^ (m // 2), y ^ (m % 2)), recv2.at[(m - 1) * n + p]).wait_recv()
            if relay(k, m):
                relay(k, m).start()

    def last():
        for k in range(n):
            p = came(k)
            parts = halves(row(p, 1 - x, 1 - y), part)
            for m in (1, 2):
                if parts[m] is not None:
                    arrival(parts[m], recv2.at[(1 + m) * n + p]).wait_recv()
        for k in range(n):
            if k:
                p = (me + k) % n
                b = dst.at[mine]
                remote(b, b, send1.at[p], recv1.at[me], at(x, p % 2, p // 2, y)).wait_send()
            for m in (1, 2):
                forward(k, m).wait_send()
                if relay(k, m):
                    relay(k, m).wait_send()

    stages = [functools.partial(step, k) for k in range(n)] + [functools.partial(pass_on, k) for k in range(n)]
    return [first] + stages + [last]


def sliced_sems(nz):
    n = 2 * nz
    return [pltpu.SemaphoreType.DMA((n,))] * 2 + [pltpu.SemaphoreType.DMA((4 * n,))] * 2


def group_gather(src, dst, send, recv, pos):
    x, c, z, y = pos
    rows = src.shape[0]
    local = pltpu.make_async_copy(src, dst.at[x * 2 + y], recv.at[0])

    def there(m):
        return dst.at[(x ^ (m // 2)) * 2 + (y ^ (m % 2))]

    def neighbour(m):
        return at(x ^ (m // 2), c, z, y ^ (m % 2))

    def out(m):
        return remote(src, dst.at[x * 2 + y], send.at[m], recv.at[m], neighbour(m))

    def relay(m):
        b = halves(there(m), rows)[m]
        return b is not None and remote(b, b, send.at[2 + m], recv.at[2 + m], neighbour(3 - m))

    def arrival(b, sem):
        return remote(b, b, send.at[0], sem, at(x, 1 - c, z, y))

    def first():
        local.start()
        for m in (1, 2):
            out(m).start()

    def pass_on():
        for m in (1, 2):
            arrival(there(m), recv.at[m]).wait_recv()
            if relay(m):
                relay(m).start()

    def last():
        local.wait()
        parts = halves(there(3), rows)
        for m in (1, 2):
            if parts[m] is not None:
                arrival(parts[m], recv.at[2 + m]).wait_recv()
            out(m).wait_send()
            if relay(m):
                relay(m).wait_send()

    return [first, pass_on, last]


def full_gather(src, dst, send, recv, nz, pos):
    x, c, z, y = pos
    rows = src.shape[0]
    sib = at(x, 1 - c, z, y)
    mine = dst.at[block_of(x, c, z, y, nz)]

    def row(core, k, m):
        return dst.at[block_of(x ^ (m // 2), core, z + k, y ^ (m % 2), nz)]

    def neighbour(m):
        return at(x ^ (m // 2), c, z, y ^ (m % 2))

    def arrival(b, sem):
        return remote(b, b, send.at[0], recv.at[sem], sib)

    def along(k, sign):
        b = row(c, k, 0)
        return remote(
            b if k else src, b, send.at[(0 if sign > 0 else nz) + z + k], recv.at[z + k], at(x, c, z + sign, y)
        )

    def forward(k, m):
        b = row(c, k, 0)
        return remote(b if k else src, b, send.at[(1 + m) * nz + z + k], recv.at[m * nz + z + k], neighbour(m))

    def relay(k, m):
        b = halves(row(c, k, m), rows)[m]
        if b is None:
            return None
        return remote(b, b, send.at[(3 + m) * nz + z + k], recv.at[(2 + m) * nz + z + k], neighbour(3 - m))

    def side(k, m):
        b = row(c, k, m)
        return remote(b if k or m else src, b, send.at[(6 + m) * nz + z + k], recv.at[(5 + m) * nz + z + k], sib)

    local = pltpu.make_async_copy(src, mine, recv.at[z])

    def first():
        local.start()
        pl.when(z < nz - 1)(along(0, 1).start)
        pl.when(z > 0)(along(0, -1).start)
        for m in (1, 2):
            forward(0, m).start()
        side(0, 0).start()

    def both(k, fn):
        @pl.when(z >= k)
        def _():
            fn(-k)

        if k:

            @pl.when(z + k < nz)
            def _():
                fn(k)

    def step(k):
        def one(k):
            arrival(row(c, k, 0), z + k).wait_recv()
            if k > 0:
                pl.when(z > 0)(along(k, -1).start)
            else:
                pl.when(z < nz - 1)(along(k, 1).start)
            for m in (1, 2):
                forward(k, m).start()
            side(k, 0).start()

        both(k, one)

    def pass_on(k):
        def one(k):
            for m in (1, 2):
                arrival(row(c, k, m), m * nz + z + k).wait_recv()
                if relay(k, m) is not None:
                    relay(k, m).start()
                side(k, m).start()

        both(k, one)

    def diagonal(k):
        def one(k):
            parts = halves(row(c, k, 3), rows)
            for m in (1, 2):
                if parts[m] is not None:
                    arrival(parts[m], (2 + m) * nz + z + k).wait_recv()
            side(k, 3).start()

        both(k, one)

    def last():
        local.wait()

        def one(k):
            for m in range(4):
                arrival(row(1 - c, k, m), (5 + m) * nz + z + k).wait_recv()
                side(k, m).wait_send()
            if k >= 0:
                pl.when(z > 0)(along(k, -1).wait_send)
            if k <= 0:
                pl.when(z < nz - 1)(along(k, 1).wait_send)
            for m in (1, 2):
                forward(k, m).wait_send()
                if relay(k, m) is not None:
                    relay(k, m).wait_send()

        for k in range(nz):
            both(k, one)

    return (
        [first]
        + [functools.partial(step, k) for k in range(1, nz)]
        + [functools.partial(pass_on, k) for k in range(nz)]
        + [functools.partial(diagonal, k) for k in range(nz)]
        + [last]
    )


def full_sems(nz):
    return [pltpu.SemaphoreType.DMA((10 * nz,)), pltpu.SemaphoreType.DMA((9 * nz,))]


def head_runs(nz, cols):
    return lambda p: [
        (block_of(x, p % 2, p // 2, 0, nz) * HD, x * cols // 2, cols // 2) for x in range(2)
    ]


def up_runs(nz, unit):
    return lambda p: [(block_of(x, p % 2, p // 2, 0, nz) * unit, x * 2 * unit, 2 * unit) for x in range(2)]


def qkv_runs(nz, width, cols):
    runs = head_runs(nz, cols)
    return lambda p: [(j * width + there, j * cols + here, size) for j in range(3) for there, here, size in runs(p)]


def fetch_kernel(
    nz, width, cols, x_in, w_qkv, w_down, vec, tab, x_all, qkv_w, down_w, vecs, tab_out, *sems
):
    pos = place()
    x, c, z, y = pos
    fsdp = 2 * nz
    devices = 4 * fsdp
    me = (x * 2 + c) * fsdp + z * 2 + y
    x_sems, qkv_sems, vec_sems, tab_sems, down_sems = sems[:2], sems[2:6], sems[6:8], sems[8:10], sems[10:]
    greet_all(devices, fsdp, me)

    def vec_copy(other):
        return remote(vec, vecs.at[me], vec_sems[0].at[other], vec_sems[1].at[me], (other // fsdp, other % fsdp))

    def each(fn):
        def body(k, _):
            fn((me + k) % devices)
            return 0

        lax.fori_loop(1, devices, body, 0)

    vec_local = pltpu.make_async_copy(vec, vecs.at[me], vec_sems[1].at[me])
    tab_local = pltpu.make_async_copy(tab, tab_out, tab_sems[1].at[0])
    tab_trade = remote(tab, tab_out, tab_sems[0].at[0], tab_sems[1].at[0], at(x, y, z, c))

    gx = line_gather(x_in, x_all, *x_sems, nz, True, pos)
    runs = qkv_runs(nz, width, cols) if len(w_qkv.shape) == 2 else None
    gq = sliced_gather(w_qkv, qkv_w, runs, qkv_sems, nz, pos)
    gx[0]()
    gq[0]()
    gx[1]()
    vec_local.start()
    each(lambda other: vec_copy(other).start())
    pl.when(c == y)(tab_local.start)
    pl.when(c != y)(tab_trade.start)
    gd = group_gather(w_down, down_w, *down_sems, pos)
    for stage in gq[1 : fsdp + 1]:
        stage()
    gx[2]()
    gd[0]()
    for stage in gx[3:-1]:
        stage()
    for stage in gq[fsdp + 1 :]:
        stage()
    gx[-1]()
    for stage in gd[1:]:
        stage()

    def vec_done(other):
        remote(vec, vecs.at[other], vec_sems[0].at[other], vec_sems[1].at[other], at(x, 1 - c, z, y)).wait_recv()
        vec_copy(other).wait_send()

    vec_local.wait()
    each(vec_done)
    tab_local.wait()
    pl.when(c != y)(tab_trade.wait_send)


def fetch(nz, x_in, w_qkv, w_down, part, vec, tab, cid):
    rows, width = x_in.shape
    n = 2 * nz
    devices = 4 * n
    cols = width // n
    shapes = [
        ((n, rows, width), BF),
        ((devices, part, 3 * cols), BF),
        ((4,) + w_down.shape, BF),
        ((devices,) + vec.shape, F32),
        (tab.shape, jnp.int32),
    ]
    return pl.pallas_call(
        functools.partial(fetch_kernel, nz, width, cols),
        out_shape=[jax.ShapeDtypeStruct(s, t) for s, t in shapes],
        in_specs=[HBM] * 5,
        out_specs=[HBM] * 5,
        scratch_shapes=gather_sems(nz)
        + sliced_sems(nz)
        + [pltpu.SemaphoreType.DMA((devices,))] * 2
        + [pltpu.SemaphoreType.DMA((1,))] * 2
        + [pltpu.SemaphoreType.DMA((5,))] * 2,
        compiler_params=params(cid),
        name="fetch",
    )(x_in, w_qkv, w_down, vec, tab)


def hand_stages(srcs, dsts, kinds, send, recv, nz, pos):
    x, c, z, y = pos
    n = 2 * nz
    count = len(kinds)

    def copies(i, m):
        gx, gy = x ^ (m // 2), y ^ (m % 2)
        sem = i * 3 + m - 1
        target = at(gx, c, z, gy)
        if not kinds[i]:
            return [remote(srcs[i].at[gx * 2 + gy], dsts[i].at[m - 1], send.at[sem], recv.at[sem], target)]
        return [
            remote(
                srcs[i].at[block_of(gx, p % 2, p // 2, gy, nz)],
                dsts[i].at[m - 1, p],
                send.at[sem],
                recv.at[sem],
                target,
            )
            for p in range(n)
        ]

    def first():
        for i in range(count):
            for m in (3, 1, 2):
                for copy in copies(i, m):
                    copy.start()

    def last():
        for i in range(count):
            for m in (1, 2, 3):
                sem = i * 3 + m - 1
                there = dsts[i].at[m - 1]
                whole = remote(there, there, send.at[sem], recv.at[sem], at(x, 1 - c, z, y))
                whole.wait_recv()
                whole.wait_send()

    return [first, last]


def hand_shapes(arrays, kinds, nz):
    return [
        jax.ShapeDtypeStruct((3, 2 * nz) + a.shape[1:] if k else (3,) + a.shape[1:], a.dtype)
        for a, k in zip(arrays, kinds)
    ]


def hand_sems(kinds):
    return [pltpu.SemaphoreType.DMA((3 * len(kinds),))] * 2


def exchange_stages(src, dst, runs, send, recv, nz, pos):
    x, c, z, y = pos
    n = 2 * nz
    me = z * 2 + c

    def give(to, p):
        if runs is None:
            return [(src.at[to], dst.at[p])]
        return [(src.at[to, :, pl.ds(here, size)], dst.at[:, pl.ds(there, size)]) for there, here, size in runs(p)]

    width = len(give(0, 0))

    def move(p):
        return [
            remote(a, b, send.at[p * width + i], recv.at[me * width + i], at(x, p % 2, p // 2, y))
            for i, (a, b) in enumerate(give(p, me))
        ]

    def come(p):
        return [
            remote(b, b, send.at[me * width + i], recv.at[p * width + i], at(x, 1 - c, z, y))
            for i, (_, b) in enumerate(give(me, p))
        ]

    local = [pltpu.make_async_copy(a, b, recv.at[me * width + i]) for i, (a, b) in enumerate(give(me, me))]

    def first():
        for copy in local:
            copy.start()
        for k in range(1, n):
            for copy in move((me + k) % n):
                copy.start()

    def last():
        for copy in local:
            copy.wait()
        for k in range(1, n):
            for copy in come((me - k + n) % n):
                copy.wait_recv()
            for copy in move((me + k) % n):
                copy.wait_send()

    return [first, last]


def exchange_sems(runs, nz):
    width = 1 if runs is None else len(runs(0))
    return [pltpu.SemaphoreType.DMA((width * 2 * nz,))] * 2


def exchange_kernel(nz, src, dst, send, recv):
    pos = place()
    greet(rank_partners(nz, pos))
    for stage in exchange_stages(src, dst, None, send, recv, nz, pos):
        stage()


def exchange(a, nz, cid, name):
    return pl.pallas_call(
        functools.partial(exchange_kernel, nz),
        out_shape=jax.ShapeDtypeStruct(a.shape, a.dtype),
        in_specs=[HBM],
        out_specs=HBM,
        scratch_shapes=exchange_sems(None, nz),
        compiler_params=params(cid),
        name=name,
    )(a)


def trade_stages(src, dst, send, recv, pos):
    x, c, z, y = pos
    local = pltpu.make_async_copy(src, dst, recv.at[0])
    trade = remote(src, dst, send.at[0], recv.at[0], at(x, y, z, c))

    def first():
        pl.when(c == y)(local.start)
        pl.when(c != y)(trade.start)

    def last():
        local.wait()
        pl.when(c != y)(trade.wait_send)

    return [first, last]


def trade_sems():
    return [pltpu.SemaphoreType.DMA((1,))] * 2


def finish_kernel(nz, runs, grad, small, qkv_s, grad_out, small_out, qkv_o, came, send, recv, *sems):
    pos = place()
    x, c, z, y = pos
    fsdp = 2 * nz
    devices = 4 * fsdp
    me = (x * 2 + c) * fsdp + z * 2 + y
    es = exchange_stages(qkv_s, qkv_o, runs, *sems[:2], nz, pos)
    ts = trade_stages(grad, grad_out, *sems[2:], pos)
    greet_all(devices, fsdp, me)

    def each(fn):
        def body(k, _):
            fn((me + k) % devices)
            return 0

        lax.fori_loop(1, devices, body, 0)

    def share(other):
        return remote(small.at[other], came.at[me], send.at[other], recv.at[me], (other // fsdp, other % fsdp))

    es[0]()
    ts[0]()
    each(lambda other: share(other).start())

    def done(other):
        remote(small.at[me], came.at[other], send.at[other], recv.at[other], at(x, 1 - c, z, y)).wait_recv()
        share(other).wait_send()

    each(done)
    came[me] = small[me]
    small_out[...] = jnp.sum(came[...], axis=0)
    ts[1]()
    es[1]()


def finish(grad, small, qkv_s, runs, nz, cid):
    devices = small.shape[0]
    out_shape = qkv_s.shape if runs is None else (qkv_s.shape[1], qkv_s.shape[0] * qkv_s.shape[2])
    return pl.pallas_call(
        functools.partial(finish_kernel, nz, runs),
        out_shape=[
            jax.ShapeDtypeStruct(grad.shape, grad.dtype),
            jax.ShapeDtypeStruct(small.shape[1:], F32),
            jax.ShapeDtypeStruct(out_shape, BF),
        ],
        in_specs=[HBM, VM, HBM],
        out_specs=[HBM, VM, HBM],
        scratch_shapes=[pltpu.VMEM(small.shape, F32)]
        + [pltpu.SemaphoreType.DMA((devices,))] * 2
        + exchange_sems(runs, nz)
        + trade_sems(),
        compiler_params=params(cid, 32 * MIB),
        name="finish",
    )(grad, small, qkv_s)


def dot(a, b, dims):
    return lax.dot_general(a, b, (dims, ((), ())), preferred_element_type=F32)


NN = ((1,), (0,))
NT = ((1,), (1,))
TN = ((0,), (0,))


def gelu_and_slope(value):
    normal = 0.5 + 0.5 * lax.erf(value * math.sqrt(0.5))
    density = jnp.exp(-0.5 * value * value) * (1.0 / math.sqrt(2.0 * math.pi))
    return value * normal, normal + value * density


def mlp_kernel(
    nz, own, cot_in, up_in, down_in, bias, out, upd_out, up_out, down_out, bias_g,
    mlp, cot, up_w, down_w, p, upd, up_g, down_g, active, gh, acc, ups, dns, gsend, grecv, ssend, srecv, lsem,
):
    pos = place()
    x, c, z, y = pos
    blocks, rows, width = mlp.shape
    units = active.shape[1]
    pair = 2 * rows
    me = z * 2 + c
    sib = at(x, 1 - c, z, y)
    up_dev, dn_dev = at(x, c, z + 1, y), at(x, c, z - 1, y)
    UP, DN, SU, SD = 0, nz, 2 * nz, 3 * nz
    S, U, D = 0, nz, 2 * nz

    def f(v):
        return v.astype(F32)

    loads = [
        pltpu.make_async_copy(a, b, lsem.at[i])
        for i, (a, b) in enumerate([(cot_in, cot), (down_in, down_w), (up_in, up_w)])
    ]
    stores = [
        pltpu.make_async_copy(a, b, lsem.at[3 + i])
        for i, (a, b) in enumerate([(upd, upd_out), (up_g, up_out), (down_g, down_out)])
    ]

    def block(b, sem, target):
        return remote(mlp.at[b], mlp.at[b], gsend.at[sem], grecv.at[sem], target)

    def up(d):
        return block((z - d) * 2 + c, UP + d, up_dev)

    def dn(d):
        return block((z + d) * 2 + c, DN + d, dn_dev)

    def side(d, below):
        return block(jnp.where(below, z - d, z + d) * 2 + c, jnp.where(below, SU, SD) + d, sib)

    def turn(i):
        both = jnp.minimum(z, nz - 1 - z)
        two = i <= 2 * both
        d = jnp.where(two, (i + 1) // 2, i - both)
        below = jnp.where(two, i % 2 == 1, z > nz - 1 - z)
        return d, below

    def arrive(i):
        if i == 0:
            block(z * 2 + 1 - c, SU, sib).wait_recv()
            return z
        d, below = turn(i)
        zi = jnp.where(below, z - d, z + d)
        block(zi * 2 + c, jnp.where(below, UP, DN) + d - 1, sib).wait_recv()
        pl.when(below & (z < nz - 1))(lambda: up(d).start())
        pl.when(jnp.logical_not(below) & (z > 0))(lambda: dn(d).start())
        side(d, below).start()
        block(zi * 2 + 1 - c, jnp.where(below, SU, SD) + d, sib).wait_recv()
        return zi

    def swap(t):
        return remote(p.at[t * 2 + 1 - c], acc.at[t], ssend.at[S + t], srecv.at[S + t], sib)

    def rise(t):
        return remote(acc.at[t], ups.at[t], ssend.at[U + t], srecv.at[U + t], up_dev)

    def fall(t):
        return remote(acc.at[t], dns.at[t], ssend.at[D + t], srecv.at[D + t], dn_dev)

    def event(t, upward):
        swap(t).wait_recv()
        acc[t] = (f(acc[t]) + f(p[t * 2 + c])).astype(BF)
        move, came = (rise, ups) if upward else (fall, dns)

        @pl.when(z > 0 if upward else z < nz - 1)
        def _():
            move(t).wait_recv()
            acc[t] = (f(acc[t]) + f(came[t])).astype(BF)

        move(t).start()

    def events(s):
        for t in range(nz):
            zz = s - t
            if 0 <= zz < t:
                pl.when(z == zz)(functools.partial(event, t, True))
            zz = 2 * (nz - 1) - s - t
            if t < zz < nz:
                pl.when(z == zz)(functools.partial(event, t, False))

    def at_rows(ref, zi):
        return ref[pl.ds(zi * 2, 2)].reshape(pair, width)

    def hidden_part(zi, early):
        here = pl.ds(pl.multiple_of(zi * pair, pair), pair)

        def tile(j, _):
            u = pl.ds(pl.multiple_of(j * 256, 256), 256)
            value = dot(at_rows(mlp, zi), up_w[:, u], NN) + bias[:, u]
            grad = dot(at_rows(cot, zi), down_w[u, :], NT)
            act, slope = gelu_and_slope(value)
            low = (grad * slope).astype(BF)
            active[here, u] = act.astype(BF)
            gh[here, u] = low
            bias_g[:, u] += jnp.sum(f(low), axis=0, keepdims=True)
            return 0

        lax.fori_loop(0, units // 256, tile, 0)

        def back(j, _):
            w = pl.ds(pl.multiple_of(j * 512, 512), 512)
            p[pl.ds(zi * 2, 2), :, w] = dot(gh[here, :], up_w[w, :], NT).astype(BF).reshape(2, rows, 512)
            return 0

        lax.fori_loop(0, width // 512, back, 0)

    def forward_part(zi):
        here = pl.ds(pl.multiple_of(zi * pair, pair), pair)

        def tile(j, _):
            w = pl.ds(pl.multiple_of(j * 512, 512), 512)
            upd[pl.ds(zi * 2, 2), :, w] = dot(active[here, :], down_w[:, w], NN).astype(BF).reshape(2, rows, 512)
            return 0

        lax.fori_loop(0, width // 512, tile, 0)

    def up_grads(first, count):
        def tile(j, _):
            w = pl.ds(pl.multiple_of(j * 256, 256), 256)
            up_g[w, :] = dot(mlp[:, :, w].reshape(blocks * rows, 256), gh[...], TN).astype(BF)
            return 0

        lax.fori_loop(first, first + count, tile, 0)

    def down_grads():
        def tile(j, _):
            u = pl.ds(pl.multiple_of(j * 256, 256), 256)
            down_g[u, :] = dot(active[:, u], cot[...].reshape(blocks * rows, width), TN).astype(BF)
            return 0

        lax.fori_loop(0, units // 256, tile, 0)

    mlp[me] = own[...]
    greet(line_partners(nz, pos))
    pl.when(z < nz - 1)(up(0).start)
    pl.when(z > 0)(dn(0).start)
    side(0, z >= 0).start()
    for copy in loads:
        copy.start()
    bias_g[...] = jnp.zeros_like(bias_g)
    for copy in loads:
        copy.wait()
    slots = 2 * nz - 1
    tiles = width // 256
    for s in range(slots):
        if s < nz:
            zi = arrive(s)
            hidden_part(zi, s)
            swap(zi).start()
        events(s)
        if s < nz:
            forward_part(zi)
        if s == nz - 1:
            stores[0].start()
            down_grads()
            stores[2].start()
        elif s == nz:
            up_grads(0, tiles // 2)
        elif s == nz + 1:
            up_grads(tiles // 2, tiles - tiles // 2)
            stores[1].start()
    swap(z).wait_recv()
    out[...] = f(acc[z]) + f(p[z * 2 + c])

    @pl.when(z > 0)
    def _():
        rise(z).wait_recv()
        out[...] += f(ups[z])

    @pl.when(z < nz - 1)
    def _():
        fall(z).wait_recv()
        out[...] += f(dns[z])

    for copy in stores:
        copy.wait()
    side(0, z >= 0).wait_send()
    pl.when(z < nz - 1)(up(0).wait_send)
    pl.when(z > 0)(dn(0).wait_send)
    for k in range(1, nz):

        @pl.when(z >= k)
        def _():
            pl.when(z < nz - 1)(up(k).wait_send)
            side(k, z >= 0).wait_send()

        @pl.when(z + k < nz)
        def _():
            pl.when(z > 0)(dn(k).wait_send)
            side(k, z < 0).wait_send()

    for t in range(nz):
        swap(t).wait_send()
        pl.when(z < t)(rise(t).wait_send)
        pl.when(z > t)(fall(t).wait_send)


def mlp_bytes(nz, rows, width, units):
    tree = 2 * nz * rows
    return 2 * (4 * tree * width + 4 * units * width + 2 * tree * units + 3 * nz * rows * width) + 8 * rows * width


def mlp_call(own, cot, up_w, down_w, bias, nz, cid):
    rows, width = own.shape
    units = down_w.shape[0]
    n = 2 * nz
    shape = jax.ShapeDtypeStruct
    return pl.pallas_call(
        functools.partial(mlp_kernel, nz),
        out_shape=[
            shape((rows, width), F32),
            shape((n, rows, width), BF),
            shape((width, units), BF),
            shape((units, width), BF),
            shape((1, units), F32),
        ],
        in_specs=[VM, HBM, HBM, HBM, VM],
        out_specs=[VM, HBM, HBM, HBM, VM],
        scratch_shapes=[
            pltpu.VMEM((n, rows, width), BF),
            pltpu.VMEM((n, rows, width), BF),
            pltpu.VMEM((width, units), BF),
            pltpu.VMEM((units, width), BF),
            pltpu.VMEM((n, rows, width), BF),
            pltpu.VMEM((n, rows, width), BF),
            pltpu.VMEM((width, units), BF),
            pltpu.VMEM((units, width), BF),
            pltpu.VMEM((n * rows, units), BF),
            pltpu.VMEM((n * rows, units), BF),
        ]
        + [pltpu.VMEM((nz, rows, width), BF)] * 3
        + gather_sems(nz)
        + [pltpu.SemaphoreType.DMA((3 * nz,))] * 2
        + [pltpu.SemaphoreType.DMA((6,))],
        compiler_params=params(cid, 62 * MIB),
        name="mlp",
    )(own, cot, up_w, down_w, bias)


def attend_kernel(
    heads, nz, unit, slopes, far, joined_q, joined, cot, w_up, w_out, out, cot_all, up_w, out_w, *sems
):
    cols = heads * HD
    step, steps = pl.program_id(0), pl.num_programs(0)
    pos = place()
    n = 2 * nz
    gc = line_gather(cot, cot_all, *sems[:2], nz, True, pos)
    gu = sliced_gather(w_up, up_w, up_runs(nz, unit), sems[2:6], nz, pos)
    go = full_gather(w_out, out_w, *sems[6:8], nz, pos)

    @pl.when(step == 0)
    def _():
        x, c, z, y = pos
        greet(rank_partners(nz, pos) + group_partners(pos) + [(c != y, at(x, y, z, c))])
        gc[0]()
        gu[0]()
        go[0]()

    @pl.when(step == 1)
    def _():
        for stage in go[1:nz]:
            stage()

    @pl.when(step == 2)
    def _():
        for stage in gu[1 : n + 1]:
            stage()
        gc[1]()

    gap = far[...]
    for h in range(heads):
        q = joined_q[:, h * HD : (h + 1) * HD]
        k = joined[:, cols + h * HD : cols + (h + 1) * HD]
        v = joined[:, 2 * cols + h * HD : 2 * cols + (h + 1) * HD]
        logits = dot(q, k, NT) * HD ** (-0.5) + slopes[h] * gap
        weights = jnp.exp(logits - jnp.max(logits, axis=1, keepdims=True))
        probs = weights * (1.0 / jnp.sum(weights, axis=1, keepdims=True))
        out[:, h * HD : (h + 1) * HD] = dot(probs.astype(BF), v, NN).astype(BF)

    @pl.when(step == steps - 1)
    def _():
        for stage in go[nz : 2 * nz]:
            stage()
        ahead, later = gc[2:-1], gu[n + 1 : -1]
        for i, stage in enumerate(ahead):
            stage()
            for other in later[i * n // len(ahead) : (i + 1) * n // len(ahead)]:
                other()
        for stage in go[2 * nz :]:
            stage()
        gc[-1]()
        gu[-1]()


def attend(slopes, far, joined, cot, w_up, w_out, unit, heads, nz, cid):
    tree = far.shape[0]
    cols = heads * HD
    rows = min(256, max(128, 2**18 // tree))
    block, width = cot.shape
    part = w_up.shape[0]
    n = 2 * nz
    shapes = [(tree, cols), (n, block, width), (4 * n, part, 4 * unit), (4 * n, part, width)]
    return pl.pallas_call(
        functools.partial(attend_kernel, heads, nz, unit),
        out_shape=[jax.ShapeDtypeStruct(s, BF) for s in shapes],
        grid=(tree // rows,),
        in_specs=[
            pl.BlockSpec(memory_space=pltpu.SMEM),
            pl.BlockSpec((rows, tree), lambda i: (i, 0)),
            pl.BlockSpec((rows, 3 * cols), lambda i: (i, 0)),
            pl.BlockSpec((tree, 3 * cols), lambda i: (0, 0)),
            HBM,
            HBM,
            HBM,
        ],
        out_specs=[pl.BlockSpec((rows, cols), lambda i: (i, 0)), HBM, HBM, HBM],
        scratch_shapes=gather_sems(nz) + sliced_sems(nz) + full_sems(nz),
        compiler_params=params(cid, 56 * MIB),
        name="attend",
    )(slopes, far, joined, joined, cot, w_up, w_out)


def attend_back_kernel(heads, nz, kinds, slopes, far, joined_q, joined, grad, branch, part_sums, *refs):
    count = len(kinds)
    srcs, refs = refs[:count], refs[count:]
    out_q, out_k, out_v, branch_all, update, refs = *refs[:5], refs[5:]
    dsts, refs = refs[:count], refs[count:]
    acc_k, acc_v, p, refs = *refs[:3], refs[3:]
    scratch, gsems, hsems, psem = refs[:5], refs[5:7], refs[7:9], refs[9]
    cols = heads * HD
    step = pl.program_id(0)
    pos = place()
    gb = line_gather(branch, branch_all, *gsems, nz, False, pos)
    hs = hand_stages(srcs, dsts, kinds, *hsems, nz, pos)
    load = pltpu.make_async_copy(part_sums, p, psem.at[0])

    @pl.when(step == 0)
    def _():
        acc_k[...] = jnp.zeros_like(acc_k)
        acc_v[...] = jnp.zeros_like(acc_v)
        greet(line_partners(nz, pos) + group_partners(pos))
        hs[0]()
        gb[0]()
        gb[1]()
        load.start()

    @pl.when(step == 3)
    def _():
        gb[2]()

    gap = far[...]
    for h in range(heads):
        here = slice(h * HD, (h + 1) * HD)
        q = joined_q[:, here]
        k = joined[:, cols + h * HD : cols + (h + 1) * HD]
        v = joined[:, 2 * cols + h * HD : 2 * cols + (h + 1) * HD]
        g = grad[:, here]
        logits = dot(k, q, NT) * HD ** (-0.5) + slopes[h] * gap
        weights = jnp.exp(logits - jnp.max(logits, axis=0, keepdims=True))
        probs = weights * (1.0 / jnp.sum(weights, axis=0, keepdims=True))
        grad_probs = dot(v, g, NT)
        delta = jnp.sum(probs * grad_probs, axis=0, keepdims=True)
        grad_raw = (probs * (grad_probs - delta) * HD ** (-0.5)).astype(BF)
        acc_v[:, here] += dot(probs.astype(BF), g, NN)
        acc_k[:, here] += dot(grad_raw, q, NN)
        out_q[:, here] = dot(grad_raw, k, TN).astype(BF)

    @pl.when(step == pl.num_programs(0) - 1)
    def _():
        out_k[...] = acc_k[...].astype(BF)
        out_v[...] = acc_v[...].astype(BF)
        for stage in gb[3:]:
            stage()
        load.wait()
        scatter_blocks(nz, pos, p, update, *scratch)
        hs[1]()


def attend_back(slopes, far_t, joined, grad, branch, part_sums, arrays, kinds, heads, nz, cid):
    tree = far_t.shape[0]
    cols = heads * HD
    rows = min(256, max(128, 2**18 // tree))
    block, width = branch.shape
    full = pl.BlockSpec((tree, cols), lambda i: (0, 0))
    part = pl.BlockSpec((rows, cols), lambda i: (i, 0))
    return pl.pallas_call(
        functools.partial(attend_back_kernel, heads, nz, kinds),
        out_shape=[jax.ShapeDtypeStruct((tree, cols), BF)] * 3
        + [jax.ShapeDtypeStruct((2 * nz, block, width), BF), jax.ShapeDtypeStruct((block, width), F32)]
        + hand_shapes(arrays, kinds, nz),
        grid=(tree // rows,),
        in_specs=[
            pl.BlockSpec(memory_space=pltpu.SMEM),
            pl.BlockSpec((tree, rows), lambda i: (0, i)),
            pl.BlockSpec((rows, 3 * cols), lambda i: (i, 0)),
            pl.BlockSpec((tree, 3 * cols), lambda i: (0, 0)),
            part,
            HBM,
            HBM,
        ]
        + [HBM] * len(arrays),
        out_specs=[part, full, full, HBM, pl.BlockSpec((block, width), lambda i: (0, 0))] + [HBM] * len(arrays),
        scratch_shapes=[pltpu.VMEM((tree, cols), F32)] * 2
        + [pltpu.VMEM((2 * nz, block, width), BF)]
        + scatter_scratch(nz, block, width)
        + gather_sems(nz)
        + hand_sems(kinds)
        + [pltpu.SemaphoreType.DMA((1,))],
        compiler_params=params(cid, 62 * MIB),
        name="attend_back",
    )(slopes, far_t, joined, joined, grad, branch, part_sums, *arrays)


def norm_parts(values):
    center = values - jnp.mean(values, axis=-1, keepdims=True)
    inverse = lax.rsqrt(jnp.mean(center * center, axis=-1, keepdims=True) + EPSILON)
    return (center * inverse, inverse)


def norm_back(grad_normed, normed, inverse):
    mean_grad = jnp.mean(grad_normed, axis=-1, keepdims=True)
    mean_cross = jnp.mean(grad_normed * normed, axis=-1, keepdims=True)
    return inverse * (grad_normed - mean_grad - normed * mean_cross)


def tree_tables(parents, seg_blocks, valid):
    segments = parents.shape[0]
    seg_tokens = jnp.broadcast_to(seg_blocks[:, None], (seg_blocks.shape[0], BLK)).reshape(-1)
    labels = jnp.arange(segments, dtype=jnp.int32)
    member = (seg_tokens[:, None] == labels[None, :]).astype(jnp.int32)
    counted = member * valid[:, None]
    before = jnp.cumsum(counted, axis=0) - counted
    rank = jnp.sum(before * member, axis=1)
    seg_len = jnp.sum(counted, axis=0)
    picked = (parents[:, None] == labels[None, :]).astype(jnp.int32)
    grand = jnp.sum(picked * parents[None, :], axis=1)
    ancestor = ((labels[None, :] == parents[:, None]) | (labels[None, :] == grand[:, None])) & (
        labels[None, :] != labels[:, None]
    )
    offset = jnp.sum(ancestor.astype(jnp.int32) * seg_len[None, :], axis=1)
    position = jnp.sum(member * offset[None, :], axis=1) + rank
    return (seg_tokens, position, ancestor.astype(jnp.float32))


def allowed_mask(seg, index, valid, ancestor):
    labels = jnp.arange(ancestor.shape[0], dtype=jnp.int32)
    member = (seg[:, None] == labels[None, :]).astype(jnp.float32)
    reach = jnp.dot(jnp.dot(member, ancestor), member.T) > 0.5
    causal = (seg[:, None] == seg[None, :]) & (index[None, :] <= index[:, None])
    visible = (valid[None, :] == 1) | (index[None, :] == index[:, None])
    return (reach | causal) & visible


def gelu_exact(value):
    return jax.nn.gelu(value, approximate=False)


def mm(spec, a, b):
    return jnp.einsum(spec, a, b, preferred_element_type=F32)


def padded(flat, lanes):
    return jnp.pad(flat, [(0, 0)] * (flat.ndim - 1) + [(0, -flat.shape[-1] % lanes)])


def per_device(
    layer_in,
    cotangent,
    w_qkv,
    w_out,
    w_up,
    w_down,
    gain_attn,
    shift_attn,
    bias_query,
    bias_value,
    bias_out,
    gain_mlp,
    shift_mlp,
    bias_up,
    bias_down,
    parents,
    seg_blocks,
    token_valid,
):
    rows, width = layer_in.shape
    fsdp = lax.axis_size("fsdp")
    nz = fsdp // 2
    devices = 4 * fsdp
    x, c, z, y = place()
    rank = z * 2 + c
    heads = H // fsdp
    cols = heads * HD
    tree = token_valid.shape[1]
    part = w_up.shape[0]
    unit = w_down.shape[0]

    vec = jnp.concatenate(
        [gain_attn, shift_attn, bias_query, bias_value, bias_out, gain_mlp, shift_mlp, bias_down, bias_up]
    ).astype(F32)
    vec = padded(vec, 1024).reshape(-1, 128)
    tab = jnp.concatenate([token_valid[0], seg_blocks[0], parents[0]])
    tab = padded(tab, 1024).reshape(-1, 128)
    aligned = part == HD and cols % 256 == 0
    if not aligned:
        w_qkv = w_qkv.reshape(part, 3, fsdp, cols).transpose(2, 0, 1, 3).reshape(fsdp, part, 3 * cols)
    x_all, qkv_w, down_w, vecs, tab = fetch(nz, layer_in, w_qkv, w_down, part, vec, tab, 1)
    down_w = down_w.reshape(4 * unit, width)
    x_all = x_all.reshape(tree, width)
    qkv_w = qkv_w.reshape(width, 3 * cols)
    vecs = vecs.reshape(devices, -1)
    (gain_one, shift_one, query_bias, value_bias, out_bias, gain_two, shift_two, down_bias) = [
        vecs[:, i * part : (i + 1) * part].reshape(-1) for i in range(8)
    ]
    up_bias = vecs[:, 8 * part : 8 * part + unit].reshape(2, 2, nz, 2, unit)
    up_bias = lax.dynamic_slice(up_bias, (0, c, z, 0, 0), (2, 1, 1, 2, unit)).reshape(-1)

    def own_rows(v):
        return lax.dynamic_slice_in_dim(v, rank * rows, rows, 0)

    normed_all, _ = norm_parts(x_all.astype(F32))
    attn_in = (normed_all * gain_one + shift_one).astype(BF)
    inputs = own_rows(x_all).astype(F32)
    normed_one, inverse_one = norm_parts(inputs)

    if aligned:

        def own_cols(v):
            v = v.reshape(2, 2, nz, 2, HD)
            return lax.dynamic_slice(v, (0, c, z, 0, 0), (2, 1, 1, 2, HD)).reshape(-1)

        def spread(v):
            v = v.reshape(2, 1, 1, 2, HD)
            return lax.dynamic_update_slice(jnp.zeros((2, 2, nz, 2, HD), F32), v, (0, c, z, 0, 0))

        numbers = block_of(jnp.arange(2)[:, None], c, z, jnp.arange(2)[None, :], nz).reshape(-1)
    else:

        def own_cols(v):
            return lax.dynamic_slice_in_dim(v, rank * cols, cols, 0)

        def spread(v):
            return lax.dynamic_update_slice_in_dim(jnp.zeros((width,), F32), v, rank * cols, 0)

        numbers = rank * heads + jnp.arange(heads)

    joined_bias = jnp.concatenate([own_cols(query_bias), jnp.zeros((cols,), F32), own_cols(value_bias)])
    joined = (jnp.dot(attn_in, qkv_w, preferred_element_type=F32) + joined_bias).astype(BF)

    tab = tab.reshape(-1)
    blocks = seg_blocks.shape[1]
    valid = tab[:tree]
    seg, position, ancestor = tree_tables(
        tab[tree + blocks : tree + blocks + parents.shape[1]], tab[tree : tree + blocks], valid
    )
    index = jnp.arange(tree, dtype=jnp.int32)
    mask = allowed_mask(seg, index, valid, ancestor)
    far = jnp.where(mask, (position[None, :] - position[:, None]).astype(F32), MASKED)
    slopes = jnp.exp2(-8.0 * (numbers.astype(F32) + 1.0) / H)
    mixed, cot, up_w, out_w = attend(slopes, far, joined, cotangent, w_up, w_out, unit, heads, nz, 9)
    out_w = out_w.reshape(width, width)
    cot = cot.reshape(tree, width)
    up_w = up_w.reshape(width, 4 * unit)

    mixed_own = exchange(mixed.reshape(fsdp, rows, cols), nz, 2, "mixed_to_tokens")
    if aligned:
        mixed_own = mixed_own.reshape(nz, 2, rows, 2, 2 * HD).transpose(2, 3, 1, 0, 4).reshape(rows, width)
    else:
        mixed_own = mixed_own.transpose(1, 0, 2).reshape(rows, width)
    branch = jnp.dot(mixed_own, out_w, preferred_element_type=F32) + out_bias
    middle = inputs + branch
    normed_two, inverse_two = norm_parts(middle)
    mlp_own = (normed_two * gain_two + shift_two).astype(BF)
    cot_blocks = cot.reshape(fsdp, rows, width)
    if mlp_bytes(nz, rows, width, 4 * unit) < 50 * MIB:
        grad_mlp_in, update, up_g, down_g, grad_bias_up = mlp_call(
            mlp_own, cot_blocks, up_w, down_w, up_bias[None], nz, 3
        )
        grad_bias_up = grad_bias_up[0]
    else:
        mlp_in = gather_tokens(mlp_own, nz, 3).reshape(tree, width)
        hidden = jnp.dot(mlp_in, up_w, preferred_element_type=F32) + up_bias
        active_float, gelu_pull = jax.vjp(gelu_exact, hidden)
        active = active_float.astype(BF)
        grad_active = mm("td,fd->tf", cot, down_w)
        grad_hidden = gelu_pull(grad_active)[0].astype(BF)
        grad_mlp_in = mm("tf,df->td", grad_hidden, up_w).astype(BF).reshape(fsdp, rows, width)
        grad_mlp_in = scatter_tokens(grad_mlp_in, nz, 4)
        update = jnp.dot(active, down_w, preferred_element_type=F32).astype(BF).reshape(fsdp, rows, width)
        down_g = mm("tf,td->fd", active, cot).astype(BF)
        up_g = mm("td,tf->df", mlp_in, grad_hidden).astype(BF)
        grad_bias_up = jnp.sum(grad_hidden.astype(F32), axis=0)
    down_g = down_g.reshape(4, unit, width)
    up_g = up_g.reshape(devices, part, 4 * unit)

    cot_own = own_rows(cot).astype(F32)
    grad_middle = cot_own + norm_back(grad_mlp_in * gain_two, normed_two, inverse_two)
    grad_branch = grad_middle.astype(BF)
    grad_mixed = mm("te,de->td", grad_branch, out_w).astype(BF)
    if not aligned:
        grad_out_w = lax.psum_scatter(
            mm("td,te->de", mixed_own, grad_branch).astype(BF), BOTH, scatter_dimension=0, tiled=True
        ).astype(F32)
    if aligned:
        grad_mixed = grad_mixed.reshape(rows, 2, 2, nz, 2 * HD).transpose(3, 2, 0, 1, 4).reshape(fsdp, rows, cols)
    else:
        grad_mixed = grad_mixed.reshape(rows, fsdp, cols).transpose(1, 0, 2)
    grad_heads = exchange(grad_mixed, nz, 5, "grad_to_heads")
    grad_heads = grad_heads.reshape(tree, cols)
    grad_q, grad_k, grad_v, branch_all, update, down_c, up_c = attend_back(
        slopes, far.T, joined, grad_heads, grad_branch, update, [down_g, up_g], (False, True), heads, nz, 6
    )
    result = middle + update + down_bias
    grad_joined = jnp.concatenate([grad_q, grad_k, grad_v], axis=1)

    def mine(g, came):
        g = g.reshape((2, 2, nz, 2) + g.shape[1:])
        g = lax.dynamic_slice(g, (x, 0, 0, y, 0, 0), (1, 2, nz, 1) + g.shape[4:])
        g = g.reshape((2, nz) + g.shape[4:]).swapaxes(0, 1)
        return (g.reshape(came.shape[1:]).astype(F32) + jnp.sum(came.astype(F32), axis=0)).astype(BF)

    def mine_flat(g, came):
        return lax.dynamic_index_in_dim(g, x * 2 + y, 0, keepdims=False).astype(F32) + jnp.sum(came.astype(F32), axis=0)

    grad_down_w = mine_flat(down_g, down_c)
    qkv_g = mm("td,te->de", attn_in, grad_joined).astype(BF).reshape(devices, part, 3 * cols)
    flat = []
    if aligned:
        flat = [mm("td,te->de", mixed, branch_all.reshape(tree, width)).astype(BF).reshape(4, part, width)]
    kinds = (True,) + (False,) * len(flat)
    grad_attn_in = mm("te,de->td", grad_joined, qkv_w).astype(BF).reshape(fsdp, rows, width)
    grad_attn_in, grad_up_w, layer_out, qkv_c, *out_c = scatter_and_hand(
        grad_attn_in, mine(up_g, up_c), up_runs(nz, unit), result.astype(BF), [qkv_g] + flat, kinds, nz, 10
    )
    grad_up_w = grad_up_w.astype(F32)
    if aligned:
        grad_out_w = mine_flat(flat[0], out_c[0])
    grad_inputs = grad_middle + norm_back(grad_attn_in * gain_one, normed_one, inverse_one)

    col = jnp.sum(grad_joined.astype(F32), axis=0)

    smalls = [
        jnp.sum(grad_attn_in * normed_one, axis=0),
        jnp.sum(grad_attn_in, axis=0),
        spread(col[:cols]),
        spread(col[2 * cols :]),
        jnp.sum(grad_branch.astype(F32), axis=0),
        jnp.sum(grad_mlp_in * normed_two, axis=0),
        jnp.sum(grad_mlp_in, axis=0),
        jnp.sum(cot_own, axis=0),
    ]
    grad_bias_up = grad_bias_up.reshape(2, 1, 1, 2, unit)
    grad_bias_up = lax.dynamic_update_slice(jnp.zeros((2, 2, nz, 2, unit), F32), grad_bias_up, (0, c, z, 0, 0))
    squares = jnp.stack([jnp.sum(result * result), jnp.sum(branch * branch)])
    packed = jnp.concatenate(
        [v.reshape(devices, part) for v in smalls]
        + [grad_bias_up.reshape(devices, unit), jnp.broadcast_to(squares, (devices, 2))],
        axis=1,
    )
    packed = padded(packed, 1024).reshape(devices, -1, 128)
    runs = qkv_runs(nz, width, cols) if aligned else None
    grad_x, packed, grad_qkv_w = finish(grad_inputs.astype(BF), packed, mine(qkv_g, qkv_c), runs, nz, 8)
    if not aligned:
        grad_qkv_w = grad_qkv_w.reshape(fsdp, part, 3, cols).transpose(1, 2, 0, 3).reshape(part, -1)
    grad_qkv_w = grad_qkv_w.astype(F32)
    packed = packed.reshape(-1)
    small = [packed[i * part : (i + 1) * part] for i in range(8)]
    up_at = 8 * part
    root_squares = jnp.sqrt(packed[up_at + unit : up_at + unit + 2] / (devices * rows * width))
    return (
        layer_out,
        grad_x,
        grad_qkv_w,
        grad_out_w,
        grad_up_w,
        grad_down_w,
        small[0],
        small[1],
        small[2],
        small[3],
        small[4],
        small[5],
        small[6],
        packed[up_at : up_at + unit],
        small[7],
        root_squares,
    )


def solution(mesh):
    matrix, vector, table = P(BOTH, None), P(BOTH), P("dp", None)
    return jax.shard_map(
        per_device,
        mesh=mesh,
        in_specs=(matrix,) * 6 + (vector,) * 9 + (table,) * 3,
        out_specs=(matrix,) * 6 + (vector,) * 9 + (P(),),
        check_vma=False,
    )
```

```python
import functools
import math

import jax
import jax.numpy as jnp
from jax import lax
from jax.experimental import pallas as pl
from jax.experimental.pallas import tpu as pltpu
from jax.sharding import PartitionSpec as P

H = 32
HD = 64
BLK = 32

EPSILON = 1e-05
MASKED = -1e30
BF = jnp.bfloat16
F32 = jnp.float32
BOTH = ("dp", "fsdp")
MESH = pl.DeviceIdType.MESH
HBM = pl.BlockSpec(memory_space=pl.ANY)
VM = pl.BlockSpec(memory_space=pltpu.VMEM)
MIB = 2**20


def place():
    d, f = lax.axis_index("dp"), lax.axis_index("fsdp")
    return d // 2, d % 2, f // 2, f % 2


def at(x, c, z, y):
    return (x * 2 + c, z * 2 + y)


def remote(src, dst, send, recv, target):
    return pltpu.make_async_remote_copy(
        src_ref=src, dst_ref=dst, send_sem=send, recv_sem=recv, device_id=target, device_id_type=MESH
    )


def greet(partners):
    barrier = pltpu.get_barrier_semaphore()
    count = 0
    for condition, device in partners:

        @pl.when(condition)
        def _():
            pl.semaphore_signal(barrier, inc=1, device_id=device, device_id_type=MESH)

        count = count + jnp.asarray(condition).astype(jnp.int32)
    pl.semaphore_wait(barrier, count)


def greet_all(devices, fsdp, me):
    barrier = pltpu.get_barrier_semaphore()

    def one(k, _):
        other = (me + k) % devices
        pl.semaphore_signal(barrier, inc=1, device_id=(other // fsdp, other % fsdp), device_id_type=MESH)
        return 0

    lax.fori_loop(1, devices, one, 0)
    pl.semaphore_wait(barrier, devices - 1)


def line_partners(nz, pos):
    x, c, z, y = pos
    return [(z >= 0, at(x, 1 - c, z, y)), (z > 0, at(x, c, z - 1, y)), (z < nz - 1, at(x, c, z + 1, y))]


def rank_partners(nz, pos):
    x, c, z, y = pos
    n = 2 * nz
    others = [(z * 2 + c + k) % n for k in range(1, n)]
    return [(z >= 0, at(x, p % 2, p // 2, y)) for p in others]


def group_partners(pos):
    x, c, z, y = pos
    return [(z >= 0, at(x ^ (m // 2), c, z, y ^ (m % 2))) for m in (1, 2, 3)]


def line_gather(src, dst, send, recv, nz, swap, pos):
    x, c, z, y = pos
    own = z * 2 + c
    sib = at(x, 1 - c, z, y)
    up_dev, dn_dev = at(x, c, z + 1, y), at(x, c, z - 1, y)
    UP, DN, SU, SD = 0, nz, 2 * nz, 3 * nz
    OWN = 4 * nz

    def block(b, moved):
        return dst.at[b] if moved else src

    def up(k):
        b = (z - k) * 2 + c
        return remote(block(b, k or swap), dst.at[b], send.at[UP + k], recv.at[UP + k], up_dev)

    def dn(k):
        b = (z + k) * 2 + c
        return remote(block(b, k or swap), dst.at[b], send.at[DN + k], recv.at[DN + k], dn_dev)

    def side(k, base, sign):
        b = (z + sign * k) * 2 + c
        return remote(block(b, k or swap), dst.at[b], send.at[base + k], recv.at[base + k], sib)

    def got(b, sem):
        return remote(dst.at[b], dst.at[b], send.at[OWN], recv.at[sem], sib)

    local = pltpu.make_async_copy(src, dst.at[own], recv.at[OWN])
    trade = remote(src, dst.at[z * 2 + y], send.at[OWN], recv.at[OWN], at(x, y, z, c))

    def first():
        if swap:
            pl.when(c == y)(local.start)
            pl.when(c != y)(trade.start)
        else:
            local.start()

    def spread():
        if swap:
            local.wait()
        pl.when(z < nz - 1)(up(0).start)
        pl.when(z > 0)(dn(0).start)
        side(0, SU, 1).start()

    def step(k):
        @pl.when(z >= k)
        def _():
            got((z - k) * 2 + c, UP + k - 1).wait_recv()
            pl.when(z < nz - 1)(up(k).start)
            side(k, SU, -1).start()

        @pl.when(z + k < nz)
        def _():
            got((z + k) * 2 + c, DN + k - 1).wait_recv()
            pl.when(z > 0)(dn(k).start)
            side(k, SD, 1).start()

    def last():
        if swap:
            pl.when(c != y)(trade.wait_send)
        else:
            local.wait()
        got(z * 2 + 1 - c, SU).wait_recv()
        pl.when(z < nz - 1)(up(0).wait_send)
        pl.when(z > 0)(dn(0).wait_send)
        side(0, SU, 1).wait_send()
        for k in range(1, nz):

            @pl.when(z >= k)
            def _():
                got((z - k) * 2 + 1 - c, SU + k).wait_recv()
                pl.when(z < nz - 1)(up(k).wait_send)
                side(k, SU, -1).wait_send()

            @pl.when(z + k < nz)
            def _():
                got((z + k) * 2 + 1 - c, SD + k).wait_recv()
                pl.when(z > 0)(dn(k).wait_send)
                side(k, SD, 1).wait_send()

    return [first, spread] + [functools.partial(step, k) for k in range(1, nz)] + [last]


def gather_sems(nz):
    return [pltpu.SemaphoreType.DMA((4 * nz + 1,))] * 2


def gather_kernel(nz, src, dst, send, recv):
    pos = place()
    greet(line_partners(nz, pos))
    for stage in line_gather(src, dst, send, recv, nz, False, pos):
        stage()


def params(cid, vmem=None):
    return pltpu.CompilerParams(collective_id=cid, has_side_effects=True, vmem_limit_bytes=vmem)


def gather_tokens(a, nz, cid):
    return pl.pallas_call(
        functools.partial(gather_kernel, nz),
        out_shape=jax.ShapeDtypeStruct((2 * nz,) + a.shape, a.dtype),
        in_specs=[HBM],
        out_specs=HBM,
        scratch_shapes=gather_sems(nz),
        compiler_params=params(cid),
        name="gather_tokens",
    )(a)


def scatter_blocks(nz, pos, p, out, acc, ups, dns, send, recv):
    x, c, z, y = pos
    sib = at(x, 1 - c, z, y)
    S, U, D = 0, nz, 2 * nz

    def f(v):
        return v.astype(F32)

    def swap(t):
        return remote(p.at[t * 2 + 1 - c], acc.at[t], send.at[S + t], recv.at[S + t], sib)

    def up(t):
        return remote(acc.at[t], ups.at[t], send.at[U + t], recv.at[U + t], at(x, c, z + 1, y))

    def dn(t):
        return remote(acc.at[t], dns.at[t], send.at[D + t], recv.at[D + t], at(x, c, z - 1, y))

    order = []
    for i in range(nz - 1):
        order += [(True, nz - 1 - i), (False, i)]
    for upward, t in order:
        pl.when(z < t if upward else z > t)(swap(t).start)
    swap(z).start()
    for upward, t in order:

        @pl.when(z < t if upward else z > t)
        def _():
            swap(t).wait_recv()
            acc[t] = (f(acc[t]) + f(p[t * 2 + c])).astype(BF)
            move, came = (up, ups) if upward else (dn, dns)

            @pl.when(z > 0 if upward else z < nz - 1)
            def _():
                move(t).wait_recv()
                acc[t] = (f(acc[t]) + f(came[t])).astype(BF)

            move(t).start()

    swap(z).wait_recv()
    out[...] = f(acc[z]) + f(p[z * 2 + c])

    @pl.when(z > 0)
    def _():
        up(z).wait_recv()
        out[...] += f(ups[z])

    @pl.when(z < nz - 1)
    def _():
        dn(z).wait_recv()
        out[...] += f(dns[z])

    for t in range(nz):
        swap(t).wait_send()
        pl.when(z < t)(up(t).wait_send)
        pl.when(z > t)(dn(t).wait_send)


def scatter_scratch(nz, rows, width):
    return [pltpu.VMEM((nz, rows, width), BF)] * 3 + [pltpu.SemaphoreType.DMA((3 * nz,))] * 2


def scatter_kernel(nz, p, out, *scratch):
    pos = place()
    greet(line_partners(nz, pos))
    scatter_blocks(nz, pos, p, out, *scratch)


def scatter_tokens(p, nz, cid):
    blocks, rows, width = p.shape
    return pl.pallas_call(
        functools.partial(scatter_kernel, nz),
        out_shape=jax.ShapeDtypeStruct((rows, width), F32),
        in_specs=[VM],
        out_specs=VM,
        scratch_shapes=scatter_scratch(nz, rows, width),
        compiler_params=params(cid, 60 * MIB),
        name="scatter_tokens",
    )(p)


def scatter_and_hand_kernel(nz, kinds, runs, p, up_s, res, *refs):
    count = len(kinds)
    srcs, refs = refs[:count], refs[count:]
    out, up_o, res_o, refs = *refs[:3], refs[3:]
    dsts, refs = refs[:count], refs[count:]
    scratch, hsems, esems, tsems = refs[:5], refs[5:7], refs[7:9], refs[9:11]
    pos = place()
    x, c, z, y = pos
    greet(rank_partners(nz, pos) + group_partners(pos) + [(c != y, at(x, y, z, c))])
    hs = hand_stages(srcs, dsts, kinds, *hsems, nz, pos)
    es = exchange_stages(up_s, up_o, runs, *esems, nz, pos)
    ts = trade_stages(res, res_o, *tsems, pos)
    hs[0]()
    es[0]()
    ts[0]()
    scatter_blocks(nz, pos, p, out, *scratch)
    hs[1]()
    es[1]()
    ts[1]()


def scatter_and_hand(p, up_s, runs, res, arrays, kinds, nz, cid):
    blocks, rows, width = p.shape
    n, part, share = up_s.shape
    return pl.pallas_call(
        functools.partial(scatter_and_hand_kernel, nz, kinds, runs),
        out_shape=[
            jax.ShapeDtypeStruct((rows, width), F32),
            jax.ShapeDtypeStruct((part, n * share), BF),
            jax.ShapeDtypeStruct(res.shape, BF),
        ]
        + hand_shapes(arrays, kinds, nz),
        in_specs=[VM] + [HBM] * (2 + len(arrays)),
        out_specs=[VM] + [HBM] * (2 + len(arrays)),
        scratch_shapes=scatter_scratch(nz, rows, width) + hand_sems(kinds) + exchange_sems(runs, nz) + trade_sems(),
        compiler_params=params(cid, 60 * MIB),
        name="scatter_and_hand",
    )(p, up_s, res, *arrays)


def block_of(x, c, z, y, nz):
    return (x * 2 + c) * 2 * nz + z * 2 + y


def halves(ref, rows):
    half = rows // 2
    if half % 16:
        return {1: None, 2: ref}
    return {1: ref.at[pl.ds(half, half)], 2: ref.at[pl.ds(0, half)]}


def sliced_gather(src, dst, runs, sems, nz, pos):
    x, c, z, y = pos
    n = 2 * nz
    me = z * 2 + c
    part = dst.shape[1]
    send1, recv1, send2, recv2 = sems

    def pieces(p):
        if runs is None:
            return [(src.at[p], slice(None))]
        return [(src.at[:, pl.ds(there, size)], pl.ds(here, size)) for there, here, size in runs(p)]

    def row(p, gx, gy):
        return dst.at[block_of(gx, p % 2, p // 2, gy, nz)]

    mine = block_of(x, c, z, y, nz)

    def out(k):
        p = (me + k) % n
        return [
            remote(a, dst.at[mine, :, b], send1.at[p], recv1.at[me], at(x, p % 2, p // 2, y))
            for a, b in pieces(p)
        ]

    local = [pltpu.make_async_copy(a, dst.at[mine, :, b], recv1.at[me]) for a, b in pieces(me)]

    def came(k):
        return (me - k + n) % n

    def arrival(b, sem):
        return remote(b, b, send1.at[me], sem, at(x, 1 - c, z, y))

    def neighbour(m):
        return at(x ^ (m // 2), c, z, y ^ (m % 2))

    def forward(k, m):
        p = came(k)
        b = row(p, x, y)
        slot = (m - 1) * n + p
        return remote(b, b, send2.at[slot], recv2.at[slot], neighbour(m))

    def relay(k, m):
        p = came(k)
        b = halves(row(p, x ^ (m // 2), y ^ (m % 2)), part)[m]
        slot = (1 + m) * n + p
        return b is not None and remote(b, b, send2.at[slot], recv2.at[slot], neighbour(3 - m))

    def first():
        for copy in local:
            copy.start()
        for k in range(1, n):
            for copy in out(k):
                copy.start()

    def step(k):
        p = came(k)
        arrival(row(p, x, y), recv1.at[p]).wait_recv()
        for m in (1, 2):
            forward(k, m).start()

    def pass_on(k):
        p = came(k)
        for m in (1, 2):
            arrival(row(p, x ^ (m // 2), y ^ (m % 2)), recv2.at[(m - 1) * n + p]).wait_recv()
            if relay(k, m):
                relay(k, m).start()

    def last():
        for k in range(n):
            p = came(k)
            parts = halves(row(p, 1 - x, 1 - y), part)
            for m in (1, 2):
                if parts[m] is not None:
                    arrival(parts[m], recv2.at[(1 + m) * n + p]).wait_recv()
        for k in range(n):
            if k:
                p = (me + k) % n
                b = dst.at[mine]
                remote(b, b, send1.at[p], recv1.at[me], at(x, p % 2, p // 2, y)).wait_send()
            for m in (1, 2):
                forward(k, m).wait_send()
                if relay(k, m):
                    relay(k, m).wait_send()

    stages = [functools.partial(step, k) for k in range(n)] + [functools.partial(pass_on, k) for k in range(n)]
    return [first] + stages + [last]


def sliced_sems(nz):
    n = 2 * nz
    return [pltpu.SemaphoreType.DMA((n,))] * 2 + [pltpu.SemaphoreType.DMA((4 * n,))] * 2


def group_gather(src, dst, send, recv, pos):
    x, c, z, y = pos
    rows = src.shape[0]
    local = pltpu.make_async_copy(src, dst.at[x * 2 + y], recv.at[0])

    def there(m):
        return dst.at[(x ^ (m // 2)) * 2 + (y ^ (m % 2))]

    def neighbour(m):
        return at(x ^ (m // 2), c, z, y ^ (m % 2))

    def out(m):
        return remote(src, dst.at[x * 2 + y], send.at[m], recv.at[m], neighbour(m))

    def relay(m):
        b = halves(there(m), rows)[m]
        return b is not None and remote(b, b, send.at[2 + m], recv.at[2 + m], neighbour(3 - m))

    def arrival(b, sem):
        return remote(b, b, send.at[0], sem, at(x, 1 - c, z, y))

    def first():
        local.start()
        for m in (1, 2):
            out(m).start()

    def pass_on():
        for m in (1, 2):
            arrival(there(m), recv.at[m]).wait_recv()
            if relay(m):
                relay(m).start()

    def last():
        local.wait()
        parts = halves(there(3), rows)
        for m in (1, 2):
            if parts[m] is not None:
                arrival(parts[m], recv.at[2 + m]).wait_recv()
            out(m).wait_send()
            if relay(m):
                relay(m).wait_send()

    return [first, pass_on, last]


def full_gather(src, dst, send, recv, nz, pos):
    x, c, z, y = pos
    rows = src.shape[0]
    sib = at(x, 1 - c, z, y)
    mine = dst.at[block_of(x, c, z, y, nz)]

    def row(core, k, m):
        return dst.at[block_of(x ^ (m // 2), core, z + k, y ^ (m % 2), nz)]

    def neighbour(m):
        return at(x ^ (m // 2), c, z, y ^ (m % 2))

    def arrival(b, sem):
        return remote(b, b, send.at[0], recv.at[sem], sib)

    def along(k, sign):
        b = row(c, k, 0)
        return remote(
            b if k else src, b, send.at[(0 if sign > 0 else nz) + z + k], recv.at[z + k], at(x, c, z + sign, y)
        )

    def forward(k, m):
        b = row(c, k, 0)
        return remote(b if k else src, b, send.at[(1 + m) * nz + z + k], recv.at[m * nz + z + k], neighbour(m))

    def relay(k, m):
        b = halves(row(c, k, m), rows)[m]
        if b is None:
            return None
        return remote(b, b, send.at[(3 + m) * nz + z + k], recv.at[(2 + m) * nz + z + k], neighbour(3 - m))

    def side(k, m):
        b = row(c, k, m)
        return remote(b if k or m else src, b, send.at[(6 + m) * nz + z + k], recv.at[(5 + m) * nz + z + k], sib)

    local = pltpu.make_async_copy(src, mine, recv.at[z])

    def first():
        local.start()
        pl.when(z < nz - 1)(along(0, 1).start)
        pl.when(z > 0)(along(0, -1).start)
        for m in (1, 2):
            forward(0, m).start()
        side(0, 0).start()

    def both(k, fn):
        @pl.when(z >= k)
        def _():
            fn(-k)

        if k:

            @pl.when(z + k < nz)
            def _():
                fn(k)

    def step(k):
        def one(k):
            arrival(row(c, k, 0), z + k).wait_recv()
            if k > 0:
                pl.when(z > 0)(along(k, -1).start)
            else:
                pl.when(z < nz - 1)(along(k, 1).start)
            for m in (1, 2):
                forward(k, m).start()
            side(k, 0).start()

        both(k, one)

    def pass_on(k):
        def one(k):
            for m in (1, 2):
                arrival(row(c, k, m), m * nz + z + k).wait_recv()
                if relay(k, m) is not None:
                    relay(k, m).start()
                side(k, m).start()

        both(k, one)

    def diagonal(k):
        def one(k):
            parts = halves(row(c, k, 3), rows)
            for m in (1, 2):
                if parts[m] is not None:
                    arrival(parts[m], (2 + m) * nz + z + k).wait_recv()
            side(k, 3).start()

        both(k, one)

    def last():
        local.wait()

        def one(k):
            for m in range(4):
                arrival(row(1 - c, k, m), (5 + m) * nz + z + k).wait_recv()
                side(k, m).wait_send()
            if k >= 0:
                pl.when(z > 0)(along(k, -1).wait_send)
            if k <= 0:
                pl.when(z < nz - 1)(along(k, 1).wait_send)
            for m in (1, 2):
                forward(k, m).wait_send()
                if relay(k, m) is not None:
                    relay(k, m).wait_send()

        for k in range(nz):
            both(k, one)

    return (
        [first]
        + [functools.partial(step, k) for k in range(1, nz)]
        + [functools.partial(pass_on, k) for k in range(nz)]
        + [functools.partial(diagonal, k) for k in range(nz)]
        + [last]
    )


def full_sems(nz):
    return [pltpu.SemaphoreType.DMA((10 * nz,)), pltpu.SemaphoreType.DMA((9 * nz,))]


def head_runs(nz, cols):
    return lambda p: [
        (block_of(x, p % 2, p // 2, 0, nz) * HD, x * cols // 2, cols // 2) for x in range(2)
    ]


def up_runs(nz, unit):
    return lambda p: [(block_of(x, p % 2, p // 2, 0, nz) * unit, x * 2 * unit, 2 * unit) for x in range(2)]


def qkv_runs(nz, width, cols):
    runs = head_runs(nz, cols)
    return lambda p: [(j * width + there, j * cols + here, size) for j in range(3) for there, here, size in runs(p)]


def fetch_kernel(
    nz, width, cols, x_in, w_qkv, w_down, vec, tab, x_all, qkv_w, down_w, vecs, tab_out, *sems
):
    pos = place()
    x, c, z, y = pos
    fsdp = 2 * nz
    devices = 4 * fsdp
    me = (x * 2 + c) * fsdp + z * 2 + y
    x_sems, qkv_sems, vec_sems, tab_sems, down_sems = sems[:2], sems[2:6], sems[6:8], sems[8:10], sems[10:]
    greet_all(devices, fsdp, me)

    def vec_copy(other):
        return remote(vec, vecs.at[me], vec_sems[0].at[other], vec_sems[1].at[me], (other // fsdp, other % fsdp))

    def each(fn):
        def body(k, _):
            fn((me + k) % devices)
            return 0

        lax.fori_loop(1, devices, body, 0)

    vec_local = pltpu.make_async_copy(vec, vecs.at[me], vec_sems[1].at[me])
    tab_local = pltpu.make_async_copy(tab, tab_out, tab_sems[1].at[0])
    tab_trade = remote(tab, tab_out, tab_sems[0].at[0], tab_sems[1].at[0], at(x, y, z, c))

    gx = line_gather(x_in, x_all, *x_sems, nz, True, pos)
    runs = qkv_runs(nz, width, cols) if len(w_qkv.shape) == 2 else None
    gq = sliced_gather(w_qkv, qkv_w, runs, qkv_sems, nz, pos)
    gx[0]()
    gq[0]()
    gx[1]()
    vec_local.start()
    each(lambda other: vec_copy(other).start())
    pl.when(c == y)(tab_local.start)
    pl.when(c != y)(tab_trade.start)
    gd = group_gather(w_down, down_w, *down_sems, pos)
    for stage in gq[1 : fsdp + 1]:
        stage()
    gx[2]()
    gd[0]()
    for stage in gx[3:-1]:
        stage()
    for stage in gq[fsdp + 1 :]:
        stage()
    gx[-1]()
    for stage in gd[1:]:
        stage()

    def vec_done(other):
        remote(vec, vecs.at[other], vec_sems[0].at[other], vec_sems[1].at[other], at(x, 1 - c, z, y)).wait_recv()
        vec_copy(other).wait_send()

    vec_local.wait()
    each(vec_done)
    tab_local.wait()
    pl.when(c != y)(tab_trade.wait_send)


def fetch(nz, x_in, w_qkv, w_down, part, vec, tab, cid):
    rows, width = x_in.shape
    n = 2 * nz
    devices = 4 * n
    cols = width // n
    shapes = [
        ((n, rows, width), BF),
        ((devices, part, 3 * cols), BF),
        ((4,) + w_down.shape, BF),
        ((devices,) + vec.shape, F32),
        (tab.shape, jnp.int32),
    ]
    return pl.pallas_call(
        functools.partial(fetch_kernel, nz, width, cols),
        out_shape=[jax.ShapeDtypeStruct(s, t) for s, t in shapes],
        in_specs=[HBM] * 5,
        out_specs=[HBM] * 5,
        scratch_shapes=gather_sems(nz)
        + sliced_sems(nz)
        + [pltpu.SemaphoreType.DMA((devices,))] * 2
        + [pltpu.SemaphoreType.DMA((1,))] * 2
        + [pltpu.SemaphoreType.DMA((5,))] * 2,
        compiler_params=params(cid),
        name="fetch",
    )(x_in, w_qkv, w_down, vec, tab)


def hand_stages(srcs, dsts, kinds, send, recv, nz, pos):
    x, c, z, y = pos
    n = 2 * nz
    count = len(kinds)

    def copies(i, m):
        gx, gy = x ^ (m // 2), y ^ (m % 2)
        sem = i * 3 + m - 1
        target = at(gx, c, z, gy)
        if not kinds[i]:
            return [remote(srcs[i].at[gx * 2 + gy], dsts[i].at[m - 1], send.at[sem], recv.at[sem], target)]
        return [
            remote(
                srcs[i].at[block_of(gx, p % 2, p // 2, gy, nz)],
                dsts[i].at[m - 1, p],
                send.at[sem],
                recv.at[sem],
                target,
            )
            for p in range(n)
        ]

    def first():
        for i in range(count):
            for m in (3, 1, 2):
                for copy in copies(i, m):
                    copy.start()

    def last():
        for i in range(count):
            for m in (1, 2, 3):
                sem = i * 3 + m - 1
                there = dsts[i].at[m - 1]
                whole = remote(there, there, send.at[sem], recv.at[sem], at(x, 1 - c, z, y))
                whole.wait_recv()
                whole.wait_send()

    return [first, last]


def hand_shapes(arrays, kinds, nz):
    return [
        jax.ShapeDtypeStruct((3, 2 * nz) + a.shape[1:] if k else (3,) + a.shape[1:], a.dtype)
        for a, k in zip(arrays, kinds)
    ]


def hand_sems(kinds):
    return [pltpu.SemaphoreType.DMA((3 * len(kinds),))] * 2


def exchange_stages(src, dst, runs, send, recv, nz, pos):
    x, c, z, y = pos
    n = 2 * nz
    me = z * 2 + c

    def give(to, p):
        if runs is None:
            return [(src.at[to], dst.at[p])]
        return [(src.at[to, :, pl.ds(here, size)], dst.at[:, pl.ds(there, size)]) for there, here, size in runs(p)]

    width = len(give(0, 0))

    def move(p):
        return [
            remote(a, b, send.at[p * width + i], recv.at[me * width + i], at(x, p % 2, p // 2, y))
            for i, (a, b) in enumerate(give(p, me))
        ]

    def come(p):
        return [
            remote(b, b, send.at[me * width + i], recv.at[p * width + i], at(x, 1 - c, z, y))
            for i, (_, b) in enumerate(give(me, p))
        ]

    local = [pltpu.make_async_copy(a, b, recv.at[me * width + i]) for i, (a, b) in enumerate(give(me, me))]

    def first():
        for copy in local:
            copy.start()
        for k in range(1, n):
            for copy in move((me + k) % n):
                copy.start()

    def last():
        for copy in local:
            copy.wait()
        for k in range(1, n):
            for copy in come((me - k + n) % n):
                copy.wait_recv()
            for copy in move((me + k) % n):
                copy.wait_send()

    return [first, last]


def exchange_sems(runs, nz):
    width = 1 if runs is None else len(runs(0))
    return [pltpu.SemaphoreType.DMA((width * 2 * nz,))] * 2


def exchange_kernel(nz, src, dst, send, recv):
    pos = place()
    greet(rank_partners(nz, pos))
    for stage in exchange_stages(src, dst, None, send, recv, nz, pos):
        stage()


def exchange(a, nz, cid, name):
    return pl.pallas_call(
        functools.partial(exchange_kernel, nz),
        out_shape=jax.ShapeDtypeStruct(a.shape, a.dtype),
        in_specs=[HBM],
        out_specs=HBM,
        scratch_shapes=exchange_sems(None, nz),
        compiler_params=params(cid),
        name=name,
    )(a)


def trade_stages(src, dst, send, recv, pos):
    x, c, z, y = pos
    local = pltpu.make_async_copy(src, dst, recv.at[0])
    trade = remote(src, dst, send.at[0], recv.at[0], at(x, y, z, c))

    def first():
        pl.when(c == y)(local.start)
        pl.when(c != y)(trade.start)

    def last():
        local.wait()
        pl.when(c != y)(trade.wait_send)

    return [first, last]


def trade_sems():
    return [pltpu.SemaphoreType.DMA((1,))] * 2


def finish_kernel(nz, runs, has, *refs):
    grad, small, *refs = refs
    qkv_s = refs.pop(0) if has else None
    grad_out, small_out, *refs = refs
    qkv_o = refs.pop(0) if has else None
    came, send, recv, *sems = refs
    pos = place()
    x, c, z, y = pos
    fsdp = 2 * nz
    devices = 4 * fsdp
    me = (x * 2 + c) * fsdp + z * 2 + y
    es = exchange_stages(qkv_s, qkv_o, runs, *sems[2:], nz, pos) if has else [lambda: None] * 2
    ts = trade_stages(grad, grad_out, *sems[:2], pos)
    greet_all(devices, fsdp, me)

    def each(fn):
        def body(k, _):
            fn((me + k) % devices)
            return 0

        lax.fori_loop(1, devices, body, 0)

    def share(other):
        return remote(small.at[other], came.at[me], send.at[other], recv.at[me], (other // fsdp, other % fsdp))

    es[0]()
    ts[0]()
    each(lambda other: share(other).start())

    def done(other):
        remote(small.at[me], came.at[other], send.at[other], recv.at[other], at(x, 1 - c, z, y)).wait_recv()
        share(other).wait_send()

    each(done)
    came[me] = small[me]
    small_out[...] = jnp.sum(came[...], axis=0)
    ts[1]()
    es[1]()


def finish(grad, small, qkv_s, runs, nz, cid):
    devices = small.shape[0]
    has = qkv_s is not None
    shapes = [jax.ShapeDtypeStruct(grad.shape, grad.dtype), jax.ShapeDtypeStruct(small.shape[1:], F32)]
    if has:
        out_shape = qkv_s.shape if runs is None else (qkv_s.shape[1], qkv_s.shape[0] * qkv_s.shape[2])
        shapes.append(jax.ShapeDtypeStruct(out_shape, BF))
    return pl.pallas_call(
        functools.partial(finish_kernel, nz, runs, has),
        out_shape=shapes,
        in_specs=[HBM, VM] + [HBM] * has,
        out_specs=[HBM, VM] + [HBM] * has,
        scratch_shapes=[pltpu.VMEM(small.shape, F32)]
        + [pltpu.SemaphoreType.DMA((devices,))] * 2
        + trade_sems()
        + (exchange_sems(runs, nz) if has else []),
        compiler_params=params(cid, 32 * MIB),
        name="finish",
    )(*((grad, small, qkv_s) if has else (grad, small)))


def dot(a, b, dims):
    return lax.dot_general(a, b, (dims, ((), ())), preferred_element_type=F32)


NN = ((1,), (0,))
NT = ((1,), (1,))
TN = ((0,), (0,))


def scatter_parts(nz, pos, own, other, acc, came, send, recv):
    x, c, z, y = pos
    S, U, D = 0, nz, 2 * nz
    sib = at(x, 1 - c, z, y)

    def f(v):
        return v.astype(F32)

    def swap(t):
        return remote(other(t), acc.at[t], send.at[S + t], recv.at[S + t], sib)

    def rise(t):
        return remote(acc.at[t], came.at[t], send.at[U + t], recv.at[U + t], at(x, c, z + 1, y))

    def fall(t):
        slot = jnp.where(z - 1 == t, nz, t)
        return remote(acc.at[t], came.at[slot], send.at[D + t], recv.at[D + t], at(x, c, z - 1, y))

    def arrival(slot, sem):
        return remote(came.at[slot], came.at[slot], send.at[S], recv.at[sem], sib)

    def event(t, upward):
        swap(t).wait_recv()

        @pl.when(z > 0 if upward else z < nz - 1)
        def _():
            arrival(t, (U if upward else D) + t).wait_recv()
            acc[t] = (f(acc[t]) + f(own(t)) + f(came[t])).astype(BF)

        @pl.when(z == 0 if upward else z == nz - 1)
        def _():
            acc[t] = (f(acc[t]) + f(own(t))).astype(BF)

        (rise if upward else fall)(t).start()

    def events(s):
        for t in range(nz):
            zz = s - t
            if 0 <= zz < t:
                pl.when(z == zz)(functools.partial(event, t, True))
            zz = 2 * (nz - 1) - s - t
            if t < zz < nz:
                pl.when(z == zz)(functools.partial(event, t, False))

    def total(out):
        swap(z).wait_recv()
        out[...] = f(acc[z]) + f(own(z))

        @pl.when(z > 0)
        def _():
            arrival(z, U + z).wait_recv()
            out[...] += f(came[z])

        @pl.when(z < nz - 1)
        def _():
            arrival(nz, D + z).wait_recv()
            out[...] += f(came[nz])

    def done():
        for t in range(nz):
            swap(t).wait_send()
            pl.when(z < t)(lambda t=t: rise(t).wait_send())
            pl.when(z > t)(lambda t=t: fall(t).wait_send())

    return swap, events, total, done


def reduce_parts(src, mine, near, far, send, recv, lsem, pos):
    x, c, z, y = pos
    half = src.shape[1] // 2

    def f(v):
        return v.astype(F32)

    def share(gx, gy, lower):
        return src.at[gx * 2 + gy, pl.ds(lower * half, half)]

    parts = [(x, y, 0), (x, y, 1), (x, 1 - y, 0), (1 - x, y, 1)]
    loads = [pltpu.make_async_copy(share(*p), mine.at[i], lsem.at[i]) for i, p in enumerate(parts)]
    along_x, along_y = at(1 - x, c, z, y), at(x, c, z, 1 - y)

    def out(i):
        a, b, target = [
            (share(1 - x, y, 0), near.at[0, 0], along_x),
            (share(1 - x, 1 - y, 0), near.at[0, 1], along_x),
            (share(x, 1 - y, 1), near.at[1, 0], along_y),
            (share(1 - x, 1 - y, 1), near.at[1, 1], along_y),
        ][i]
        return remote(a, b, send.at[i], recv.at[i], target)

    def on(i):
        return remote(near.at[i, 1], far.at[i], send.at[4 + i], recv.at[4 + i], [along_y, along_x][i])

    def first():
        for i in (1, 3, 0, 2):
            out(i).start()
        for copy in loads:
            copy.start()

    def second():
        for copy in loads:
            copy.wait()
        for i in range(2):
            out(2 * i + 1).wait_recv()
            near[i, 1] = (f(near[i, 1]) + f(mine[2 + i])).astype(BF)
            on(i).start()

    def total(put):
        for i in range(2):
            out(2 * i).wait_recv()
            on(i).wait_recv()
            put(i, f(mine[i]) + f(near[i, 0]) + f(far[i]))

    def done():
        for i in range(4):
            out(i).wait_send()
        for i in range(2):
            on(i).wait_send()

    return first, second, total, done


def reduce_scratch(rows, width):
    half = rows // 2
    return [
        pltpu.VMEM((4, half, width), BF),
        pltpu.VMEM((2, 2, half, width), BF),
        pltpu.VMEM((2, half, width), BF),
        pltpu.SemaphoreType.DMA((6,)),
        pltpu.SemaphoreType.DMA((6,)),
        pltpu.SemaphoreType.DMA((4,)),
    ]


def tail_kernel(
    heads, nz, runs_up, runs_qkv, slopes, far_in, grad_in, joined, a1_in, mixed, qkv_in, branch, upd_in, up_src, down_src,
    base, grad_out, down_o, out_o, col_o, square_o, up_o, qkv_o, branch_all, layer_o, grad_s, *refs,
):
    refs = list(refs)

    def take(n):
        got = refs[:n]
        del refs[:n]
        return got

    gap_s, tokens, qkv_w, grad_joined, acc_k, acc_v = take(6)
    upd_own, upd_acc, upd_came, upd_send, upd_recv = take(5)
    att_p, att_acc, att_came, att_send, att_recv = take(5)
    up_refs, down_refs, qkv_refs, out_refs = take(6), take(6), take(6), take(6)
    up_sum, qkv_sum, qkv_g, out_g, res, res_low = take(6)
    gsems, esems, esems_up, esems_qkv, tsems = take(2), take(2), take(2), take(2), take(2)
    gap_sem, load_sem = take(2)

    pos = place()
    x, c, z, y = pos
    n = 2 * nz
    tree, cols = mixed.shape
    rows, width = branch.shape
    part = up_sum.shape[1]
    rank = z * 2 + c
    step = gap_s.shape[2]

    es = exchange_stages(grad_in, grad_s, None, *esems, nz, pos)
    gb = line_gather(branch, branch_all, *gsems, nz, False, pos)
    up1, up2, up_total, up_done = reduce_parts(up_src, *up_refs, pos)
    down1, down2, down_total, down_done = reduce_parts(down_src, *down_refs, pos)
    qkv1, qkv2, qkv_total, qkv_done = reduce_parts(qkv_g, *qkv_refs, pos)
    out1, out2, out_total, out_done = reduce_parts(out_g, *out_refs, pos)
    upd_swap, upd_events, upd_total, upd_done = scatter_parts(
        nz, pos, lambda t: upd_own[t], lambda t: upd_in.at[t * 2 + 1 - c], upd_acc, upd_came, upd_send, upd_recv
    )
    att_swap, att_events, att_total, att_done = scatter_parts(
        nz, pos, lambda t: att_p[t * 2 + c], lambda t: att_p.at[t * 2 + 1 - c], att_acc, att_came, att_send, att_recv
    )
    ex_up = exchange_stages(up_sum, up_o, runs_up, *esems_up, nz, pos)
    ex_qkv = exchange_stages(qkv_sum, qkv_o, runs_qkv, *esems_qkv, nz, pos)
    home = trade_stages(res_low, layer_o, *tsems, pos)
    loads = [pltpu.make_async_copy(upd_in.at[t * 2 + c], upd_own.at[t], load_sem.at[t]) for t in range(nz)]
    load_w = pltpu.make_async_copy(qkv_in, qkv_w, load_sem.at[nz])
    load_a = pltpu.make_async_copy(a1_in, tokens, load_sem.at[nz + 1])
    load_b = pltpu.make_async_copy(branch_all, tokens, load_sem.at[nz + 2])

    def gap_load(i, slot):
        return pltpu.make_async_copy(
            far_in.at[:, pl.ds(pl.multiple_of(i * step, step), step)], gap_s.at[slot], gap_sem.at[slot]
        )

    greet(rank_partners(nz, pos) + group_partners(pos) + [(c != y, at(x, y, z, c))])
    es[0]()
    up1()
    gb[0]()
    gb[1]()
    for t in list(range(nz - 1, 0, -1)) + [0]:
        upd_swap(t).start()
    gap_load(0, 0).start()
    for copy in loads + [load_w, load_a]:
        copy.start()
    acc_k[...] = jnp.zeros_like(acc_k)
    acc_v[...] = jnp.zeros_like(acc_v)
    for copy in loads:
        copy.wait()
    es[1]()

    steps = tree // step

    def attend_step(i, _):
        slot = i % 2
        gap_load(i, slot).wait()
        pl.when(i + 1 < steps)(lambda: gap_load(i + 1, 1 - slot).start())
        gap = gap_s[slot]
        here = pl.ds(pl.multiple_of(i * step, step), step)
        per = step // rows
        grads = grad_s[pl.ds(i * per, per)].reshape(step, cols)
        for h in range(heads):
            lane = slice(h * HD, (h + 1) * HD)
            q = joined[here, lane]
            k = joined[:, cols + h * HD : cols + (h + 1) * HD]
            v = joined[:, 2 * cols + h * HD : 2 * cols + (h + 1) * HD]
            g = grads[:, lane]
            logits = dot(k, q, NT) * HD ** (-0.5) + slopes[h] * gap
            weights = jnp.exp(logits - jnp.max(logits, axis=0, keepdims=True))
            probs = weights * (1.0 / jnp.sum(weights, axis=0, keepdims=True))
            grad_probs = dot(v, g, NT)
            delta = jnp.sum(probs * grad_probs, axis=0, keepdims=True)
            grad_raw = (probs * (grad_probs - delta) * HD ** (-0.5)).astype(BF)
            acc_v[:, lane] += dot(probs.astype(BF), g, NN)
            acc_k[:, lane] += dot(grad_raw, q, NN)
            grad_joined[here, lane] = dot(grad_raw, k, TN).astype(BF)

        def later(k, fns):
            @pl.when(i == k)
            def _():
                for fn in fns:
                    fn()

        later(0, [down1, lambda: upd_events(0)])
        later(1, [gb[2], lambda: upd_events(1)])
        later(2, [up2] + gb[3:4] + [lambda: upd_events(2)])
        later(3, gb[4:5] + [lambda: upd_events(3)])
        return 0

    lax.fori_loop(0, steps, attend_step, 0)
    grad_joined[:, cols : 2 * cols] = acc_k[...].astype(BF)
    grad_joined[:, 2 * cols :] = acc_v[...].astype(BF)
    load_w.wait()

    def back(t, _):
        here = pl.ds(pl.multiple_of(t * 2 * rows, 2 * rows), 2 * rows)

        def tile(j, _):
            w = pl.ds(pl.multiple_of(j * 512, 512), 512)
            att_p[pl.ds(t * 2, 2), :, w] = dot(grad_joined[here, :], qkv_w[w, :], NT).astype(BF).reshape(2, rows, 512)
            return 0

        lax.fori_loop(0, width // 512, tile, 0)
        att_swap(t).start()
        return 0

    lax.fori_loop(0, nz, back, 0)
    col_o[...] = jnp.sum(grad_joined[...].astype(F32), axis=0, keepdims=True)
    load_a.wait()
    blocks = 256 // part

    def qkv_tile(j, _):
        w = pl.ds(pl.multiple_of(j * 256, 256), 256)
        value = dot(tokens[:, :, w].reshape(tree, 256), grad_joined[...], TN).astype(BF)
        for i in range(blocks):
            r = j * blocks + i
            d, f = r // n, r % n
            p = f // 2 * 2 + d % 2
            qkv_g[d // 2 * 2 + f % 2, pl.ds(pl.multiple_of(p * part, part), part), :] = value[i * part : (i + 1) * part]
        return 0

    att_events(0)
    lax.fori_loop(0, width // 256, qkv_tile, 0)
    qkv1()
    upd_events(4)
    att_events(1)
    down2()
    for stage in gb[5:]:
        stage()
    load_b.start()
    load_b.wait()

    def out_tile(j, _):
        w = pl.ds(pl.multiple_of(j * 512, 512), 512)
        value = dot(mixed[...], tokens[:, :, w].reshape(tree, 512), TN).astype(BF)
        out_g[:, :, w] = value.reshape(4, cols // 4, 512)
        return 0

    lax.fori_loop(0, width // 512, out_tile, 0)
    out1()
    upd_events(5)
    att_events(2)

    def put_ranks(dest):
        def put(lower, value):
            dest[pl.ds(lower * nz, nz)] = value.astype(BF).reshape(nz, part, -1)

        return put

    up_total(put_ranks(up_sum))
    ex_up[0]()
    upd_events(6)
    upd_total(res)
    res[...] += base[...]
    res_low[...] = res[...].astype(BF)
    home[0]()
    square_o[...] = jnp.sum(res[...] * res[...], axis=0, keepdims=True)
    att_events(3)
    qkv2()
    att_events(4)
    out2()

    def put_down(lower, value):
        half = value.shape[0]
        down_o[pl.ds(lower * half, half), :] = value

    down_total(put_down)
    att_events(5)
    att_events(6)
    att_total(grad_out)
    ex_up[1]()

    def put_out(lower, value):
        half = value.shape[0]
        out_o[pl.ds(lower * half, half), :] = value

    out_total(put_out)
    qkv_total(put_ranks(qkv_sum))
    ex_qkv[0]()
    home[1]()
    ex_qkv[1]()
    for fn in (up_done, down_done, qkv_done, out_done, upd_done, att_done):
        fn()


def tail_call(slopes, far_t, grad, joined, a1, mixed, qkv_w, branch, upd, up_g, down_g, base, runs, heads, nz, cid):
    tree, cols = mixed.shape
    rows, width = branch.shape
    n = 2 * nz
    part = width // (4 * n)
    unit = down_g.shape[1]
    step = 256
    runs_up, runs_qkv = runs
    shape = jax.ShapeDtypeStruct

    def scatter_refs(own):
        return [
            pltpu.VMEM((own, rows, width), BF),
            pltpu.VMEM((nz, rows, width), BF),
            pltpu.VMEM((nz + 1, rows, width), BF),
            pltpu.SemaphoreType.DMA((3 * nz,)),
            pltpu.SemaphoreType.DMA((3 * nz,)),
        ]

    return pl.pallas_call(
        functools.partial(tail_kernel, heads, nz, runs_up, runs_qkv),
        out_shape=[
            shape((rows, width), F32),
            shape((unit, width), F32),
            shape((part, width), F32),
            shape((1, 3 * cols), F32),
            shape((1, width), F32),
            shape((part, 4 * n * unit), BF),
            shape((part, 3 * width), BF),
            shape((n, rows, width), BF),
            shape((rows, width), BF),
        ],
        in_specs=[pl.BlockSpec(memory_space=pltpu.SMEM), HBM, HBM, VM, HBM, VM, HBM, HBM, HBM, HBM, HBM, VM],
        out_specs=[VM] * 5 + [HBM] * 4,
        scratch_shapes=[
            pltpu.VMEM((n, rows, cols), BF),
            pltpu.VMEM((2, tree, step), F32),
            pltpu.VMEM((n, rows, width), BF),
            pltpu.VMEM((width, 3 * cols), BF),
            pltpu.VMEM((tree, 3 * cols), BF),
            pltpu.VMEM((tree, cols), F32),
            pltpu.VMEM((tree, cols), F32),
        ]
        + scatter_refs(nz)
        + scatter_refs(n)
        + reduce_scratch(n * part, 4 * unit)
        + reduce_scratch(unit, width)
        + reduce_scratch(n * part, 3 * cols)
        + reduce_scratch(part, width)
        + [
            pltpu.VMEM((n, part, 4 * unit), BF),
            pltpu.VMEM((n, part, 3 * cols), BF),
            pltpu.VMEM((4, n * part, 3 * cols), BF),
            pltpu.VMEM((4, part, width), BF),
            pltpu.VMEM((rows, width), F32),
            pltpu.VMEM((rows, width), BF),
        ]
        + gather_sems(nz)
        + exchange_sems(None, nz)
        + exchange_sems(runs_up, nz)
        + exchange_sems(runs_qkv, nz)
        + trade_sems()
        + [pltpu.SemaphoreType.DMA((2,)), pltpu.SemaphoreType.DMA((nz + 3,))],
        compiler_params=params(cid, 63 * MIB),
        name="tail",
    )(slopes, far_t, grad, joined, a1, mixed, qkv_w, branch, upd, up_g, down_g, base)


def gelu_and_slope(value):
    normal = 0.5 + 0.5 * lax.erf(value * math.sqrt(0.5))
    density = jnp.exp(-0.5 * value * value) * (1.0 / math.sqrt(2.0 * math.pi))
    return value * normal, normal + value * density


def mlp_kernel(
    nz, own, cot_in, up_in, down_in, bias, out, upd_out, up_out, down_out, bias_g,
    mlp, cot, up_w, down_w, p, upd, up_g, down_g, active, gh, acc, ups, dns, gsend, grecv, ssend, srecv, lsem,
):
    pos = place()
    x, c, z, y = pos
    blocks, rows, width = mlp.shape
    units = active.shape[1]
    pair = 2 * rows
    me = z * 2 + c
    sib = at(x, 1 - c, z, y)
    up_dev, dn_dev = at(x, c, z + 1, y), at(x, c, z - 1, y)
    UP, DN, SU, SD = 0, nz, 2 * nz, 3 * nz
    S, U, D = 0, nz, 2 * nz

    def f(v):
        return v.astype(F32)

    loads = [
        pltpu.make_async_copy(a, b, lsem.at[i])
        for i, (a, b) in enumerate([(cot_in, cot), (down_in, down_w), (up_in, up_w)])
    ]
    part = up_out.shape[1] // blocks

    def rank_rows(r):
        d, f = r // blocks, r % blocks
        return up_out.at[d // 2 * 2 + f % 2, pl.ds((f // 2 * 2 + d % 2) * part, part)]

    stores = [
        [pltpu.make_async_copy(upd, upd_out, lsem.at[3])],
        [
            pltpu.make_async_copy(up_g.at[pl.ds(r * part, part)], rank_rows(r), lsem.at[5 + r])
            for r in range(4 * blocks)
        ],
        [pltpu.make_async_copy(down_g, down_out, lsem.at[4])],
    ]

    def store(i):
        for copy in stores[i]:
            copy.start()


    def block(b, sem, target):
        return remote(mlp.at[b], mlp.at[b], gsend.at[sem], grecv.at[sem], target)

    def up(d):
        return block((z - d) * 2 + c, UP + d, up_dev)

    def dn(d):
        return block((z + d) * 2 + c, DN + d, dn_dev)

    def side(d, below):
        return block(jnp.where(below, z - d, z + d) * 2 + c, jnp.where(below, SU, SD) + d, sib)

    def turn(i):
        both = jnp.minimum(z, nz - 1 - z)
        two = i <= 2 * both
        d = jnp.where(two, (i + 1) // 2, i - both)
        below = jnp.where(two, i % 2 == 1, z > nz - 1 - z)
        return d, below

    def arrive(i):
        if i == 0:
            block(z * 2 + 1 - c, SU, sib).wait_recv()
            return z
        d, below = turn(i)
        zi = jnp.where(below, z - d, z + d)
        block(zi * 2 + c, jnp.where(below, UP, DN) + d - 1, sib).wait_recv()
        pl.when(below & (z < nz - 1))(lambda: up(d).start())
        pl.when(jnp.logical_not(below) & (z > 0))(lambda: dn(d).start())
        side(d, below).start()
        block(zi * 2 + 1 - c, jnp.where(below, SU, SD) + d, sib).wait_recv()
        return zi

    def swap(t):
        return remote(p.at[t * 2 + 1 - c], acc.at[t], ssend.at[S + t], srecv.at[S + t], sib)

    def rise(t):
        return remote(acc.at[t], ups.at[t], ssend.at[U + t], srecv.at[U + t], up_dev)

    def fall(t):
        return remote(acc.at[t], dns.at[t], ssend.at[D + t], srecv.at[D + t], dn_dev)

    def event(t, upward):
        swap(t).wait_recv()
        acc[t] = (f(acc[t]) + f(p[t * 2 + c])).astype(BF)
        move, came = (rise, ups) if upward else (fall, dns)

        @pl.when(z > 0 if upward else z < nz - 1)
        def _():
            move(t).wait_recv()
            acc[t] = (f(acc[t]) + f(came[t])).astype(BF)

        move(t).start()

    def events(s):
        for t in range(nz):
            zz = s - t
            if 0 <= zz < t:
                pl.when(z == zz)(functools.partial(event, t, True))
            zz = 2 * (nz - 1) - s - t
            if t < zz < nz:
                pl.when(z == zz)(functools.partial(event, t, False))

    def at_rows(ref, zi):
        return ref[pl.ds(zi * 2, 2)].reshape(pair, width)

    def hidden_part(zi, early):
        here = pl.ds(pl.multiple_of(zi * pair, pair), pair)

        def tile(j, _):
            u = pl.ds(pl.multiple_of(j * 256, 256), 256)
            value = dot(at_rows(mlp, zi), up_w[:, u], NN) + bias[:, u]
            grad = dot(at_rows(cot, zi), down_w[u, :], NT)
            act, slope = gelu_and_slope(value)
            low = (grad * slope).astype(BF)
            active[here, u] = act.astype(BF)
            gh[here, u] = low
            bias_g[:, u] += jnp.sum(f(low), axis=0, keepdims=True)
            return 0

        lax.fori_loop(0, units // 256, tile, 0)

        def back(j, _):
            w = pl.ds(pl.multiple_of(j * 512, 512), 512)
            p[pl.ds(zi * 2, 2), :, w] = dot(gh[here, :], up_w[w, :], NT).astype(BF).reshape(2, rows, 512)
            return 0

        lax.fori_loop(0, width // 512, back, 0)

    def forward_part(zi):
        here = pl.ds(pl.multiple_of(zi * pair, pair), pair)

        def tile(j, _):
            w = pl.ds(pl.multiple_of(j * 512, 512), 512)
            upd[pl.ds(zi * 2, 2), :, w] = dot(active[here, :], down_w[:, w], NN).astype(BF).reshape(2, rows, 512)
            return 0

        lax.fori_loop(0, width // 512, tile, 0)

    def up_grads(first, count):
        def tile(j, _):
            w = pl.ds(pl.multiple_of(j * 256, 256), 256)
            up_g[w, :] = dot(mlp[:, :, w].reshape(blocks * rows, 256), gh[...], TN).astype(BF)
            return 0

        lax.fori_loop(first, first + count, tile, 0)

    def down_grads():
        def tile(j, _):
            u = pl.ds(pl.multiple_of(j * 256, 256), 256)
            down_g[u, :] = dot(active[:, u], cot[...].reshape(blocks * rows, width), TN).astype(BF)
            return 0

        lax.fori_loop(0, units // 256, tile, 0)

    mlp[me] = own[...]
    greet(line_partners(nz, pos))
    pl.when(z < nz - 1)(up(0).start)
    pl.when(z > 0)(dn(0).start)
    side(0, z >= 0).start()
    for copy in loads:
        copy.start()
    bias_g[...] = jnp.zeros_like(bias_g)
    for copy in loads:
        copy.wait()
    slots = 2 * nz - 1
    tiles = width // 256
    for s in range(slots):
        if s < nz:
            zi = arrive(s)
            hidden_part(zi, s)
            swap(zi).start()
        events(s)
        if s < nz:
            forward_part(zi)
        if s == nz - 1:
            store(0)
            down_grads()
            store(2)
        elif s == nz:
            up_grads(0, tiles // 2)
        elif s == nz + 1:
            up_grads(tiles // 2, tiles - tiles // 2)
            store(1)
    swap(z).wait_recv()
    out[...] = f(acc[z]) + f(p[z * 2 + c])

    @pl.when(z > 0)
    def _():
        rise(z).wait_recv()
        out[...] += f(ups[z])

    @pl.when(z < nz - 1)
    def _():
        fall(z).wait_recv()
        out[...] += f(dns[z])

    for copies in stores:
        for copy in copies:
            copy.wait()
    side(0, z >= 0).wait_send()
    pl.when(z < nz - 1)(up(0).wait_send)
    pl.when(z > 0)(dn(0).wait_send)
    for k in range(1, nz):

        @pl.when(z >= k)
        def _():
            pl.when(z < nz - 1)(up(k).wait_send)
            side(k, z >= 0).wait_send()

        @pl.when(z + k < nz)
        def _():
            pl.when(z > 0)(dn(k).wait_send)
            side(k, z < 0).wait_send()

    for t in range(nz):
        swap(t).wait_send()
        pl.when(z < t)(rise(t).wait_send)
        pl.when(z > t)(fall(t).wait_send)


def mlp_bytes(nz, rows, width, units):
    tree = 2 * nz * rows
    return 2 * (4 * tree * width + 4 * units * width + 2 * tree * units + 3 * nz * rows * width) + 8 * rows * width


def mlp_call(own, cot, up_w, down_w, bias, nz, cid):
    rows, width = own.shape
    units = down_w.shape[0]
    n = 2 * nz
    shape = jax.ShapeDtypeStruct
    return pl.pallas_call(
        functools.partial(mlp_kernel, nz),
        out_shape=[
            shape((rows, width), F32),
            shape((n, rows, width), BF),
            shape((4, width // 4, units), BF),
            shape((units, width), BF),
            shape((1, units), F32),
        ],
        in_specs=[VM, HBM, HBM, HBM, VM],
        out_specs=[VM, HBM, HBM, HBM, VM],
        scratch_shapes=[
            pltpu.VMEM((n, rows, width), BF),
            pltpu.VMEM((n, rows, width), BF),
            pltpu.VMEM((width, units), BF),
            pltpu.VMEM((units, width), BF),
            pltpu.VMEM((n, rows, width), BF),
            pltpu.VMEM((n, rows, width), BF),
            pltpu.VMEM((width, units), BF),
            pltpu.VMEM((units, width), BF),
            pltpu.VMEM((n * rows, units), BF),
            pltpu.VMEM((n * rows, units), BF),
        ]
        + [pltpu.VMEM((nz, rows, width), BF)] * 3
        + gather_sems(nz)
        + [pltpu.SemaphoreType.DMA((3 * nz,))] * 2
        + [pltpu.SemaphoreType.DMA((5 + 4 * n,))],
        compiler_params=params(cid, 62 * MIB),
        name="mlp",
    )(own, cot, up_w, down_w, bias)


def attend_kernel(
    heads, nz, unit, slopes, far, joined_q, joined, cot, w_up, w_out, out, cot_all, up_w, out_w, *sems
):
    cols = heads * HD
    step, steps = pl.program_id(0), pl.num_programs(0)
    pos = place()
    n = 2 * nz
    gc = line_gather(cot, cot_all, *sems[:2], nz, True, pos)
    gu = sliced_gather(w_up, up_w, up_runs(nz, unit), sems[2:6], nz, pos)
    go = full_gather(w_out, out_w, *sems[6:8], nz, pos)

    @pl.when(step == 0)
    def _():
        x, c, z, y = pos
        greet(rank_partners(nz, pos) + group_partners(pos) + [(c != y, at(x, y, z, c))])
        gc[0]()
        gu[0]()
        go[0]()

    @pl.when(step == 1)
    def _():
        for stage in go[1:nz]:
            stage()

    @pl.when(step == 2)
    def _():
        for stage in gu[1 : n + 1]:
            stage()
        gc[1]()

    gap = far[...]
    for h in range(heads):
        q = joined_q[:, h * HD : (h + 1) * HD]
        k = joined[:, cols + h * HD : cols + (h + 1) * HD]
        v = joined[:, 2 * cols + h * HD : 2 * cols + (h + 1) * HD]
        logits = dot(q, k, NT) * HD ** (-0.5) + slopes[h] * gap
        weights = jnp.exp(logits - jnp.max(logits, axis=1, keepdims=True))
        probs = weights * (1.0 / jnp.sum(weights, axis=1, keepdims=True))
        out[:, h * HD : (h + 1) * HD] = dot(probs.astype(BF), v, NN).astype(BF)

    @pl.when(step == steps - 1)
    def _():
        for stage in go[nz : 2 * nz]:
            stage()
        ahead, later = gc[2:-1], gu[n + 1 : -1]
        for i, stage in enumerate(ahead):
            stage()
            for other in later[i * n // len(ahead) : (i + 1) * n // len(ahead)]:
                other()
        for stage in go[2 * nz :]:
            stage()
        gc[-1]()
        gu[-1]()


def attend(slopes, far, joined, cot, w_up, w_out, unit, heads, nz, cid):
    tree = far.shape[0]
    cols = heads * HD
    rows = min(256, max(128, 2**18 // tree))
    block, width = cot.shape
    part = w_up.shape[0]
    n = 2 * nz
    shapes = [(tree, cols), (n, block, width), (4 * n, part, 4 * unit), (4 * n, part, width)]
    return pl.pallas_call(
        functools.partial(attend_kernel, heads, nz, unit),
        out_shape=[jax.ShapeDtypeStruct(s, BF) for s in shapes],
        grid=(tree // rows,),
        in_specs=[
            pl.BlockSpec(memory_space=pltpu.SMEM),
            pl.BlockSpec((rows, tree), lambda i: (i, 0)),
            pl.BlockSpec((rows, 3 * cols), lambda i: (i, 0)),
            pl.BlockSpec((tree, 3 * cols), lambda i: (0, 0)),
            HBM,
            HBM,
            HBM,
        ],
        out_specs=[pl.BlockSpec((rows, cols), lambda i: (i, 0)), HBM, HBM, HBM],
        scratch_shapes=gather_sems(nz) + sliced_sems(nz) + full_sems(nz),
        compiler_params=params(cid, 56 * MIB),
        name="attend",
    )(slopes, far, joined, joined, cot, w_up, w_out)


def attend_back_kernel(heads, nz, kinds, slopes, far, joined_q, joined, grad, branch, part_sums, *refs):
    count = len(kinds)
    srcs, refs = refs[:count], refs[count:]
    out_q, out_k, out_v, branch_all, update, refs = *refs[:5], refs[5:]
    dsts, refs = refs[:count], refs[count:]
    acc_k, acc_v, p, refs = *refs[:3], refs[3:]
    scratch, gsems, hsems, psem = refs[:5], refs[5:7], refs[7:9], refs[9]
    cols = heads * HD
    step = pl.program_id(0)
    pos = place()
    gb = line_gather(branch, branch_all, *gsems, nz, False, pos)
    hs = hand_stages(srcs, dsts, kinds, *hsems, nz, pos)
    load = pltpu.make_async_copy(part_sums, p, psem.at[0])

    @pl.when(step == 0)
    def _():
        acc_k[...] = jnp.zeros_like(acc_k)
        acc_v[...] = jnp.zeros_like(acc_v)
        greet(line_partners(nz, pos) + group_partners(pos))
        hs[0]()
        gb[0]()
        gb[1]()
        load.start()

    @pl.when(step == 3)
    def _():
        gb[2]()

    gap = far[...]
    for h in range(heads):
        here = slice(h * HD, (h + 1) * HD)
        q = joined_q[:, here]
        k = joined[:, cols + h * HD : cols + (h + 1) * HD]
        v = joined[:, 2 * cols + h * HD : 2 * cols + (h + 1) * HD]
        g = grad[:, here]
        logits = dot(k, q, NT) * HD ** (-0.5) + slopes[h] * gap
        weights = jnp.exp(logits - jnp.max(logits, axis=0, keepdims=True))
        probs = weights * (1.0 / jnp.sum(weights, axis=0, keepdims=True))
        grad_probs = dot(v, g, NT)
        delta = jnp.sum(probs * grad_probs, axis=0, keepdims=True)
        grad_raw = (probs * (grad_probs - delta) * HD ** (-0.5)).astype(BF)
        acc_v[:, here] += dot(probs.astype(BF), g, NN)
        acc_k[:, here] += dot(grad_raw, q, NN)
        out_q[:, here] = dot(grad_raw, k, TN).astype(BF)

    @pl.when(step == pl.num_programs(0) - 1)
    def _():
        out_k[...] = acc_k[...].astype(BF)
        out_v[...] = acc_v[...].astype(BF)
        for stage in gb[3:]:
            stage()
        load.wait()
        scatter_blocks(nz, pos, p, update, *scratch)
        hs[1]()


def attend_back(slopes, far_t, joined, grad, branch, part_sums, arrays, kinds, heads, nz, cid):
    tree = far_t.shape[0]
    cols = heads * HD
    rows = min(256, max(128, 2**18 // tree))
    block, width = branch.shape
    full = pl.BlockSpec((tree, cols), lambda i: (0, 0))
    part = pl.BlockSpec((rows, cols), lambda i: (i, 0))
    return pl.pallas_call(
        functools.partial(attend_back_kernel, heads, nz, kinds),
        out_shape=[jax.ShapeDtypeStruct((tree, cols), BF)] * 3
        + [jax.ShapeDtypeStruct((2 * nz, block, width), BF), jax.ShapeDtypeStruct((block, width), F32)]
        + hand_shapes(arrays, kinds, nz),
        grid=(tree // rows,),
        in_specs=[
            pl.BlockSpec(memory_space=pltpu.SMEM),
            pl.BlockSpec((tree, rows), lambda i: (0, i)),
            pl.BlockSpec((rows, 3 * cols), lambda i: (i, 0)),
            pl.BlockSpec((tree, 3 * cols), lambda i: (0, 0)),
            part,
            HBM,
            HBM,
        ]
        + [HBM] * len(arrays),
        out_specs=[part, full, full, HBM, pl.BlockSpec((block, width), lambda i: (0, 0))] + [HBM] * len(arrays),
        scratch_shapes=[pltpu.VMEM((tree, cols), F32)] * 2
        + [pltpu.VMEM((2 * nz, block, width), BF)]
        + scatter_scratch(nz, block, width)
        + gather_sems(nz)
        + hand_sems(kinds)
        + [pltpu.SemaphoreType.DMA((1,))],
        compiler_params=params(cid, 62 * MIB),
        name="attend_back",
    )(slopes, far_t, joined, joined, grad, branch, part_sums, *arrays)


def norm_parts(values):
    center = values - jnp.mean(values, axis=-1, keepdims=True)
    inverse = lax.rsqrt(jnp.mean(center * center, axis=-1, keepdims=True) + EPSILON)
    return (center * inverse, inverse)


def norm_back(grad_normed, normed, inverse):
    mean_grad = jnp.mean(grad_normed, axis=-1, keepdims=True)
    mean_cross = jnp.mean(grad_normed * normed, axis=-1, keepdims=True)
    return inverse * (grad_normed - mean_grad - normed * mean_cross)


def tree_tables(parents, seg_blocks, valid):
    segments = parents.shape[0]
    seg_tokens = jnp.broadcast_to(seg_blocks[:, None], (seg_blocks.shape[0], BLK)).reshape(-1)
    labels = jnp.arange(segments, dtype=jnp.int32)
    member = (seg_tokens[:, None] == labels[None, :]).astype(jnp.int32)
    counted = member * valid[:, None]
    before = jnp.cumsum(counted, axis=0) - counted
    rank = jnp.sum(before * member, axis=1)
    seg_len = jnp.sum(counted, axis=0)
    picked = (parents[:, None] == labels[None, :]).astype(jnp.int32)
    grand = jnp.sum(picked * parents[None, :], axis=1)
    ancestor = ((labels[None, :] == parents[:, None]) | (labels[None, :] == grand[:, None])) & (
        labels[None, :] != labels[:, None]
    )
    offset = jnp.sum(ancestor.astype(jnp.int32) * seg_len[None, :], axis=1)
    position = jnp.sum(member * offset[None, :], axis=1) + rank
    return (seg_tokens, position, ancestor.astype(jnp.float32))


def allowed_mask(seg, index, valid, ancestor):
    labels = jnp.arange(ancestor.shape[0], dtype=jnp.int32)
    member = (seg[:, None] == labels[None, :]).astype(jnp.float32)
    reach = jnp.dot(jnp.dot(member, ancestor), member.T) > 0.5
    causal = (seg[:, None] == seg[None, :]) & (index[None, :] <= index[:, None])
    visible = (valid[None, :] == 1) | (index[None, :] == index[:, None])
    return (reach | causal) & visible


def gelu_exact(value):
    return jax.nn.gelu(value, approximate=False)


def mm(spec, a, b):
    return jnp.einsum(spec, a, b, preferred_element_type=F32)


def padded(flat, lanes):
    return jnp.pad(flat, [(0, 0)] * (flat.ndim - 1) + [(0, -flat.shape[-1] % lanes)])


def per_device(
    layer_in,
    cotangent,
    w_qkv,
    w_out,
    w_up,
    w_down,
    gain_attn,
    shift_attn,
    bias_query,
    bias_value,
    bias_out,
    gain_mlp,
    shift_mlp,
    bias_up,
    bias_down,
    parents,
    seg_blocks,
    token_valid,
):
    rows, width = layer_in.shape
    fsdp = lax.axis_size("fsdp")
    nz = fsdp // 2
    devices = 4 * fsdp
    x, c, z, y = place()
    rank = z * 2 + c
    heads = H // fsdp
    cols = heads * HD
    tree = token_valid.shape[1]
    part = w_up.shape[0]
    unit = w_down.shape[0]

    vec = jnp.concatenate(
        [gain_attn, shift_attn, bias_query, bias_value, bias_out, gain_mlp, shift_mlp, bias_down, bias_up]
    ).astype(F32)
    vec = padded(vec, 1024).reshape(-1, 128)
    tab = jnp.concatenate([token_valid[0], seg_blocks[0], parents[0]])
    tab = padded(tab, 1024).reshape(-1, 128)
    aligned = part == HD and cols % 256 == 0
    if not aligned:
        w_qkv = w_qkv.reshape(part, 3, fsdp, cols).transpose(2, 0, 1, 3).reshape(fsdp, part, 3 * cols)
    x_all, qkv_w, down_w, vecs, tab = fetch(nz, layer_in, w_qkv, w_down, part, vec, tab, 1)
    down_w = down_w.reshape(4 * unit, width)
    x_all = x_all.reshape(tree, width)
    qkv_w = qkv_w.reshape(width, 3 * cols)
    vecs = vecs.reshape(devices, -1)
    (gain_one, shift_one, query_bias, value_bias, out_bias, gain_two, shift_two, down_bias) = [
        vecs[:, i * part : (i + 1) * part].reshape(-1) for i in range(8)
    ]
    up_bias = vecs[:, 8 * part : 8 * part + unit].reshape(2, 2, nz, 2, unit)
    up_bias = lax.dynamic_slice(up_bias, (0, c, z, 0, 0), (2, 1, 1, 2, unit)).reshape(-1)

    def own_rows(v):
        return lax.dynamic_slice_in_dim(v, rank * rows, rows, 0)

    normed_all, _ = norm_parts(x_all.astype(F32))
    attn_in = (normed_all * gain_one + shift_one).astype(BF)
    inputs = own_rows(x_all).astype(F32)
    normed_one, inverse_one = norm_parts(inputs)

    if aligned:

        def own_cols(v):
            v = v.reshape(2, 2, nz, 2, HD)
            return lax.dynamic_slice(v, (0, c, z, 0, 0), (2, 1, 1, 2, HD)).reshape(-1)

        def spread(v):
            v = v.reshape(2, 1, 1, 2, HD)
            return lax.dynamic_update_slice(jnp.zeros((2, 2, nz, 2, HD), F32), v, (0, c, z, 0, 0))

        numbers = block_of(jnp.arange(2)[:, None], c, z, jnp.arange(2)[None, :], nz).reshape(-1)
    else:

        def own_cols(v):
            return lax.dynamic_slice_in_dim(v, rank * cols, cols, 0)

        def spread(v):
            return lax.dynamic_update_slice_in_dim(jnp.zeros((width,), F32), v, rank * cols, 0)

        numbers = rank * heads + jnp.arange(heads)

    joined_bias = jnp.concatenate([own_cols(query_bias), jnp.zeros((cols,), F32), own_cols(value_bias)])
    joined = (jnp.dot(attn_in, qkv_w, preferred_element_type=F32) + joined_bias).astype(BF)

    tab = tab.reshape(-1)
    blocks = seg_blocks.shape[1]
    valid = tab[:tree]
    seg, position, ancestor = tree_tables(
        tab[tree + blocks : tree + blocks + parents.shape[1]], tab[tree : tree + blocks], valid
    )
    index = jnp.arange(tree, dtype=jnp.int32)
    mask = allowed_mask(seg, index, valid, ancestor)
    far = jnp.where(mask, (position[None, :] - position[:, None]).astype(F32), MASKED)
    slopes = jnp.exp2(-8.0 * (numbers.astype(F32) + 1.0) / H)
    mixed, cot, up_w, out_w = attend(slopes, far, joined, cotangent, w_up, w_out, unit, heads, nz, 9)
    out_w = out_w.reshape(width, width)
    cot = cot.reshape(tree, width)
    up_w = up_w.reshape(width, 4 * unit)

    mixed_own = exchange(mixed.reshape(fsdp, rows, cols), nz, 2, "mixed_to_tokens")
    if aligned:
        mixed_own = mixed_own.reshape(nz, 2, rows, 2, 2 * HD).transpose(2, 3, 1, 0, 4).reshape(rows, width)
    else:
        mixed_own = mixed_own.transpose(1, 0, 2).reshape(rows, width)
    branch = jnp.dot(mixed_own, out_w, preferred_element_type=F32) + out_bias
    middle = inputs + branch
    normed_two, inverse_two = norm_parts(middle)
    mlp_own = (normed_two * gain_two + shift_two).astype(BF)
    cot_blocks = cot.reshape(fsdp, rows, width)
    fused = aligned and nz == 4 and mlp_bytes(nz, rows, width, 4 * unit) < 50 * MIB
    if fused:
        grad_mlp_in, update, up_g, down_g, grad_bias_up = mlp_call(
            mlp_own, cot_blocks, up_w, down_w, up_bias[None], nz, 3
        )
        grad_bias_up = grad_bias_up[0]
    else:
        mlp_in = gather_tokens(mlp_own, nz, 3).reshape(tree, width)
        hidden = jnp.dot(mlp_in, up_w, preferred_element_type=F32) + up_bias
        active_float, gelu_pull = jax.vjp(gelu_exact, hidden)
        active = active_float.astype(BF)
        grad_active = mm("td,fd->tf", cot, down_w)
        grad_hidden = gelu_pull(grad_active)[0].astype(BF)
        grad_mlp_in = mm("tf,df->td", grad_hidden, up_w).astype(BF).reshape(fsdp, rows, width)
        grad_mlp_in = scatter_tokens(grad_mlp_in, nz, 4)
        update = jnp.dot(active, down_w, preferred_element_type=F32).astype(BF).reshape(fsdp, rows, width)
        down_g = mm("tf,td->fd", active, cot).astype(BF)
        up_g = mm("td,tf->df", mlp_in, grad_hidden).astype(BF)
        grad_bias_up = jnp.sum(grad_hidden.astype(F32), axis=0)
    down_g = down_g.reshape(4, unit, width)
    cot_own = own_rows(cot).astype(F32)
    grad_middle = cot_own + norm_back(grad_mlp_in * gain_two, normed_two, inverse_two)
    grad_branch = grad_middle.astype(BF)
    grad_mixed = mm("te,de->td", grad_branch, out_w).astype(BF)
    if not aligned:
        grad_out_w = lax.psum_scatter(
            mm("td,te->de", mixed_own, grad_branch).astype(BF), BOTH, scatter_dimension=0, tiled=True
        ).astype(F32)
    if aligned:
        grad_mixed = grad_mixed.reshape(rows, 2, 2, nz, 2 * HD).transpose(3, 2, 0, 1, 4).reshape(fsdp, rows, cols)
    else:
        grad_mixed = grad_mixed.reshape(rows, fsdp, cols).transpose(1, 0, 2)
    if fused:
        runs = up_runs(nz, unit), qkv_runs(nz, width, cols)
        grad_attn_in, grad_down_w, grad_out_w, col, square, grad_up_w, grad_qkv_w, _, layer_out = tail_call(
            slopes, far.T, grad_mixed, joined, attn_in.reshape(fsdp, rows, width), mixed, qkv_w, grad_branch,
            update, up_g, down_g, middle + down_bias, runs, heads, nz, 6,
        )
        col, square = col[0], jnp.sum(square)
    else:
        up_g = up_g.reshape(devices, part, 4 * unit)
        grad_heads = exchange(grad_mixed, nz, 5, "grad_to_heads")
        grad_heads = grad_heads.reshape(tree, cols)
        grad_q, grad_k, grad_v, branch_all, update, down_c, up_c = attend_back(
            slopes, far.T, joined, grad_heads, grad_branch, update, [down_g, up_g], (False, True), heads, nz, 6
        )
        result = middle + update + down_bias
        grad_joined = jnp.concatenate([grad_q, grad_k, grad_v], axis=1)

        def mine(g, came):
            g = g.reshape((2, 2, nz, 2) + g.shape[1:])
            g = lax.dynamic_slice(g, (x, 0, 0, y, 0, 0), (1, 2, nz, 1) + g.shape[4:])
            g = g.reshape((2, nz) + g.shape[4:]).swapaxes(0, 1)
            return (g.reshape(came.shape[1:]).astype(F32) + jnp.sum(came.astype(F32), axis=0)).astype(BF)

        def mine_flat(g, came):
            return lax.dynamic_index_in_dim(g, x * 2 + y, 0, keepdims=False).astype(F32) + jnp.sum(came.astype(F32), axis=0)

        grad_down_w = mine_flat(down_g, down_c)
        qkv_g = mm("td,te->de", attn_in, grad_joined).astype(BF).reshape(devices, part, 3 * cols)
        flat = []
        if aligned:
            flat = [mm("td,te->de", mixed, branch_all.reshape(tree, width)).astype(BF).reshape(4, part, width)]
        kinds = (True,) + (False,) * len(flat)
        grad_attn_in = mm("te,de->td", grad_joined, qkv_w).astype(BF).reshape(fsdp, rows, width)
        grad_attn_in, grad_up_w, layer_out, qkv_c, *out_c = scatter_and_hand(
            grad_attn_in, mine(up_g, up_c), up_runs(nz, unit), result.astype(BF), [qkv_g] + flat, kinds, nz, 10
        )
        grad_up_w = grad_up_w.astype(F32)
        if aligned:
            grad_out_w = mine_flat(flat[0], out_c[0])
        col, square = jnp.sum(grad_joined.astype(F32), axis=0), jnp.sum(result * result)
    grad_up_w = grad_up_w.astype(F32)
    grad_inputs = grad_middle + norm_back(grad_attn_in * gain_one, normed_one, inverse_one)

    smalls = [
        jnp.sum(grad_attn_in * normed_one, axis=0),
        jnp.sum(grad_attn_in, axis=0),
        spread(col[:cols]),
        spread(col[2 * cols :]),
        jnp.sum(grad_branch.astype(F32), axis=0),
        jnp.sum(grad_mlp_in * normed_two, axis=0),
        jnp.sum(grad_mlp_in, axis=0),
        jnp.sum(cot_own, axis=0),
    ]
    grad_bias_up = grad_bias_up.reshape(2, 1, 1, 2, unit)
    grad_bias_up = lax.dynamic_update_slice(jnp.zeros((2, 2, nz, 2, unit), F32), grad_bias_up, (0, c, z, 0, 0))
    squares = jnp.stack([square, jnp.sum(branch * branch)])
    packed = jnp.concatenate(
        [v.reshape(devices, part) for v in smalls]
        + [grad_bias_up.reshape(devices, unit), jnp.broadcast_to(squares, (devices, 2))],
        axis=1,
    )
    packed = padded(packed, 1024).reshape(devices, -1, 128)
    if fused:
        grad_x, packed = finish(grad_inputs.astype(BF), packed, None, None, nz, 8)
    else:
        runs = qkv_runs(nz, width, cols) if aligned else None
        grad_x, packed, grad_qkv_w = finish(grad_inputs.astype(BF), packed, mine(qkv_g, qkv_c), runs, nz, 8)
    if not aligned:
        grad_qkv_w = grad_qkv_w.reshape(fsdp, part, 3, cols).transpose(1, 2, 0, 3).reshape(part, -1)
    grad_qkv_w = grad_qkv_w.astype(F32)
    packed = packed.reshape(-1)
    small = [packed[i * part : (i + 1) * part] for i in range(8)]
    up_at = 8 * part
    root_squares = jnp.sqrt(packed[up_at + unit : up_at + unit + 2] / (devices * rows * width))
    return (
        layer_out,
        grad_x,
        grad_qkv_w,
        grad_out_w,
        grad_up_w,
        grad_down_w,
        small[0],
        small[1],
        small[2],
        small[3],
        small[4],
        small[5],
        small[6],
        packed[up_at : up_at + unit],
        small[7],
        root_squares,
    )


def solution(mesh):
    matrix, vector, table = P(BOTH, None), P(BOTH), P("dp", None)
    return jax.shard_map(
        per_device,
        mesh=mesh,
        in_specs=(matrix,) * 6 + (vector,) * 9 + (table,) * 3,
        out_specs=(matrix,) * 6 + (vector,) * 9 + (P(),),
        check_vma=False,
    )
```

```python
import functools
import math

import jax
import jax.numpy as jnp
import numpy as np
from jax import lax
from jax.experimental import pallas as pl
from jax.experimental.pallas import tpu as pltpu
from jax.sharding import PartitionSpec as P

H = 32
HD = 64
BLK = 32

EPSILON = 1e-05
MASKED = -1e30
BF = jnp.bfloat16
F32 = jnp.float32
BOTH = ("dp", "fsdp")
MESH = pl.DeviceIdType.MESH
HBM = pl.BlockSpec(memory_space=pl.ANY)
VM = pl.BlockSpec(memory_space=pltpu.VMEM)
MIB = 2**20


def place():
    d, f = lax.axis_index("dp"), lax.axis_index("fsdp")
    return d // 2, d % 2, f // 2, f % 2


def at(x, c, z, y):
    return (x * 2 + c, z * 2 + y)


def remote(src, dst, send, recv, target):
    return pltpu.make_async_remote_copy(
        src_ref=src, dst_ref=dst, send_sem=send, recv_sem=recv, device_id=target, device_id_type=MESH
    )


def greet(partners):
    barrier = pltpu.get_barrier_semaphore()
    count = 0
    for condition, device in partners:

        @pl.when(condition)
        def _():
            pl.semaphore_signal(barrier, inc=1, device_id=device, device_id_type=MESH)

        count = count + jnp.asarray(condition).astype(jnp.int32)
    pl.semaphore_wait(barrier, count)


def greet_all(devices, fsdp, me):
    barrier = pltpu.get_barrier_semaphore()

    def one(k, _):
        other = (me + k) % devices
        pl.semaphore_signal(barrier, inc=1, device_id=(other // fsdp, other % fsdp), device_id_type=MESH)
        return 0

    lax.fori_loop(1, devices, one, 0)
    pl.semaphore_wait(barrier, devices - 1)


def line_partners(nz, pos):
    x, c, z, y = pos
    return [(z >= 0, at(x, 1 - c, z, y)), (z > 0, at(x, c, z - 1, y)), (z < nz - 1, at(x, c, z + 1, y))]


def rank_partners(nz, pos):
    x, c, z, y = pos
    n = 2 * nz
    others = [(z * 2 + c + k) % n for k in range(1, n)]
    return [(z >= 0, at(x, p % 2, p // 2, y)) for p in others]


def group_partners(pos):
    x, c, z, y = pos
    return [(z >= 0, at(x ^ (m // 2), c, z, y ^ (m % 2))) for m in (1, 2, 3)]


def line_gather(src, dst, send, recv, nz, swap, pos):
    x, c, z, y = pos
    own = z * 2 + c
    sib = at(x, 1 - c, z, y)
    up_dev, dn_dev = at(x, c, z + 1, y), at(x, c, z - 1, y)
    UP, DN, SU, SD = 0, nz, 2 * nz, 3 * nz
    OWN = 4 * nz

    def block(b, moved):
        return dst.at[b] if moved else src

    def up(k):
        b = (z - k) * 2 + c
        return remote(block(b, k or swap), dst.at[b], send.at[UP + k], recv.at[UP + k], up_dev)

    def dn(k):
        b = (z + k) * 2 + c
        return remote(block(b, k or swap), dst.at[b], send.at[DN + k], recv.at[DN + k], dn_dev)

    def side(k, base, sign):
        b = (z + sign * k) * 2 + c
        return remote(block(b, k or swap), dst.at[b], send.at[base + k], recv.at[base + k], sib)

    def got(b, sem):
        return remote(dst.at[b], dst.at[b], send.at[OWN], recv.at[sem], sib)

    local = pltpu.make_async_copy(src, dst.at[own], recv.at[OWN])
    trade = remote(src, dst.at[z * 2 + y], send.at[OWN], recv.at[OWN], at(x, y, z, c))

    def first():
        if swap:
            pl.when(c == y)(local.start)
            pl.when(c != y)(trade.start)
        else:
            local.start()

    def spread():
        if swap:
            local.wait()
        pl.when(z < nz - 1)(up(0).start)
        pl.when(z > 0)(dn(0).start)
        side(0, SU, 1).start()

    def step(k):
        @pl.when(z >= k)
        def _():
            got((z - k) * 2 + c, UP + k - 1).wait_recv()
            pl.when(z < nz - 1)(up(k).start)
            side(k, SU, -1).start()

        @pl.when(z + k < nz)
        def _():
            got((z + k) * 2 + c, DN + k - 1).wait_recv()
            pl.when(z > 0)(dn(k).start)
            side(k, SD, 1).start()

    def last():
        if swap:
            pl.when(c != y)(trade.wait_send)
        else:
            local.wait()
        got(z * 2 + 1 - c, SU).wait_recv()
        pl.when(z < nz - 1)(up(0).wait_send)
        pl.when(z > 0)(dn(0).wait_send)
        side(0, SU, 1).wait_send()
        for k in range(1, nz):

            @pl.when(z >= k)
            def _():
                got((z - k) * 2 + 1 - c, SU + k).wait_recv()
                pl.when(z < nz - 1)(up(k).wait_send)
                side(k, SU, -1).wait_send()

            @pl.when(z + k < nz)
            def _():
                got((z + k) * 2 + 1 - c, SD + k).wait_recv()
                pl.when(z > 0)(dn(k).wait_send)
                side(k, SD, 1).wait_send()

    return [first, spread] + [functools.partial(step, k) for k in range(1, nz)] + [last]


def gather_sems(nz):
    return [pltpu.SemaphoreType.DMA((4 * nz + 1,))] * 2


def gather_kernel(nz, src, dst, send, recv):
    pos = place()
    greet(line_partners(nz, pos))
    for stage in line_gather(src, dst, send, recv, nz, False, pos):
        stage()


def params(cid, vmem=None):
    return pltpu.CompilerParams(collective_id=cid, has_side_effects=True, vmem_limit_bytes=vmem)


def gather_tokens(a, nz, cid):
    return pl.pallas_call(
        functools.partial(gather_kernel, nz),
        out_shape=jax.ShapeDtypeStruct((2 * nz,) + a.shape, a.dtype),
        in_specs=[HBM],
        out_specs=HBM,
        scratch_shapes=gather_sems(nz),
        compiler_params=params(cid),
        name="gather_tokens",
    )(a)


def scatter_blocks(nz, pos, p, out, acc, ups, dns, send, recv):
    x, c, z, y = pos
    sib = at(x, 1 - c, z, y)
    S, U, D = 0, nz, 2 * nz

    def f(v):
        return v.astype(F32)

    def swap(t):
        return remote(p.at[t * 2 + 1 - c], acc.at[t], send.at[S + t], recv.at[S + t], sib)

    def up(t):
        return remote(acc.at[t], ups.at[t], send.at[U + t], recv.at[U + t], at(x, c, z + 1, y))

    def dn(t):
        return remote(acc.at[t], dns.at[t], send.at[D + t], recv.at[D + t], at(x, c, z - 1, y))

    order = []
    for i in range(nz - 1):
        order += [(True, nz - 1 - i), (False, i)]
    for upward, t in order:
        pl.when(z < t if upward else z > t)(swap(t).start)
    swap(z).start()
    for upward, t in order:

        @pl.when(z < t if upward else z > t)
        def _():
            swap(t).wait_recv()
            acc[t] = (f(acc[t]) + f(p[t * 2 + c])).astype(BF)
            move, came = (up, ups) if upward else (dn, dns)

            @pl.when(z > 0 if upward else z < nz - 1)
            def _():
                move(t).wait_recv()
                acc[t] = (f(acc[t]) + f(came[t])).astype(BF)

            move(t).start()

    swap(z).wait_recv()
    out[...] = f(acc[z]) + f(p[z * 2 + c])

    @pl.when(z > 0)
    def _():
        up(z).wait_recv()
        out[...] += f(ups[z])

    @pl.when(z < nz - 1)
    def _():
        dn(z).wait_recv()
        out[...] += f(dns[z])

    for t in range(nz):
        swap(t).wait_send()
        pl.when(z < t)(up(t).wait_send)
        pl.when(z > t)(dn(t).wait_send)


def scatter_scratch(nz, rows, width):
    return [pltpu.VMEM((nz, rows, width), BF)] * 3 + [pltpu.SemaphoreType.DMA((3 * nz,))] * 2


def scatter_kernel(nz, p, out, *scratch):
    pos = place()
    greet(line_partners(nz, pos))
    scatter_blocks(nz, pos, p, out, *scratch)


def scatter_tokens(p, nz, cid):
    blocks, rows, width = p.shape
    return pl.pallas_call(
        functools.partial(scatter_kernel, nz),
        out_shape=jax.ShapeDtypeStruct((rows, width), F32),
        in_specs=[VM],
        out_specs=VM,
        scratch_shapes=scatter_scratch(nz, rows, width),
        compiler_params=params(cid, 60 * MIB),
        name="scatter_tokens",
    )(p)


def scatter_and_hand_kernel(nz, kinds, runs, p, up_s, res, *refs):
    count = len(kinds)
    srcs, refs = refs[:count], refs[count:]
    out, up_o, res_o, refs = *refs[:3], refs[3:]
    dsts, refs = refs[:count], refs[count:]
    scratch, hsems, esems, tsems = refs[:5], refs[5:7], refs[7:9], refs[9:11]
    pos = place()
    x, c, z, y = pos
    greet(rank_partners(nz, pos) + group_partners(pos) + [(c != y, at(x, y, z, c))])
    hs = hand_stages(srcs, dsts, kinds, *hsems, nz, pos)
    es = exchange_stages(up_s, up_o, runs, *esems, nz, pos)
    ts = trade_stages(res, res_o, *tsems, pos)
    hs[0]()
    es[0]()
    ts[0]()
    scatter_blocks(nz, pos, p, out, *scratch)
    hs[1]()
    es[1]()
    ts[1]()


def scatter_and_hand(p, up_s, runs, res, arrays, kinds, nz, cid):
    blocks, rows, width = p.shape
    n, part, share = up_s.shape
    return pl.pallas_call(
        functools.partial(scatter_and_hand_kernel, nz, kinds, runs),
        out_shape=[
            jax.ShapeDtypeStruct((rows, width), F32),
            jax.ShapeDtypeStruct((part, n * share), BF),
            jax.ShapeDtypeStruct(res.shape, BF),
        ]
        + hand_shapes(arrays, kinds, nz),
        in_specs=[VM] + [HBM] * (2 + len(arrays)),
        out_specs=[VM] + [HBM] * (2 + len(arrays)),
        scratch_shapes=scatter_scratch(nz, rows, width) + hand_sems(kinds) + exchange_sems(runs, nz) + trade_sems(),
        compiler_params=params(cid, 60 * MIB),
        name="scatter_and_hand",
    )(p, up_s, res, *arrays)


def block_of(x, c, z, y, nz):
    return (x * 2 + c) * 2 * nz + z * 2 + y


def halves(ref, rows):
    half = rows // 2
    if half % 16:
        return {1: None, 2: ref}
    return {1: ref.at[pl.ds(half, half)], 2: ref.at[pl.ds(0, half)]}


def sliced_gather(src, dst, runs, sems, nz, pos):
    x, c, z, y = pos
    n = 2 * nz
    me = z * 2 + c
    part = dst.shape[1]
    send1, recv1, send2, recv2 = sems

    def pieces(p):
        if runs is None:
            return [(src.at[p], slice(None))]
        return [(src.at[:, pl.ds(there, size)], pl.ds(here, size)) for there, here, size in runs(p)]

    def row(p, gx, gy):
        return dst.at[block_of(gx, p % 2, p // 2, gy, nz)]

    mine = block_of(x, c, z, y, nz)

    def out(k):
        p = (me + k) % n
        return [
            remote(a, dst.at[mine, :, b], send1.at[p], recv1.at[me], at(x, p % 2, p // 2, y))
            for a, b in pieces(p)
        ]

    local = [pltpu.make_async_copy(a, dst.at[mine, :, b], recv1.at[me]) for a, b in pieces(me)]

    def came(k):
        return (me - k + n) % n

    def arrival(b, sem):
        return remote(b, b, send1.at[me], sem, at(x, 1 - c, z, y))

    def neighbour(m):
        return at(x ^ (m // 2), c, z, y ^ (m % 2))

    def forward(k, m):
        p = came(k)
        b = row(p, x, y)
        slot = (m - 1) * n + p
        return remote(b, b, send2.at[slot], recv2.at[slot], neighbour(m))

    def relay(k, m):
        p = came(k)
        b = halves(row(p, x ^ (m // 2), y ^ (m % 2)), part)[m]
        slot = (1 + m) * n + p
        return b is not None and remote(b, b, send2.at[slot], recv2.at[slot], neighbour(3 - m))

    def first():
        for copy in local:
            copy.start()
        for k in range(1, n):
            for copy in out(k):
                copy.start()

    def step(k):
        p = came(k)
        arrival(row(p, x, y), recv1.at[p]).wait_recv()
        for m in (1, 2):
            forward(k, m).start()

    def pass_on(k):
        p = came(k)
        for m in (1, 2):
            arrival(row(p, x ^ (m // 2), y ^ (m % 2)), recv2.at[(m - 1) * n + p]).wait_recv()
            if relay(k, m):
                relay(k, m).start()

    def last():
        for k in range(n):
            p = came(k)
            parts = halves(row(p, 1 - x, 1 - y), part)
            for m in (1, 2):
                if parts[m] is not None:
                    arrival(parts[m], recv2.at[(1 + m) * n + p]).wait_recv()
        for k in range(n):
            if k:
                p = (me + k) % n
                b = dst.at[mine]
                remote(b, b, send1.at[p], recv1.at[me], at(x, p % 2, p // 2, y)).wait_send()
            for m in (1, 2):
                forward(k, m).wait_send()
                if relay(k, m):
                    relay(k, m).wait_send()

    stages = [functools.partial(step, k) for k in range(n)] + [functools.partial(pass_on, k) for k in range(n)]
    return [first] + stages + [last]


def sliced_sems(nz):
    n = 2 * nz
    return [pltpu.SemaphoreType.DMA((n,))] * 2 + [pltpu.SemaphoreType.DMA((4 * n,))] * 2


def group_gather(src, dst, send, recv, pos):
    x, c, z, y = pos
    rows = src.shape[0]
    local = pltpu.make_async_copy(src, dst.at[x * 2 + y], recv.at[0])

    def there(m):
        return dst.at[(x ^ (m // 2)) * 2 + (y ^ (m % 2))]

    def neighbour(m):
        return at(x ^ (m // 2), c, z, y ^ (m % 2))

    def out(m):
        return remote(src, dst.at[x * 2 + y], send.at[m], recv.at[m], neighbour(m))

    def relay(m):
        b = halves(there(m), rows)[m]
        return b is not None and remote(b, b, send.at[2 + m], recv.at[2 + m], neighbour(3 - m))

    def arrival(b, sem):
        return remote(b, b, send.at[0], sem, at(x, 1 - c, z, y))

    def first():
        local.start()
        for m in (1, 2):
            out(m).start()

    def pass_on():
        for m in (1, 2):
            arrival(there(m), recv.at[m]).wait_recv()
            if relay(m):
                relay(m).start()

    def last():
        local.wait()
        parts = halves(there(3), rows)
        for m in (1, 2):
            if parts[m] is not None:
                arrival(parts[m], recv.at[2 + m]).wait_recv()
            out(m).wait_send()
            if relay(m):
                relay(m).wait_send()

    return [first, pass_on, last]


def full_gather(src, dst, send, recv, nz, pos):
    x, c, z, y = pos
    rows = src.shape[0]
    sib = at(x, 1 - c, z, y)
    mine = dst.at[block_of(x, c, z, y, nz)]

    def row(core, k, m):
        return dst.at[block_of(x ^ (m // 2), core, z + k, y ^ (m % 2), nz)]

    def neighbour(m):
        return at(x ^ (m // 2), c, z, y ^ (m % 2))

    def arrival(b, sem):
        return remote(b, b, send.at[0], recv.at[sem], sib)

    def along(k, sign):
        b = row(c, k, 0)
        return remote(
            b if k else src, b, send.at[(0 if sign > 0 else nz) + z + k], recv.at[z + k], at(x, c, z + sign, y)
        )

    def forward(k, m):
        b = row(c, k, 0)
        return remote(b if k else src, b, send.at[(1 + m) * nz + z + k], recv.at[m * nz + z + k], neighbour(m))

    def relay(k, m):
        b = halves(row(c, k, m), rows)[m]
        if b is None:
            return None
        return remote(b, b, send.at[(3 + m) * nz + z + k], recv.at[(2 + m) * nz + z + k], neighbour(3 - m))

    def side(k, m):
        b = row(c, k, m)
        return remote(b if k or m else src, b, send.at[(6 + m) * nz + z + k], recv.at[(5 + m) * nz + z + k], sib)

    local = pltpu.make_async_copy(src, mine, recv.at[z])

    def first():
        local.start()
        pl.when(z < nz - 1)(along(0, 1).start)
        pl.when(z > 0)(along(0, -1).start)
        for m in (1, 2):
            forward(0, m).start()
        side(0, 0).start()

    def both(k, fn):
        @pl.when(z >= k)
        def _():
            fn(-k)

        if k:

            @pl.when(z + k < nz)
            def _():
                fn(k)

    def step(k):
        def one(k):
            arrival(row(c, k, 0), z + k).wait_recv()
            if k > 0:
                pl.when(z > 0)(along(k, -1).start)
            else:
                pl.when(z < nz - 1)(along(k, 1).start)
            for m in (1, 2):
                forward(k, m).start()
            side(k, 0).start()

        both(k, one)

    def pass_on(k):
        def one(k):
            for m in (1, 2):
                arrival(row(c, k, m), m * nz + z + k).wait_recv()
                if relay(k, m) is not None:
                    relay(k, m).start()
                side(k, m).start()

        both(k, one)

    def diagonal(k):
        def one(k):
            parts = halves(row(c, k, 3), rows)
            for m in (1, 2):
                if parts[m] is not None:
                    arrival(parts[m], (2 + m) * nz + z + k).wait_recv()
            side(k, 3).start()

        both(k, one)

    def last():
        local.wait()

        def one(k):
            for m in range(4):
                arrival(row(1 - c, k, m), (5 + m) * nz + z + k).wait_recv()
                side(k, m).wait_send()
            if k >= 0:
                pl.when(z > 0)(along(k, -1).wait_send)
            if k <= 0:
                pl.when(z < nz - 1)(along(k, 1).wait_send)
            for m in (1, 2):
                forward(k, m).wait_send()
                if relay(k, m) is not None:
                    relay(k, m).wait_send()

        for k in range(nz):
            both(k, one)

    return (
        [first]
        + [functools.partial(step, k) for k in range(1, nz)]
        + [functools.partial(pass_on, k) for k in range(nz)]
        + [functools.partial(diagonal, k) for k in range(nz)]
        + [last]
    )


def full_sems(nz):
    return [pltpu.SemaphoreType.DMA((10 * nz,)), pltpu.SemaphoreType.DMA((9 * nz,))]


def head_runs(nz, cols):
    return lambda p: [
        (block_of(x, p % 2, p // 2, 0, nz) * HD, x * cols // 2, cols // 2) for x in range(2)
    ]


def up_runs(nz, unit):
    return lambda p: [(block_of(x, p % 2, p // 2, 0, nz) * unit, x * 2 * unit, 2 * unit) for x in range(2)]


def qkv_runs(nz, width, cols):
    runs = head_runs(nz, cols)
    return lambda p: [(j * width + there, j * cols + here, size) for j in range(3) for there, here, size in runs(p)]


def fetch_kernel(
    nz, width, cols, x_in, w_qkv, w_down, vec, tab, x_all, qkv_w, down_w, vecs, tab_out, *sems
):
    pos = place()
    x, c, z, y = pos
    fsdp = 2 * nz
    devices = 4 * fsdp
    me = (x * 2 + c) * fsdp + z * 2 + y
    x_sems, qkv_sems, vec_sems, tab_sems, down_sems = sems[:2], sems[2:6], sems[6:8], sems[8:10], sems[10:]
    greet_all(devices, fsdp, me)

    def vec_copy(other):
        return remote(vec, vecs.at[me], vec_sems[0].at[other], vec_sems[1].at[me], (other // fsdp, other % fsdp))

    def each(fn):
        def body(k, _):
            fn((me + k) % devices)
            return 0

        lax.fori_loop(1, devices, body, 0)

    vec_local = pltpu.make_async_copy(vec, vecs.at[me], vec_sems[1].at[me])
    tab_local = pltpu.make_async_copy(tab, tab_out, tab_sems[1].at[0])
    tab_trade = remote(tab, tab_out, tab_sems[0].at[0], tab_sems[1].at[0], at(x, y, z, c))

    gx = line_gather(x_in, x_all, *x_sems, nz, True, pos)
    runs = qkv_runs(nz, width, cols) if len(w_qkv.shape) == 2 else None
    gq = sliced_gather(w_qkv, qkv_w, runs, qkv_sems, nz, pos)
    gx[0]()
    gq[0]()
    gx[1]()
    vec_local.start()
    each(lambda other: vec_copy(other).start())
    pl.when(c == y)(tab_local.start)
    pl.when(c != y)(tab_trade.start)
    gd = group_gather(w_down, down_w, *down_sems, pos)
    for stage in gq[1 : fsdp + 1]:
        stage()
    gx[2]()
    gd[0]()
    for stage in gx[3:-1]:
        stage()
    for stage in gq[fsdp + 1 :]:
        stage()
    gx[-1]()
    for stage in gd[1:]:
        stage()

    def vec_done(other):
        remote(vec, vecs.at[other], vec_sems[0].at[other], vec_sems[1].at[other], at(x, 1 - c, z, y)).wait_recv()
        vec_copy(other).wait_send()

    vec_local.wait()
    each(vec_done)
    tab_local.wait()
    pl.when(c != y)(tab_trade.wait_send)


def fetch(nz, x_in, w_qkv, w_down, part, vec, tab, cid):
    rows, width = x_in.shape
    n = 2 * nz
    devices = 4 * n
    cols = width // n
    shapes = [
        ((n, rows, width), BF),
        ((devices, part, 3 * cols), BF),
        ((4,) + w_down.shape, BF),
        ((devices,) + vec.shape, F32),
        (tab.shape, jnp.int32),
    ]
    return pl.pallas_call(
        functools.partial(fetch_kernel, nz, width, cols),
        out_shape=[jax.ShapeDtypeStruct(s, t) for s, t in shapes],
        in_specs=[HBM] * 5,
        out_specs=[HBM] * 5,
        scratch_shapes=gather_sems(nz)
        + sliced_sems(nz)
        + [pltpu.SemaphoreType.DMA((devices,))] * 2
        + [pltpu.SemaphoreType.DMA((1,))] * 2
        + [pltpu.SemaphoreType.DMA((5,))] * 2,
        compiler_params=params(cid),
        name="fetch",
    )(x_in, w_qkv, w_down, vec, tab)


def hand_stages(srcs, dsts, kinds, send, recv, nz, pos):
    x, c, z, y = pos
    n = 2 * nz
    count = len(kinds)

    def copies(i, m):
        gx, gy = x ^ (m // 2), y ^ (m % 2)
        sem = i * 3 + m - 1
        target = at(gx, c, z, gy)
        if not kinds[i]:
            return [remote(srcs[i].at[gx * 2 + gy], dsts[i].at[m - 1], send.at[sem], recv.at[sem], target)]
        return [
            remote(
                srcs[i].at[block_of(gx, p % 2, p // 2, gy, nz)],
                dsts[i].at[m - 1, p],
                send.at[sem],
                recv.at[sem],
                target,
            )
            for p in range(n)
        ]

    def first():
        for i in range(count):
            for m in (3, 1, 2):
                for copy in copies(i, m):
                    copy.start()

    def last():
        for i in range(count):
            for m in (1, 2, 3):
                sem = i * 3 + m - 1
                there = dsts[i].at[m - 1]
                whole = remote(there, there, send.at[sem], recv.at[sem], at(x, 1 - c, z, y))
                whole.wait_recv()
                whole.wait_send()

    return [first, last]


def hand_shapes(arrays, kinds, nz):
    return [
        jax.ShapeDtypeStruct((3, 2 * nz) + a.shape[1:] if k else (3,) + a.shape[1:], a.dtype)
        for a, k in zip(arrays, kinds)
    ]


def hand_sems(kinds):
    return [pltpu.SemaphoreType.DMA((3 * len(kinds),))] * 2


def exchange_stages(src, dst, runs, send, recv, nz, pos):
    x, c, z, y = pos
    n = 2 * nz
    me = z * 2 + c

    def give(to, p):
        if runs is None:
            return [(src.at[to], dst.at[p])]
        return [(src.at[to, :, pl.ds(here, size)], dst.at[:, pl.ds(there, size)]) for there, here, size in runs(p)]

    width = len(give(0, 0))

    def move(p):
        return [
            remote(a, b, send.at[p * width + i], recv.at[me * width + i], at(x, p % 2, p // 2, y))
            for i, (a, b) in enumerate(give(p, me))
        ]

    def come(p):
        return [
            remote(b, b, send.at[me * width + i], recv.at[p * width + i], at(x, 1 - c, z, y))
            for i, (_, b) in enumerate(give(me, p))
        ]

    local = [pltpu.make_async_copy(a, b, recv.at[me * width + i]) for i, (a, b) in enumerate(give(me, me))]

    def first():
        for copy in local:
            copy.start()
        for k in range(1, n):
            for copy in move((me + k) % n):
                copy.start()

    def last():
        for copy in local:
            copy.wait()
        for k in range(1, n):
            for copy in come((me - k + n) % n):
                copy.wait_recv()
            for copy in move((me + k) % n):
                copy.wait_send()

    return [first, last]


def exchange_sems(runs, nz):
    width = 1 if runs is None else len(runs(0))
    return [pltpu.SemaphoreType.DMA((width * 2 * nz,))] * 2


def exchange_kernel(nz, src, dst, send, recv):
    pos = place()
    greet(rank_partners(nz, pos))
    for stage in exchange_stages(src, dst, None, send, recv, nz, pos):
        stage()


def exchange(a, nz, cid, name):
    return pl.pallas_call(
        functools.partial(exchange_kernel, nz),
        out_shape=jax.ShapeDtypeStruct(a.shape, a.dtype),
        in_specs=[HBM],
        out_specs=HBM,
        scratch_shapes=exchange_sems(None, nz),
        compiler_params=params(cid),
        name=name,
    )(a)


def trade_stages(src, dst, send, recv, pos):
    x, c, z, y = pos
    local = pltpu.make_async_copy(src, dst, recv.at[0])
    trade = remote(src, dst, send.at[0], recv.at[0], at(x, y, z, c))

    def first():
        pl.when(c == y)(local.start)
        pl.when(c != y)(trade.start)

    def last():
        local.wait()
        pl.when(c != y)(trade.wait_send)

    return [first, last]


def trade_sems():
    return [pltpu.SemaphoreType.DMA((1,))] * 2


def finish_kernel(nz, runs, has, *refs):
    grad, small, *refs = refs
    qkv_s = refs.pop(0) if has else None
    grad_out, small_out, *refs = refs
    qkv_o = refs.pop(0) if has else None
    came, send, recv, *sems = refs
    pos = place()
    x, c, z, y = pos
    fsdp = 2 * nz
    devices = 4 * fsdp
    me = (x * 2 + c) * fsdp + z * 2 + y
    es = exchange_stages(qkv_s, qkv_o, runs, *sems[2:], nz, pos) if has else [lambda: None] * 2
    ts = trade_stages(grad, grad_out, *sems[:2], pos)
    greet_all(devices, fsdp, me)

    def each(fn):
        def body(k, _):
            fn((me + k) % devices)
            return 0

        lax.fori_loop(1, devices, body, 0)

    def share(other):
        return remote(small.at[other], came.at[me], send.at[other], recv.at[me], (other // fsdp, other % fsdp))

    es[0]()
    ts[0]()
    each(lambda other: share(other).start())

    def done(other):
        remote(small.at[me], came.at[other], send.at[other], recv.at[other], at(x, 1 - c, z, y)).wait_recv()
        share(other).wait_send()

    each(done)
    came[me] = small[me]
    small_out[...] = jnp.sum(came[...], axis=0)
    ts[1]()
    es[1]()


def finish(grad, small, qkv_s, runs, nz, cid):
    devices = small.shape[0]
    has = qkv_s is not None
    shapes = [jax.ShapeDtypeStruct(grad.shape, grad.dtype), jax.ShapeDtypeStruct(small.shape[1:], F32)]
    if has:
        out_shape = qkv_s.shape if runs is None else (qkv_s.shape[1], qkv_s.shape[0] * qkv_s.shape[2])
        shapes.append(jax.ShapeDtypeStruct(out_shape, BF))
    return pl.pallas_call(
        functools.partial(finish_kernel, nz, runs, has),
        out_shape=shapes,
        in_specs=[HBM, VM] + [HBM] * has,
        out_specs=[HBM, VM] + [HBM] * has,
        scratch_shapes=[pltpu.VMEM(small.shape, F32)]
        + [pltpu.SemaphoreType.DMA((devices,))] * 2
        + trade_sems()
        + (exchange_sems(runs, nz) if has else []),
        compiler_params=params(cid, 32 * MIB),
        name="finish",
    )(*((grad, small, qkv_s) if has else (grad, small)))


def dot(a, b, dims):
    return lax.dot_general(a, b, (dims, ((), ())), preferred_element_type=F32)


NN = ((1,), (0,))
NT = ((1,), (1,))
TN = ((0,), (0,))


def head_number(h, heads, nz, pos):
    x, c, z, y = pos
    return block_of(h // (heads // 2), c, z, h % (heads // 2), nz)


def head_kernel(heads, nz, runs_qkv, runs_up, runs_out, *refs):
    refs = list(refs)

    def take(n):
        got = refs[:n]
        del refs[:n]
        return got

    slopes, valid_in, blocks_in, parents_in = take(4)
    vectors, bias_up = take(8), take(1)[0]
    x_in, cot, w_qkv, w_up, w_out, w_down = take(6)
    joined, mixed, mixed_own, x_own, rows_o, up_bias = take(6)
    a1_o, far_o, cot_all, qkv_o, up_w, out_w, down_w = take(7)
    pack, vecs, tab, tab_in, table, columns, member_s, reach_s, far_s, x_all, a1, qkv_w, bias_s = take(13)
    x_sems, cot_sems, qkv_sems, up_sems, out_sems, down_sems = take(2), take(2), take(4), take(4), take(2), take(2)
    vec_sems, tab_sems, mix_sems, (local_sem, far_sem) = take(2), take(2), take(2), take(2)

    pos = place()
    x, c, z, y = pos
    n = 2 * nz
    devices = 4 * n
    me = block_of(x, c, z, y, nz)
    rank = z * 2 + c
    tree, cols = joined.shape[0], joined.shape[1] // 3
    rows, width = x_own.shape
    part = w_out.shape[0]

    gx = line_gather(x_in, x_all, *x_sems, nz, True, pos)
    gc = line_gather(cot, cot_all, *cot_sems, nz, True, pos)
    gq = sliced_gather(w_qkv, qkv_w, runs_qkv, qkv_sems, nz, pos)
    gu = sliced_gather(w_up, up_w, runs_up, up_sems, nz, pos)
    go = full_gather(w_out, out_w, *out_sems, nz, pos)
    gd = group_gather(w_down, down_w, *down_sems, pos)
    ex = exchange_stages(mixed, mixed_own, runs_out, *mix_sems, nz, pos)
    ts = trade_stages(tab, tab_in, *tab_sems, pos)
    store_a = pltpu.make_async_copy(a1, a1_o, local_sem.at[0])
    store_q = pltpu.make_async_copy(qkv_w, qkv_o, local_sem.at[1])

    def each(fn):
        def body(k, _):
            fn((me + k) % devices)
            return 0

        lax.fori_loop(1, devices, body, 0)

    def vec_copy(other):
        return remote(pack, vecs.at[me], vec_sems[0].at[other], vec_sems[1].at[me], (other // n, other % n))

    def vec_come(other):
        remote(vecs.at[other], vecs.at[other], vec_sems[0].at[me], vec_sems[1].at[other], at(x, 1 - c, z, y)).wait_recv()

    pack[...] = jnp.zeros_like(pack)
    for i, v in enumerate(vectors):
        pack[i : i + 1, 0:part] = v[...].astype(F32).reshape(1, part)
    lined = pack[...]
    pack[...] = jnp.where(y == 1, pltpu.roll(lined, part, 1), lined)
    for i in range(bias_up.shape[0] // 128):
        pack[8 + i : 9 + i, :] = bias_up[i * 128 : (i + 1) * 128].astype(F32).reshape(1, 128)
    tab[...] = jnp.full_like(tab, -1)
    tab[0:1, :] = valid_in[...]
    tab[1:2, 0 : blocks_in.shape[1]] = blocks_in[...]
    tab[2:3, 0 : parents_in.shape[1]] = parents_in[...]

    greet_all(devices, n, me)
    gx[0]()
    gq[0]()
    ts[0]()
    go[0]()
    gd[0]()
    each(lambda other: vec_copy(other).start())
    vecs[me] = pack[...]
    gx[1]()

    ts[1]()
    seg = lax.broadcasted_iota(jnp.int32, (128, 128), 0)
    lane = lax.broadcasted_iota(jnp.int32, (128, 128), 1)

    def low(v):
        return v.astype(F32).astype(BF)

    parent = low(seg == tab_in[2:3, 0:128])
    above = (parent.astype(F32) + dot(parent, parent, NN)) > 0.5
    ancestor = low(above & (seg != lane))
    owner = low(seg == tab_in[1:2, 0:128])
    spread = low(
        lax.shift_right_logical(lax.broadcasted_iota(jnp.int32, (128, tree), 1), BLK.bit_length() - 1)
        == lax.broadcasted_iota(jnp.int32, (128, tree), 0)
    )
    member = dot(owner, spread, NN)
    valid = tab_in[0:1, :].astype(F32)
    counted = member * valid
    member_s[...] = member.astype(BF)
    reach_s[...] = (2.0 * dot(ancestor, member_s[...], NN) + member).astype(BF)
    lens = jnp.broadcast_to(jnp.sum(counted, axis=1, keepdims=True), (128, 128))
    offset = lax.dot_general(
        ancestor.astype(F32), lens, (TN, ((), ())), precision=lax.Precision.HIGHEST, preferred_element_type=F32
    )
    table[...] = jnp.zeros_like(table)
    table[1:2, :] = valid
    for j in range(tree // 256):
        here = slice(j * 256, (j + 1) * 256)
        earlier = low(
            lax.broadcasted_iota(jnp.int32, (tree, 256), 0) < lax.broadcasted_iota(jnp.int32, (tree, 256), 1) + j * 256
        )
        before = dot(counted.astype(BF), earlier, NN) + offset[:, 0:1]
        table[0:1, here] = jnp.sum(before * member[:, here], axis=0, keepdims=True)
    columns[...] = table[...].T

    step = far_s.shape[2]
    steps = tree // step
    far_store = [
        pltpu.make_async_copy(far_s.at[i % 2], far_o.at[:, pl.ds(i * step, step)], far_sem.at[i % 2]) for i in range(steps)
    ]

    def allow(value, key, query, key_valid):
        return ((value > 1.5) | ((value > 0.5) & (key <= query))) & ((key_valid > 0.5) | (key == query))

    def far_blocks():
        for i in range(steps):
            here = slice(i * step, (i + 1) * step)
            key = lax.broadcasted_iota(jnp.int32, (tree, step), 0)
            query = lax.broadcasted_iota(jnp.int32, (tree, step), 1) + i * step
            allowed = allow(dot(member_s[...], reach_s[:, here], TN), key, query, columns[:, 1:2])
            if i >= 2:
                far_store[i - 2].wait()
            far_s[i % 2] = jnp.where(allowed, columns[:, 0:1], MASKED)
            far_store[i].start()

    def whole_vectors():
        each(vec_come)
        for i in range(devices // 2):
            rows_o[:, i * 128 : (i + 1) * 128] = vecs[2 * i, 0:8] + vecs[2 * i + 1, 0:8]
        per = bias_up.shape[0] // 128
        for g in range(4):
            r = block_of(g // 2, c, z, g % 2, nz)
            for i in range(per):
                up_bias[:, (g * per + i) * 128 : (g * per + i + 1) * 128] = vecs[r, 8 + i : 9 + i]
        bias_s[...] = jnp.zeros_like(bias_s)
        for there, here, size in runs_out(rank):
            there = pl.multiple_of(there, 128)
            bias_s[:, here : here + size] = rows_o[2:3, pl.ds(there, size)]
            bias_s[:, 2 * cols + here : 2 * cols + here + size] = rows_o[3:4, pl.ds(there, size)]

    def norm(b):
        def tile(j, _):
            here = pl.ds(pl.multiple_of(j * 32, 32), 32)
            normed, _ = norm_parts(x_all[b, here].astype(F32))
            a1[b, here] = (normed * rows_o[0:1, :] + rows_o[1:2, :]).astype(BF)
            return 0

        lax.fori_loop(0, rows // 32, tile, 0)

    def norm_at(k, core):
        pl.when(z >= k)(lambda: norm((z - k) * 2 + core))
        if k:
            pl.when(z + k < nz)(lambda: norm((z + k) * 2 + core))

    for stage in gq[1 : n + 1]:
        stage()
    gx[2]()
    go[1]()
    gd[1]()
    far_blocks()
    whole_vectors()
    norm_at(0, c)
    norm_at(1, c)
    gx[3]()
    gu[0]()
    gc[0]()
    norm_at(2, c)
    go[2]()
    for stage in gq[n + 1 : 2 * n + 1]:
        stage()
    gx[4]()
    gc[1]()
    norm_at(3, c)
    go[3]()
    gx[-1]()
    x_own[...] = x_all[rank]
    for k in range(nz):
        norm_at(k, 1 - c)
    store_a.start()
    gq[-1]()
    store_q.start()
    for stage in gu[1 : n + 1]:
        stage()

    def project(i, _):
        here = pl.ds(pl.multiple_of(i * 2 * rows, 2 * rows), 2 * rows)
        tokens = a1[pl.ds(2 * i, 2)].reshape(2 * rows, width)

        def tile(j, _):
            u = pl.ds(pl.multiple_of(j * 256, 256), 256)
            value = dot(tokens, qkv_w[:, :, u].reshape(width, 256), NN) + bias_s[:, u]
            joined[here, u] = value.astype(BF)
            return 0

        lax.fori_loop(0, 3 * cols // 256, tile, 0)
        return 0

    lax.fori_loop(0, nz, project, 0)
    slope = [slopes[head_number(h, heads, nz, pos)] for h in range(heads)]

    gc[2]()
    def attend_step(i, _):
        here = pl.ds(pl.multiple_of(i * step, step), step)
        per = step // rows
        key = lax.broadcasted_iota(jnp.int32, (step, tree), 1)
        query = lax.broadcasted_iota(jnp.int32, (step, tree), 0) + i * step
        allowed = allow(dot(reach_s[:, here], member_s[...], TN), key, query, table[1:2, :])
        gap = jnp.where(allowed, table[0:1, :], MASKED)
        for h in range(heads):
            lanes = slice(h * HD, (h + 1) * HD)
            q = joined[here, lanes]
            k = joined[:, cols + h * HD : cols + (h + 1) * HD]
            v = joined[:, 2 * cols + h * HD : 2 * cols + (h + 1) * HD]
            logits = dot(q, k, NT) * HD ** (-0.5) + slope[h] * gap
            weights = jnp.exp(logits - jnp.max(logits, axis=1, keepdims=True))
            probs = weights * (1.0 / jnp.sum(weights, axis=1, keepdims=True))
            mixed[pl.ds(i * per, per), :, lanes] = dot(probs.astype(BF), v, NN).astype(BF).reshape(per, rows, HD)

        def later(k, fns):
            @pl.when(i == k)
            def _():
                for fn in fns:
                    fn()

        later(0, go[nz : 2 * nz])
        later(1, gc[3:4] + gu[n + 1 : n + 1 + n // 2])
        later(2, gc[4:5] + gu[n + 1 + n // 2 : 2 * n + 1])
        later(3, go[2 * nz : 3 * nz])
        return 0

    lax.fori_loop(0, steps, attend_step, 0)
    ex[0]()
    ex[1]()
    for stage in (go[-1], gc[-1], gu[-1], gd[-1]):
        stage()
    each(lambda other: vec_copy(other).wait_send())
    for i in range(max(0, steps - 2), steps):
        far_store[i].wait()
    store_a.wait()
    store_q.wait()


def head_call(slopes, tables, vectors, bias_up, layer_in, cot, w_qkv, w_up, w_out, w_down, heads, nz, cid):
    rows, width = layer_in.shape
    n = 2 * nz
    devices = 4 * n
    tree = n * rows
    cols = heads * HD
    part, unit = w_out.shape[0], w_down.shape[0]
    step = 256
    runs_qkv, runs_up, runs_out = qkv_runs(nz, width, cols), up_runs(nz, unit), head_runs(nz, cols)
    shape = jax.ShapeDtypeStruct
    return pl.pallas_call(
        functools.partial(head_kernel, heads, nz, runs_qkv, runs_up, runs_out),
        out_shape=[
            shape((tree, 3 * cols), BF),
            shape((n, rows, cols), BF),
            shape((rows, width), BF),
            shape((rows, width), BF),
            shape((8, width), F32),
            shape((1, 4 * unit), F32),
            shape((n, rows, width), BF),
            shape((tree, tree), F32),
            shape((n, rows, width), BF),
            shape((devices, part, 3 * cols), BF),
            shape((devices, part, 4 * unit), BF),
            shape((devices, part, width), BF),
            shape((4, unit, width), BF),
        ],
        in_specs=[pl.BlockSpec(memory_space=pltpu.SMEM)] + [VM] * 12 + [HBM] * 6,
        out_specs=[VM] * 6 + [HBM] * 7,
        scratch_shapes=[
            pltpu.VMEM((16, 128), F32),
            pltpu.VMEM((devices, 16, 128), F32),
            pltpu.VMEM((8, tree), jnp.int32),
            pltpu.VMEM((8, tree), jnp.int32),
            pltpu.VMEM((128, tree), F32),
            pltpu.VMEM((tree, 128), F32),
            pltpu.VMEM((128, tree), BF),
            pltpu.VMEM((128, tree), BF),
            pltpu.VMEM((2, tree, step), F32),
            pltpu.VMEM((n, rows, width), BF),
            pltpu.VMEM((n, rows, width), BF),
            pltpu.VMEM((devices, part, 3 * cols), BF),
            pltpu.VMEM((1, 3 * cols), F32),
        ]
        + gather_sems(nz) * 2
        + sliced_sems(nz) * 2
        + full_sems(nz)
        + [pltpu.SemaphoreType.DMA((5,))] * 2
        + [pltpu.SemaphoreType.DMA((devices,))] * 2
        + trade_sems()
        + exchange_sems(runs_out, nz)
        + [pltpu.SemaphoreType.DMA((2,))] * 2,
        compiler_params=params(cid, 60 * MIB),
        name="head",
    )(slopes, *tables, *vectors, bias_up, layer_in, cot, w_qkv, w_up, w_out, w_down)


def scatter_parts(nz, pos, own, other, acc, came, send, recv):
    x, c, z, y = pos
    S, U, D = 0, nz, 2 * nz
    sib = at(x, 1 - c, z, y)

    def f(v):
        return v.astype(F32)

    def swap(t):
        return remote(other(t), acc.at[t], send.at[S + t], recv.at[S + t], sib)

    def rise(t):
        return remote(acc.at[t], came.at[t], send.at[U + t], recv.at[U + t], at(x, c, z + 1, y))

    def fall(t):
        slot = jnp.where(z - 1 == t, nz, t)
        return remote(acc.at[t], came.at[slot], send.at[D + t], recv.at[D + t], at(x, c, z - 1, y))

    def arrival(slot, sem):
        return remote(came.at[slot], came.at[slot], send.at[S], recv.at[sem], sib)

    def event(t, upward):
        swap(t).wait_recv()

        @pl.when(z > 0 if upward else z < nz - 1)
        def _():
            arrival(t, (U if upward else D) + t).wait_recv()
            acc[t] = (f(acc[t]) + f(own(t)) + f(came[t])).astype(BF)

        @pl.when(z == 0 if upward else z == nz - 1)
        def _():
            acc[t] = (f(acc[t]) + f(own(t))).astype(BF)

        (rise if upward else fall)(t).start()

    def begin():
        for i in range(nz - 1):
            pl.when(z == 0)(functools.partial(event, nz - 1 - i, True))
            pl.when(z == nz - 1)(functools.partial(event, i, False))

    def near(i):
        t = nz - 1 - i
        pl.when((z > 0) & (z < nz // 2) & (z < t))(functools.partial(event, t, True))
        pl.when((z >= nz // 2) & (z < nz - 1) & (z > i))(functools.partial(event, i, False))

    def far():
        for i in range(nz - 1):
            t = nz - 1 - i
            pl.when((z >= nz // 2) & (z < t))(functools.partial(event, t, True))
            pl.when((z < nz // 2) & (z > i))(functools.partial(event, i, False))

    def total(out):
        swap(z).wait_recv()
        out[...] = f(acc[z]) + f(own(z))

        @pl.when(z > 0)
        def _():
            arrival(z, U + z).wait_recv()
            out[...] += f(came[z])

        @pl.when(z < nz - 1)
        def _():
            arrival(nz, D + z).wait_recv()
            out[...] += f(came[nz])

    def done():
        for t in range(nz):
            swap(t).wait_send()
            pl.when(z < t)(lambda t=t: rise(t).wait_send())
            pl.when(z > t)(lambda t=t: fall(t).wait_send())

    return swap, begin, near, far, total, done


def reduce_parts(src, mine, near, far, send, recv, lsem, pos):
    x, c, z, y = pos
    half = src.shape[1] // 2

    def f(v):
        return v.astype(F32)

    def share(gx, gy, lower):
        return src.at[gx * 2 + gy, pl.ds(lower * half, half)]

    parts = [(x, y, 0), (x, y, 1), (x, 1 - y, 0), (1 - x, y, 1)]
    loads = [pltpu.make_async_copy(share(*p), mine.at[i], lsem.at[i]) for i, p in enumerate(parts)]
    along_x, along_y = at(1 - x, c, z, y), at(x, c, z, 1 - y)

    def out(i):
        a, b, target = [
            (share(1 - x, y, 0), near.at[0, 0], along_x),
            (share(1 - x, 1 - y, 0), near.at[0, 1], along_x),
            (share(x, 1 - y, 1), near.at[1, 0], along_y),
            (share(1 - x, 1 - y, 1), near.at[1, 1], along_y),
        ][i]
        return remote(a, b, send.at[i], recv.at[i], target)

    def on(i):
        return remote(near.at[i, 1], far.at[i], send.at[4 + i], recv.at[4 + i], [along_y, along_x][i])

    def first():
        for i in (1, 3, 0, 2):
            out(i).start()
        for copy in loads:
            copy.start()

    def second():
        for copy in loads:
            copy.wait()
        for i in range(2):
            out(2 * i + 1).wait_recv()
            near[i, 1] = (f(near[i, 1]) + f(mine[2 + i])).astype(BF)
            on(i).start()

    def total(put):
        for i in range(2):
            out(2 * i).wait_recv()
            on(i).wait_recv()
            put(i, f(mine[i]) + f(near[i, 0]) + f(far[i]))

    def done():
        for i in range(4):
            out(i).wait_send()
        for i in range(2):
            on(i).wait_send()

    return first, second, total, done


def reduce_scratch(rows, width):
    half = rows // 2
    return [
        pltpu.VMEM((4, half, width), BF),
        pltpu.VMEM((2, 2, half, width), BF),
        pltpu.VMEM((2, half, width), BF),
        pltpu.SemaphoreType.DMA((6,)),
        pltpu.SemaphoreType.DMA((6,)),
        pltpu.SemaphoreType.DMA((4,)),
    ]


def tail_kernel(
    heads, nz, runs_up, runs_qkv, slopes, far_in, grad_in, joined, a1_in, mixed, qkv_in, branch, upd_in, up_src, down_src,
    base, grad_out, down_o, out_o, col_o, square_o, up_o, qkv_o, branch_all, layer_o, grad_s, *refs,
):
    refs = list(refs)

    def take(n):
        got = refs[:n]
        del refs[:n]
        return got

    gap_s, tokens, qkv_w, grad_joined, acc_k, acc_v = take(6)
    upd_own, upd_acc, upd_came, upd_send, upd_recv = take(5)
    att_p, att_acc, att_came, att_send, att_recv = take(5)
    up_refs, down_refs, qkv_refs, out_refs = take(6), take(6), take(6), take(6)
    up_sum, qkv_sum, qkv_g, out_g, res, res_low = take(6)
    gsems, esems, esems_up, esems_qkv, tsems = take(2), take(2), take(2), take(2), take(2)
    gap_sem, load_sem = take(2)

    pos = place()
    x, c, z, y = pos
    n = 2 * nz
    tree, cols = mixed.shape
    rows, width = branch.shape
    part = up_sum.shape[1]
    rank = z * 2 + c
    step = gap_s.shape[2]

    es = exchange_stages(grad_in, grad_s, None, *esems, nz, pos)
    gb = line_gather(branch, branch_all, *gsems, nz, False, pos)
    up1, up2, up_total, up_done = reduce_parts(up_src, *up_refs, pos)
    down1, down2, down_total, down_done = reduce_parts(down_src, *down_refs, pos)
    qkv1, qkv2, qkv_total, qkv_done = reduce_parts(qkv_g, *qkv_refs, pos)
    out1, out2, out_total, out_done = reduce_parts(out_g, *out_refs, pos)
    upd_swap, upd_begin, upd_near, upd_far, upd_total, upd_done = scatter_parts(
        nz, pos, lambda t: upd_own[t], lambda t: upd_in.at[t * 2 + 1 - c], upd_acc, upd_came, upd_send, upd_recv
    )
    att_swap, att_begin, att_near, att_far, att_total, att_done = scatter_parts(
        nz, pos, lambda t: att_p[t * 2 + c], lambda t: att_p.at[t * 2 + 1 - c], att_acc, att_came, att_send, att_recv
    )
    ex_up = exchange_stages(up_sum, up_o, runs_up, *esems_up, nz, pos)
    ex_qkv = exchange_stages(qkv_sum, qkv_o, runs_qkv, *esems_qkv, nz, pos)
    home = trade_stages(res_low, layer_o, *tsems, pos)
    loads = [pltpu.make_async_copy(upd_in.at[t * 2 + c], upd_own.at[t], load_sem.at[t]) for t in range(nz)]
    load_w = pltpu.make_async_copy(qkv_in, qkv_w, load_sem.at[nz])
    load_a = pltpu.make_async_copy(a1_in, tokens, load_sem.at[nz + 1])
    load_b = pltpu.make_async_copy(branch_all, tokens, load_sem.at[nz + 2])

    def gap_load(i, slot):
        return pltpu.make_async_copy(
            far_in.at[:, pl.ds(pl.multiple_of(i * step, step), step)], gap_s.at[slot], gap_sem.at[slot]
        )

    greet(rank_partners(nz, pos) + group_partners(pos) + [(c != y, at(x, y, z, c))])
    es[0]()
    up1()
    for t in range(nz):
        upd_swap(t).start()
    gap_load(0, 0).start()
    for copy in loads + [load_w, load_a]:
        copy.start()
    acc_k[...] = jnp.zeros_like(acc_k)
    acc_v[...] = jnp.zeros_like(acc_v)
    for copy in loads:
        copy.wait()
    es[1]()
    gb[0]()
    gb[1]()
    upd_begin()

    steps = tree // step
    slope = [slopes[head_number(h, heads, nz, pos)] for h in range(heads)]

    def attend_step(i, _):
        slot = i % 2
        gap_load(i, slot).wait()
        pl.when(i + 1 < steps)(lambda: gap_load(i + 1, 1 - slot).start())
        gap = gap_s[slot]
        here = pl.ds(pl.multiple_of(i * step, step), step)
        per = step // rows
        grads = grad_s[pl.ds(i * per, per)].reshape(step, cols)
        for h in range(heads):
            lane = slice(h * HD, (h + 1) * HD)
            q = joined[here, lane]
            k = joined[:, cols + h * HD : cols + (h + 1) * HD]
            v = joined[:, 2 * cols + h * HD : 2 * cols + (h + 1) * HD]
            g = grads[:, lane]
            logits = dot(k, q, NT) * HD ** (-0.5) + slope[h] * gap
            weights = jnp.exp(logits - jnp.max(logits, axis=0, keepdims=True))
            probs = weights * (1.0 / jnp.sum(weights, axis=0, keepdims=True))
            grad_probs = dot(v, g, NT)
            delta = jnp.sum(probs * grad_probs, axis=0, keepdims=True)
            grad_raw = (probs * (grad_probs - delta) * HD ** (-0.5)).astype(BF)
            acc_v[:, lane] += dot(probs.astype(BF), g, NN)
            acc_k[:, lane] += dot(grad_raw, q, NN)
            grad_joined[here, lane] = dot(grad_raw, k, TN).astype(BF)

        def later(k, fns):
            @pl.when(i == k)
            def _():
                for fn in fns:
                    fn()

        later(0, [down1])
        later(1, [gb[2], lambda: upd_near(0)])
        later(2, [up2, gb[3], lambda: upd_near(1)])
        later(3, [gb[4], upd_far])
        return 0

    lax.fori_loop(0, steps, attend_step, 0)
    grad_joined[:, cols : 2 * cols] = acc_k[...].astype(BF)
    grad_joined[:, 2 * cols :] = acc_v[...].astype(BF)
    load_w.wait()

    def back(t, _):
        here = pl.ds(pl.multiple_of(t * 2 * rows, 2 * rows), 2 * rows)

        def tile(j, _):
            w = pl.ds(pl.multiple_of(j * 512, 512), 512)
            att_p[pl.ds(t * 2, 2), :, w] = dot(grad_joined[here, :], qkv_w[w, :], NT).astype(BF).reshape(2, rows, 512)
            return 0

        lax.fori_loop(0, width // 512, tile, 0)
        att_swap(t).start()
        return 0

    lax.fori_loop(0, nz, back, 0)
    col_o[...] = jnp.sum(grad_joined[...].astype(F32), axis=0, keepdims=True)
    load_a.wait()
    blocks = 256 // part

    def qkv_tile(j, _):
        w = pl.ds(pl.multiple_of(j * 256, 256), 256)
        value = dot(tokens[:, :, w].reshape(tree, 256), grad_joined[...], TN).astype(BF)
        for i in range(blocks):
            r = j * blocks + i
            d, f = r // n, r % n
            p = f // 2 * 2 + d % 2
            qkv_g[d // 2 * 2 + f % 2, pl.ds(pl.multiple_of(p * part, part), part), :] = value[i * part : (i + 1) * part]
        return 0

    att_begin()
    lax.fori_loop(0, width // 256, qkv_tile, 0)
    qkv1()
    down2()
    att_near(0)

    def put_ranks(dest):
        def put(lower, value):
            dest[pl.ds(lower * nz, nz)] = value.astype(BF).reshape(nz, part, -1)

        return put

    up_total(put_ranks(up_sum))
    ex_up[0]()
    att_near(1)
    qkv2()
    att_far()
    upd_total(res)
    res[...] += base[...]
    res_low[...] = res[...].astype(BF)
    home[0]()
    square_o[...] = jnp.sum(res[...] * res[...], axis=0, keepdims=True)
    for stage in gb[5:]:
        stage()
    load_b.start()
    load_b.wait()

    def out_tile(j, _):
        w = pl.ds(pl.multiple_of(j * 512, 512), 512)
        value = dot(mixed[...], tokens[:, :, w].reshape(tree, 512), TN).astype(BF)
        out_g[:, :, w] = value.reshape(4, cols // 4, 512)
        return 0

    lax.fori_loop(0, width // 512, out_tile, 0)
    out1()
    qkv_total(put_ranks(qkv_sum))
    ex_qkv[0]()
    att_total(grad_out)
    out2()

    def put_down(lower, value):
        half = value.shape[0]
        down_o[pl.ds(lower * half, half), :] = value

    down_total(put_down)
    def put_out(lower, value):
        half = value.shape[0]
        out_o[pl.ds(lower * half, half), :] = value

    out_total(put_out)
    ex_up[1]()
    home[1]()
    ex_qkv[1]()
    for fn in (up_done, down_done, qkv_done, out_done, upd_done, att_done):
        fn()


def tail_call(slopes, far_t, grad, joined, a1, mixed, qkv_w, branch, upd, up_g, down_g, base, runs, heads, nz, cid):
    tree, cols = mixed.shape
    rows, width = branch.shape
    n = 2 * nz
    part = width // (4 * n)
    unit = down_g.shape[1]
    step = 256
    runs_up, runs_qkv = runs
    shape = jax.ShapeDtypeStruct

    def scatter_refs(own):
        return [
            pltpu.VMEM((own, rows, width), BF),
            pltpu.VMEM((nz, rows, width), BF),
            pltpu.VMEM((nz + 1, rows, width), BF),
            pltpu.SemaphoreType.DMA((3 * nz,)),
            pltpu.SemaphoreType.DMA((3 * nz,)),
        ]

    return pl.pallas_call(
        functools.partial(tail_kernel, heads, nz, runs_up, runs_qkv),
        out_shape=[
            shape((rows, width), F32),
            shape((unit, width), F32),
            shape((part, width), F32),
            shape((1, 3 * cols), F32),
            shape((1, width), F32),
            shape((part, 4 * n * unit), BF),
            shape((part, 3 * width), BF),
            shape((n, rows, width), BF),
            shape((rows, width), BF),
        ],
        in_specs=[pl.BlockSpec(memory_space=pltpu.SMEM), HBM, HBM, VM, HBM, VM, HBM, HBM, HBM, HBM, HBM, VM],
        out_specs=[VM] * 5 + [HBM] * 4,
        scratch_shapes=[
            pltpu.VMEM((n, rows, cols), BF),
            pltpu.VMEM((2, tree, step), F32),
            pltpu.VMEM((n, rows, width), BF),
            pltpu.VMEM((width, 3 * cols), BF),
            pltpu.VMEM((tree, 3 * cols), BF),
            pltpu.VMEM((tree, cols), F32),
            pltpu.VMEM((tree, cols), F32),
        ]
        + scatter_refs(nz)
        + scatter_refs(n)
        + reduce_scratch(n * part, 4 * unit)
        + reduce_scratch(unit, width)
        + reduce_scratch(n * part, 3 * cols)
        + reduce_scratch(part, width)
        + [
            pltpu.VMEM((n, part, 4 * unit), BF),
            pltpu.VMEM((n, part, 3 * cols), BF),
            pltpu.VMEM((4, n * part, 3 * cols), BF),
            pltpu.VMEM((4, part, width), BF),
            pltpu.VMEM((rows, width), F32),
            pltpu.VMEM((rows, width), BF),
        ]
        + gather_sems(nz)
        + exchange_sems(None, nz)
        + exchange_sems(runs_up, nz)
        + exchange_sems(runs_qkv, nz)
        + trade_sems()
        + [pltpu.SemaphoreType.DMA((2,)), pltpu.SemaphoreType.DMA((nz + 3,))],
        compiler_params=params(cid, 63 * MIB),
        name="tail",
    )(slopes, far_t, grad, joined, a1, mixed, qkv_w, branch, upd, up_g, down_g, base)


def gelu_and_slope(value):
    normal = 0.5 + 0.5 * lax.erf(value * math.sqrt(0.5))
    density = jnp.exp(-0.5 * value * value) * (1.0 / math.sqrt(2.0 * math.pi))
    return value * normal, normal + value * density


def mlp_kernel(
    nz, own, cot_in, up_in, down_in, bias, out, upd_out, up_out, down_out, bias_g,
    mlp, cot, up_w, down_w, p, upd, up_g, down_g, active, gh, acc, ups, dns, gsend, grecv, ssend, srecv, lsem,
):
    pos = place()
    x, c, z, y = pos
    blocks, rows, width = mlp.shape
    units = active.shape[1]
    pair = 2 * rows
    me = z * 2 + c
    sib = at(x, 1 - c, z, y)
    up_dev, dn_dev = at(x, c, z + 1, y), at(x, c, z - 1, y)
    UP, DN, SU, SD = 0, nz, 2 * nz, 3 * nz
    S, U, D = 0, nz, 2 * nz

    def f(v):
        return v.astype(F32)

    loads = [
        pltpu.make_async_copy(a, b, lsem.at[i])
        for i, (a, b) in enumerate([(cot_in, cot), (down_in, down_w), (up_in, up_w)])
    ]
    part = up_out.shape[1] // blocks

    def rank_rows(r):
        d, f = r // blocks, r % blocks
        return up_out.at[d // 2 * 2 + f % 2, pl.ds((f // 2 * 2 + d % 2) * part, part)]

    stores = [
        [pltpu.make_async_copy(upd, upd_out, lsem.at[3])],
        [
            pltpu.make_async_copy(up_g.at[pl.ds(r * part, part)], rank_rows(r), lsem.at[5 + r])
            for r in range(4 * blocks)
        ],
        [pltpu.make_async_copy(down_g, down_out, lsem.at[4])],
    ]

    def store(i):
        for copy in stores[i]:
            copy.start()


    def block(b, sem, target):
        return remote(mlp.at[b], mlp.at[b], gsend.at[sem], grecv.at[sem], target)

    def up(d):
        return block((z - d) * 2 + c, UP + d, up_dev)

    def dn(d):
        return block((z + d) * 2 + c, DN + d, dn_dev)

    def side(d, below):
        return block(jnp.where(below, z - d, z + d) * 2 + c, jnp.where(below, SU, SD) + d, sib)

    def turn(i):
        both = jnp.minimum(z, nz - 1 - z)
        two = i <= 2 * both
        d = jnp.where(two, (i + 1) // 2, i - both)
        below = jnp.where(two, i % 2 == 1, z > nz - 1 - z)
        return d, below

    def arrive(i):
        if i == 0:
            block(z * 2 + 1 - c, SU, sib).wait_recv()
            return z
        d, below = turn(i)
        zi = jnp.where(below, z - d, z + d)
        block(zi * 2 + c, jnp.where(below, UP, DN) + d - 1, sib).wait_recv()
        pl.when(below & (z < nz - 1))(lambda: up(d).start())
        pl.when(jnp.logical_not(below) & (z > 0))(lambda: dn(d).start())
        side(d, below).start()
        block(zi * 2 + 1 - c, jnp.where(below, SU, SD) + d, sib).wait_recv()
        return zi

    def swap(t):
        return remote(p.at[t * 2 + 1 - c], acc.at[t], ssend.at[S + t], srecv.at[S + t], sib)

    def rise(t):
        return remote(acc.at[t], ups.at[t], ssend.at[U + t], srecv.at[U + t], up_dev)

    def fall(t):
        return remote(acc.at[t], dns.at[t], ssend.at[D + t], srecv.at[D + t], dn_dev)

    def event(t, upward):
        swap(t).wait_recv()
        acc[t] = (f(acc[t]) + f(p[t * 2 + c])).astype(BF)
        move, came = (rise, ups) if upward else (fall, dns)

        @pl.when(z > 0 if upward else z < nz - 1)
        def _():
            move(t).wait_recv()
            acc[t] = (f(acc[t]) + f(came[t])).astype(BF)

        move(t).start()

    def events(s):
        for t in range(nz):
            zz = s - t
            if 0 <= zz < t:
                pl.when(z == zz)(functools.partial(event, t, True))
            zz = 2 * (nz - 1) - s - t
            if t < zz < nz:
                pl.when(z == zz)(functools.partial(event, t, False))

    def at_rows(ref, zi):
        return ref[pl.ds(zi * 2, 2)].reshape(pair, width)

    def hidden_part(zi, early):
        here = pl.ds(pl.multiple_of(zi * pair, pair), pair)

        def tile(j, _):
            u = pl.ds(pl.multiple_of(j * 256, 256), 256)
            value = dot(at_rows(mlp, zi), up_w[:, u], NN) + bias[:, u]
            grad = dot(at_rows(cot, zi), down_w[u, :], NT)
            act, slope = gelu_and_slope(value)
            low = (grad * slope).astype(BF)
            active[here, u] = act.astype(BF)
            gh[here, u] = low
            bias_g[:, u] += jnp.sum(f(low), axis=0, keepdims=True)
            return 0

        lax.fori_loop(0, units // 256, tile, 0)

        def back(j, _):
            w = pl.ds(pl.multiple_of(j * 512, 512), 512)
            p[pl.ds(zi * 2, 2), :, w] = dot(gh[here, :], up_w[w, :], NT).astype(BF).reshape(2, rows, 512)
            return 0

        lax.fori_loop(0, width // 512, back, 0)

    def forward_part(zi):
        here = pl.ds(pl.multiple_of(zi * pair, pair), pair)

        def tile(j, _):
            w = pl.ds(pl.multiple_of(j * 512, 512), 512)
            upd[pl.ds(zi * 2, 2), :, w] = dot(active[here, :], down_w[:, w], NN).astype(BF).reshape(2, rows, 512)
            return 0

        lax.fori_loop(0, width // 512, tile, 0)

    def up_grads(first, count):
        def tile(j, _):
            w = pl.ds(pl.multiple_of(j * 256, 256), 256)
            up_g[w, :] = dot(mlp[:, :, w].reshape(blocks * rows, 256), gh[...], TN).astype(BF)
            return 0

        lax.fori_loop(first, first + count, tile, 0)

    def down_grads():
        def tile(j, _):
            u = pl.ds(pl.multiple_of(j * 256, 256), 256)
            down_g[u, :] = dot(active[:, u], cot[...].reshape(blocks * rows, width), TN).astype(BF)
            return 0

        lax.fori_loop(0, units // 256, tile, 0)

    mlp[me] = own[...]
    greet(line_partners(nz, pos))
    pl.when(z < nz - 1)(up(0).start)
    pl.when(z > 0)(dn(0).start)
    side(0, z >= 0).start()
    for copy in loads:
        copy.start()
    bias_g[...] = jnp.zeros_like(bias_g)
    for copy in loads:
        copy.wait()
    slots = 2 * nz - 1
    tiles = width // 256
    for s in range(slots):
        if s < nz:
            zi = arrive(s)
            hidden_part(zi, s)
            swap(zi).start()
        events(s)
        if s < nz:
            forward_part(zi)
        if s == nz - 1:
            store(0)
            down_grads()
            store(2)
        elif s == nz:
            up_grads(0, tiles // 2)
        elif s == nz + 1:
            up_grads(tiles // 2, tiles - tiles // 2)
            store(1)
    swap(z).wait_recv()
    out[...] = f(acc[z]) + f(p[z * 2 + c])

    @pl.when(z > 0)
    def _():
        rise(z).wait_recv()
        out[...] += f(ups[z])

    @pl.when(z < nz - 1)
    def _():
        fall(z).wait_recv()
        out[...] += f(dns[z])

    for copies in stores:
        for copy in copies:
            copy.wait()
    side(0, z >= 0).wait_send()
    pl.when(z < nz - 1)(up(0).wait_send)
    pl.when(z > 0)(dn(0).wait_send)
    for k in range(1, nz):

        @pl.when(z >= k)
        def _():
            pl.when(z < nz - 1)(up(k).wait_send)
            side(k, z >= 0).wait_send()

        @pl.when(z + k < nz)
        def _():
            pl.when(z > 0)(dn(k).wait_send)
            side(k, z < 0).wait_send()

    for t in range(nz):
        swap(t).wait_send()
        pl.when(z < t)(rise(t).wait_send)
        pl.when(z > t)(fall(t).wait_send)


def mlp_bytes(nz, rows, width, units):
    tree = 2 * nz * rows
    return 2 * (4 * tree * width + 4 * units * width + 2 * tree * units + 3 * nz * rows * width) + 8 * rows * width


def mlp_call(own, cot, up_w, down_w, bias, nz, cid):
    rows, width = own.shape
    units = down_w.shape[0]
    n = 2 * nz
    shape = jax.ShapeDtypeStruct
    return pl.pallas_call(
        functools.partial(mlp_kernel, nz),
        out_shape=[
            shape((rows, width), F32),
            shape((n, rows, width), BF),
            shape((4, width // 4, units), BF),
            shape((units, width), BF),
            shape((1, units), F32),
        ],
        in_specs=[VM, HBM, HBM, HBM, VM],
        out_specs=[VM, HBM, HBM, HBM, VM],
        scratch_shapes=[
            pltpu.VMEM((n, rows, width), BF),
            pltpu.VMEM((n, rows, width), BF),
            pltpu.VMEM((width, units), BF),
            pltpu.VMEM((units, width), BF),
            pltpu.VMEM((n, rows, width), BF),
            pltpu.VMEM((n, rows, width), BF),
            pltpu.VMEM((width, units), BF),
            pltpu.VMEM((units, width), BF),
            pltpu.VMEM((n * rows, units), BF),
            pltpu.VMEM((n * rows, units), BF),
        ]
        + [pltpu.VMEM((nz, rows, width), BF)] * 3
        + gather_sems(nz)
        + [pltpu.SemaphoreType.DMA((3 * nz,))] * 2
        + [pltpu.SemaphoreType.DMA((5 + 4 * n,))],
        compiler_params=params(cid, 62 * MIB),
        name="mlp",
    )(own, cot, up_w, down_w, bias)


def attend_kernel(
    heads, nz, unit, slopes, far, joined_q, joined, cot, w_up, w_out, out, cot_all, up_w, out_w, *sems
):
    cols = heads * HD
    step, steps = pl.program_id(0), pl.num_programs(0)
    pos = place()
    n = 2 * nz
    gc = line_gather(cot, cot_all, *sems[:2], nz, True, pos)
    gu = sliced_gather(w_up, up_w, up_runs(nz, unit), sems[2:6], nz, pos)
    go = full_gather(w_out, out_w, *sems[6:8], nz, pos)

    @pl.when(step == 0)
    def _():
        x, c, z, y = pos
        greet(rank_partners(nz, pos) + group_partners(pos) + [(c != y, at(x, y, z, c))])
        gc[0]()
        gu[0]()
        go[0]()

    @pl.when(step == 1)
    def _():
        for stage in go[1:nz]:
            stage()

    @pl.when(step == 2)
    def _():
        for stage in gu[1 : n + 1]:
            stage()
        gc[1]()

    gap = far[...]
    for h in range(heads):
        q = joined_q[:, h * HD : (h + 1) * HD]
        k = joined[:, cols + h * HD : cols + (h + 1) * HD]
        v = joined[:, 2 * cols + h * HD : 2 * cols + (h + 1) * HD]
        logits = dot(q, k, NT) * HD ** (-0.5) + slopes[h] * gap
        weights = jnp.exp(logits - jnp.max(logits, axis=1, keepdims=True))
        probs = weights * (1.0 / jnp.sum(weights, axis=1, keepdims=True))
        out[:, h * HD : (h + 1) * HD] = dot(probs.astype(BF), v, NN).astype(BF)

    @pl.when(step == steps - 1)
    def _():
        for stage in go[nz : 2 * nz]:
            stage()
        ahead, later = gc[2:-1], gu[n + 1 : -1]
        for i, stage in enumerate(ahead):
            stage()
            for other in later[i * n // len(ahead) : (i + 1) * n // len(ahead)]:
                other()
        for stage in go[2 * nz :]:
            stage()
        gc[-1]()
        gu[-1]()


def attend(slopes, far, joined, cot, w_up, w_out, unit, heads, nz, cid):
    tree = far.shape[0]
    cols = heads * HD
    rows = min(256, max(128, 2**18 // tree))
    block, width = cot.shape
    part = w_up.shape[0]
    n = 2 * nz
    shapes = [(tree, cols), (n, block, width), (4 * n, part, 4 * unit), (4 * n, part, width)]
    return pl.pallas_call(
        functools.partial(attend_kernel, heads, nz, unit),
        out_shape=[jax.ShapeDtypeStruct(s, BF) for s in shapes],
        grid=(tree // rows,),
        in_specs=[
            pl.BlockSpec(memory_space=pltpu.SMEM),
            pl.BlockSpec((rows, tree), lambda i: (i, 0)),
            pl.BlockSpec((rows, 3 * cols), lambda i: (i, 0)),
            pl.BlockSpec((tree, 3 * cols), lambda i: (0, 0)),
            HBM,
            HBM,
            HBM,
        ],
        out_specs=[pl.BlockSpec((rows, cols), lambda i: (i, 0)), HBM, HBM, HBM],
        scratch_shapes=gather_sems(nz) + sliced_sems(nz) + full_sems(nz),
        compiler_params=params(cid, 56 * MIB),
        name="attend",
    )(slopes, far, joined, joined, cot, w_up, w_out)


def attend_back_kernel(heads, nz, kinds, slopes, far, joined_q, joined, grad, branch, part_sums, *refs):
    count = len(kinds)
    srcs, refs = refs[:count], refs[count:]
    out_q, out_k, out_v, branch_all, update, refs = *refs[:5], refs[5:]
    dsts, refs = refs[:count], refs[count:]
    acc_k, acc_v, p, refs = *refs[:3], refs[3:]
    scratch, gsems, hsems, psem = refs[:5], refs[5:7], refs[7:9], refs[9]
    cols = heads * HD
    step = pl.program_id(0)
    pos = place()
    gb = line_gather(branch, branch_all, *gsems, nz, False, pos)
    hs = hand_stages(srcs, dsts, kinds, *hsems, nz, pos)
    load = pltpu.make_async_copy(part_sums, p, psem.at[0])

    @pl.when(step == 0)
    def _():
        acc_k[...] = jnp.zeros_like(acc_k)
        acc_v[...] = jnp.zeros_like(acc_v)
        greet(line_partners(nz, pos) + group_partners(pos))
        hs[0]()
        gb[0]()
        gb[1]()
        load.start()

    @pl.when(step == 3)
    def _():
        gb[2]()

    gap = far[...]
    for h in range(heads):
        here = slice(h * HD, (h + 1) * HD)
        q = joined_q[:, here]
        k = joined[:, cols + h * HD : cols + (h + 1) * HD]
        v = joined[:, 2 * cols + h * HD : 2 * cols + (h + 1) * HD]
        g = grad[:, here]
        logits = dot(k, q, NT) * HD ** (-0.5) + slopes[h] * gap
        weights = jnp.exp(logits - jnp.max(logits, axis=0, keepdims=True))
        probs = weights * (1.0 / jnp.sum(weights, axis=0, keepdims=True))
        grad_probs = dot(v, g, NT)
        delta = jnp.sum(probs * grad_probs, axis=0, keepdims=True)
        grad_raw = (probs * (grad_probs - delta) * HD ** (-0.5)).astype(BF)
        acc_v[:, here] += dot(probs.astype(BF), g, NN)
        acc_k[:, here] += dot(grad_raw, q, NN)
        out_q[:, here] = dot(grad_raw, k, TN).astype(BF)

    @pl.when(step == pl.num_programs(0) - 1)
    def _():
        out_k[...] = acc_k[...].astype(BF)
        out_v[...] = acc_v[...].astype(BF)
        for stage in gb[3:]:
            stage()
        load.wait()
        scatter_blocks(nz, pos, p, update, *scratch)
        hs[1]()


def attend_back(slopes, far_t, joined, grad, branch, part_sums, arrays, kinds, heads, nz, cid):
    tree = far_t.shape[0]
    cols = heads * HD
    rows = min(256, max(128, 2**18 // tree))
    block, width = branch.shape
    full = pl.BlockSpec((tree, cols), lambda i: (0, 0))
    part = pl.BlockSpec((rows, cols), lambda i: (i, 0))
    return pl.pallas_call(
        functools.partial(attend_back_kernel, heads, nz, kinds),
        out_shape=[jax.ShapeDtypeStruct((tree, cols), BF)] * 3
        + [jax.ShapeDtypeStruct((2 * nz, block, width), BF), jax.ShapeDtypeStruct((block, width), F32)]
        + hand_shapes(arrays, kinds, nz),
        grid=(tree // rows,),
        in_specs=[
            pl.BlockSpec(memory_space=pltpu.SMEM),
            pl.BlockSpec((tree, rows), lambda i: (0, i)),
            pl.BlockSpec((rows, 3 * cols), lambda i: (i, 0)),
            pl.BlockSpec((tree, 3 * cols), lambda i: (0, 0)),
            part,
            HBM,
            HBM,
        ]
        + [HBM] * len(arrays),
        out_specs=[part, full, full, HBM, pl.BlockSpec((block, width), lambda i: (0, 0))] + [HBM] * len(arrays),
        scratch_shapes=[pltpu.VMEM((tree, cols), F32)] * 2
        + [pltpu.VMEM((2 * nz, block, width), BF)]
        + scatter_scratch(nz, block, width)
        + gather_sems(nz)
        + hand_sems(kinds)
        + [pltpu.SemaphoreType.DMA((1,))],
        compiler_params=params(cid, 62 * MIB),
        name="attend_back",
    )(slopes, far_t, joined, joined, grad, branch, part_sums, *arrays)


def norm_parts(values):
    center = values - jnp.mean(values, axis=-1, keepdims=True)
    inverse = lax.rsqrt(jnp.mean(center * center, axis=-1, keepdims=True) + EPSILON)
    return (center * inverse, inverse)


def norm_back(grad_normed, normed, inverse):
    mean_grad = jnp.mean(grad_normed, axis=-1, keepdims=True)
    mean_cross = jnp.mean(grad_normed * normed, axis=-1, keepdims=True)
    return inverse * (grad_normed - mean_grad - normed * mean_cross)


def tree_tables(parents, seg_blocks, valid):
    segments = parents.shape[0]
    seg_tokens = jnp.broadcast_to(seg_blocks[:, None], (seg_blocks.shape[0], BLK)).reshape(-1)
    labels = jnp.arange(segments, dtype=jnp.int32)
    member = (seg_tokens[:, None] == labels[None, :]).astype(jnp.int32)
    counted = member * valid[:, None]
    before = jnp.cumsum(counted, axis=0) - counted
    rank = jnp.sum(before * member, axis=1)
    seg_len = jnp.sum(counted, axis=0)
    picked = (parents[:, None] == labels[None, :]).astype(jnp.int32)
    grand = jnp.sum(picked * parents[None, :], axis=1)
    ancestor = ((labels[None, :] == parents[:, None]) | (labels[None, :] == grand[:, None])) & (
        labels[None, :] != labels[:, None]
    )
    offset = jnp.sum(ancestor.astype(jnp.int32) * seg_len[None, :], axis=1)
    position = jnp.sum(member * offset[None, :], axis=1) + rank
    return (seg_tokens, position, ancestor.astype(jnp.float32))


def allowed_mask(seg, index, valid, ancestor):
    labels = jnp.arange(ancestor.shape[0], dtype=jnp.int32)
    member = (seg[:, None] == labels[None, :]).astype(jnp.float32)
    reach = jnp.dot(jnp.dot(member, ancestor), member.T) > 0.5
    causal = (seg[:, None] == seg[None, :]) & (index[None, :] <= index[:, None])
    visible = (valid[None, :] == 1) | (index[None, :] == index[:, None])
    return (reach | causal) & visible


def gelu_exact(value):
    return jax.nn.gelu(value, approximate=False)


def mm(spec, a, b):
    return jnp.einsum(spec, a, b, preferred_element_type=F32)


def padded(flat, lanes):
    return jnp.pad(flat, [(0, 0)] * (flat.ndim - 1) + [(0, -flat.shape[-1] % lanes)])


def by_steps(
    layer_in,
    cotangent,
    w_qkv,
    w_out,
    w_up,
    w_down,
    gain_attn,
    shift_attn,
    bias_query,
    bias_value,
    bias_out,
    gain_mlp,
    shift_mlp,
    bias_up,
    bias_down,
    parents,
    seg_blocks,
    token_valid,
):
    rows, width = layer_in.shape
    fsdp = lax.axis_size("fsdp")
    nz = fsdp // 2
    devices = 4 * fsdp
    x, c, z, y = place()
    rank = z * 2 + c
    heads = H // fsdp
    cols = heads * HD
    tree = token_valid.shape[1]
    part = w_up.shape[0]
    unit = w_down.shape[0]

    vec = jnp.concatenate(
        [gain_attn, shift_attn, bias_query, bias_value, bias_out, gain_mlp, shift_mlp, bias_down, bias_up]
    ).astype(F32)
    vec = padded(vec, 1024).reshape(-1, 128)
    tab = jnp.concatenate([token_valid[0], seg_blocks[0], parents[0]])
    tab = padded(tab, 1024).reshape(-1, 128)
    aligned = part == HD and cols % 256 == 0
    if not aligned:
        w_qkv = w_qkv.reshape(part, 3, fsdp, cols).transpose(2, 0, 1, 3).reshape(fsdp, part, 3 * cols)
    x_all, qkv_w, down_w, vecs, tab = fetch(nz, layer_in, w_qkv, w_down, part, vec, tab, 1)
    down_w = down_w.reshape(4 * unit, width)
    x_all = x_all.reshape(tree, width)
    qkv_w = qkv_w.reshape(width, 3 * cols)
    vecs = vecs.reshape(devices, -1)
    (gain_one, shift_one, query_bias, value_bias, out_bias, gain_two, shift_two, down_bias) = [
        vecs[:, i * part : (i + 1) * part].reshape(-1) for i in range(8)
    ]
    up_bias = vecs[:, 8 * part : 8 * part + unit].reshape(2, 2, nz, 2, unit)
    up_bias = lax.dynamic_slice(up_bias, (0, c, z, 0, 0), (2, 1, 1, 2, unit)).reshape(-1)

    def own_rows(v):
        return lax.dynamic_slice_in_dim(v, rank * rows, rows, 0)

    normed_all, _ = norm_parts(x_all.astype(F32))
    attn_in = (normed_all * gain_one + shift_one).astype(BF)
    inputs = own_rows(x_all).astype(F32)
    normed_one, inverse_one = norm_parts(inputs)

    if aligned:

        def own_cols(v):
            v = v.reshape(2, 2, nz, 2, HD)
            return lax.dynamic_slice(v, (0, c, z, 0, 0), (2, 1, 1, 2, HD)).reshape(-1)

        def spread(v):
            v = v.reshape(2, 1, 1, 2, HD)
            return lax.dynamic_update_slice(jnp.zeros((2, 2, nz, 2, HD), F32), v, (0, c, z, 0, 0))

        numbers = block_of(jnp.arange(2)[:, None], c, z, jnp.arange(2)[None, :], nz).reshape(-1)
    else:

        def own_cols(v):
            return lax.dynamic_slice_in_dim(v, rank * cols, cols, 0)

        def spread(v):
            return lax.dynamic_update_slice_in_dim(jnp.zeros((width,), F32), v, rank * cols, 0)

        numbers = rank * heads + jnp.arange(heads)

    joined_bias = jnp.concatenate([own_cols(query_bias), jnp.zeros((cols,), F32), own_cols(value_bias)])
    joined = (jnp.dot(attn_in, qkv_w, preferred_element_type=F32) + joined_bias).astype(BF)

    tab = tab.reshape(-1)
    blocks = seg_blocks.shape[1]
    valid = tab[:tree]
    seg, position, ancestor = tree_tables(
        tab[tree + blocks : tree + blocks + parents.shape[1]], tab[tree : tree + blocks], valid
    )
    index = jnp.arange(tree, dtype=jnp.int32)
    mask = allowed_mask(seg, index, valid, ancestor)
    far = jnp.where(mask, (position[None, :] - position[:, None]).astype(F32), MASKED)
    slopes = jnp.exp2(-8.0 * (numbers.astype(F32) + 1.0) / H)
    mixed, cot, up_w, out_w = attend(slopes, far, joined, cotangent, w_up, w_out, unit, heads, nz, 9)
    out_w = out_w.reshape(width, width)
    cot = cot.reshape(tree, width)
    up_w = up_w.reshape(width, 4 * unit)

    mixed_own = exchange(mixed.reshape(fsdp, rows, cols), nz, 2, "mixed_to_tokens")
    if aligned:
        mixed_own = mixed_own.reshape(nz, 2, rows, 2, 2 * HD).transpose(2, 3, 1, 0, 4).reshape(rows, width)
    else:
        mixed_own = mixed_own.transpose(1, 0, 2).reshape(rows, width)
    branch = jnp.dot(mixed_own, out_w, preferred_element_type=F32) + out_bias
    middle = inputs + branch
    normed_two, inverse_two = norm_parts(middle)
    mlp_own = (normed_two * gain_two + shift_two).astype(BF)
    cot_blocks = cot.reshape(fsdp, rows, width)
    mlp_in = gather_tokens(mlp_own, nz, 3).reshape(tree, width)
    hidden = jnp.dot(mlp_in, up_w, preferred_element_type=F32) + up_bias
    active_float, gelu_pull = jax.vjp(gelu_exact, hidden)
    active = active_float.astype(BF)
    grad_active = mm("td,fd->tf", cot, down_w)
    grad_hidden = gelu_pull(grad_active)[0].astype(BF)
    grad_mlp_in = mm("tf,df->td", grad_hidden, up_w).astype(BF).reshape(fsdp, rows, width)
    grad_mlp_in = scatter_tokens(grad_mlp_in, nz, 4)
    update = jnp.dot(active, down_w, preferred_element_type=F32).astype(BF).reshape(fsdp, rows, width)
    down_g = mm("tf,td->fd", active, cot).astype(BF)
    up_g = mm("td,tf->df", mlp_in, grad_hidden).astype(BF)
    grad_bias_up = jnp.sum(grad_hidden.astype(F32), axis=0)
    down_g = down_g.reshape(4, unit, width)
    cot_own = own_rows(cot).astype(F32)
    grad_middle = cot_own + norm_back(grad_mlp_in * gain_two, normed_two, inverse_two)
    grad_branch = grad_middle.astype(BF)
    grad_mixed = mm("te,de->td", grad_branch, out_w).astype(BF)
    if not aligned:
        grad_out_w = lax.psum_scatter(
            mm("td,te->de", mixed_own, grad_branch).astype(BF), BOTH, scatter_dimension=0, tiled=True
        ).astype(F32)
    if aligned:
        grad_mixed = grad_mixed.reshape(rows, 2, 2, nz, 2 * HD).transpose(3, 2, 0, 1, 4).reshape(fsdp, rows, cols)
    else:
        grad_mixed = grad_mixed.reshape(rows, fsdp, cols).transpose(1, 0, 2)
    up_g = up_g.reshape(devices, part, 4 * unit)
    grad_heads = exchange(grad_mixed, nz, 5, "grad_to_heads")
    grad_heads = grad_heads.reshape(tree, cols)
    grad_q, grad_k, grad_v, branch_all, update, down_c, up_c = attend_back(
        slopes, far.T, joined, grad_heads, grad_branch, update, [down_g, up_g], (False, True), heads, nz, 6
    )
    result = middle + update + down_bias
    grad_joined = jnp.concatenate([grad_q, grad_k, grad_v], axis=1)

    def mine(g, came):
        g = g.reshape((2, 2, nz, 2) + g.shape[1:])
        g = lax.dynamic_slice(g, (x, 0, 0, y, 0, 0), (1, 2, nz, 1) + g.shape[4:])
        g = g.reshape((2, nz) + g.shape[4:]).swapaxes(0, 1)
        return (g.reshape(came.shape[1:]).astype(F32) + jnp.sum(came.astype(F32), axis=0)).astype(BF)

    def mine_flat(g, came):
        return lax.dynamic_index_in_dim(g, x * 2 + y, 0, keepdims=False).astype(F32) + jnp.sum(came.astype(F32), axis=0)

    grad_down_w = mine_flat(down_g, down_c)
    qkv_g = mm("td,te->de", attn_in, grad_joined).astype(BF).reshape(devices, part, 3 * cols)
    flat = []
    if aligned:
        flat = [mm("td,te->de", mixed, branch_all.reshape(tree, width)).astype(BF).reshape(4, part, width)]
    kinds = (True,) + (False,) * len(flat)
    grad_attn_in = mm("te,de->td", grad_joined, qkv_w).astype(BF).reshape(fsdp, rows, width)
    grad_attn_in, grad_up_w, layer_out, qkv_c, *out_c = scatter_and_hand(
        grad_attn_in, mine(up_g, up_c), up_runs(nz, unit), result.astype(BF), [qkv_g] + flat, kinds, nz, 10
    )
    if aligned:
        grad_out_w = mine_flat(flat[0], out_c[0])
    col, square = jnp.sum(grad_joined.astype(F32), axis=0), jnp.sum(result * result)
    grad_up_w = grad_up_w.astype(F32)
    grad_inputs = grad_middle + norm_back(grad_attn_in * gain_one, normed_one, inverse_one)

    smalls = [
        jnp.sum(grad_attn_in * normed_one, axis=0),
        jnp.sum(grad_attn_in, axis=0),
        spread(col[:cols]),
        spread(col[2 * cols :]),
        jnp.sum(grad_branch.astype(F32), axis=0),
        jnp.sum(grad_mlp_in * normed_two, axis=0),
        jnp.sum(grad_mlp_in, axis=0),
        jnp.sum(cot_own, axis=0),
    ]
    grad_bias_up = grad_bias_up.reshape(2, 1, 1, 2, unit)
    grad_bias_up = lax.dynamic_update_slice(jnp.zeros((2, 2, nz, 2, unit), F32), grad_bias_up, (0, c, z, 0, 0))
    squares = jnp.stack([square, jnp.sum(branch * branch)])
    packed = jnp.concatenate(
        [v.reshape(devices, part) for v in smalls]
        + [grad_bias_up.reshape(devices, unit), jnp.broadcast_to(squares, (devices, 2))],
        axis=1,
    )
    packed = padded(packed, 1024).reshape(devices, -1, 128)
    runs = qkv_runs(nz, width, cols) if aligned else None
    grad_x, packed, grad_qkv_w = finish(grad_inputs.astype(BF), packed, mine(qkv_g, qkv_c), runs, nz, 8)
    if not aligned:
        grad_qkv_w = grad_qkv_w.reshape(fsdp, part, 3, cols).transpose(1, 2, 0, 3).reshape(part, -1)
    grad_qkv_w = grad_qkv_w.astype(F32)
    packed = packed.reshape(-1)
    small = [packed[i * part : (i + 1) * part] for i in range(8)]
    up_at = 8 * part
    root_squares = jnp.sqrt(packed[up_at + unit : up_at + unit + 2] / (devices * rows * width))
    return (
        layer_out,
        grad_x,
        grad_qkv_w,
        grad_out_w,
        grad_up_w,
        grad_down_w,
        small[0],
        small[1],
        small[2],
        small[3],
        small[4],
        small[5],
        small[6],
        packed[up_at : up_at + unit],
        small[7],
        root_squares,
    )


def by_kernels(
    layer_in,
    cotangent,
    w_qkv,
    w_out,
    w_up,
    w_down,
    gain_attn,
    shift_attn,
    bias_query,
    bias_value,
    bias_out,
    gain_mlp,
    shift_mlp,
    bias_up,
    bias_down,
    parents,
    seg_blocks,
    token_valid,
):
    rows, width = layer_in.shape
    fsdp = lax.axis_size("fsdp")
    nz = fsdp // 2
    devices = 4 * fsdp
    x, c, z, y = place()
    rank = z * 2 + c
    heads = H // fsdp
    cols = heads * HD
    tree = token_valid.shape[1]
    part = w_up.shape[0]
    unit = w_down.shape[0]

    slopes = jnp.asarray(np.exp2(-8.0 * (np.arange(H) + 1.0) / H).astype(np.float32))
    vectors = (gain_attn, shift_attn, bias_query, bias_value, bias_out, gain_mlp, shift_mlp, bias_down)
    joined, mixed, mixed_own, own, whole, up_bias, attn_in, far, cot, qkv_w, up_w, out_w, down_w = head_call(
        slopes, (token_valid, seg_blocks, parents), vectors, bias_up, layer_in, cotangent, w_qkv, w_up, w_out, w_down,
        heads, nz, 1,
    )
    qkv_w = qkv_w.reshape(width, 3 * cols)
    up_w = up_w.reshape(width, 4 * unit)
    out_w = out_w.reshape(width, width)
    down_w = down_w.reshape(4 * unit, width)
    gain_one, out_bias, gain_two, shift_two, down_bias = [whole[i] for i in (0, 4, 5, 6, 7)]

    inputs = own.astype(F32)
    normed_one, inverse_one = norm_parts(inputs)
    branch = jnp.dot(mixed_own, out_w, preferred_element_type=F32) + out_bias
    middle = inputs + branch
    normed_two, inverse_two = norm_parts(middle)
    mlp_own = (normed_two * gain_two + shift_two).astype(BF)
    grad_mlp_in, update, up_g, down_g, grad_bias_up = mlp_call(mlp_own, cot, up_w, down_w, up_bias, nz, 3)
    down_g = down_g.reshape(4, unit, width)

    cot_own = lax.dynamic_index_in_dim(cot, rank, 0, keepdims=False).astype(F32)
    grad_middle = cot_own + norm_back(grad_mlp_in * gain_two, normed_two, inverse_two)
    grad_branch = grad_middle.astype(BF)
    grad_mixed = mm("te,de->td", grad_branch, out_w).astype(BF)
    grad_mixed = grad_mixed.reshape(rows, 2, 2, nz, 2 * HD).transpose(3, 2, 0, 1, 4).reshape(fsdp, rows, cols)
    runs = up_runs(nz, unit), qkv_runs(nz, width, cols)
    grad_attn_in, grad_down_w, grad_out_w, col, square, grad_up_w, grad_qkv_w, _, layer_out = tail_call(
        slopes, far, grad_mixed, joined, attn_in, mixed.reshape(tree, cols), qkv_w, grad_branch,
        update, up_g, down_g, middle + down_bias, runs, heads, nz, 6,
    )
    grad_inputs = grad_middle + norm_back(grad_attn_in * gain_one, normed_one, inverse_one)

    def spread(v):
        v = v.reshape(2, 1, 1, 2, HD)
        return lax.dynamic_update_slice(jnp.zeros((2, 2, nz, 2, HD), F32), v, (0, c, z, 0, 0))

    smalls = [
        jnp.sum(grad_attn_in * normed_one, axis=0),
        jnp.sum(grad_attn_in, axis=0),
        spread(col[0, :cols]),
        spread(col[0, 2 * cols :]),
        jnp.sum(grad_branch.astype(F32), axis=0),
        jnp.sum(grad_mlp_in * normed_two, axis=0),
        jnp.sum(grad_mlp_in, axis=0),
        jnp.sum(cot_own, axis=0),
    ]
    grad_bias_up = grad_bias_up.reshape(2, 1, 1, 2, unit)
    grad_bias_up = lax.dynamic_update_slice(jnp.zeros((2, 2, nz, 2, unit), F32), grad_bias_up, (0, c, z, 0, 0))
    squares = jnp.stack([jnp.sum(square), jnp.sum(branch * branch)])
    packed = jnp.concatenate(
        [v.reshape(devices, part) for v in smalls]
        + [grad_bias_up.reshape(devices, unit), jnp.broadcast_to(squares, (devices, 2))],
        axis=1,
    )
    packed = padded(packed, 1024).reshape(devices, -1, 128)
    grad_x, packed = finish(grad_inputs.astype(BF), packed, None, None, nz, 8)
    packed = packed.reshape(-1)
    small = [packed[i * part : (i + 1) * part] for i in range(8)]
    up_at = 8 * part
    root_squares = jnp.sqrt(packed[up_at + unit : up_at + unit + 2] / (devices * rows * width))
    return (
        layer_out,
        grad_x,
        grad_qkv_w.astype(F32),
        grad_out_w,
        grad_up_w.astype(F32),
        grad_down_w,
        small[0],
        small[1],
        small[2],
        small[3],
        small[4],
        small[5],
        small[6],
        packed[up_at : up_at + unit],
        small[7],
        root_squares,
    )


def per_device(*args):
    layer_in, w_down, token_valid = args[0], args[5], args[17]
    fsdp = lax.axis_size("fsdp")
    rows, width = layer_in.shape
    unit = w_down.shape[0]
    fits = mlp_bytes(fsdp // 2, rows, width, 4 * unit) < 50 * MIB
    whole_heads = args[2].shape[0] == HD and H // fsdp == 4 and width == H * HD
    if fsdp == 8 and fits and whole_heads and unit % 128 == 0 and token_valid.shape[1] % 256 == 0 and rows == 128:
        return by_kernels(*args)
    return by_steps(*args)


def solution(mesh):
    matrix, vector, table = P(BOTH, None), P(BOTH), P("dp", None)
    return jax.shard_map(
        per_device,
        mesh=mesh,
        in_specs=(matrix,) * 6 + (vector,) * 9 + (table,) * 3,
        out_specs=(matrix,) * 6 + (vector,) * 9 + (P(),),
        check_vma=False,
    )
```

```python
import functools
import math

import jax
import jax.numpy as jnp
import numpy as np
from jax import lax
from jax.experimental import pallas as pl
from jax.experimental.pallas import tpu as pltpu
from jax.sharding import PartitionSpec as P

H = 32
HD = 64
BLK = 32

EPSILON = 1e-05
MASKED = -1e30
BF = jnp.bfloat16
F32 = jnp.float32
BOTH = ("dp", "fsdp")
MESH = pl.DeviceIdType.MESH
HBM = pl.BlockSpec(memory_space=pl.ANY)
VM = pl.BlockSpec(memory_space=pltpu.VMEM)
MIB = 2**20


def place():
    d, f = lax.axis_index("dp"), lax.axis_index("fsdp")
    return d // 2, d % 2, f // 2, f % 2


def at(x, c, z, y):
    return (x * 2 + c, z * 2 + y)


def remote(src, dst, send, recv, target):
    return pltpu.make_async_remote_copy(
        src_ref=src, dst_ref=dst, send_sem=send, recv_sem=recv, device_id=target, device_id_type=MESH
    )


def greet(partners):
    barrier = pltpu.get_barrier_semaphore()
    count = 0
    for condition, device in partners:

        @pl.when(condition)
        def _():
            pl.semaphore_signal(barrier, inc=1, device_id=device, device_id_type=MESH)

        count = count + jnp.asarray(condition).astype(jnp.int32)
    pl.semaphore_wait(barrier, count)


def greet_all(devices, fsdp, me):
    barrier = pltpu.get_barrier_semaphore()

    def one(k, _):
        other = (me + k) % devices
        pl.semaphore_signal(barrier, inc=1, device_id=(other // fsdp, other % fsdp), device_id_type=MESH)
        return 0

    lax.fori_loop(1, devices, one, 0)
    pl.semaphore_wait(barrier, devices - 1)


def line_partners(nz, pos):
    x, c, z, y = pos
    return [(z >= 0, at(x, 1 - c, z, y)), (z > 0, at(x, c, z - 1, y)), (z < nz - 1, at(x, c, z + 1, y))]


def rank_partners(nz, pos):
    x, c, z, y = pos
    n = 2 * nz
    others = [(z * 2 + c + k) % n for k in range(1, n)]
    return [(z >= 0, at(x, p % 2, p // 2, y)) for p in others]


def group_partners(pos):
    x, c, z, y = pos
    return [(z >= 0, at(x ^ (m // 2), c, z, y ^ (m % 2))) for m in (1, 2, 3)]


def line_gather(src, dst, send, recv, nz, swap, pos):
    x, c, z, y = pos
    own = z * 2 + c
    sib = at(x, 1 - c, z, y)
    up_dev, dn_dev = at(x, c, z + 1, y), at(x, c, z - 1, y)
    UP, DN, SU, SD = 0, nz, 2 * nz, 3 * nz
    OWN = 4 * nz

    def block(b, moved):
        return dst.at[b] if moved else src

    def up(k):
        b = (z - k) * 2 + c
        return remote(block(b, k or swap), dst.at[b], send.at[UP + k], recv.at[UP + k], up_dev)

    def dn(k):
        b = (z + k) * 2 + c
        return remote(block(b, k or swap), dst.at[b], send.at[DN + k], recv.at[DN + k], dn_dev)

    def side(k, base, sign):
        b = (z + sign * k) * 2 + c
        return remote(block(b, k or swap), dst.at[b], send.at[base + k], recv.at[base + k], sib)

    def got(b, sem):
        return remote(dst.at[b], dst.at[b], send.at[OWN], recv.at[sem], sib)

    local = pltpu.make_async_copy(src, dst.at[own], recv.at[OWN])
    trade = remote(src, dst.at[z * 2 + y], send.at[OWN], recv.at[OWN], at(x, y, z, c))

    def first():
        if swap:
            pl.when(c == y)(local.start)
            pl.when(c != y)(trade.start)
        else:
            local.start()

    def spread():
        if swap:
            local.wait()
        pl.when(z < nz - 1)(up(0).start)
        pl.when(z > 0)(dn(0).start)
        side(0, SU, 1).start()

    def step(k):
        @pl.when(z >= k)
        def _():
            got((z - k) * 2 + c, UP + k - 1).wait_recv()
            pl.when(z < nz - 1)(up(k).start)
            side(k, SU, -1).start()

        @pl.when(z + k < nz)
        def _():
            got((z + k) * 2 + c, DN + k - 1).wait_recv()
            pl.when(z > 0)(dn(k).start)
            side(k, SD, 1).start()

    def last():
        if swap:
            pl.when(c != y)(trade.wait_send)
        else:
            local.wait()
        got(z * 2 + 1 - c, SU).wait_recv()
        pl.when(z < nz - 1)(up(0).wait_send)
        pl.when(z > 0)(dn(0).wait_send)
        side(0, SU, 1).wait_send()
        for k in range(1, nz):

            @pl.when(z >= k)
            def _():
                got((z - k) * 2 + 1 - c, SU + k).wait_recv()
                pl.when(z < nz - 1)(up(k).wait_send)
                side(k, SU, -1).wait_send()

            @pl.when(z + k < nz)
            def _():
                got((z + k) * 2 + 1 - c, SD + k).wait_recv()
                pl.when(z > 0)(dn(k).wait_send)
                side(k, SD, 1).wait_send()

    return [first, spread] + [functools.partial(step, k) for k in range(1, nz)] + [last]


def gather_sems(nz):
    return [pltpu.SemaphoreType.DMA((4 * nz + 1,))] * 2


def gather_kernel(nz, src, dst, send, recv):
    pos = place()
    greet(line_partners(nz, pos))
    for stage in line_gather(src, dst, send, recv, nz, False, pos):
        stage()


def params(cid, vmem=None):
    return pltpu.CompilerParams(collective_id=cid, has_side_effects=True, vmem_limit_bytes=vmem)


def gather_tokens(a, nz, cid):
    return pl.pallas_call(
        functools.partial(gather_kernel, nz),
        out_shape=jax.ShapeDtypeStruct((2 * nz,) + a.shape, a.dtype),
        in_specs=[HBM],
        out_specs=HBM,
        scratch_shapes=gather_sems(nz),
        compiler_params=params(cid),
        name="gather_tokens",
    )(a)


def scatter_blocks(nz, pos, p, out, acc, ups, dns, send, recv):
    x, c, z, y = pos
    sib = at(x, 1 - c, z, y)
    S, U, D = 0, nz, 2 * nz

    def f(v):
        return v.astype(F32)

    def swap(t):
        return remote(p.at[t * 2 + 1 - c], acc.at[t], send.at[S + t], recv.at[S + t], sib)

    def up(t):
        return remote(acc.at[t], ups.at[t], send.at[U + t], recv.at[U + t], at(x, c, z + 1, y))

    def dn(t):
        return remote(acc.at[t], dns.at[t], send.at[D + t], recv.at[D + t], at(x, c, z - 1, y))

    order = []
    for i in range(nz - 1):
        order += [(True, nz - 1 - i), (False, i)]
    for upward, t in order:
        pl.when(z < t if upward else z > t)(swap(t).start)
    swap(z).start()
    for upward, t in order:

        @pl.when(z < t if upward else z > t)
        def _():
            swap(t).wait_recv()
            acc[t] = (f(acc[t]) + f(p[t * 2 + c])).astype(BF)
            move, came = (up, ups) if upward else (dn, dns)

            @pl.when(z > 0 if upward else z < nz - 1)
            def _():
                move(t).wait_recv()
                acc[t] = (f(acc[t]) + f(came[t])).astype(BF)

            move(t).start()

    swap(z).wait_recv()
    out[...] = f(acc[z]) + f(p[z * 2 + c])

    @pl.when(z > 0)
    def _():
        up(z).wait_recv()
        out[...] += f(ups[z])

    @pl.when(z < nz - 1)
    def _():
        dn(z).wait_recv()
        out[...] += f(dns[z])

    for t in range(nz):
        swap(t).wait_send()
        pl.when(z < t)(up(t).wait_send)
        pl.when(z > t)(dn(t).wait_send)


def scatter_scratch(nz, rows, width):
    return [pltpu.VMEM((nz, rows, width), BF)] * 3 + [pltpu.SemaphoreType.DMA((3 * nz,))] * 2


def scatter_kernel(nz, p, out, *scratch):
    pos = place()
    greet(line_partners(nz, pos))
    scatter_blocks(nz, pos, p, out, *scratch)


def scatter_tokens(p, nz, cid):
    blocks, rows, width = p.shape
    return pl.pallas_call(
        functools.partial(scatter_kernel, nz),
        out_shape=jax.ShapeDtypeStruct((rows, width), F32),
        in_specs=[VM],
        out_specs=VM,
        scratch_shapes=scatter_scratch(nz, rows, width),
        compiler_params=params(cid, 60 * MIB),
        name="scatter_tokens",
    )(p)


def scatter_and_hand_kernel(nz, kinds, runs, p, up_s, res, *refs):
    count = len(kinds)
    srcs, refs = refs[:count], refs[count:]
    out, up_o, res_o, refs = *refs[:3], refs[3:]
    dsts, refs = refs[:count], refs[count:]
    scratch, hsems, esems, tsems = refs[:5], refs[5:7], refs[7:9], refs[9:11]
    pos = place()
    x, c, z, y = pos
    greet(rank_partners(nz, pos) + group_partners(pos) + [(c != y, at(x, y, z, c))])
    hs = hand_stages(srcs, dsts, kinds, *hsems, nz, pos)
    es = exchange_stages(up_s, up_o, runs, *esems, nz, pos)
    ts = trade_stages(res, res_o, *tsems, pos)
    hs[0]()
    es[0]()
    ts[0]()
    scatter_blocks(nz, pos, p, out, *scratch)
    hs[1]()
    es[1]()
    ts[1]()


def scatter_and_hand(p, up_s, runs, res, arrays, kinds, nz, cid):
    blocks, rows, width = p.shape
    n, part, share = up_s.shape
    return pl.pallas_call(
        functools.partial(scatter_and_hand_kernel, nz, kinds, runs),
        out_shape=[
            jax.ShapeDtypeStruct((rows, width), F32),
            jax.ShapeDtypeStruct((part, n * share), BF),
            jax.ShapeDtypeStruct(res.shape, BF),
        ]
        + hand_shapes(arrays, kinds, nz),
        in_specs=[VM] + [HBM] * (2 + len(arrays)),
        out_specs=[VM] + [HBM] * (2 + len(arrays)),
        scratch_shapes=scatter_scratch(nz, rows, width) + hand_sems(kinds) + exchange_sems(runs, nz) + trade_sems(),
        compiler_params=params(cid, 60 * MIB),
        name="scatter_and_hand",
    )(p, up_s, res, *arrays)


def block_of(x, c, z, y, nz):
    return (x * 2 + c) * 2 * nz + z * 2 + y


def halves(ref, rows):
    half = rows // 2
    if half % 16:
        return {1: None, 2: ref}
    return {1: ref.at[pl.ds(half, half)], 2: ref.at[pl.ds(0, half)]}


def sliced_gather(src, dst, runs, sems, nz, pos):
    x, c, z, y = pos
    n = 2 * nz
    me = z * 2 + c
    part = dst.shape[1]
    send1, recv1, send2, recv2 = sems

    def pieces(p):
        if runs is None:
            return [(src.at[p], slice(None))]
        return [(src.at[:, pl.ds(there, size)], pl.ds(here, size)) for there, here, size in runs(p)]

    def row(p, gx, gy):
        return dst.at[block_of(gx, p % 2, p // 2, gy, nz)]

    mine = block_of(x, c, z, y, nz)

    def out(k):
        p = (me + k) % n
        return [
            remote(a, dst.at[mine, :, b], send1.at[p], recv1.at[me], at(x, p % 2, p // 2, y))
            for a, b in pieces(p)
        ]

    local = [pltpu.make_async_copy(a, dst.at[mine, :, b], recv1.at[me]) for a, b in pieces(me)]

    def came(k):
        return (me - k + n) % n

    def arrival(b, sem):
        return remote(b, b, send1.at[me], sem, at(x, 1 - c, z, y))

    def neighbour(m):
        return at(x ^ (m // 2), c, z, y ^ (m % 2))

    def forward(k, m):
        p = came(k)
        b = row(p, x, y)
        slot = (m - 1) * n + p
        return remote(b, b, send2.at[slot], recv2.at[slot], neighbour(m))

    def relay(k, m):
        p = came(k)
        b = halves(row(p, x ^ (m // 2), y ^ (m % 2)), part)[m]
        slot = (1 + m) * n + p
        return b is not None and remote(b, b, send2.at[slot], recv2.at[slot], neighbour(3 - m))

    def first():
        for copy in local:
            copy.start()
        for k in range(1, n):
            for copy in out(k):
                copy.start()

    def step(k):
        p = came(k)
        arrival(row(p, x, y), recv1.at[p]).wait_recv()
        for m in (1, 2):
            forward(k, m).start()

    def pass_on(k):
        p = came(k)
        for m in (1, 2):
            arrival(row(p, x ^ (m // 2), y ^ (m % 2)), recv2.at[(m - 1) * n + p]).wait_recv()
            if relay(k, m):
                relay(k, m).start()

    def last():
        for k in range(n):
            p = came(k)
            parts = halves(row(p, 1 - x, 1 - y), part)
            for m in (1, 2):
                if parts[m] is not None:
                    arrival(parts[m], recv2.at[(1 + m) * n + p]).wait_recv()
        for k in range(n):
            if k:
                p = (me + k) % n
                b = dst.at[mine]
                remote(b, b, send1.at[p], recv1.at[me], at(x, p % 2, p // 2, y)).wait_send()
            for m in (1, 2):
                forward(k, m).wait_send()
                if relay(k, m):
                    relay(k, m).wait_send()

    stages = [functools.partial(step, k) for k in range(n)] + [functools.partial(pass_on, k) for k in range(n)]
    return [first] + stages + [last]


def sliced_sems(nz):
    n = 2 * nz
    return [pltpu.SemaphoreType.DMA((n,))] * 2 + [pltpu.SemaphoreType.DMA((4 * n,))] * 2


def group_gather(src, dst, send, recv, pos):
    x, c, z, y = pos
    rows = src.shape[0]
    local = pltpu.make_async_copy(src, dst.at[x * 2 + y], recv.at[0])

    def there(m):
        return dst.at[(x ^ (m // 2)) * 2 + (y ^ (m % 2))]

    def neighbour(m):
        return at(x ^ (m // 2), c, z, y ^ (m % 2))

    def out(m):
        return remote(src, dst.at[x * 2 + y], send.at[m], recv.at[m], neighbour(m))

    def relay(m):
        b = halves(there(m), rows)[m]
        return b is not None and remote(b, b, send.at[2 + m], recv.at[2 + m], neighbour(3 - m))

    def arrival(b, sem):
        return remote(b, b, send.at[0], sem, at(x, 1 - c, z, y))

    def first():
        local.start()
        for m in (1, 2):
            out(m).start()

    def pass_on():
        for m in (1, 2):
            arrival(there(m), recv.at[m]).wait_recv()
            if relay(m):
                relay(m).start()

    def last():
        local.wait()
        parts = halves(there(3), rows)
        for m in (1, 2):
            if parts[m] is not None:
                arrival(parts[m], recv.at[2 + m]).wait_recv()
            out(m).wait_send()
            if relay(m):
                relay(m).wait_send()

    return [first, pass_on, last]


def full_gather(src, dst, send, recv, nz, pos):
    x, c, z, y = pos
    rows = src.shape[0]
    sib = at(x, 1 - c, z, y)
    mine = dst.at[block_of(x, c, z, y, nz)]

    def row(core, k, m):
        return dst.at[block_of(x ^ (m // 2), core, z + k, y ^ (m % 2), nz)]

    def neighbour(m):
        return at(x ^ (m // 2), c, z, y ^ (m % 2))

    def arrival(b, sem):
        return remote(b, b, send.at[0], recv.at[sem], sib)

    def along(k, sign):
        b = row(c, k, 0)
        return remote(
            b if k else src, b, send.at[(0 if sign > 0 else nz) + z + k], recv.at[z + k], at(x, c, z + sign, y)
        )

    def forward(k, m):
        b = row(c, k, 0)
        return remote(b if k else src, b, send.at[(1 + m) * nz + z + k], recv.at[m * nz + z + k], neighbour(m))

    def relay(k, m):
        b = halves(row(c, k, m), rows)[m]
        if b is None:
            return None
        return remote(b, b, send.at[(3 + m) * nz + z + k], recv.at[(2 + m) * nz + z + k], neighbour(3 - m))

    def side(k, m):
        b = row(c, k, m)
        return remote(b if k or m else src, b, send.at[(6 + m) * nz + z + k], recv.at[(5 + m) * nz + z + k], sib)

    local = pltpu.make_async_copy(src, mine, recv.at[z])

    def first():
        local.start()
        pl.when(z < nz - 1)(along(0, 1).start)
        pl.when(z > 0)(along(0, -1).start)
        for m in (1, 2):
            forward(0, m).start()
        side(0, 0).start()

    def both(k, fn):
        @pl.when(z >= k)
        def _():
            fn(-k)

        if k:

            @pl.when(z + k < nz)
            def _():
                fn(k)

    def step(k):
        def one(k):
            arrival(row(c, k, 0), z + k).wait_recv()
            if k > 0:
                pl.when(z > 0)(along(k, -1).start)
            else:
                pl.when(z < nz - 1)(along(k, 1).start)
            for m in (1, 2):
                forward(k, m).start()
            side(k, 0).start()

        both(k, one)

    def pass_on(k):
        def one(k):
            for m in (1, 2):
                arrival(row(c, k, m), m * nz + z + k).wait_recv()
                if relay(k, m) is not None:
                    relay(k, m).start()
                side(k, m).start()

        both(k, one)

    def diagonal(k):
        def one(k):
            parts = halves(row(c, k, 3), rows)
            for m in (1, 2):
                if parts[m] is not None:
                    arrival(parts[m], (2 + m) * nz + z + k).wait_recv()
            side(k, 3).start()

        both(k, one)

    def last():
        local.wait()

        def one(k):
            for m in range(4):
                arrival(row(1 - c, k, m), (5 + m) * nz + z + k).wait_recv()
                side(k, m).wait_send()
            if k >= 0:
                pl.when(z > 0)(along(k, -1).wait_send)
            if k <= 0:
                pl.when(z < nz - 1)(along(k, 1).wait_send)
            for m in (1, 2):
                forward(k, m).wait_send()
                if relay(k, m) is not None:
                    relay(k, m).wait_send()

        for k in range(nz):
            both(k, one)

    return (
        [first]
        + [functools.partial(step, k) for k in range(1, nz)]
        + [functools.partial(pass_on, k) for k in range(nz)]
        + [functools.partial(diagonal, k) for k in range(nz)]
        + [last]
    )


def full_sems(nz):
    return [pltpu.SemaphoreType.DMA((10 * nz,)), pltpu.SemaphoreType.DMA((9 * nz,))]


def head_runs(nz, cols):
    return lambda p: [
        (block_of(x, p % 2, p // 2, 0, nz) * HD, x * cols // 2, cols // 2) for x in range(2)
    ]


def up_runs(nz, unit):
    return lambda p: [(block_of(x, p % 2, p // 2, 0, nz) * unit, x * 2 * unit, 2 * unit) for x in range(2)]


def qkv_runs(nz, width, cols):
    runs = head_runs(nz, cols)
    return lambda p: [(j * width + there, j * cols + here, size) for j in range(3) for there, here, size in runs(p)]


def fetch_kernel(
    nz, width, cols, x_in, w_qkv, w_down, vec, tab, x_all, qkv_w, down_w, vecs, tab_out, *sems
):
    pos = place()
    x, c, z, y = pos
    fsdp = 2 * nz
    devices = 4 * fsdp
    me = (x * 2 + c) * fsdp + z * 2 + y
    x_sems, qkv_sems, vec_sems, tab_sems, down_sems = sems[:2], sems[2:6], sems[6:8], sems[8:10], sems[10:]
    greet_all(devices, fsdp, me)

    def vec_copy(other):
        return remote(vec, vecs.at[me], vec_sems[0].at[other], vec_sems[1].at[me], (other // fsdp, other % fsdp))

    def each(fn):
        def body(k, _):
            fn((me + k) % devices)
            return 0

        lax.fori_loop(1, devices, body, 0)

    vec_local = pltpu.make_async_copy(vec, vecs.at[me], vec_sems[1].at[me])
    tab_local = pltpu.make_async_copy(tab, tab_out, tab_sems[1].at[0])
    tab_trade = remote(tab, tab_out, tab_sems[0].at[0], tab_sems[1].at[0], at(x, y, z, c))

    gx = line_gather(x_in, x_all, *x_sems, nz, True, pos)
    runs = qkv_runs(nz, width, cols) if len(w_qkv.shape) == 2 else None
    gq = sliced_gather(w_qkv, qkv_w, runs, qkv_sems, nz, pos)
    gx[0]()
    gq[0]()
    gx[1]()
    vec_local.start()
    each(lambda other: vec_copy(other).start())
    pl.when(c == y)(tab_local.start)
    pl.when(c != y)(tab_trade.start)
    gd = group_gather(w_down, down_w, *down_sems, pos)
    for stage in gq[1 : fsdp + 1]:
        stage()
    gx[2]()
    gd[0]()
    for stage in gx[3:-1]:
        stage()
    for stage in gq[fsdp + 1 :]:
        stage()
    gx[-1]()
    for stage in gd[1:]:
        stage()

    def vec_done(other):
        remote(vec, vecs.at[other], vec_sems[0].at[other], vec_sems[1].at[other], at(x, 1 - c, z, y)).wait_recv()
        vec_copy(other).wait_send()

    vec_local.wait()
    each(vec_done)
    tab_local.wait()
    pl.when(c != y)(tab_trade.wait_send)


def fetch(nz, x_in, w_qkv, w_down, part, vec, tab, cid):
    rows, width = x_in.shape
    n = 2 * nz
    devices = 4 * n
    cols = width // n
    shapes = [
        ((n, rows, width), BF),
        ((devices, part, 3 * cols), BF),
        ((4,) + w_down.shape, BF),
        ((devices,) + vec.shape, F32),
        (tab.shape, jnp.int32),
    ]
    return pl.pallas_call(
        functools.partial(fetch_kernel, nz, width, cols),
        out_shape=[jax.ShapeDtypeStruct(s, t) for s, t in shapes],
        in_specs=[HBM] * 5,
        out_specs=[HBM] * 5,
        scratch_shapes=gather_sems(nz)
        + sliced_sems(nz)
        + [pltpu.SemaphoreType.DMA((devices,))] * 2
        + [pltpu.SemaphoreType.DMA((1,))] * 2
        + [pltpu.SemaphoreType.DMA((5,))] * 2,
        compiler_params=params(cid),
        name="fetch",
    )(x_in, w_qkv, w_down, vec, tab)


def hand_stages(srcs, dsts, kinds, send, recv, nz, pos):
    x, c, z, y = pos
    n = 2 * nz
    count = len(kinds)

    def copies(i, m):
        gx, gy = x ^ (m // 2), y ^ (m % 2)
        sem = i * 3 + m - 1
        target = at(gx, c, z, gy)
        if not kinds[i]:
            return [remote(srcs[i].at[gx * 2 + gy], dsts[i].at[m - 1], send.at[sem], recv.at[sem], target)]
        return [
            remote(
                srcs[i].at[block_of(gx, p % 2, p // 2, gy, nz)],
                dsts[i].at[m - 1, p],
                send.at[sem],
                recv.at[sem],
                target,
            )
            for p in range(n)
        ]

    def first():
        for i in range(count):
            for m in (3, 1, 2):
                for copy in copies(i, m):
                    copy.start()

    def last():
        for i in range(count):
            for m in (1, 2, 3):
                sem = i * 3 + m - 1
                there = dsts[i].at[m - 1]
                whole = remote(there, there, send.at[sem], recv.at[sem], at(x, 1 - c, z, y))
                whole.wait_recv()
                whole.wait_send()

    return [first, last]


def hand_shapes(arrays, kinds, nz):
    return [
        jax.ShapeDtypeStruct((3, 2 * nz) + a.shape[1:] if k else (3,) + a.shape[1:], a.dtype)
        for a, k in zip(arrays, kinds)
    ]


def hand_sems(kinds):
    return [pltpu.SemaphoreType.DMA((3 * len(kinds),))] * 2


def exchange_stages(src, dst, runs, send, recv, nz, pos):
    x, c, z, y = pos
    n = 2 * nz
    me = z * 2 + c

    def give(to, p):
        if runs is None:
            return [(src.at[to], dst.at[p])]
        return [(src.at[to, :, pl.ds(here, size)], dst.at[:, pl.ds(there, size)]) for there, here, size in runs(p)]

    width = len(give(0, 0))

    def move(p):
        return [
            remote(a, b, send.at[p * width + i], recv.at[me * width + i], at(x, p % 2, p // 2, y))
            for i, (a, b) in enumerate(give(p, me))
        ]

    def come(p):
        return [
            remote(b, b, send.at[me * width + i], recv.at[p * width + i], at(x, 1 - c, z, y))
            for i, (_, b) in enumerate(give(me, p))
        ]

    local = [pltpu.make_async_copy(a, b, recv.at[me * width + i]) for i, (a, b) in enumerate(give(me, me))]

    def first():
        for copy in local:
            copy.start()
        for k in range(1, n):
            for copy in move((me + k) % n):
                copy.start()

    def last():
        for copy in local:
            copy.wait()
        for k in range(1, n):
            for copy in come((me - k + n) % n):
                copy.wait_recv()
            for copy in move((me + k) % n):
                copy.wait_send()

    return [first, last]


def exchange_sems(runs, nz):
    width = 1 if runs is None else len(runs(0))
    return [pltpu.SemaphoreType.DMA((width * 2 * nz,))] * 2


def exchange_kernel(nz, src, dst, send, recv):
    pos = place()
    greet(rank_partners(nz, pos))
    for stage in exchange_stages(src, dst, None, send, recv, nz, pos):
        stage()


def exchange(a, nz, cid, name):
    return pl.pallas_call(
        functools.partial(exchange_kernel, nz),
        out_shape=jax.ShapeDtypeStruct(a.shape, a.dtype),
        in_specs=[HBM],
        out_specs=HBM,
        scratch_shapes=exchange_sems(None, nz),
        compiler_params=params(cid),
        name=name,
    )(a)


def trade_stages(src, dst, send, recv, pos):
    x, c, z, y = pos
    local = pltpu.make_async_copy(src, dst, recv.at[0])
    trade = remote(src, dst, send.at[0], recv.at[0], at(x, y, z, c))

    def first():
        pl.when(c == y)(local.start)
        pl.when(c != y)(trade.start)

    def last():
        local.wait()
        pl.when(c != y)(trade.wait_send)

    return [first, last]


def trade_sems():
    return [pltpu.SemaphoreType.DMA((1,))] * 2


def finish_kernel(nz, runs, has, *refs):
    grad, small, *refs = refs
    qkv_s = refs.pop(0) if has else None
    grad_out, small_out, *refs = refs
    qkv_o = refs.pop(0) if has else None
    came, send, recv, *sems = refs
    pos = place()
    x, c, z, y = pos
    fsdp = 2 * nz
    devices = 4 * fsdp
    me = (x * 2 + c) * fsdp + z * 2 + y
    es = exchange_stages(qkv_s, qkv_o, runs, *sems[2:], nz, pos) if has else [lambda: None] * 2
    ts = trade_stages(grad, grad_out, *sems[:2], pos)
    greet_all(devices, fsdp, me)

    def each(fn):
        def body(k, _):
            fn((me + k) % devices)
            return 0

        lax.fori_loop(1, devices, body, 0)

    def share(other):
        return remote(small.at[other], came.at[me], send.at[other], recv.at[me], (other // fsdp, other % fsdp))

    es[0]()
    ts[0]()
    each(lambda other: share(other).start())

    def done(other):
        remote(small.at[me], came.at[other], send.at[other], recv.at[other], at(x, 1 - c, z, y)).wait_recv()
        share(other).wait_send()

    each(done)
    came[me] = small[me]
    small_out[...] = jnp.sum(came[...], axis=0)
    ts[1]()
    es[1]()


def finish(grad, small, qkv_s, runs, nz, cid):
    devices = small.shape[0]
    has = qkv_s is not None
    shapes = [jax.ShapeDtypeStruct(grad.shape, grad.dtype), jax.ShapeDtypeStruct(small.shape[1:], F32)]
    if has:
        out_shape = qkv_s.shape if runs is None else (qkv_s.shape[1], qkv_s.shape[0] * qkv_s.shape[2])
        shapes.append(jax.ShapeDtypeStruct(out_shape, BF))
    return pl.pallas_call(
        functools.partial(finish_kernel, nz, runs, has),
        out_shape=shapes,
        in_specs=[HBM, VM] + [HBM] * has,
        out_specs=[HBM, VM] + [HBM] * has,
        scratch_shapes=[pltpu.VMEM(small.shape, F32)]
        + [pltpu.SemaphoreType.DMA((devices,))] * 2
        + trade_sems()
        + (exchange_sems(runs, nz) if has else []),
        compiler_params=params(cid, 32 * MIB),
        name="finish",
    )(*((grad, small, qkv_s) if has else (grad, small)))


def dot(a, b, dims):
    return lax.dot_general(a, b, (dims, ((), ())), preferred_element_type=F32)


NN = ((1,), (0,))
NT = ((1,), (1,))
TN = ((0,), (0,))


def head_number(h, heads, nz, pos):
    x, c, z, y = pos
    return block_of(h // (heads // 2), c, z, h % (heads // 2), nz)


def head_kernel(heads, nz, runs_qkv, runs_up, runs_out, *refs):
    refs = list(refs)

    def take(n):
        got = refs[:n]
        del refs[:n]
        return got

    slopes, valid_in, blocks_in, parents_in = take(4)
    vectors, bias_up = take(8), take(1)[0]
    x_in, cot, w_qkv, w_up, w_out, w_down = take(6)
    joined, mixed, mixed_own, x_own, rows_o, up_bias = take(6)
    a1_o, far_o, cot_all, qkv_o, up_w, out_w, down_w = take(7)
    pack, vecs, tab, tab_in, table, columns, member_s, reach_s, far_s, x_all, a1, qkv_w, bias_s = take(13)
    x_sems, cot_sems, qkv_sems, up_sems, out_sems, down_sems = take(2), take(2), take(4), take(4), take(2), take(2)
    vec_sems, tab_sems, mix_sems, (local_sem, far_sem) = take(2), take(2), take(2), take(2)

    pos = place()
    x, c, z, y = pos
    n = 2 * nz
    devices = 4 * n
    me = block_of(x, c, z, y, nz)
    rank = z * 2 + c
    tree, cols = joined.shape[0], joined.shape[1] // 3
    rows, width = x_own.shape
    part = w_out.shape[0]

    gx = line_gather(x_in, x_all, *x_sems, nz, True, pos)
    gc = line_gather(cot, cot_all, *cot_sems, nz, True, pos)
    gq = sliced_gather(w_qkv, qkv_w, runs_qkv, qkv_sems, nz, pos)
    gu = sliced_gather(w_up, up_w, runs_up, up_sems, nz, pos)
    go = full_gather(w_out, out_w, *out_sems, nz, pos)
    gd = group_gather(w_down, down_w, *down_sems, pos)
    ex = exchange_stages(mixed, mixed_own, runs_out, *mix_sems, nz, pos)
    ts = trade_stages(tab, tab_in, *tab_sems, pos)
    store_a = pltpu.make_async_copy(a1, a1_o, local_sem.at[0])
    store_q = pltpu.make_async_copy(qkv_w, qkv_o, local_sem.at[1])

    def each(fn):
        def body(k, _):
            fn((me + k) % devices)
            return 0

        lax.fori_loop(1, devices, body, 0)

    def vec_copy(other):
        return remote(pack, vecs.at[me], vec_sems[0].at[other], vec_sems[1].at[me], (other // n, other % n))

    def vec_come(other):
        remote(vecs.at[other], vecs.at[other], vec_sems[0].at[me], vec_sems[1].at[other], at(x, 1 - c, z, y)).wait_recv()

    pack[...] = jnp.zeros_like(pack)
    for i, v in enumerate(vectors):
        pack[i : i + 1, 0:part] = v[...].astype(F32).reshape(1, part)
    lined = pack[...]
    pack[...] = jnp.where(y == 1, pltpu.roll(lined, part, 1), lined)
    for i in range(bias_up.shape[0] // 128):
        pack[8 + i : 9 + i, :] = bias_up[i * 128 : (i + 1) * 128].astype(F32).reshape(1, 128)
    tab[...] = jnp.full_like(tab, -1)
    tab[0:1, :] = valid_in[...]
    tab[1:2, 0 : blocks_in.shape[1]] = blocks_in[...]
    tab[2:3, 0 : parents_in.shape[1]] = parents_in[...]

    greet_all(devices, n, me)
    gx[0]()
    gq[0]()
    ts[0]()
    go[0]()
    gd[0]()
    each(lambda other: vec_copy(other).start())
    vecs[me] = pack[...]
    gx[1]()

    ts[1]()
    seg = lax.broadcasted_iota(jnp.int32, (128, 128), 0)
    lane = lax.broadcasted_iota(jnp.int32, (128, 128), 1)

    def low(v):
        return v.astype(F32).astype(BF)

    parent = low(seg == tab_in[2:3, 0:128])
    above = (parent.astype(F32) + dot(parent, parent, NN)) > 0.5
    ancestor = low(above & (seg != lane))
    owner = low(seg == tab_in[1:2, 0:128])
    spread = low(
        lax.shift_right_logical(lax.broadcasted_iota(jnp.int32, (128, tree), 1), BLK.bit_length() - 1)
        == lax.broadcasted_iota(jnp.int32, (128, tree), 0)
    )
    member = dot(owner, spread, NN)
    valid = tab_in[0:1, :].astype(F32)
    counted = member * valid
    member_s[...] = member.astype(BF)
    reach_s[...] = (2.0 * dot(ancestor, member_s[...], NN) + member).astype(BF)
    lens = jnp.broadcast_to(jnp.sum(counted, axis=1, keepdims=True), (128, 128))
    offset = lax.dot_general(
        ancestor.astype(F32), lens, (TN, ((), ())), precision=lax.Precision.HIGHEST, preferred_element_type=F32
    )
    table[...] = jnp.zeros_like(table)
    table[1:2, :] = valid
    for j in range(tree // 256):
        here = slice(j * 256, (j + 1) * 256)
        earlier = low(
            lax.broadcasted_iota(jnp.int32, (tree, 256), 0) < lax.broadcasted_iota(jnp.int32, (tree, 256), 1) + j * 256
        )
        before = dot(counted.astype(BF), earlier, NN) + offset[:, 0:1]
        table[0:1, here] = jnp.sum(before * member[:, here], axis=0, keepdims=True)
    columns[...] = table[...].T

    step = far_s.shape[2]
    steps = tree // step
    far_store = [
        pltpu.make_async_copy(far_s.at[i % 2], far_o.at[:, pl.ds(i * step, step)], far_sem.at[i % 2]) for i in range(steps)
    ]

    def allow(value, key, query, key_valid):
        return ((value > 1.5) | ((value > 0.5) & (key <= query))) & ((key_valid > 0.5) | (key == query))

    def far_blocks():
        for i in range(steps):
            here = slice(i * step, (i + 1) * step)
            key = lax.broadcasted_iota(jnp.int32, (tree, step), 0)
            query = lax.broadcasted_iota(jnp.int32, (tree, step), 1) + i * step
            allowed = allow(dot(member_s[...], reach_s[:, here], TN), key, query, columns[:, 1:2])
            if i >= 2:
                far_store[i - 2].wait()
            far_s[i % 2] = jnp.where(allowed, columns[:, 0:1], MASKED)
            far_store[i].start()

    def whole_vectors():
        each(vec_come)
        for i in range(devices // 2):
            rows_o[:, i * 128 : (i + 1) * 128] = vecs[2 * i, 0:8] + vecs[2 * i + 1, 0:8]
        per = bias_up.shape[0] // 128
        for g in range(4):
            r = block_of(g // 2, c, z, g % 2, nz)
            for i in range(per):
                up_bias[:, (g * per + i) * 128 : (g * per + i + 1) * 128] = vecs[r, 8 + i : 9 + i]
        bias_s[...] = jnp.zeros_like(bias_s)
        for there, here, size in runs_out(rank):
            there = pl.multiple_of(there, 128)
            bias_s[:, here : here + size] = rows_o[2:3, pl.ds(there, size)]
            bias_s[:, 2 * cols + here : 2 * cols + here + size] = rows_o[3:4, pl.ds(there, size)]

    def norm(b):
        def tile(j, _):
            here = pl.ds(pl.multiple_of(j * 32, 32), 32)
            normed, _ = norm_parts(x_all[b, here].astype(F32))
            a1[b, here] = (normed * rows_o[0:1, :] + rows_o[1:2, :]).astype(BF)
            return 0

        lax.fori_loop(0, rows // 32, tile, 0)

    def norm_at(k, core):
        pl.when(z >= k)(lambda: norm((z - k) * 2 + core))
        if k:
            pl.when(z + k < nz)(lambda: norm((z + k) * 2 + core))

    for stage in gq[1 : n + 1]:
        stage()
    gx[2]()
    go[1]()
    gd[1]()
    far_blocks()
    whole_vectors()
    norm_at(0, c)
    norm_at(1, c)
    gx[3]()
    gu[0]()
    gc[0]()
    norm_at(2, c)
    go[2]()
    for stage in gq[n + 1 : 2 * n + 1]:
        stage()
    gx[4]()
    gc[1]()
    norm_at(3, c)
    go[3]()
    gx[-1]()
    x_own[...] = x_all[rank]
    for k in range(nz):
        norm_at(k, 1 - c)
    store_a.start()
    gq[-1]()
    store_q.start()
    for stage in gu[1 : n + 1]:
        stage()

    def project(i, _):
        here = pl.ds(pl.multiple_of(i * 2 * rows, 2 * rows), 2 * rows)
        tokens = a1[pl.ds(2 * i, 2)].reshape(2 * rows, width)

        def tile(j, _):
            u = pl.ds(pl.multiple_of(j * 256, 256), 256)
            value = dot(tokens, qkv_w[:, :, u].reshape(width, 256), NN) + bias_s[:, u]
            joined[here, u] = value.astype(BF)
            return 0

        lax.fori_loop(0, 3 * cols // 256, tile, 0)
        return 0

    lax.fori_loop(0, nz, project, 0)
    slope = [slopes[head_number(h, heads, nz, pos)] for h in range(heads)]

    gc[2]()
    def attend_step(i, _):
        here = pl.ds(pl.multiple_of(i * step, step), step)
        per = step // rows
        key = lax.broadcasted_iota(jnp.int32, (step, tree), 1)
        query = lax.broadcasted_iota(jnp.int32, (step, tree), 0) + i * step
        allowed = allow(dot(reach_s[:, here], member_s[...], TN), key, query, table[1:2, :])
        gap = jnp.where(allowed, table[0:1, :], MASKED)
        for h in range(heads):
            lanes = slice(h * HD, (h + 1) * HD)
            q = joined[here, lanes]
            k = joined[:, cols + h * HD : cols + (h + 1) * HD]
            v = joined[:, 2 * cols + h * HD : 2 * cols + (h + 1) * HD]
            logits = dot(q, k, NT) * HD ** (-0.5) + slope[h] * gap
            weights = jnp.exp(logits - jnp.max(logits, axis=1, keepdims=True))
            probs = weights * (1.0 / jnp.sum(weights, axis=1, keepdims=True))
            mixed[pl.ds(i * per, per), :, lanes] = dot(probs.astype(BF), v, NN).astype(BF).reshape(per, rows, HD)

        def later(k, fns):
            @pl.when(i == k)
            def _():
                for fn in fns:
                    fn()

        later(0, go[nz : 2 * nz])
        later(1, gc[3:4] + gu[n + 1 : n + 1 + n // 2])
        later(2, gc[4:5] + gu[n + 1 + n // 2 : 2 * n + 1])
        later(3, go[2 * nz : 3 * nz])
        return 0

    lax.fori_loop(0, steps, attend_step, 0)
    ex[0]()
    ex[1]()
    for stage in (go[-1], gc[-1], gu[-1], gd[-1]):
        stage()
    each(lambda other: vec_copy(other).wait_send())
    for i in range(max(0, steps - 2), steps):
        far_store[i].wait()
    store_a.wait()
    store_q.wait()


def head_call(slopes, tables, vectors, bias_up, layer_in, cot, w_qkv, w_up, w_out, w_down, heads, nz, cid):
    rows, width = layer_in.shape
    n = 2 * nz
    devices = 4 * n
    tree = n * rows
    cols = heads * HD
    part, unit = w_out.shape[0], w_down.shape[0]
    step = 256
    runs_qkv, runs_up, runs_out = qkv_runs(nz, width, cols), up_runs(nz, unit), head_runs(nz, cols)
    shape = jax.ShapeDtypeStruct
    return pl.pallas_call(
        functools.partial(head_kernel, heads, nz, runs_qkv, runs_up, runs_out),
        out_shape=[
            shape((tree, 3 * cols), BF),
            shape((n, rows, cols), BF),
            shape((rows, width), BF),
            shape((rows, width), BF),
            shape((8, width), F32),
            shape((1, 4 * unit), F32),
            shape((n, rows, width), BF),
            shape((tree, tree), F32),
            shape((n, rows, width), BF),
            shape((devices, part, 3 * cols), BF),
            shape((devices, part, 4 * unit), BF),
            shape((devices, part, width), BF),
            shape((4, unit, width), BF),
        ],
        in_specs=[pl.BlockSpec(memory_space=pltpu.SMEM)] + [VM] * 12 + [HBM] * 6,
        out_specs=[VM] * 6 + [HBM] * 7,
        scratch_shapes=[
            pltpu.VMEM((16, 128), F32),
            pltpu.VMEM((devices, 16, 128), F32),
            pltpu.VMEM((8, tree), jnp.int32),
            pltpu.VMEM((8, tree), jnp.int32),
            pltpu.VMEM((128, tree), F32),
            pltpu.VMEM((tree, 128), F32),
            pltpu.VMEM((128, tree), BF),
            pltpu.VMEM((128, tree), BF),
            pltpu.VMEM((2, tree, step), F32),
            pltpu.VMEM((n, rows, width), BF),
            pltpu.VMEM((n, rows, width), BF),
            pltpu.VMEM((devices, part, 3 * cols), BF),
            pltpu.VMEM((1, 3 * cols), F32),
        ]
        + gather_sems(nz) * 2
        + sliced_sems(nz) * 2
        + full_sems(nz)
        + [pltpu.SemaphoreType.DMA((5,))] * 2
        + [pltpu.SemaphoreType.DMA((devices,))] * 2
        + trade_sems()
        + exchange_sems(runs_out, nz)
        + [pltpu.SemaphoreType.DMA((2,))] * 2,
        compiler_params=params(cid, 60 * MIB),
        name="head",
    )(slopes, *tables, *vectors, bias_up, layer_in, cot, w_qkv, w_up, w_out, w_down)


def scatter_parts(nz, pos, own, other, acc, came, send, recv):
    x, c, z, y = pos
    S, U, D = 0, nz, 3 * nz
    sib = at(x, 1 - c, z, y)
    half = acc.shape[1] // 2

    def f(v):
        return v.astype(F32)

    def swap(t):
        return remote(other(t), acc.at[t], send.at[S + t], recv.at[S + t], sib)

    def piece(ref, t, h):
        return ref.at[t, pl.ds(h * half, half)]

    def rise(t, h):
        sem = U + t * 2 + h
        return remote(piece(acc, t, h), piece(came, t, h), send.at[sem], recv.at[sem], at(x, c, z + 1, y))

    def fall(t, h):
        slot = jnp.where(z - 1 == t, nz, t)
        sem = D + t * 2 + h
        return remote(piece(acc, t, h), piece(came, slot, h), send.at[sem], recv.at[sem], at(x, c, z - 1, y))

    def arrival(slot, h, sem):
        there = piece(came, slot, h)
        return remote(there, there, send.at[S], recv.at[sem], sib)

    def event(t, upward):
        swap(t).wait_recv()
        acc[t] = (f(acc[t]) + f(own(t))).astype(BF)
        for h in range(2):

            @pl.when(z > 0 if upward else z < nz - 1)
            def _():
                arrival(t, h, (U if upward else D) + t * 2 + h).wait_recv()
                here = slice(h * half, (h + 1) * half)
                acc[t, here] = (f(acc[t, here]) + f(came[t, here])).astype(BF)

            (rise if upward else fall)(t, h).start()

    def slot(k):
        for t in range(nz):
            zz = k - t
            if 0 <= zz < t:
                pl.when(z == zz)(functools.partial(event, t, True))
            zz = 2 * (nz - 1) - k - t
            if t < zz < nz:
                pl.when(z == zz)(functools.partial(event, t, False))

    def begin():
        for i in range(nz - 1):
            pl.when(z == 0)(functools.partial(event, nz - 1 - i, True))
            pl.when(z == nz - 1)(functools.partial(event, i, False))

    def near(i):
        t = nz - 1 - i
        pl.when((z > 0) & (z < nz // 2) & (z < t))(functools.partial(event, t, True))
        pl.when((z >= nz // 2) & (z < nz - 1) & (z > i))(functools.partial(event, i, False))

    def far():
        for i in range(nz - 1):
            t = nz - 1 - i
            pl.when((z >= nz // 2) & (z < t))(functools.partial(event, t, True))
            pl.when((z < nz // 2) & (z > i))(functools.partial(event, i, False))

    def total(out):
        swap(z).wait_recv()
        out[...] = f(acc[z]) + f(own(z))
        for upward, slot, base in ((True, z, U), (False, nz, D)):

            @pl.when(z > 0 if upward else z < nz - 1)
            def _():
                for h in range(2):
                    here = slice(h * half, (h + 1) * half)
                    arrival(slot, h, base + z * 2 + h).wait_recv()
                    out[here, :] += f(came[slot, here])

    def done():
        for t in range(nz):
            swap(t).wait_send()
            for h in range(2):
                pl.when(z < t)(lambda: rise(t, h).wait_send())
                pl.when(z > t)(lambda: fall(t, h).wait_send())

    return swap, slot, begin, near, far, total, done


def reduce_parts(src, mine, near, far, send, recv, lsem, pos):
    x, c, z, y = pos
    half = src.shape[1] // 2

    def f(v):
        return v.astype(F32)

    def share(gx, gy, lower):
        return src.at[gx * 2 + gy, pl.ds(lower * half, half)]

    parts = [(x, y, 0), (x, y, 1), (x, 1 - y, 0), (1 - x, y, 1)]
    loads = [pltpu.make_async_copy(share(*p), mine.at[i], lsem.at[i]) for i, p in enumerate(parts)]
    along_x, along_y = at(1 - x, c, z, y), at(x, c, z, 1 - y)

    def out(i):
        a, b, target = [
            (share(1 - x, y, 0), near.at[0, 0], along_x),
            (share(1 - x, 1 - y, 0), near.at[0, 1], along_x),
            (share(x, 1 - y, 1), near.at[1, 0], along_y),
            (share(1 - x, 1 - y, 1), near.at[1, 1], along_y),
        ][i]
        return remote(a, b, send.at[i], recv.at[i], target)

    def on(i):
        return remote(near.at[i, 1], far.at[i], send.at[4 + i], recv.at[4 + i], [along_y, along_x][i])

    def first():
        for i in (1, 3, 0, 2):
            out(i).start()
        for copy in loads:
            copy.start()

    def second():
        for copy in loads:
            copy.wait()
        for i in range(2):
            out(2 * i + 1).wait_recv()
            near[i, 1] = (f(near[i, 1]) + f(mine[2 + i])).astype(BF)
            on(i).start()

    def total(put):
        for i in range(2):
            out(2 * i).wait_recv()
            on(i).wait_recv()
            put(i, f(mine[i]) + f(near[i, 0]) + f(far[i]))

    def done():
        for i in range(4):
            out(i).wait_send()
        for i in range(2):
            on(i).wait_send()

    return first, second, total, done


def reduce_scratch(rows, width):
    half = rows // 2
    return [
        pltpu.VMEM((4, half, width), BF),
        pltpu.VMEM((2, 2, half, width), BF),
        pltpu.VMEM((2, half, width), BF),
        pltpu.SemaphoreType.DMA((6,)),
        pltpu.SemaphoreType.DMA((6,)),
        pltpu.SemaphoreType.DMA((4,)),
    ]


def tail_kernel(
    heads, nz, runs_up, runs_qkv, slopes, far_in, grad_in, joined, a1_in, mixed, qkv_in, branch, upd_in, up_src, down_src,
    middle, x_own, whole, grad_middle, sums, bias_g,
    down_o, out_o, small_o, bias_o, up_o, qkv_o, branch_all, layer_o, grad_o, grad_s, *refs,
):
    refs = list(refs)

    def take(n):
        got = refs[:n]
        del refs[:n]
        return got

    gap_s, tokens, qkv_w, grad_joined, acc_k, acc_v = take(6)
    upd_own, upd_acc, upd_came, upd_send, upd_recv = take(5)
    att_p, att_acc, att_came, att_send, att_recv = take(5)
    up_refs, down_refs, qkv_refs, out_refs = take(6), take(6), take(6), take(6)
    up_sum, qkv_sum, qkv_g, out_g, res, res_low = take(6)
    grad_low, vec, came, bias_t, bias_c = take(5)
    gsems, esems, esems_up, esems_qkv, tsems, tsems_x = take(2), take(2), take(2), take(2), take(2), take(2)
    vsems, bsems = take(2), take(2)
    gap_sem, load_sem = take(2)

    pos = place()
    x, c, z, y = pos
    n = 2 * nz
    tree, cols = mixed.shape
    rows, width = branch.shape
    part = up_sum.shape[1]
    rank = z * 2 + c
    step = gap_s.shape[2]

    es = exchange_stages(grad_in, grad_s, None, *esems, nz, pos)
    gb = line_gather(branch, branch_all, *gsems, nz, False, pos)
    up1, up2, up_total, up_done = reduce_parts(up_src, *up_refs, pos)
    down1, down2, down_total, down_done = reduce_parts(down_src, *down_refs, pos)
    qkv1, qkv2, qkv_total, qkv_done = reduce_parts(qkv_g, *qkv_refs, pos)
    out1, out2, out_total, out_done = reduce_parts(out_g, *out_refs, pos)
    upd_swap, _, upd_begin, upd_near, upd_far, upd_total, upd_done = scatter_parts(
        nz, pos, lambda t: upd_own[t], lambda t: upd_in.at[t * 2 + 1 - c], upd_acc, upd_came, upd_send, upd_recv
    )
    att_swap, _, att_begin, att_near, att_far, att_total, att_done = scatter_parts(
        nz, pos, lambda t: att_p[t * 2 + c], lambda t: att_p.at[t * 2 + 1 - c], att_acc, att_came, att_send, att_recv
    )
    ex_up = exchange_stages(up_sum, up_o, runs_up, *esems_up, nz, pos)
    ex_qkv = exchange_stages(qkv_sum, qkv_o, runs_qkv, *esems_qkv, nz, pos)
    home = trade_stages(res_low, layer_o, *tsems, pos)
    home_x = trade_stages(grad_low, grad_o, *tsems_x, pos)
    devices = 4 * n
    me = block_of(x, c, z, y, nz)
    group = x * 2 + y

    def each(fn):
        def body(k, _):
            fn((me + k) % devices)
            return 0

        lax.fori_loop(1, devices, body, 0)

    def share(other):
        tile = vec.at[:, pl.ds(pl.multiple_of(other // 2 * 128, 128), 128)]
        return remote(tile, came.at[me], vsems[0].at[other], vsems[1].at[me], (other // n, other % n))

    def share_come(other):
        there = came.at[other]
        remote(there, there, vsems[0].at[me], vsems[1].at[other], at(x, 1 - c, z, y)).wait_recv()

    def bias_share(m):
        target = at(x ^ (m // 2), c, z, y ^ (m % 2))
        return remote(bias_t.at[group ^ m], bias_c.at[m - 1], bsems[0].at[m - 1], bsems[1].at[m - 1], target)
    loads = [pltpu.make_async_copy(upd_in.at[t * 2 + c], upd_own.at[t], load_sem.at[t]) for t in range(nz)]
    load_w = pltpu.make_async_copy(qkv_in, qkv_w, load_sem.at[nz])
    load_a = pltpu.make_async_copy(a1_in, tokens, load_sem.at[nz + 1])
    load_b = pltpu.make_async_copy(branch_all, tokens, load_sem.at[nz + 2])

    def gap_load(i, slot):
        return pltpu.make_async_copy(
            far_in.at[:, pl.ds(pl.multiple_of(i * step, step), step)], gap_s.at[slot], gap_sem.at[slot]
        )

    greet_all(devices, n, me)
    es[0]()
    up1()
    for t in range(nz):
        upd_swap(t).start()
    gap_load(0, 0).start()
    for copy in loads + [load_w, load_a]:
        copy.start()
    acc_k[...] = jnp.zeros_like(acc_k)
    acc_v[...] = jnp.zeros_like(acc_v)
    for copy in loads:
        copy.wait()
    es[1]()
    gb[0]()
    gb[1]()
    upd_begin()

    steps = tree // step
    slope = [slopes[head_number(h, heads, nz, pos)] for h in range(heads)]

    def attend_step(i, _):
        slot = i % 2
        gap_load(i, slot).wait()
        pl.when(i + 1 < steps)(lambda: gap_load(i + 1, 1 - slot).start())
        gap = gap_s[slot]
        here = pl.ds(pl.multiple_of(i * step, step), step)
        per = step // rows
        grads = grad_s[pl.ds(i * per, per)].reshape(step, cols)
        for h in range(heads):
            lane = slice(h * HD, (h + 1) * HD)
            q = joined[here, lane]
            k = joined[:, cols + h * HD : cols + (h + 1) * HD]
            v = joined[:, 2 * cols + h * HD : 2 * cols + (h + 1) * HD]
            g = grads[:, lane]
            logits = dot(k, q, NT) * HD ** (-0.5) + slope[h] * gap
            weights = jnp.exp(logits - jnp.max(logits, axis=0, keepdims=True))
            probs = weights * (1.0 / jnp.sum(weights, axis=0, keepdims=True))
            grad_probs = dot(v, g, NT)
            delta = jnp.sum(probs * grad_probs, axis=0, keepdims=True)
            grad_raw = (probs * (grad_probs - delta) * HD ** (-0.5)).astype(BF)
            acc_v[:, lane] += dot(probs.astype(BF), g, NN)
            acc_k[:, lane] += dot(grad_raw, q, NN)
            grad_joined[here, lane] = dot(grad_raw, k, TN).astype(BF)

        def later(k, fns):
            @pl.when(i == k)
            def _():
                for fn in fns:
                    fn()

        later(1, [gb[2]])
        later(2, [up2])
        later(3, [down1, lambda: upd_near(0)])
        return 0

    lax.fori_loop(0, steps, attend_step, 0)
    grad_joined[:, cols : 2 * cols] = acc_k[...].astype(BF)
    grad_joined[:, 2 * cols :] = acc_v[...].astype(BF)
    load_w.wait()

    def put_ranks(dest):
        def put(lower, value):
            dest[pl.ds(lower * nz, nz)] = value.astype(BF).reshape(nz, part, -1)

        return put

    def back(t, _):
        here = pl.ds(pl.multiple_of(t * 2 * rows, 2 * rows), 2 * rows)

        def tile(j, _):
            w = pl.ds(pl.multiple_of(j * 512, 512), 512)
            att_p[pl.ds(t * 2, 2), :, w] = dot(grad_joined[here, :], qkv_w[w, :], NT).astype(BF).reshape(2, rows, 512)
            return 0

        lax.fori_loop(0, width // 512, tile, 0)
        att_swap(t).start()
        return 0

    lax.fori_loop(0, nz, back, 0)
    load_a.wait()
    blocks = 256 // part

    def qkv_tile(j, _):
        w = pl.ds(pl.multiple_of(j * 256, 256), 256)
        value = dot(tokens[:, :, w].reshape(tree, 256), grad_joined[...], TN).astype(BF)
        for i in range(blocks):
            r = j * blocks + i
            d, f = r // n, r % n
            p = f // 2 * 2 + d % 2
            qkv_g[d // 2 * 2 + f % 2, pl.ds(pl.multiple_of(p * part, part), part), :] = value[i * part : (i + 1) * part]
        return 0

    att_begin()
    col = jnp.sum(grad_joined[...].astype(F32), axis=0, keepdims=True)
    vec[...] = jnp.zeros_like(vec)
    for there, here, size in head_runs(nz, cols)(rank):
        there = pl.multiple_of(there, 128)
        vec[2:3, pl.ds(there, size)] = col[:, here : here + size]
        vec[3:4, pl.ds(there, size)] = col[:, 2 * cols + here : 2 * cols + here + size]
    for i, k in enumerate((2, 0, 1, 3)):
        vec[4 + i : 5 + i, :] = sums[k : k + 1, :]
    vec[9:10, :] = jnp.broadcast_to(jnp.sum(sums[4:5, :], axis=1, keepdims=True), (1, width))
    bias_t[...] = jnp.zeros_like(bias_t)
    per = bias_g.shape[1] // 512
    for g in range(4):
        for i in range(per):
            bias_t[g, i : i + 1, :] = bias_g[:, (g * per + i) * 128 : (g * per + i + 1) * 128]
    for m in (1, 2, 3):
        bias_share(m).start()
    gb[3]()
    lax.fori_loop(0, width // 256, qkv_tile, 0)
    qkv1()
    upd_near(1)
    gb[4]()
    up_total(put_ranks(up_sum))
    ex_up[0]()
    upd_far()
    att_near(0)
    att_near(1)
    qkv2()
    att_far()
    down2()
    for stage in gb[5:]:
        stage()
    load_b.start()
    load_b.wait()

    def out_tile(j, _):
        w = pl.ds(pl.multiple_of(j * 512, 512), 512)
        value = dot(mixed[...], tokens[:, :, w].reshape(tree, 512), TN).astype(BF)
        out_g[:, :, w] = value.reshape(4, cols // 4, 512)
        return 0

    lax.fori_loop(0, width // 512, out_tile, 0)
    out1()
    qkv_total(put_ranks(qkv_sum))
    ex_qkv[0]()
    att_total(res)

    def norm(j, _):
        here = pl.ds(pl.multiple_of(j * 32, 32), 32)
        normed, inverse = norm_parts(x_own[here, :].astype(F32))
        value = res[here, :]
        through = grad_middle[here, :] + norm_back(value * whole[0:1, :], normed, inverse)
        grad_low[here, :] = through.astype(BF)
        vec[0:1, :] += jnp.sum(value * normed, axis=0, keepdims=True)
        vec[1:2, :] += jnp.sum(value, axis=0, keepdims=True)
        return 0

    lax.fori_loop(0, rows // 32, norm, 0)
    home_x[0]()
    upd_total(res)
    res[...] += middle[...] + whole[7:8, :]
    res_low[...] = res[...].astype(BF)
    home[0]()
    square = jnp.sum(jnp.sum(res[...] * res[...], axis=0, keepdims=True), axis=1, keepdims=True)
    vec[8:9, :] = jnp.broadcast_to(square, (1, width))
    each(lambda other: share(other).start())
    out2()

    def put_down(lower, value):
        half = value.shape[0]
        down_o[pl.ds(lower * half, half), :] = value

    down_total(put_down)
    def put_out(lower, value):
        half = value.shape[0]
        out_o[pl.ds(lower * half, half), :] = value

    out_total(put_out)
    each(share_come)
    came[me] = vec[:, pl.ds(pl.multiple_of(me // 2 * 128, 128), 128)]
    summed = jnp.sum(came[...], axis=0)
    small_o[...] = jnp.where(y == 1, pltpu.roll(summed, 64, 1), summed)
    for m in (1, 2, 3):
        bias_share(m).wait_recv()
    bias_o[...] = bias_t[group] + jnp.sum(bias_c[...], axis=0)
    ex_up[1]()
    home[1]()
    home_x[1]()
    ex_qkv[1]()
    each(lambda other: share(other).wait_send())
    for m in (1, 2, 3):
        bias_share(m).wait_send()
    for fn in (up_done, down_done, qkv_done, out_done, upd_done, att_done):
        fn()


def tail_call(
    slopes, far_t, grad, joined, a1, mixed, qkv_w, branch, upd, up_g, down_g, middle, x_own, whole, grad_middle, sums, bias_g,
    runs, heads, nz, cid,
):
    tree, cols = mixed.shape
    rows, width = branch.shape
    n = 2 * nz
    part = width // (4 * n)
    unit = down_g.shape[1]
    step = 256
    runs_up, runs_qkv = runs
    shape = jax.ShapeDtypeStruct

    def scatter_refs(own):
        return [
            pltpu.VMEM((own, rows, width), BF),
            pltpu.VMEM((nz, rows, width), BF),
            pltpu.VMEM((nz + 1, rows, width), BF),
            pltpu.SemaphoreType.DMA((5 * nz,)),
            pltpu.SemaphoreType.DMA((5 * nz,)),
        ]

    return pl.pallas_call(
        functools.partial(tail_kernel, heads, nz, runs_up, runs_qkv),
        out_shape=[
            shape((unit, width), F32),
            shape((part, width), F32),
            shape((16, 128), F32),
            shape((8, 128), F32),
            shape((part, 4 * n * unit), BF),
            shape((part, 3 * width), BF),
            shape((n, rows, width), BF),
            shape((rows, width), BF),
            shape((rows, width), BF),
        ],
        in_specs=[pl.BlockSpec(memory_space=pltpu.SMEM), HBM, HBM, VM, HBM, VM] + [HBM] * 5 + [VM] * 6,
        out_specs=[VM] * 4 + [HBM] * 5,
        scratch_shapes=[
            pltpu.VMEM((n, rows, cols), BF),
            pltpu.VMEM((2, tree, step), F32),
            pltpu.VMEM((n, rows, width), BF),
            pltpu.VMEM((width, 3 * cols), BF),
            pltpu.VMEM((tree, 3 * cols), BF),
            pltpu.VMEM((tree, cols), F32),
            pltpu.VMEM((tree, cols), F32),
        ]
        + scatter_refs(nz)
        + scatter_refs(n)
        + reduce_scratch(n * part, 4 * unit)
        + reduce_scratch(unit, width)
        + reduce_scratch(n * part, 3 * cols)
        + reduce_scratch(part, width)
        + [
            pltpu.VMEM((n, part, 4 * unit), BF),
            pltpu.VMEM((n, part, 3 * cols), BF),
            pltpu.VMEM((4, n * part, 3 * cols), BF),
            pltpu.VMEM((4, part, width), BF),
            pltpu.VMEM((rows, width), F32),
            pltpu.VMEM((rows, width), BF),
            pltpu.VMEM((rows, width), BF),
            pltpu.VMEM((16, width), F32),
            pltpu.VMEM((4 * n, 16, 128), F32),
            pltpu.VMEM((4, 8, 128), F32),
            pltpu.VMEM((3, 8, 128), F32),
        ]
        + gather_sems(nz)
        + exchange_sems(None, nz)
        + exchange_sems(runs_up, nz)
        + exchange_sems(runs_qkv, nz)
        + trade_sems() * 2
        + [pltpu.SemaphoreType.DMA((4 * n,))] * 2
        + [pltpu.SemaphoreType.DMA((3,))] * 2
        + [pltpu.SemaphoreType.DMA((2,)), pltpu.SemaphoreType.DMA((nz + 3,))],
        compiler_params=params(cid, 63 * MIB),
        name="tail",
    )(
        slopes, far_t, grad, joined, a1, mixed, qkv_w, branch, upd, up_g, down_g,
        middle, x_own, whole, grad_middle, sums, bias_g,
    )


def gelu_and_slope(value):
    normal = 0.5 + 0.5 * lax.erf(value * math.sqrt(0.5))
    density = jnp.exp(-0.5 * value * value) * (1.0 / math.sqrt(2.0 * math.pi))
    return value * normal, normal + value * density


def mlp_kernel(
    nz, mixed, x_own, whole, out_in, cot_in, up_in, down_in, bias,
    middle, grad_middle, grad_branch, grad_mixed, sums, bias_g, upd_out, up_out, down_out,
    mlp, cot, up_w, down_w, p, upd, up_g, down_g, out_w, active, gh, grad, acc, came, gsend, grecv, ssend, srecv, lsem,
):
    pos = place()
    x, c, z, y = pos
    blocks, rows, width = mlp.shape
    units = active.shape[1]
    pair = 2 * rows
    me = z * 2 + c
    sib = at(x, 1 - c, z, y)
    up_dev, dn_dev = at(x, c, z + 1, y), at(x, c, z - 1, y)
    UP, DN, SU, SD = 0, nz, 2 * nz, 3 * nz
    part = out_w.shape[1]

    def f(v):
        return v.astype(F32)

    loads = [
        pltpu.make_async_copy(a, b, lsem.at[i])
        for i, (a, b) in enumerate([(out_in, out_w), (up_in, up_w), (cot_in, cot), (down_in, down_w)])
    ]

    def rank_rows(r):
        d, f = r // blocks, r % blocks
        return up_out.at[d // 2 * 2 + f % 2, pl.ds((f // 2 * 2 + d % 2) * part, part)]

    stores = [
        [pltpu.make_async_copy(upd, upd_out, lsem.at[4])],
        [
            pltpu.make_async_copy(up_g.at[pl.ds(r * part, part)], rank_rows(r), lsem.at[6 + r])
            for r in range(4 * blocks)
        ],
        [pltpu.make_async_copy(down_g, down_out, lsem.at[5])],
    ]

    def store(i):
        for copy in stores[i]:
            copy.start()


    def block(b, sem, target):
        return remote(mlp.at[b], mlp.at[b], gsend.at[sem], grecv.at[sem], target)

    def up(d):
        return block((z - d) * 2 + c, UP + d, up_dev)

    def dn(d):
        return block((z + d) * 2 + c, DN + d, dn_dev)

    def side(d, below):
        return block(jnp.where(below, z - d, z + d) * 2 + c, jnp.where(below, SU, SD) + d, sib)

    def turn(i):
        both = jnp.minimum(z, nz - 1 - z)
        two = i <= 2 * both
        d = jnp.where(two, (i + 1) // 2, i - both)
        below = jnp.where(two, i % 2 == 1, z > nz - 1 - z)
        return d, below

    def arrive(i):
        if i == 0:
            block(z * 2 + 1 - c, SU, sib).wait_recv()
            return z
        d, below = turn(i)
        zi = jnp.where(below, z - d, z + d)
        block(zi * 2 + c, jnp.where(below, UP, DN) + d - 1, sib).wait_recv()
        pl.when(below & (z < nz - 1))(lambda: up(d).start())
        pl.when(jnp.logical_not(below) & (z > 0))(lambda: dn(d).start())
        side(d, below).start()
        block(zi * 2 + 1 - c, jnp.where(below, SU, SD) + d, sib).wait_recv()
        return zi

    swap, slot, _, _, _, total, done = scatter_parts(
        nz, pos, lambda t: p[t * 2 + c], lambda t: p.at[t * 2 + 1 - c], acc, came, ssend, srecv
    )

    def at_rows(ref, zi):
        return ref[pl.ds(zi * 2, 2)].reshape(pair, width)

    def hidden_part(zi, early):
        here = pl.ds(pl.multiple_of(zi * pair, pair), pair)

        def tile(j, _):
            u = pl.ds(pl.multiple_of(j * 256, 256), 256)
            value = dot(at_rows(mlp, zi), up_w[:, u], NN) + bias[:, u]
            grad = dot(at_rows(cot, zi), down_w[u, :], NT)
            act, slope = gelu_and_slope(value)
            low = (grad * slope).astype(BF)
            active[here, u] = act.astype(BF)
            gh[here, u] = low
            bias_g[:, u] += jnp.sum(f(low), axis=0, keepdims=True)
            return 0

        lax.fori_loop(0, units // 256, tile, 0)

        def back(j, _):
            w = pl.ds(pl.multiple_of(j * 512, 512), 512)
            p[pl.ds(zi * 2, 2), :, w] = dot(gh[here, :], up_w[w, :], NT).astype(BF).reshape(2, rows, 512)
            return 0

        lax.fori_loop(0, width // 512, back, 0)

    def forward_part(zi):
        here = pl.ds(pl.multiple_of(zi * pair, pair), pair)

        def tile(j, _):
            w = pl.ds(pl.multiple_of(j * 512, 512), 512)
            upd[pl.ds(zi * 2, 2), :, w] = dot(active[here, :], down_w[:, w], NN).astype(BF).reshape(2, rows, 512)
            return 0

        lax.fori_loop(0, width // 512, tile, 0)

    def up_grads(first, count):
        def tile(j, _):
            w = pl.ds(pl.multiple_of(j * 256, 256), 256)
            up_g[w, :] = dot(mlp[:, :, w].reshape(blocks * rows, 256), gh[...], TN).astype(BF)
            return 0

        lax.fori_loop(first, first + count, tile, 0)

    def down_grads():
        def tile(j, _):
            u = pl.ds(pl.multiple_of(j * 256, 256), 256)
            down_g[u, :] = dot(active[:, u], cot[...].reshape(blocks * rows, width), TN).astype(BF)
            return 0

        lax.fori_loop(0, units // 256, tile, 0)

    def project():
        def tile(j, _):
            w = pl.ds(pl.multiple_of(j * 512, 512), 512)
            branch = dot(mixed[...], out_w[:, :, w].reshape(width, 512), NN) + whole[4:5, w]
            sums[4:5, w] = jnp.sum(branch * branch, axis=0, keepdims=True)
            middle[:, w] = f(x_own[:, w]) + branch
            return 0

        lax.fori_loop(0, width // 512, tile, 0)

        def norm(j, _):
            here = pl.ds(pl.multiple_of(j * 32, 32), 32)
            normed, _ = norm_parts(middle[here, :])
            mlp[me, here] = (normed * whole[5:6, :] + whole[6:7, :]).astype(BF)
            return 0

        lax.fori_loop(0, rows // 32, norm, 0)

    def finish_rows():
        def norm(j, _):
            here = pl.ds(pl.multiple_of(j * 32, 32), 32)
            normed, inverse = norm_parts(middle[here, :])
            value, own = grad[here, :], f(cot[me, here])
            through = own + norm_back(value * whole[5:6, :], normed, inverse)
            low = through.astype(BF)
            grad_middle[here, :] = through
            grad_branch[here, :] = low
            for i, v in enumerate((value * normed, value, f(low), own)):
                sums[i : i + 1, :] += jnp.sum(v, axis=0, keepdims=True)
            return 0

        lax.fori_loop(0, rows // 32, norm, 0)
        each = 256 // part

        def tile(j, _):
            value = dot(grad_branch[...], out_w[pl.ds(j * each, each)].reshape(256, width), NT).astype(BF)
            for i in range(2):
                r = j * each + i * (each // 2)
                d, fs = r // blocks, r % blocks
                grad_mixed[fs // 2 * 2 + d % 2, :, pl.ds(pl.multiple_of(d // 2 * 128, 128), 128)] = value[
                    :, i * 128 : (i + 1) * 128
                ]
            return 0

        lax.fori_loop(0, width // 256, tile, 0)

    for copy in loads:
        copy.start()
    bias_g[...] = jnp.zeros_like(bias_g)
    sums[...] = jnp.zeros_like(sums)
    greet(line_partners(nz, pos))
    loads[0].wait()
    project()
    pl.when(z < nz - 1)(up(0).start)
    pl.when(z > 0)(dn(0).start)
    side(0, z >= 0).start()
    for copy in loads[1:]:
        copy.wait()
    slots = 2 * nz - 1
    tiles = width // 256
    for s in range(slots):
        if s < nz:
            zi = arrive(s)
            hidden_part(zi, s)
            swap(zi).start()
        slot(s)
        if s < nz:
            forward_part(zi)
        if s == nz - 1:
            store(0)
            down_grads()
            store(2)
        elif s == nz:
            up_grads(0, tiles // 2)
        elif s == nz + 1:
            up_grads(tiles // 2, tiles - tiles // 2)
            store(1)
    total(grad)
    finish_rows()
    for copies in stores:
        for copy in copies:
            copy.wait()
    side(0, z >= 0).wait_send()
    pl.when(z < nz - 1)(up(0).wait_send)
    pl.when(z > 0)(dn(0).wait_send)
    for k in range(1, nz):

        @pl.when(z >= k)
        def _():
            pl.when(z < nz - 1)(up(k).wait_send)
            side(k, z >= 0).wait_send()

        @pl.when(z + k < nz)
        def _():
            pl.when(z > 0)(dn(k).wait_send)
            side(k, z < 0).wait_send()

    done()


def mlp_bytes(nz, rows, width, units):
    tree = 2 * nz * rows
    kept = 4 * tree * width + 4 * units * width + 2 * tree * units + 2 * nz * rows * width + width * width
    return 2 * kept + 14 * rows * width


def mlp_call(mixed, x_own, whole, out_w, cot, up_w, down_w, bias, nz, cid):
    rows, width = x_own.shape
    units = down_w.shape[0]
    n = 2 * nz
    shape = jax.ShapeDtypeStruct
    return pl.pallas_call(
        functools.partial(mlp_kernel, nz),
        out_shape=[
            shape((rows, width), F32),
            shape((rows, width), F32),
            shape((rows, width), BF),
            shape((n, rows, width // n), BF),
            shape((8, width), F32),
            shape((1, units), F32),
            shape((n, rows, width), BF),
            shape((4, width // 4, units), BF),
            shape((units, width), BF),
        ],
        in_specs=[VM] * 3 + [HBM] * 4 + [VM],
        out_specs=[VM] * 6 + [HBM] * 3,
        scratch_shapes=[
            pltpu.VMEM((n, rows, width), BF),
            pltpu.VMEM((n, rows, width), BF),
            pltpu.VMEM((width, units), BF),
            pltpu.VMEM((units, width), BF),
            pltpu.VMEM((n, rows, width), BF),
            pltpu.VMEM((n, rows, width), BF),
            pltpu.VMEM((width, units), BF),
            pltpu.VMEM((units, width), BF),
            pltpu.VMEM(out_w.shape, BF),
            pltpu.VMEM((n * rows, units), BF),
            pltpu.VMEM((n * rows, units), BF),
            pltpu.VMEM((rows, width), F32),
            pltpu.VMEM((nz, rows, width), BF),
            pltpu.VMEM((nz + 1, rows, width), BF),
        ]
        + gather_sems(nz)
        + [pltpu.SemaphoreType.DMA((5 * nz,))] * 2
        + [pltpu.SemaphoreType.DMA((6 + 4 * n,))],
        compiler_params=params(cid, 63 * MIB),
        name="mlp",
    )(mixed, x_own, whole, out_w, cot, up_w, down_w, bias)


def attend_kernel(
    heads, nz, unit, slopes, far, joined_q, joined, cot, w_up, w_out, out, cot_all, up_w, out_w, *sems
):
    cols = heads * HD
    step, steps = pl.program_id(0), pl.num_programs(0)
    pos = place()
    n = 2 * nz
    gc = line_gather(cot, cot_all, *sems[:2], nz, True, pos)
    gu = sliced_gather(w_up, up_w, up_runs(nz, unit), sems[2:6], nz, pos)
    go = full_gather(w_out, out_w, *sems[6:8], nz, pos)

    @pl.when(step == 0)
    def _():
        x, c, z, y = pos
        greet(rank_partners(nz, pos) + group_partners(pos) + [(c != y, at(x, y, z, c))])
        gc[0]()
        gu[0]()
        go[0]()

    @pl.when(step == 1)
    def _():
        for stage in go[1:nz]:
            stage()

    @pl.when(step == 2)
    def _():
        for stage in gu[1 : n + 1]:
            stage()
        gc[1]()

    gap = far[...]
    for h in range(heads):
        q = joined_q[:, h * HD : (h + 1) * HD]
        k = joined[:, cols + h * HD : cols + (h + 1) * HD]
        v = joined[:, 2 * cols + h * HD : 2 * cols + (h + 1) * HD]
        logits = dot(q, k, NT) * HD ** (-0.5) + slopes[h] * gap
        weights = jnp.exp(logits - jnp.max(logits, axis=1, keepdims=True))
        probs = weights * (1.0 / jnp.sum(weights, axis=1, keepdims=True))
        out[:, h * HD : (h + 1) * HD] = dot(probs.astype(BF), v, NN).astype(BF)

    @pl.when(step == steps - 1)
    def _():
        for stage in go[nz : 2 * nz]:
            stage()
        ahead, later = gc[2:-1], gu[n + 1 : -1]
        for i, stage in enumerate(ahead):
            stage()
            for other in later[i * n // len(ahead) : (i + 1) * n // len(ahead)]:
                other()
        for stage in go[2 * nz :]:
            stage()
        gc[-1]()
        gu[-1]()


def attend(slopes, far, joined, cot, w_up, w_out, unit, heads, nz, cid):
    tree = far.shape[0]
    cols = heads * HD
    rows = min(256, max(128, 2**18 // tree))
    block, width = cot.shape
    part = w_up.shape[0]
    n = 2 * nz
    shapes = [(tree, cols), (n, block, width), (4 * n, part, 4 * unit), (4 * n, part, width)]
    return pl.pallas_call(
        functools.partial(attend_kernel, heads, nz, unit),
        out_shape=[jax.ShapeDtypeStruct(s, BF) for s in shapes],
        grid=(tree // rows,),
        in_specs=[
            pl.BlockSpec(memory_space=pltpu.SMEM),
            pl.BlockSpec((rows, tree), lambda i: (i, 0)),
            pl.BlockSpec((rows, 3 * cols), lambda i: (i, 0)),
            pl.BlockSpec((tree, 3 * cols), lambda i: (0, 0)),
            HBM,
            HBM,
            HBM,
        ],
        out_specs=[pl.BlockSpec((rows, cols), lambda i: (i, 0)), HBM, HBM, HBM],
        scratch_shapes=gather_sems(nz) + sliced_sems(nz) + full_sems(nz),
        compiler_params=params(cid, 56 * MIB),
        name="attend",
    )(slopes, far, joined, joined, cot, w_up, w_out)


def attend_back_kernel(heads, nz, kinds, slopes, far, joined_q, joined, grad, branch, part_sums, *refs):
    count = len(kinds)
    srcs, refs = refs[:count], refs[count:]
    out_q, out_k, out_v, branch_all, update, refs = *refs[:5], refs[5:]
    dsts, refs = refs[:count], refs[count:]
    acc_k, acc_v, p, refs = *refs[:3], refs[3:]
    scratch, gsems, hsems, psem = refs[:5], refs[5:7], refs[7:9], refs[9]
    cols = heads * HD
    step = pl.program_id(0)
    pos = place()
    gb = line_gather(branch, branch_all, *gsems, nz, False, pos)
    hs = hand_stages(srcs, dsts, kinds, *hsems, nz, pos)
    load = pltpu.make_async_copy(part_sums, p, psem.at[0])

    @pl.when(step == 0)
    def _():
        acc_k[...] = jnp.zeros_like(acc_k)
        acc_v[...] = jnp.zeros_like(acc_v)
        greet(line_partners(nz, pos) + group_partners(pos))
        hs[0]()
        gb[0]()
        gb[1]()
        load.start()

    @pl.when(step == 3)
    def _():
        gb[2]()

    gap = far[...]
    for h in range(heads):
        here = slice(h * HD, (h + 1) * HD)
        q = joined_q[:, here]
        k = joined[:, cols + h * HD : cols + (h + 1) * HD]
        v = joined[:, 2 * cols + h * HD : 2 * cols + (h + 1) * HD]
        g = grad[:, here]
        logits = dot(k, q, NT) * HD ** (-0.5) + slopes[h] * gap
        weights = jnp.exp(logits - jnp.max(logits, axis=0, keepdims=True))
        probs = weights * (1.0 / jnp.sum(weights, axis=0, keepdims=True))
        grad_probs = dot(v, g, NT)
        delta = jnp.sum(probs * grad_probs, axis=0, keepdims=True)
        grad_raw = (probs * (grad_probs - delta) * HD ** (-0.5)).astype(BF)
        acc_v[:, here] += dot(probs.astype(BF), g, NN)
        acc_k[:, here] += dot(grad_raw, q, NN)
        out_q[:, here] = dot(grad_raw, k, TN).astype(BF)

    @pl.when(step == pl.num_programs(0) - 1)
    def _():
        out_k[...] = acc_k[...].astype(BF)
        out_v[...] = acc_v[...].astype(BF)
        for stage in gb[3:]:
            stage()
        load.wait()
        scatter_blocks(nz, pos, p, update, *scratch)
        hs[1]()


def attend_back(slopes, far_t, joined, grad, branch, part_sums, arrays, kinds, heads, nz, cid):
    tree = far_t.shape[0]
    cols = heads * HD
    rows = min(256, max(128, 2**18 // tree))
    block, width = branch.shape
    full = pl.BlockSpec((tree, cols), lambda i: (0, 0))
    part = pl.BlockSpec((rows, cols), lambda i: (i, 0))
    return pl.pallas_call(
        functools.partial(attend_back_kernel, heads, nz, kinds),
        out_shape=[jax.ShapeDtypeStruct((tree, cols), BF)] * 3
        + [jax.ShapeDtypeStruct((2 * nz, block, width), BF), jax.ShapeDtypeStruct((block, width), F32)]
        + hand_shapes(arrays, kinds, nz),
        grid=(tree // rows,),
        in_specs=[
            pl.BlockSpec(memory_space=pltpu.SMEM),
            pl.BlockSpec((tree, rows), lambda i: (0, i)),
            pl.BlockSpec((rows, 3 * cols), lambda i: (i, 0)),
            pl.BlockSpec((tree, 3 * cols), lambda i: (0, 0)),
            part,
            HBM,
            HBM,
        ]
        + [HBM] * len(arrays),
        out_specs=[part, full, full, HBM, pl.BlockSpec((block, width), lambda i: (0, 0))] + [HBM] * len(arrays),
        scratch_shapes=[pltpu.VMEM((tree, cols), F32)] * 2
        + [pltpu.VMEM((2 * nz, block, width), BF)]
        + scatter_scratch(nz, block, width)
        + gather_sems(nz)
        + hand_sems(kinds)
        + [pltpu.SemaphoreType.DMA((1,))],
        compiler_params=params(cid, 62 * MIB),
        name="attend_back",
    )(slopes, far_t, joined, joined, grad, branch, part_sums, *arrays)


def norm_parts(values):
    center = values - jnp.mean(values, axis=-1, keepdims=True)
    inverse = lax.rsqrt(jnp.mean(center * center, axis=-1, keepdims=True) + EPSILON)
    return (center * inverse, inverse)


def norm_back(grad_normed, normed, inverse):
    mean_grad = jnp.mean(grad_normed, axis=-1, keepdims=True)
    mean_cross = jnp.mean(grad_normed * normed, axis=-1, keepdims=True)
    return inverse * (grad_normed - mean_grad - normed * mean_cross)


def tree_tables(parents, seg_blocks, valid):
    segments = parents.shape[0]
    seg_tokens = jnp.broadcast_to(seg_blocks[:, None], (seg_blocks.shape[0], BLK)).reshape(-1)
    labels = jnp.arange(segments, dtype=jnp.int32)
    member = (seg_tokens[:, None] == labels[None, :]).astype(jnp.int32)
    counted = member * valid[:, None]
    before = jnp.cumsum(counted, axis=0) - counted
    rank = jnp.sum(before * member, axis=1)
    seg_len = jnp.sum(counted, axis=0)
    picked = (parents[:, None] == labels[None, :]).astype(jnp.int32)
    grand = jnp.sum(picked * parents[None, :], axis=1)
    ancestor = ((labels[None, :] == parents[:, None]) | (labels[None, :] == grand[:, None])) & (
        labels[None, :] != labels[:, None]
    )
    offset = jnp.sum(ancestor.astype(jnp.int32) * seg_len[None, :], axis=1)
    position = jnp.sum(member * offset[None, :], axis=1) + rank
    return (seg_tokens, position, ancestor.astype(jnp.float32))


def allowed_mask(seg, index, valid, ancestor):
    labels = jnp.arange(ancestor.shape[0], dtype=jnp.int32)
    member = (seg[:, None] == labels[None, :]).astype(jnp.float32)
    reach = jnp.dot(jnp.dot(member, ancestor), member.T) > 0.5
    causal = (seg[:, None] == seg[None, :]) & (index[None, :] <= index[:, None])
    visible = (valid[None, :] == 1) | (index[None, :] == index[:, None])
    return (reach | causal) & visible


def gelu_exact(value):
    return jax.nn.gelu(value, approximate=False)


def mm(spec, a, b):
    return jnp.einsum(spec, a, b, preferred_element_type=F32)


def padded(flat, lanes):
    return jnp.pad(flat, [(0, 0)] * (flat.ndim - 1) + [(0, -flat.shape[-1] % lanes)])


def by_steps(
    layer_in,
    cotangent,
    w_qkv,
    w_out,
    w_up,
    w_down,
    gain_attn,
    shift_attn,
    bias_query,
    bias_value,
    bias_out,
    gain_mlp,
    shift_mlp,
    bias_up,
    bias_down,
    parents,
    seg_blocks,
    token_valid,
):
    rows, width = layer_in.shape
    fsdp = lax.axis_size("fsdp")
    nz = fsdp // 2
    devices = 4 * fsdp
    x, c, z, y = place()
    rank = z * 2 + c
    heads = H // fsdp
    cols = heads * HD
    tree = token_valid.shape[1]
    part = w_up.shape[0]
    unit = w_down.shape[0]

    vec = jnp.concatenate(
        [gain_attn, shift_attn, bias_query, bias_value, bias_out, gain_mlp, shift_mlp, bias_down, bias_up]
    ).astype(F32)
    vec = padded(vec, 1024).reshape(-1, 128)
    tab = jnp.concatenate([token_valid[0], seg_blocks[0], parents[0]])
    tab = padded(tab, 1024).reshape(-1, 128)
    aligned = part == HD and cols % 256 == 0
    if not aligned:
        w_qkv = w_qkv.reshape(part, 3, fsdp, cols).transpose(2, 0, 1, 3).reshape(fsdp, part, 3 * cols)
    x_all, qkv_w, down_w, vecs, tab = fetch(nz, layer_in, w_qkv, w_down, part, vec, tab, 1)
    down_w = down_w.reshape(4 * unit, width)
    x_all = x_all.reshape(tree, width)
    qkv_w = qkv_w.reshape(width, 3 * cols)
    vecs = vecs.reshape(devices, -1)
    (gain_one, shift_one, query_bias, value_bias, out_bias, gain_two, shift_two, down_bias) = [
        vecs[:, i * part : (i + 1) * part].reshape(-1) for i in range(8)
    ]
    up_bias = vecs[:, 8 * part : 8 * part + unit].reshape(2, 2, nz, 2, unit)
    up_bias = lax.dynamic_slice(up_bias, (0, c, z, 0, 0), (2, 1, 1, 2, unit)).reshape(-1)

    def own_rows(v):
        return lax.dynamic_slice_in_dim(v, rank * rows, rows, 0)

    normed_all, _ = norm_parts(x_all.astype(F32))
    attn_in = (normed_all * gain_one + shift_one).astype(BF)
    inputs = own_rows(x_all).astype(F32)
    normed_one, inverse_one = norm_parts(inputs)

    if aligned:

        def own_cols(v):
            v = v.reshape(2, 2, nz, 2, HD)
            return lax.dynamic_slice(v, (0, c, z, 0, 0), (2, 1, 1, 2, HD)).reshape(-1)

        def spread(v):
            v = v.reshape(2, 1, 1, 2, HD)
            return lax.dynamic_update_slice(jnp.zeros((2, 2, nz, 2, HD), F32), v, (0, c, z, 0, 0))

        numbers = block_of(jnp.arange(2)[:, None], c, z, jnp.arange(2)[None, :], nz).reshape(-1)
    else:

        def own_cols(v):
            return lax.dynamic_slice_in_dim(v, rank * cols, cols, 0)

        def spread(v):
            return lax.dynamic_update_slice_in_dim(jnp.zeros((width,), F32), v, rank * cols, 0)

        numbers = rank * heads + jnp.arange(heads)

    joined_bias = jnp.concatenate([own_cols(query_bias), jnp.zeros((cols,), F32), own_cols(value_bias)])
    joined = (jnp.dot(attn_in, qkv_w, preferred_element_type=F32) + joined_bias).astype(BF)

    tab = tab.reshape(-1)
    blocks = seg_blocks.shape[1]
    valid = tab[:tree]
    seg, position, ancestor = tree_tables(
        tab[tree + blocks : tree + blocks + parents.shape[1]], tab[tree : tree + blocks], valid
    )
    index = jnp.arange(tree, dtype=jnp.int32)
    mask = allowed_mask(seg, index, valid, ancestor)
    far = jnp.where(mask, (position[None, :] - position[:, None]).astype(F32), MASKED)
    slopes = jnp.exp2(-8.0 * (numbers.astype(F32) + 1.0) / H)
    mixed, cot, up_w, out_w = attend(slopes, far, joined, cotangent, w_up, w_out, unit, heads, nz, 9)
    out_w = out_w.reshape(width, width)
    cot = cot.reshape(tree, width)
    up_w = up_w.reshape(width, 4 * unit)

    mixed_own = exchange(mixed.reshape(fsdp, rows, cols), nz, 2, "mixed_to_tokens")
    if aligned:
        mixed_own = mixed_own.reshape(nz, 2, rows, 2, 2 * HD).transpose(2, 3, 1, 0, 4).reshape(rows, width)
    else:
        mixed_own = mixed_own.transpose(1, 0, 2).reshape(rows, width)
    branch = jnp.dot(mixed_own, out_w, preferred_element_type=F32) + out_bias
    middle = inputs + branch
    normed_two, inverse_two = norm_parts(middle)
    mlp_own = (normed_two * gain_two + shift_two).astype(BF)
    cot_blocks = cot.reshape(fsdp, rows, width)
    mlp_in = gather_tokens(mlp_own, nz, 3).reshape(tree, width)
    hidden = jnp.dot(mlp_in, up_w, preferred_element_type=F32) + up_bias
    active_float, gelu_pull = jax.vjp(gelu_exact, hidden)
    active = active_float.astype(BF)
    grad_active = mm("td,fd->tf", cot, down_w)
    grad_hidden = gelu_pull(grad_active)[0].astype(BF)
    grad_mlp_in = mm("tf,df->td", grad_hidden, up_w).astype(BF).reshape(fsdp, rows, width)
    grad_mlp_in = scatter_tokens(grad_mlp_in, nz, 4)
    update = jnp.dot(active, down_w, preferred_element_type=F32).astype(BF).reshape(fsdp, rows, width)
    down_g = mm("tf,td->fd", active, cot).astype(BF)
    up_g = mm("td,tf->df", mlp_in, grad_hidden).astype(BF)
    grad_bias_up = jnp.sum(grad_hidden.astype(F32), axis=0)
    down_g = down_g.reshape(4, unit, width)
    cot_own = own_rows(cot).astype(F32)
    grad_middle = cot_own + norm_back(grad_mlp_in * gain_two, normed_two, inverse_two)
    grad_branch = grad_middle.astype(BF)
    grad_mixed = mm("te,de->td", grad_branch, out_w).astype(BF)
    if not aligned:
        grad_out_w = lax.psum_scatter(
            mm("td,te->de", mixed_own, grad_branch).astype(BF), BOTH, scatter_dimension=0, tiled=True
        ).astype(F32)
    if aligned:
        grad_mixed = grad_mixed.reshape(rows, 2, 2, nz, 2 * HD).transpose(3, 2, 0, 1, 4).reshape(fsdp, rows, cols)
    else:
        grad_mixed = grad_mixed.reshape(rows, fsdp, cols).transpose(1, 0, 2)
    up_g = up_g.reshape(devices, part, 4 * unit)
    grad_heads = exchange(grad_mixed, nz, 5, "grad_to_heads")
    grad_heads = grad_heads.reshape(tree, cols)
    grad_q, grad_k, grad_v, branch_all, update, down_c, up_c = attend_back(
        slopes, far.T, joined, grad_heads, grad_branch, update, [down_g, up_g], (False, True), heads, nz, 6
    )
    result = middle + update + down_bias
    grad_joined = jnp.concatenate([grad_q, grad_k, grad_v], axis=1)

    def mine(g, came):
        g = g.reshape((2, 2, nz, 2) + g.shape[1:])
        g = lax.dynamic_slice(g, (x, 0, 0, y, 0, 0), (1, 2, nz, 1) + g.shape[4:])
        g = g.reshape((2, nz) + g.shape[4:]).swapaxes(0, 1)
        return (g.reshape(came.shape[1:]).astype(F32) + jnp.sum(came.astype(F32), axis=0)).astype(BF)

    def mine_flat(g, came):
        return lax.dynamic_index_in_dim(g, x * 2 + y, 0, keepdims=False).astype(F32) + jnp.sum(came.astype(F32), axis=0)

    grad_down_w = mine_flat(down_g, down_c)
    qkv_g = mm("td,te->de", attn_in, grad_joined).astype(BF).reshape(devices, part, 3 * cols)
    flat = []
    if aligned:
        flat = [mm("td,te->de", mixed, branch_all.reshape(tree, width)).astype(BF).reshape(4, part, width)]
    kinds = (True,) + (False,) * len(flat)
    grad_attn_in = mm("te,de->td", grad_joined, qkv_w).astype(BF).reshape(fsdp, rows, width)
    grad_attn_in, grad_up_w, layer_out, qkv_c, *out_c = scatter_and_hand(
        grad_attn_in, mine(up_g, up_c), up_runs(nz, unit), result.astype(BF), [qkv_g] + flat, kinds, nz, 10
    )
    if aligned:
        grad_out_w = mine_flat(flat[0], out_c[0])
    col, square = jnp.sum(grad_joined.astype(F32), axis=0), jnp.sum(result * result)
    grad_up_w = grad_up_w.astype(F32)
    grad_inputs = grad_middle + norm_back(grad_attn_in * gain_one, normed_one, inverse_one)

    smalls = [
        jnp.sum(grad_attn_in * normed_one, axis=0),
        jnp.sum(grad_attn_in, axis=0),
        spread(col[:cols]),
        spread(col[2 * cols :]),
        jnp.sum(grad_branch.astype(F32), axis=0),
        jnp.sum(grad_mlp_in * normed_two, axis=0),
        jnp.sum(grad_mlp_in, axis=0),
        jnp.sum(cot_own, axis=0),
    ]
    grad_bias_up = grad_bias_up.reshape(2, 1, 1, 2, unit)
    grad_bias_up = lax.dynamic_update_slice(jnp.zeros((2, 2, nz, 2, unit), F32), grad_bias_up, (0, c, z, 0, 0))
    squares = jnp.stack([square, jnp.sum(branch * branch)])
    packed = jnp.concatenate(
        [v.reshape(devices, part) for v in smalls]
        + [grad_bias_up.reshape(devices, unit), jnp.broadcast_to(squares, (devices, 2))],
        axis=1,
    )
    packed = padded(packed, 1024).reshape(devices, -1, 128)
    runs = qkv_runs(nz, width, cols) if aligned else None
    grad_x, packed, grad_qkv_w = finish(grad_inputs.astype(BF), packed, mine(qkv_g, qkv_c), runs, nz, 8)
    if not aligned:
        grad_qkv_w = grad_qkv_w.reshape(fsdp, part, 3, cols).transpose(1, 2, 0, 3).reshape(part, -1)
    grad_qkv_w = grad_qkv_w.astype(F32)
    packed = packed.reshape(-1)
    small = [packed[i * part : (i + 1) * part] for i in range(8)]
    up_at = 8 * part
    root_squares = jnp.sqrt(packed[up_at + unit : up_at + unit + 2] / (devices * rows * width))
    return (
        layer_out,
        grad_x,
        grad_qkv_w,
        grad_out_w,
        grad_up_w,
        grad_down_w,
        small[0],
        small[1],
        small[2],
        small[3],
        small[4],
        small[5],
        small[6],
        packed[up_at : up_at + unit],
        small[7],
        root_squares,
    )


def by_kernels(
    layer_in,
    cotangent,
    w_qkv,
    w_out,
    w_up,
    w_down,
    gain_attn,
    shift_attn,
    bias_query,
    bias_value,
    bias_out,
    gain_mlp,
    shift_mlp,
    bias_up,
    bias_down,
    parents,
    seg_blocks,
    token_valid,
):
    rows, width = layer_in.shape
    fsdp = lax.axis_size("fsdp")
    nz = fsdp // 2
    devices = 4 * fsdp
    heads = H // fsdp
    cols = heads * HD
    tree = token_valid.shape[1]
    part = w_up.shape[0]
    unit = w_down.shape[0]

    slopes = jnp.asarray(np.exp2(-8.0 * (np.arange(H) + 1.0) / H).astype(np.float32))
    vectors = (gain_attn, shift_attn, bias_query, bias_value, bias_out, gain_mlp, shift_mlp, bias_down)
    joined, mixed, mixed_own, own, whole, up_bias, attn_in, far, cot, qkv_w, up_w, out_w, down_w = head_call(
        slopes, (token_valid, seg_blocks, parents), vectors, bias_up, layer_in, cotangent, w_qkv, w_up, w_out, w_down,
        heads, nz, 1,
    )
    qkv_w = qkv_w.reshape(width, 3 * cols)
    up_w = up_w.reshape(width, 4 * unit)
    down_w = down_w.reshape(4 * unit, width)
    middle, grad_middle, grad_branch, grad_mixed, sums, grad_bias_up, update, up_g, down_g = mlp_call(
        mixed_own, own, whole, out_w, cot, up_w, down_w, up_bias, nz, 3
    )
    down_g = down_g.reshape(4, unit, width)
    runs = up_runs(nz, unit), qkv_runs(nz, width, cols)
    grad_down_w, grad_out_w, small, bias, grad_up_w, grad_qkv_w, _, layer_out, grad_x = tail_call(
        slopes, far, grad_mixed, joined, attn_in, mixed.reshape(tree, cols), qkv_w, grad_branch, update, up_g, down_g,
        middle, own, whole, grad_middle, sums, grad_bias_up, runs, heads, nz, 6,
    )
    root_squares = jnp.sqrt(small[8:10, 0] / (devices * rows * width))
    vectors = [small[i, :part] for i in range(8)]
    return (
        layer_out,
        grad_x,
        grad_qkv_w.astype(F32),
        grad_out_w,
        grad_up_w.astype(F32),
        grad_down_w,
        *vectors[:7],
        bias.reshape(-1)[:unit],
        vectors[7],
        root_squares,
    )


def per_device(*args):
    layer_in, w_down, token_valid = args[0], args[5], args[17]
    fsdp = lax.axis_size("fsdp")
    rows, width = layer_in.shape
    unit = w_down.shape[0]
    fits = mlp_bytes(fsdp // 2, rows, width, 4 * unit) < 60 * MIB
    whole_heads = args[2].shape[0] == HD and H // fsdp == 4 and width == H * HD
    if fsdp == 8 and fits and whole_heads and unit % 128 == 0 and token_valid.shape[1] % 256 == 0 and rows == 128:
        return by_kernels(*args)
    return by_steps(*args)


def solution(mesh):
    matrix, vector, table = P(BOTH, None), P(BOTH), P("dp", None)
    return jax.shard_map(
        per_device,
        mesh=mesh,
        in_specs=(matrix,) * 6 + (vector,) * 9 + (table,) * 3,
        out_specs=(matrix,) * 6 + (vector,) * 9 + (P(),),
        check_vma=False,
    )
```

```python
import functools
import math

import jax
import jax.numpy as jnp
import numpy as np
from jax import lax
from jax.experimental import pallas as pl
from jax.experimental.pallas import tpu as pltpu
from jax.sharding import PartitionSpec as P

H = 32
HD = 64
BLK = 32

EPSILON = 1e-05
MASKED = -1e30
BF = jnp.bfloat16
F32 = jnp.float32
BOTH = ("dp", "fsdp")
MESH = pl.DeviceIdType.MESH
HBM = pl.BlockSpec(memory_space=pl.ANY)
VM = pl.BlockSpec(memory_space=pltpu.VMEM)
MIB = 2**20


def place():
    d, f = lax.axis_index("dp"), lax.axis_index("fsdp")
    return d // 2, d % 2, f // 2, f % 2


def at(x, c, z, y):
    return (x * 2 + c, z * 2 + y)


def remote(src, dst, send, recv, target):
    return pltpu.make_async_remote_copy(
        src_ref=src, dst_ref=dst, send_sem=send, recv_sem=recv, device_id=target, device_id_type=MESH
    )


def greet(partners):
    barrier = pltpu.get_barrier_semaphore()
    count = 0
    for condition, device in partners:

        @pl.when(condition)
        def _():
            pl.semaphore_signal(barrier, inc=1, device_id=device, device_id_type=MESH)

        count = count + jnp.asarray(condition).astype(jnp.int32)
    pl.semaphore_wait(barrier, count)


def greet_all(devices, fsdp, me):
    barrier = pltpu.get_barrier_semaphore()

    def one(k, _):
        other = (me + k) % devices
        pl.semaphore_signal(barrier, inc=1, device_id=(other // fsdp, other % fsdp), device_id_type=MESH)
        return 0

    lax.fori_loop(1, devices, one, 0)
    pl.semaphore_wait(barrier, devices - 1)


def line_partners(nz, pos):
    x, c, z, y = pos
    return [(z >= 0, at(x, 1 - c, z, y)), (z > 0, at(x, c, z - 1, y)), (z < nz - 1, at(x, c, z + 1, y))]


def rank_partners(nz, pos):
    x, c, z, y = pos
    n = 2 * nz
    others = [(z * 2 + c + k) % n for k in range(1, n)]
    return [(z >= 0, at(x, p % 2, p // 2, y)) for p in others]


def group_partners(pos):
    x, c, z, y = pos
    return [(z >= 0, at(x ^ (m // 2), c, z, y ^ (m % 2))) for m in (1, 2, 3)]


def line_gather(src, dst, send, recv, nz, swap, pos):
    x, c, z, y = pos
    own = z * 2 + c
    sib = at(x, 1 - c, z, y)
    up_dev, dn_dev = at(x, c, z + 1, y), at(x, c, z - 1, y)
    UP, DN, SU, SD = 0, nz, 2 * nz, 3 * nz
    OWN = 4 * nz

    def block(b, moved):
        return dst.at[b] if moved else src

    def up(k):
        b = (z - k) * 2 + c
        return remote(block(b, k or swap), dst.at[b], send.at[UP + k], recv.at[UP + k], up_dev)

    def dn(k):
        b = (z + k) * 2 + c
        return remote(block(b, k or swap), dst.at[b], send.at[DN + k], recv.at[DN + k], dn_dev)

    def side(k, base, sign):
        b = (z + sign * k) * 2 + c
        return remote(block(b, k or swap), dst.at[b], send.at[base + k], recv.at[base + k], sib)

    def got(b, sem):
        return remote(dst.at[b], dst.at[b], send.at[OWN], recv.at[sem], sib)

    local = pltpu.make_async_copy(src, dst.at[own], recv.at[OWN])
    trade = remote(src, dst.at[z * 2 + y], send.at[OWN], recv.at[OWN], at(x, y, z, c))

    def first():
        if swap:
            pl.when(c == y)(local.start)
            pl.when(c != y)(trade.start)
        else:
            local.start()

    def spread():
        if swap:
            local.wait()
        pl.when(z < nz - 1)(up(0).start)
        pl.when(z > 0)(dn(0).start)
        side(0, SU, 1).start()

    def step(k):
        @pl.when(z >= k)
        def _():
            got((z - k) * 2 + c, UP + k - 1).wait_recv()
            pl.when(z < nz - 1)(up(k).start)
            side(k, SU, -1).start()

        @pl.when(z + k < nz)
        def _():
            got((z + k) * 2 + c, DN + k - 1).wait_recv()
            pl.when(z > 0)(dn(k).start)
            side(k, SD, 1).start()

    def last():
        if swap:
            pl.when(c != y)(trade.wait_send)
        else:
            local.wait()
        got(z * 2 + 1 - c, SU).wait_recv()
        pl.when(z < nz - 1)(up(0).wait_send)
        pl.when(z > 0)(dn(0).wait_send)
        side(0, SU, 1).wait_send()
        for k in range(1, nz):

            @pl.when(z >= k)
            def _():
                got((z - k) * 2 + 1 - c, SU + k).wait_recv()
                pl.when(z < nz - 1)(up(k).wait_send)
                side(k, SU, -1).wait_send()

            @pl.when(z + k < nz)
            def _():
                got((z + k) * 2 + 1 - c, SD + k).wait_recv()
                pl.when(z > 0)(dn(k).wait_send)
                side(k, SD, 1).wait_send()

    return [first, spread] + [functools.partial(step, k) for k in range(1, nz)] + [last]


def gather_sems(nz):
    return [pltpu.SemaphoreType.DMA((4 * nz + 1,))] * 2


def gather_kernel(nz, src, dst, send, recv):
    pos = place()
    greet(line_partners(nz, pos))
    for stage in line_gather(src, dst, send, recv, nz, False, pos):
        stage()


def params(cid, vmem=None):
    return pltpu.CompilerParams(collective_id=cid, has_side_effects=True, vmem_limit_bytes=vmem)


def gather_tokens(a, nz, cid):
    return pl.pallas_call(
        functools.partial(gather_kernel, nz),
        out_shape=jax.ShapeDtypeStruct((2 * nz,) + a.shape, a.dtype),
        in_specs=[HBM],
        out_specs=HBM,
        scratch_shapes=gather_sems(nz),
        compiler_params=params(cid),
        name="gather_tokens",
    )(a)


def scatter_blocks(nz, pos, p, out, acc, ups, dns, send, recv):
    x, c, z, y = pos
    sib = at(x, 1 - c, z, y)
    S, U, D = 0, nz, 2 * nz

    def f(v):
        return v.astype(F32)

    def swap(t):
        return remote(p.at[t * 2 + 1 - c], acc.at[t], send.at[S + t], recv.at[S + t], sib)

    def up(t):
        return remote(acc.at[t], ups.at[t], send.at[U + t], recv.at[U + t], at(x, c, z + 1, y))

    def dn(t):
        return remote(acc.at[t], dns.at[t], send.at[D + t], recv.at[D + t], at(x, c, z - 1, y))

    order = []
    for i in range(nz - 1):
        order += [(True, nz - 1 - i), (False, i)]
    for upward, t in order:
        pl.when(z < t if upward else z > t)(swap(t).start)
    swap(z).start()
    for upward, t in order:

        @pl.when(z < t if upward else z > t)
        def _():
            swap(t).wait_recv()
            acc[t] = (f(acc[t]) + f(p[t * 2 + c])).astype(BF)
            move, came = (up, ups) if upward else (dn, dns)

            @pl.when(z > 0 if upward else z < nz - 1)
            def _():
                move(t).wait_recv()
                acc[t] = (f(acc[t]) + f(came[t])).astype(BF)

            move(t).start()

    swap(z).wait_recv()
    out[...] = f(acc[z]) + f(p[z * 2 + c])

    @pl.when(z > 0)
    def _():
        up(z).wait_recv()
        out[...] += f(ups[z])

    @pl.when(z < nz - 1)
    def _():
        dn(z).wait_recv()
        out[...] += f(dns[z])

    for t in range(nz):
        swap(t).wait_send()
        pl.when(z < t)(up(t).wait_send)
        pl.when(z > t)(dn(t).wait_send)


def scatter_scratch(nz, rows, width):
    return [pltpu.VMEM((nz, rows, width), BF)] * 3 + [pltpu.SemaphoreType.DMA((3 * nz,))] * 2


def scatter_kernel(nz, p, out, *scratch):
    pos = place()
    greet(line_partners(nz, pos))
    scatter_blocks(nz, pos, p, out, *scratch)


def scatter_tokens(p, nz, cid):
    blocks, rows, width = p.shape
    return pl.pallas_call(
        functools.partial(scatter_kernel, nz),
        out_shape=jax.ShapeDtypeStruct((rows, width), F32),
        in_specs=[VM],
        out_specs=VM,
        scratch_shapes=scatter_scratch(nz, rows, width),
        compiler_params=params(cid, 60 * MIB),
        name="scatter_tokens",
    )(p)


def scatter_and_hand_kernel(nz, kinds, runs, p, up_s, res, *refs):
    count = len(kinds)
    srcs, refs = refs[:count], refs[count:]
    out, up_o, res_o, refs = *refs[:3], refs[3:]
    dsts, refs = refs[:count], refs[count:]
    scratch, hsems, esems, tsems = refs[:5], refs[5:7], refs[7:9], refs[9:11]
    pos = place()
    x, c, z, y = pos
    greet(rank_partners(nz, pos) + group_partners(pos) + [(c != y, at(x, y, z, c))])
    hs = hand_stages(srcs, dsts, kinds, *hsems, nz, pos)
    es = exchange_stages(up_s, up_o, runs, *esems, nz, pos)
    ts = trade_stages(res, res_o, *tsems, pos)
    hs[0]()
    es[0]()
    ts[0]()
    scatter_blocks(nz, pos, p, out, *scratch)
    hs[1]()
    es[1]()
    ts[1]()


def scatter_and_hand(p, up_s, runs, res, arrays, kinds, nz, cid):
    blocks, rows, width = p.shape
    n, part, share = up_s.shape
    return pl.pallas_call(
        functools.partial(scatter_and_hand_kernel, nz, kinds, runs),
        out_shape=[
            jax.ShapeDtypeStruct((rows, width), F32),
            jax.ShapeDtypeStruct((part, n * share), BF),
            jax.ShapeDtypeStruct(res.shape, BF),
        ]
        + hand_shapes(arrays, kinds, nz),
        in_specs=[VM] + [HBM] * (2 + len(arrays)),
        out_specs=[VM] + [HBM] * (2 + len(arrays)),
        scratch_shapes=scatter_scratch(nz, rows, width) + hand_sems(kinds) + exchange_sems(runs, nz) + trade_sems(),
        compiler_params=params(cid, 60 * MIB),
        name="scatter_and_hand",
    )(p, up_s, res, *arrays)


def block_of(x, c, z, y, nz):
    return (x * 2 + c) * 2 * nz + z * 2 + y


def halves(ref, rows, cut=2):
    half = rows // cut
    if half % 16:
        return {1: None, 2: ref}
    return {1: ref.at[pl.ds(half, rows - half)], 2: ref.at[pl.ds(0, half)]}


def sliced_gather(src, dst, runs, sems, nz, pos):
    x, c, z, y = pos
    n = 2 * nz
    me = z * 2 + c
    part = dst.shape[1]
    send1, recv1, send2, recv2 = sems

    def pieces(p):
        if runs is None:
            return [(src.at[p], slice(None))]
        return [(src.at[:, pl.ds(there, size)], pl.ds(here, size)) for there, here, size in runs(p)]

    def row(p, gx, gy):
        return dst.at[block_of(gx, p % 2, p // 2, gy, nz)]

    mine = block_of(x, c, z, y, nz)

    def out(k):
        p = (me + k) % n
        return [
            remote(a, dst.at[mine, :, b], send1.at[p], recv1.at[me], at(x, p % 2, p // 2, y))
            for a, b in pieces(p)
        ]

    local = [pltpu.make_async_copy(a, dst.at[mine, :, b], recv1.at[me]) for a, b in pieces(me)]

    def came(k):
        return (me - k + n) % n

    def arrival(b, sem):
        return remote(b, b, send1.at[me], sem, at(x, 1 - c, z, y))

    def neighbour(m):
        return at(x ^ (m // 2), c, z, y ^ (m % 2))

    def forward(k, m):
        p = came(k)
        b = row(p, x, y)
        slot = (m - 1) * n + p
        return remote(b, b, send2.at[slot], recv2.at[slot], neighbour(m))

    def relay(k, m):
        p = came(k)
        b = halves(row(p, x ^ (m // 2), y ^ (m % 2)), part)[m]
        slot = (1 + m) * n + p
        return b is not None and remote(b, b, send2.at[slot], recv2.at[slot], neighbour(3 - m))

    def first():
        for copy in local:
            copy.start()
        for k in range(1, n):
            for copy in out(k):
                copy.start()

    def step(k):
        p = came(k)
        arrival(row(p, x, y), recv1.at[p]).wait_recv()
        for m in (1, 2):
            forward(k, m).start()

    def pass_on(k):
        p = came(k)
        for m in (1, 2):
            arrival(row(p, x ^ (m // 2), y ^ (m % 2)), recv2.at[(m - 1) * n + p]).wait_recv()
            if relay(k, m):
                relay(k, m).start()

    def last():
        for k in range(n):
            p = came(k)
            parts = halves(row(p, 1 - x, 1 - y), part)
            for m in (1, 2):
                if parts[m] is not None:
                    arrival(parts[m], recv2.at[(1 + m) * n + p]).wait_recv()
        for k in range(n):
            if k:
                p = (me + k) % n
                b = dst.at[mine]
                remote(b, b, send1.at[p], recv1.at[me], at(x, p % 2, p // 2, y)).wait_send()
            for m in (1, 2):
                forward(k, m).wait_send()
                if relay(k, m):
                    relay(k, m).wait_send()

    stages = [functools.partial(step, k) for k in range(n)] + [functools.partial(pass_on, k) for k in range(n)]
    return [first] + stages + [last]


def sliced_sems(nz):
    n = 2 * nz
    return [pltpu.SemaphoreType.DMA((n,))] * 2 + [pltpu.SemaphoreType.DMA((4 * n,))] * 2


def group_gather(src, dst, send, recv, pos):
    x, c, z, y = pos
    rows = src.shape[0]
    local = pltpu.make_async_copy(src, dst.at[x * 2 + y], recv.at[0])

    def there(m):
        return dst.at[(x ^ (m // 2)) * 2 + (y ^ (m % 2))]

    def neighbour(m):
        return at(x ^ (m // 2), c, z, y ^ (m % 2))

    def out(m):
        return remote(src, dst.at[x * 2 + y], send.at[m], recv.at[m], neighbour(m))

    def relay(m):
        b = halves(there(m), rows, 4)[m]
        return b is not None and remote(b, b, send.at[2 + m], recv.at[2 + m], neighbour(3 - m))

    def arrival(b, sem):
        return remote(b, b, send.at[0], sem, at(x, 1 - c, z, y))

    def first():
        local.start()
        for m in (1, 2):
            out(m).start()

    def pass_on():
        for m in (1, 2):
            arrival(there(m), recv.at[m]).wait_recv()
            if relay(m):
                relay(m).start()

    def last():
        local.wait()
        parts = halves(there(3), rows, 4)
        for m in (1, 2):
            if parts[m] is not None:
                arrival(parts[m], recv.at[2 + m]).wait_recv()
            out(m).wait_send()
            if relay(m):
                relay(m).wait_send()

    return [first, pass_on, last]


def full_gather(src, dst, send, recv, nz, pos):
    x, c, z, y = pos
    rows = src.shape[0]
    sib = at(x, 1 - c, z, y)
    mine = dst.at[block_of(x, c, z, y, nz)]

    def row(core, k, m):
        return dst.at[block_of(x ^ (m // 2), core, z + k, y ^ (m % 2), nz)]

    def neighbour(m):
        return at(x ^ (m // 2), c, z, y ^ (m % 2))

    def arrival(b, sem):
        return remote(b, b, send.at[0], recv.at[sem], sib)

    def along(k, sign):
        b = row(c, k, 0)
        return remote(
            b if k else src, b, send.at[(0 if sign > 0 else nz) + z + k], recv.at[z + k], at(x, c, z + sign, y)
        )

    def forward(k, m):
        b = row(c, k, 0)
        return remote(b if k else src, b, send.at[(1 + m) * nz + z + k], recv.at[m * nz + z + k], neighbour(m))

    def relay(k, m):
        b = halves(row(c, k, m), rows)[m]
        if b is None:
            return None
        return remote(b, b, send.at[(3 + m) * nz + z + k], recv.at[(2 + m) * nz + z + k], neighbour(3 - m))

    def side(k, m):
        b = row(c, k, m)
        return remote(b if k or m else src, b, send.at[(6 + m) * nz + z + k], recv.at[(5 + m) * nz + z + k], sib)

    local = pltpu.make_async_copy(src, mine, recv.at[z])

    def first():
        local.start()
        pl.when(z < nz - 1)(along(0, 1).start)
        pl.when(z > 0)(along(0, -1).start)
        for m in (1, 2):
            forward(0, m).start()
        side(0, 0).start()

    def both(k, fn):
        @pl.when(z >= k)
        def _():
            fn(-k)

        if k:

            @pl.when(z + k < nz)
            def _():
                fn(k)

    def step(k):
        def one(k):
            arrival(row(c, k, 0), z + k).wait_recv()
            if k > 0:
                pl.when(z > 0)(along(k, -1).start)
            else:
                pl.when(z < nz - 1)(along(k, 1).start)
            for m in (1, 2):
                forward(k, m).start()
            side(k, 0).start()

        both(k, one)

    def pass_on(k):
        def one(k):
            for m in (1, 2):
                arrival(row(c, k, m), m * nz + z + k).wait_recv()
                if relay(k, m) is not None:
                    relay(k, m).start()
                side(k, m).start()

        both(k, one)

    def diagonal(k):
        def one(k):
            parts = halves(row(c, k, 3), rows)
            for m in (1, 2):
                if parts[m] is not None:
                    arrival(parts[m], (2 + m) * nz + z + k).wait_recv()
            side(k, 3).start()

        both(k, one)

    def last():
        local.wait()

        def one(k):
            for m in range(4):
                arrival(row(1 - c, k, m), (5 + m) * nz + z + k).wait_recv()
                side(k, m).wait_send()
            if k >= 0:
                pl.when(z > 0)(along(k, -1).wait_send)
            if k <= 0:
                pl.when(z < nz - 1)(along(k, 1).wait_send)
            for m in (1, 2):
                forward(k, m).wait_send()
                if relay(k, m) is not None:
                    relay(k, m).wait_send()

        for k in range(nz):
            both(k, one)

    return (
        [first]
        + [functools.partial(step, k) for k in range(1, nz)]
        + [functools.partial(pass_on, k) for k in range(nz)]
        + [functools.partial(diagonal, k) for k in range(nz)]
        + [last]
    )


def full_sems(nz):
    return [pltpu.SemaphoreType.DMA((10 * nz,)), pltpu.SemaphoreType.DMA((9 * nz,))]


def head_runs(nz, cols):
    return lambda p: [
        (block_of(x, p % 2, p // 2, 0, nz) * HD, x * cols // 2, cols // 2) for x in range(2)
    ]


def up_runs(nz, unit):
    return lambda p: [(block_of(x, p % 2, p // 2, 0, nz) * unit, x * 2 * unit, 2 * unit) for x in range(2)]


def qkv_runs(nz, width, cols):
    runs = head_runs(nz, cols)
    return lambda p: [(j * width + there, j * cols + here, size) for j in range(3) for there, here, size in runs(p)]


def fetch_kernel(
    nz, width, cols, x_in, w_qkv, w_down, vec, tab, x_all, qkv_w, down_w, vecs, tab_out, *sems
):
    pos = place()
    x, c, z, y = pos
    fsdp = 2 * nz
    devices = 4 * fsdp
    me = (x * 2 + c) * fsdp + z * 2 + y
    x_sems, qkv_sems, vec_sems, tab_sems, down_sems = sems[:2], sems[2:6], sems[6:8], sems[8:10], sems[10:]
    greet_all(devices, fsdp, me)

    def vec_copy(other):
        return remote(vec, vecs.at[me], vec_sems[0].at[other], vec_sems[1].at[me], (other // fsdp, other % fsdp))

    def each(fn):
        def body(k, _):
            fn((me + k) % devices)
            return 0

        lax.fori_loop(1, devices, body, 0)

    vec_local = pltpu.make_async_copy(vec, vecs.at[me], vec_sems[1].at[me])
    tab_local = pltpu.make_async_copy(tab, tab_out, tab_sems[1].at[0])
    tab_trade = remote(tab, tab_out, tab_sems[0].at[0], tab_sems[1].at[0], at(x, y, z, c))

    gx = line_gather(x_in, x_all, *x_sems, nz, True, pos)
    runs = qkv_runs(nz, width, cols) if len(w_qkv.shape) == 2 else None
    gq = sliced_gather(w_qkv, qkv_w, runs, qkv_sems, nz, pos)
    gx[0]()
    gq[0]()
    gx[1]()
    vec_local.start()
    each(lambda other: vec_copy(other).start())
    pl.when(c == y)(tab_local.start)
    pl.when(c != y)(tab_trade.start)
    gd = group_gather(w_down, down_w, *down_sems, pos)
    for stage in gq[1 : fsdp + 1]:
        stage()
    gx[2]()
    gd[0]()
    for stage in gx[3:-1]:
        stage()
    for stage in gq[fsdp + 1 :]:
        stage()
    gx[-1]()
    for stage in gd[1:]:
        stage()

    def vec_done(other):
        remote(vec, vecs.at[other], vec_sems[0].at[other], vec_sems[1].at[other], at(x, 1 - c, z, y)).wait_recv()
        vec_copy(other).wait_send()

    vec_local.wait()
    each(vec_done)
    tab_local.wait()
    pl.when(c != y)(tab_trade.wait_send)


def fetch(nz, x_in, w_qkv, w_down, part, vec, tab, cid):
    rows, width = x_in.shape
    n = 2 * nz
    devices = 4 * n
    cols = width // n
    shapes = [
        ((n, rows, width), BF),
        ((devices, part, 3 * cols), BF),
        ((4,) + w_down.shape, BF),
        ((devices,) + vec.shape, F32),
        (tab.shape, jnp.int32),
    ]
    return pl.pallas_call(
        functools.partial(fetch_kernel, nz, width, cols),
        out_shape=[jax.ShapeDtypeStruct(s, t) for s, t in shapes],
        in_specs=[HBM] * 5,
        out_specs=[HBM] * 5,
        scratch_shapes=gather_sems(nz)
        + sliced_sems(nz)
        + [pltpu.SemaphoreType.DMA((devices,))] * 2
        + [pltpu.SemaphoreType.DMA((1,))] * 2
        + [pltpu.SemaphoreType.DMA((5,))] * 2,
        compiler_params=params(cid),
        name="fetch",
    )(x_in, w_qkv, w_down, vec, tab)


def hand_stages(srcs, dsts, kinds, send, recv, nz, pos):
    x, c, z, y = pos
    n = 2 * nz
    count = len(kinds)

    def copies(i, m):
        gx, gy = x ^ (m // 2), y ^ (m % 2)
        sem = i * 3 + m - 1
        target = at(gx, c, z, gy)
        if not kinds[i]:
            return [remote(srcs[i].at[gx * 2 + gy], dsts[i].at[m - 1], send.at[sem], recv.at[sem], target)]
        return [
            remote(
                srcs[i].at[block_of(gx, p % 2, p // 2, gy, nz)],
                dsts[i].at[m - 1, p],
                send.at[sem],
                recv.at[sem],
                target,
            )
            for p in range(n)
        ]

    def first():
        for i in range(count):
            for m in (3, 1, 2):
                for copy in copies(i, m):
                    copy.start()

    def last():
        for i in range(count):
            for m in (1, 2, 3):
                sem = i * 3 + m - 1
                there = dsts[i].at[m - 1]
                whole = remote(there, there, send.at[sem], recv.at[sem], at(x, 1 - c, z, y))
                whole.wait_recv()
                whole.wait_send()

    return [first, last]


def hand_shapes(arrays, kinds, nz):
    return [
        jax.ShapeDtypeStruct((3, 2 * nz) + a.shape[1:] if k else (3,) + a.shape[1:], a.dtype)
        for a, k in zip(arrays, kinds)
    ]


def hand_sems(kinds):
    return [pltpu.SemaphoreType.DMA((3 * len(kinds),))] * 2


def exchange_stages(src, dst, runs, send, recv, nz, pos):
    x, c, z, y = pos
    n = 2 * nz
    me = z * 2 + c

    def give(to, p):
        if runs is None:
            return [(src.at[to], dst.at[p])]
        return [(src.at[to, :, pl.ds(here, size)], dst.at[:, pl.ds(there, size)]) for there, here, size in runs(p)]

    width = len(give(0, 0))

    def move(p):
        return [
            remote(a, b, send.at[p * width + i], recv.at[me * width + i], at(x, p % 2, p // 2, y))
            for i, (a, b) in enumerate(give(p, me))
        ]

    def come(p):
        return [
            remote(b, b, send.at[me * width + i], recv.at[p * width + i], at(x, 1 - c, z, y))
            for i, (_, b) in enumerate(give(me, p))
        ]

    local = [pltpu.make_async_copy(a, b, recv.at[me * width + i]) for i, (a, b) in enumerate(give(me, me))]

    def first():
        for copy in local:
            copy.start()
        for k in range(1, n):
            for copy in move((me + k) % n):
                copy.start()

    def last():
        for copy in local:
            copy.wait()
        for k in range(1, n):
            for copy in come((me - k + n) % n):
                copy.wait_recv()
            for copy in move((me + k) % n):
                copy.wait_send()

    return [first, last]


def exchange_sems(runs, nz):
    width = 1 if runs is None else len(runs(0))
    return [pltpu.SemaphoreType.DMA((width * 2 * nz,))] * 2


def exchange_kernel(nz, src, dst, send, recv):
    pos = place()
    greet(rank_partners(nz, pos))
    for stage in exchange_stages(src, dst, None, send, recv, nz, pos):
        stage()


def exchange(a, nz, cid, name):
    return pl.pallas_call(
        functools.partial(exchange_kernel, nz),
        out_shape=jax.ShapeDtypeStruct(a.shape, a.dtype),
        in_specs=[HBM],
        out_specs=HBM,
        scratch_shapes=exchange_sems(None, nz),
        compiler_params=params(cid),
        name=name,
    )(a)


def trade_stages(src, dst, send, recv, pos):
    x, c, z, y = pos
    local = pltpu.make_async_copy(src, dst, recv.at[0])
    trade = remote(src, dst, send.at[0], recv.at[0], at(x, y, z, c))

    def first():
        pl.when(c == y)(local.start)
        pl.when(c != y)(trade.start)

    def last():
        local.wait()
        pl.when(c != y)(trade.wait_send)

    return [first, last]


def trade_sems():
    return [pltpu.SemaphoreType.DMA((1,))] * 2


def finish_kernel(nz, runs, has, *refs):
    grad, small, *refs = refs
    qkv_s = refs.pop(0) if has else None
    grad_out, small_out, *refs = refs
    qkv_o = refs.pop(0) if has else None
    came, send, recv, *sems = refs
    pos = place()
    x, c, z, y = pos
    fsdp = 2 * nz
    devices = 4 * fsdp
    me = (x * 2 + c) * fsdp + z * 2 + y
    es = exchange_stages(qkv_s, qkv_o, runs, *sems[2:], nz, pos) if has else [lambda: None] * 2
    ts = trade_stages(grad, grad_out, *sems[:2], pos)
    greet_all(devices, fsdp, me)

    def each(fn):
        def body(k, _):
            fn((me + k) % devices)
            return 0

        lax.fori_loop(1, devices, body, 0)

    def share(other):
        return remote(small.at[other], came.at[me], send.at[other], recv.at[me], (other // fsdp, other % fsdp))

    es[0]()
    ts[0]()
    each(lambda other: share(other).start())

    def done(other):
        remote(small.at[me], came.at[other], send.at[other], recv.at[other], at(x, 1 - c, z, y)).wait_recv()
        share(other).wait_send()

    each(done)
    came[me] = small[me]
    small_out[...] = jnp.sum(came[...], axis=0)
    ts[1]()
    es[1]()


def finish(grad, small, qkv_s, runs, nz, cid):
    devices = small.shape[0]
    has = qkv_s is not None
    shapes = [jax.ShapeDtypeStruct(grad.shape, grad.dtype), jax.ShapeDtypeStruct(small.shape[1:], F32)]
    if has:
        out_shape = qkv_s.shape if runs is None else (qkv_s.shape[1], qkv_s.shape[0] * qkv_s.shape[2])
        shapes.append(jax.ShapeDtypeStruct(out_shape, BF))
    return pl.pallas_call(
        functools.partial(finish_kernel, nz, runs, has),
        out_shape=shapes,
        in_specs=[HBM, VM] + [HBM] * has,
        out_specs=[HBM, VM] + [HBM] * has,
        scratch_shapes=[pltpu.VMEM(small.shape, F32)]
        + [pltpu.SemaphoreType.DMA((devices,))] * 2
        + trade_sems()
        + (exchange_sems(runs, nz) if has else []),
        compiler_params=params(cid, 32 * MIB),
        name="finish",
    )(*((grad, small, qkv_s) if has else (grad, small)))


def dot(a, b, dims):
    return lax.dot_general(a, b, (dims, ((), ())), preferred_element_type=F32)


NN = ((1,), (0,))
NT = ((1,), (1,))
TN = ((0,), (0,))


def head_number(h, heads, nz, pos):
    x, c, z, y = pos
    return block_of(h // (heads // 2), c, z, h % (heads // 2), nz)


def head_kernel(heads, nz, runs_qkv, runs_up, runs_out, *refs):
    refs = list(refs)

    def take(n):
        got = refs[:n]
        del refs[:n]
        return got

    slopes, valid_in, blocks_in, parents_in = take(4)
    vectors, bias_up = take(8), take(1)[0]
    x_in, cot, w_qkv, w_up, w_out, w_down = take(6)
    joined, mixed, mixed_own, x_own, rows_o, up_bias = take(6)
    a1_o, far_o, cot_all, qkv_o, up_w, out_w, down_w = take(7)
    pack, vecs, tab, tab_in, table, columns, member_s, reach_s, far_s, x_all, a1, qkv_w, bias_s = take(13)
    x_sems, cot_sems, qkv_sems, up_sems, out_sems, down_sems = take(2), take(2), take(4), take(4), take(2), take(2)
    vec_sems, tab_sems, mix_sems, (local_sem, far_sem) = take(2), take(2), take(2), take(2)

    pos = place()
    x, c, z, y = pos
    n = 2 * nz
    devices = 4 * n
    me = block_of(x, c, z, y, nz)
    rank = z * 2 + c
    tree, cols = joined.shape[0], joined.shape[1] // 3
    rows, width = x_own.shape
    part = w_out.shape[0]

    gx = line_gather(x_in, x_all, *x_sems, nz, True, pos)
    gc = line_gather(cot, cot_all, *cot_sems, nz, True, pos)
    gq = sliced_gather(w_qkv, qkv_w, runs_qkv, qkv_sems, nz, pos)
    gu = sliced_gather(w_up, up_w, runs_up, up_sems, nz, pos)
    go = full_gather(w_out, out_w, *out_sems, nz, pos)
    gd = group_gather(w_down, down_w, *down_sems, pos)
    ex = exchange_stages(mixed, mixed_own, runs_out, *mix_sems, nz, pos)
    ts = trade_stages(tab, tab_in, *tab_sems, pos)
    store_a = pltpu.make_async_copy(a1, a1_o, local_sem.at[0])
    store_q = pltpu.make_async_copy(qkv_w, qkv_o, local_sem.at[1])

    def each(fn):
        def body(k, _):
            fn((me + k) % devices)
            return 0

        lax.fori_loop(1, devices, body, 0)

    def vec_copy(other):
        return remote(pack, vecs.at[me], vec_sems[0].at[other], vec_sems[1].at[me], (other // n, other % n))

    def vec_come(other):
        remote(vecs.at[other], vecs.at[other], vec_sems[0].at[me], vec_sems[1].at[other], at(x, 1 - c, z, y)).wait_recv()

    pack[...] = jnp.zeros_like(pack)
    for i, v in enumerate(vectors):
        pack[i : i + 1, 0:part] = v[...].astype(F32).reshape(1, part)
    lined = pack[...]
    pack[...] = jnp.where(y == 1, pltpu.roll(lined, part, 1), lined)
    for i in range(bias_up.shape[0] // 128):
        pack[8 + i : 9 + i, :] = bias_up[i * 128 : (i + 1) * 128].astype(F32).reshape(1, 128)
    tab[...] = jnp.full_like(tab, -1)
    tab[0:1, :] = valid_in[...]
    tab[1:2, 0 : blocks_in.shape[1]] = blocks_in[...]
    tab[2:3, 0 : parents_in.shape[1]] = parents_in[...]

    greet_all(devices, n, me)
    gx[0]()
    gq[0]()
    ts[0]()
    go[0]()
    gd[0]()
    each(lambda other: vec_copy(other).start())
    vecs[me] = pack[...]
    gx[1]()

    ts[1]()
    seg = lax.broadcasted_iota(jnp.int32, (128, 128), 0)
    lane = lax.broadcasted_iota(jnp.int32, (128, 128), 1)

    def low(v):
        return v.astype(F32).astype(BF)

    parent = low(seg == tab_in[2:3, 0:128])
    above = (parent.astype(F32) + dot(parent, parent, NN)) > 0.5
    ancestor = low(above & (seg != lane))
    owner = low(seg == tab_in[1:2, 0:128])
    spread = low(
        lax.shift_right_logical(lax.broadcasted_iota(jnp.int32, (128, tree), 1), BLK.bit_length() - 1)
        == lax.broadcasted_iota(jnp.int32, (128, tree), 0)
    )
    member = dot(owner, spread, NN)
    valid = tab_in[0:1, :].astype(F32)
    counted = member * valid
    member_s[...] = member.astype(BF)
    reach_s[...] = (2.0 * dot(ancestor, member_s[...], NN) + member).astype(BF)
    lens = jnp.broadcast_to(jnp.sum(counted, axis=1, keepdims=True), (128, 128))
    offset = lax.dot_general(
        ancestor.astype(F32), lens, (TN, ((), ())), precision=lax.Precision.HIGHEST, preferred_element_type=F32
    )
    table[...] = jnp.zeros_like(table)
    table[1:2, :] = valid
    for j in range(tree // 256):
        here = slice(j * 256, (j + 1) * 256)
        earlier = low(
            lax.broadcasted_iota(jnp.int32, (tree, 256), 0) < lax.broadcasted_iota(jnp.int32, (tree, 256), 1) + j * 256
        )
        before = dot(counted.astype(BF), earlier, NN) + offset[:, 0:1]
        table[0:1, here] = jnp.sum(before * member[:, here], axis=0, keepdims=True)
    columns[...] = table[...].T

    step = far_s.shape[2]
    steps = tree // step
    far_store = [
        pltpu.make_async_copy(far_s.at[i % 2], far_o.at[:, pl.ds(i * step, step)], far_sem.at[i % 2]) for i in range(steps)
    ]

    def allow(value, key, query, key_valid):
        return ((value > 1.5) | ((value > 0.5) & (key <= query))) & ((key_valid > 0.5) | (key == query))

    def far_blocks():
        for i in range(steps):
            here = slice(i * step, (i + 1) * step)
            key = lax.broadcasted_iota(jnp.int32, (tree, step), 0)
            query = lax.broadcasted_iota(jnp.int32, (tree, step), 1) + i * step
            allowed = allow(dot(member_s[...], reach_s[:, here], TN), key, query, columns[:, 1:2])
            if i >= 2:
                far_store[i - 2].wait()
            far_s[i % 2] = jnp.where(allowed, columns[:, 0:1], MASKED)
            far_store[i].start()

    def whole_vectors():
        each(vec_come)
        for i in range(devices // 2):
            rows_o[:, i * 128 : (i + 1) * 128] = vecs[2 * i, 0:8] + vecs[2 * i + 1, 0:8]
        per = bias_up.shape[0] // 128
        for g in range(4):
            r = block_of(g // 2, c, z, g % 2, nz)
            for i in range(per):
                up_bias[:, (g * per + i) * 128 : (g * per + i + 1) * 128] = vecs[r, 8 + i : 9 + i]
        bias_s[...] = jnp.zeros_like(bias_s)
        for there, here, size in runs_out(rank):
            there = pl.multiple_of(there, 128)
            bias_s[:, here : here + size] = rows_o[2:3, pl.ds(there, size)]
            bias_s[:, 2 * cols + here : 2 * cols + here + size] = rows_o[3:4, pl.ds(there, size)]

    def norm(b):
        def tile(j, _):
            here = pl.ds(pl.multiple_of(j * 32, 32), 32)
            normed, _ = norm_parts(x_all[b, here].astype(F32))
            a1[b, here] = (normed * rows_o[0:1, :] + rows_o[1:2, :]).astype(BF)
            return 0

        lax.fori_loop(0, rows // 32, tile, 0)

    def norm_at(k, core):
        pl.when(z >= k)(lambda: norm((z - k) * 2 + core))
        if k:
            pl.when(z + k < nz)(lambda: norm((z + k) * 2 + core))

    for stage in gq[1 : n + 1]:
        stage()
    gx[2]()
    go[1]()
    gd[1]()
    far_blocks()
    whole_vectors()
    norm_at(0, c)
    norm_at(1, c)
    gx[3]()
    gu[0]()
    gc[0]()
    norm_at(2, c)
    go[2]()
    for stage in gq[n + 1 : 2 * n + 1]:
        stage()
    gx[4]()
    gc[1]()
    norm_at(3, c)
    go[3]()
    gx[-1]()
    x_own[...] = x_all[rank]
    for k in range(nz):
        norm_at(k, 1 - c)
    store_a.start()
    gq[-1]()
    store_q.start()
    for stage in gu[1 : n + 1]:
        stage()

    def project(i, _):
        here = pl.ds(pl.multiple_of(i * 2 * rows, 2 * rows), 2 * rows)
        tokens = a1[pl.ds(2 * i, 2)].reshape(2 * rows, width)

        def tile(j, _):
            u = pl.ds(pl.multiple_of(j * 256, 256), 256)
            value = dot(tokens, qkv_w[:, :, u].reshape(width, 256), NN) + bias_s[:, u]
            joined[here, u] = value.astype(BF)
            return 0

        lax.fori_loop(0, 3 * cols // 256, tile, 0)
        return 0

    lax.fori_loop(0, nz, project, 0)
    slope = [slopes[head_number(h, heads, nz, pos)] for h in range(heads)]

    gc[2]()
    def attend_step(i, _):
        here = pl.ds(pl.multiple_of(i * step, step), step)
        per = step // rows
        key = lax.broadcasted_iota(jnp.int32, (step, tree), 1)
        query = lax.broadcasted_iota(jnp.int32, (step, tree), 0) + i * step
        allowed = allow(dot(reach_s[:, here], member_s[...], TN), key, query, table[1:2, :])
        gap = jnp.where(allowed, table[0:1, :], MASKED)
        for h in range(heads):
            lanes = slice(h * HD, (h + 1) * HD)
            q = joined[here, lanes] * BF(HD ** (-0.5))
            k = joined[:, cols + h * HD : cols + (h + 1) * HD]
            v = joined[:, 2 * cols + h * HD : 2 * cols + (h + 1) * HD]
            logits = dot(q, k, NT) + slope[h] * gap
            weights = jnp.exp(logits - jnp.max(logits, axis=1, keepdims=True))
            probs = weights * (1.0 / jnp.sum(weights, axis=1, keepdims=True))
            mixed[pl.ds(i * per, per), :, lanes] = dot(probs.astype(BF), v, NN).astype(BF).reshape(per, rows, HD)

        def later(k, fns):
            @pl.when(i == k)
            def _():
                for fn in fns:
                    fn()

        later(0, go[nz : 2 * nz])
        later(1, gc[3:4] + gu[n + 1 : n + 1 + n // 2])
        later(2, gc[4:5] + gu[n + 1 + n // 2 : 2 * n + 1])
        return 0

    lax.fori_loop(0, steps, attend_step, 0)
    ex[0]()
    for stage in go[2 * nz : 3 * nz]:
        stage()
    ex[1]()
    for stage in (go[-1], gc[-1], gu[-1], gd[-1]):
        stage()
    each(lambda other: vec_copy(other).wait_send())
    for i in range(max(0, steps - 2), steps):
        far_store[i].wait()
    store_a.wait()
    store_q.wait()


def head_call(slopes, tables, vectors, bias_up, layer_in, cot, w_qkv, w_up, w_out, w_down, heads, nz, cid):
    rows, width = layer_in.shape
    n = 2 * nz
    devices = 4 * n
    tree = n * rows
    cols = heads * HD
    part, unit = w_out.shape[0], w_down.shape[0]
    step = 256
    runs_qkv, runs_up, runs_out = qkv_runs(nz, width, cols), up_runs(nz, unit), head_runs(nz, cols)
    shape = jax.ShapeDtypeStruct
    return pl.pallas_call(
        functools.partial(head_kernel, heads, nz, runs_qkv, runs_up, runs_out),
        out_shape=[
            shape((tree, 3 * cols), BF),
            shape((n, rows, cols), BF),
            shape((rows, width), BF),
            shape((rows, width), BF),
            shape((8, width), F32),
            shape((1, 4 * unit), F32),
            shape((n, rows, width), BF),
            shape((tree, tree), F32),
            shape((n, rows, width), BF),
            shape((devices, part, 3 * cols), BF),
            shape((devices, part, 4 * unit), BF),
            shape((devices, part, width), BF),
            shape((4, unit, width), BF),
        ],
        in_specs=[pl.BlockSpec(memory_space=pltpu.SMEM)] + [VM] * 12 + [HBM] * 6,
        out_specs=[VM] * 6 + [HBM] * 7,
        scratch_shapes=[
            pltpu.VMEM((16, 128), F32),
            pltpu.VMEM((devices, 16, 128), F32),
            pltpu.VMEM((8, tree), jnp.int32),
            pltpu.VMEM((8, tree), jnp.int32),
            pltpu.VMEM((128, tree), F32),
            pltpu.VMEM((tree, 128), F32),
            pltpu.VMEM((128, tree), BF),
            pltpu.VMEM((128, tree), BF),
            pltpu.VMEM((2, tree, step), F32),
            pltpu.VMEM((n, rows, width), BF),
            pltpu.VMEM((n, rows, width), BF),
            pltpu.VMEM((devices, part, 3 * cols), BF),
            pltpu.VMEM((1, 3 * cols), F32),
        ]
        + gather_sems(nz) * 2
        + sliced_sems(nz) * 2
        + full_sems(nz)
        + [pltpu.SemaphoreType.DMA((5,))] * 2
        + [pltpu.SemaphoreType.DMA((devices,))] * 2
        + trade_sems()
        + exchange_sems(runs_out, nz)
        + [pltpu.SemaphoreType.DMA((2,))] * 2,
        compiler_params=params(cid, 60 * MIB),
        name="head",
    )(slopes, *tables, *vectors, bias_up, layer_in, cot, w_qkv, w_up, w_out, w_down)


def scatter_parts(nz, pos, own, other, acc, came, send, recv):
    x, c, z, y = pos
    S, U, D = 0, nz, 3 * nz
    sib = at(x, 1 - c, z, y)
    half = acc.shape[1] // 2

    def f(v):
        return v.astype(F32)

    def swap(t):
        return remote(other(t), acc.at[t], send.at[S + t], recv.at[S + t], sib)

    def piece(ref, t, h):
        return ref.at[t, pl.ds(h * half, half)]

    def rise(t, h):
        sem = U + t * 2 + h
        return remote(piece(acc, t, h), piece(came, t, h), send.at[sem], recv.at[sem], at(x, c, z + 1, y))

    def fall(t, h):
        slot = jnp.where(z - 1 == t, nz, t)
        sem = D + t * 2 + h
        return remote(piece(acc, t, h), piece(came, slot, h), send.at[sem], recv.at[sem], at(x, c, z - 1, y))

    def arrival(slot, h, sem):
        there = piece(came, slot, h)
        return remote(there, there, send.at[S], recv.at[sem], sib)

    def event(t, upward):
        swap(t).wait_recv()
        acc[t] = (f(acc[t]) + f(own(t))).astype(BF)
        for h in range(2):

            @pl.when(z > 0 if upward else z < nz - 1)
            def _():
                arrival(t, h, (U if upward else D) + t * 2 + h).wait_recv()
                here = slice(h * half, (h + 1) * half)
                acc[t, here] = (f(acc[t, here]) + f(came[t, here])).astype(BF)

            (rise if upward else fall)(t, h).start()

    def slot(k):
        for t in range(nz):
            zz = k - t
            if 0 <= zz < t:
                pl.when(z == zz)(functools.partial(event, t, True))
            zz = 2 * (nz - 1) - k - t
            if t < zz < nz:
                pl.when(z == zz)(functools.partial(event, t, False))

    def begin(i):
        pl.when(z == 0)(functools.partial(event, nz - 1 - i, True))
        pl.when(z == nz - 1)(functools.partial(event, i, False))

    def near(i):
        t = nz - 1 - i
        pl.when((z > 0) & (z < nz // 2) & (z < t))(functools.partial(event, t, True))
        pl.when((z >= nz // 2) & (z < nz - 1) & (z > i))(functools.partial(event, i, False))

    def far():
        for i in range(nz - 1):
            t = nz - 1 - i
            pl.when((z >= nz // 2) & (z < t))(functools.partial(event, t, True))
            pl.when((z < nz // 2) & (z > i))(functools.partial(event, i, False))

    def total(out):
        swap(z).wait_recv()
        out[...] = f(acc[z]) + f(own(z))
        for upward, slot, base in ((True, z, U), (False, nz, D)):

            @pl.when(z > 0 if upward else z < nz - 1)
            def _():
                for h in range(2):
                    here = slice(h * half, (h + 1) * half)
                    arrival(slot, h, base + z * 2 + h).wait_recv()
                    out[here, :] += f(came[slot, here])

    def done():
        for t in range(nz):
            swap(t).wait_send()
            for h in range(2):
                pl.when(z < t)(lambda: rise(t, h).wait_send())
                pl.when(z > t)(lambda: fall(t, h).wait_send())

    return swap, slot, begin, near, far, total, done


def reduce_parts(src, mine, near, far, send, recv, lsem, pos):
    x, c, z, y = pos
    half = src.shape[1] // 2

    def f(v):
        return v.astype(F32)

    def share(gx, gy, lower):
        return src.at[gx * 2 + gy, pl.ds(lower * half, half)]

    parts = [(x, y, 0), (x, y, 1), (x, 1 - y, 0), (1 - x, y, 1)]
    loads = [pltpu.make_async_copy(share(*p), mine.at[i], lsem.at[i]) for i, p in enumerate(parts)]
    along_x, along_y = at(1 - x, c, z, y), at(x, c, z, 1 - y)

    def out(i):
        a, b, target = [
            (share(1 - x, y, 0), near.at[0, 0], along_x),
            (share(1 - x, 1 - y, 0), near.at[0, 1], along_x),
            (share(x, 1 - y, 1), near.at[1, 0], along_y),
            (share(1 - x, 1 - y, 1), near.at[1, 1], along_y),
        ][i]
        return remote(a, b, send.at[i], recv.at[i], target)

    def on(i):
        return remote(near.at[i, 1], far.at[i], send.at[4 + i], recv.at[4 + i], [along_y, along_x][i])

    def first():
        for i in (1, 3, 0, 2):
            out(i).start()
        for copy in loads:
            copy.start()

    def second():
        for copy in loads:
            copy.wait()
        for i in range(2):
            out(2 * i + 1).wait_recv()
            near[i, 1] = (f(near[i, 1]) + f(mine[2 + i])).astype(BF)
            on(i).start()

    def total(put):
        for i in range(2):
            out(2 * i).wait_recv()
            on(i).wait_recv()
            put(i, f(mine[i]) + f(near[i, 0]) + f(far[i]))

    def done():
        for i in range(4):
            out(i).wait_send()
        for i in range(2):
            on(i).wait_send()

    return first, second, total, done


def reduce_scratch(rows, width):
    half = rows // 2
    return [
        pltpu.VMEM((4, half, width), BF),
        pltpu.VMEM((2, 2, half, width), BF),
        pltpu.VMEM((2, half, width), BF),
        pltpu.SemaphoreType.DMA((6,)),
        pltpu.SemaphoreType.DMA((6,)),
        pltpu.SemaphoreType.DMA((4,)),
    ]


def tail_kernel(
    heads, nz, runs_up, runs_qkv, slopes, far_in, grad_in, joined, a1_in, mixed_in, qkv_in, branch, upd_in, up_src, down_src,
    middle_in, x_in, whole, grad_in_middle, sums, bias_g,
    down_o, out_o, small_o, bias_o, up_o, qkv_o, branch_all, layer_o, grad_o, grad_s, *refs,
):
    refs = list(refs)

    def take(n):
        got = refs[:n]
        del refs[:n]
        return got

    gap_s, tokens, qkv_w, grad_joined, acc_k, acc_v = take(6)
    upd_own, upd_acc, upd_came, upd_send, upd_recv = take(5)
    att_p, att_acc, att_came, att_send, att_recv = take(5)
    up_refs, down_refs, qkv_refs, out_refs = take(6), take(6), take(6), take(6)
    up_sum, qkv_sum, qkv_g, out_g, res, res_low = take(6)
    grad_low, vec, came, bias_t, bias_c, mixed, middle, x_own, grad_middle = take(9)
    gsems, esems, esems_up, esems_qkv, tsems, tsems_x = take(2), take(2), take(2), take(2), take(2), take(2)
    vsems, bsems = take(2), take(2)
    gap_sem, load_sem = take(2)

    pos = place()
    x, c, z, y = pos
    n = 2 * nz
    tree, cols = mixed_in.shape
    rows, width = branch.shape
    part = up_sum.shape[1]
    rank = z * 2 + c
    step = gap_s.shape[2]

    es = exchange_stages(grad_in, grad_s, None, *esems, nz, pos)
    gb = line_gather(branch, branch_all, *gsems, nz, False, pos)
    up1, up2, up_total, up_done = reduce_parts(up_src, *up_refs, pos)
    down1, down2, down_total, down_done = reduce_parts(down_src, *down_refs, pos)
    qkv1, qkv2, qkv_total, qkv_done = reduce_parts(qkv_g, *qkv_refs, pos)
    out1, out2, out_total, out_done = reduce_parts(out_g, *out_refs, pos)
    upd_swap, _, upd_begin, upd_near, upd_far, upd_total, upd_done = scatter_parts(
        nz, pos, lambda t: upd_own[t], lambda t: upd_in.at[t * 2 + 1 - c], upd_acc, upd_came, upd_send, upd_recv
    )
    att_swap, _, att_begin, att_near, att_far, att_total, att_done = scatter_parts(
        nz, pos, lambda t: att_p[t * 2 + c], lambda t: att_p.at[t * 2 + 1 - c], att_acc, att_came, att_send, att_recv
    )
    ex_up = exchange_stages(up_sum, up_o, runs_up, *esems_up, nz, pos)
    ex_qkv = exchange_stages(qkv_sum, qkv_o, runs_qkv, *esems_qkv, nz, pos)
    home = trade_stages(res_low, layer_o, *tsems, pos)
    home_x = trade_stages(grad_low, grad_o, *tsems_x, pos)
    devices = 4 * n
    me = block_of(x, c, z, y, nz)
    group = x * 2 + y

    def each(fn):
        def body(k, _):
            fn((me + k) % devices)
            return 0

        lax.fori_loop(1, devices, body, 0)

    def share(other):
        tile = vec.at[:, pl.ds(pl.multiple_of(other // 2 * 128, 128), 128)]
        return remote(tile, came.at[me], vsems[0].at[other], vsems[1].at[me], (other // n, other % n))

    def share_come(other):
        there = came.at[other]
        remote(there, there, vsems[0].at[me], vsems[1].at[other], at(x, 1 - c, z, y)).wait_recv()

    def bias_share(m):
        target = at(x ^ (m // 2), c, z, y ^ (m % 2))
        return remote(bias_t.at[group ^ m], bias_c.at[m - 1], bsems[0].at[m - 1], bsems[1].at[m - 1], target)
    loads = [pltpu.make_async_copy(upd_in.at[t * 2 + c], upd_own.at[t], load_sem.at[t]) for t in range(nz)]
    load_w = pltpu.make_async_copy(qkv_in, qkv_w, load_sem.at[nz])
    load_a = pltpu.make_async_copy(a1_in, tokens, load_sem.at[nz + 1])
    load_b = pltpu.make_async_copy(branch_all, tokens, load_sem.at[nz + 2])

    def gap_load(i, slot):
        return pltpu.make_async_copy(
            far_in.at[:, pl.ds(pl.multiple_of(i * step, step), step)], gap_s.at[slot], gap_sem.at[slot]
        )

    greet_all(devices, n, me)
    es[0]()
    up1()
    for t in range(nz):
        upd_swap(t).start()
    gap_load(0, 0).start()
    lates = [
        pltpu.make_async_copy(a, b, load_sem.at[nz + 3 + i])
        for i, (a, b) in enumerate([(mixed_in, mixed), (middle_in, middle), (x_in, x_own), (grad_in_middle, grad_middle)])
    ]
    for copy in loads + [load_w, load_a] + lates:
        copy.start()
    acc_k[...] = jnp.zeros_like(acc_k)
    acc_v[...] = jnp.zeros_like(acc_v)
    for copy in loads:
        copy.wait()
    es[1]()
    gb[0]()
    gb[1]()
    for i in range(nz - 1):
        upd_begin(i)

    steps = tree // step
    slope = [slopes[head_number(h, heads, nz, pos)] for h in range(heads)]

    def attend_step(i, _):
        slot = i % 2
        gap_load(i, slot).wait()
        pl.when(i + 1 < steps)(lambda: gap_load(i + 1, 1 - slot).start())
        gap = gap_s[slot]
        here = pl.ds(pl.multiple_of(i * step, step), step)
        per = step // rows
        grads = grad_s[pl.ds(i * per, per)].reshape(step, cols)
        for h in range(heads):
            lane = slice(h * HD, (h + 1) * HD)
            q = joined[here, lane]
            scale = BF(HD ** (-0.5))
            k = joined[:, cols + h * HD : cols + (h + 1) * HD]
            v = joined[:, 2 * cols + h * HD : 2 * cols + (h + 1) * HD]
            g = grads[:, lane]
            logits = dot(k, q * scale, NT) + slope[h] * gap
            weights = jnp.exp(logits - jnp.max(logits, axis=0, keepdims=True))
            probs = weights * (1.0 / jnp.sum(weights, axis=0, keepdims=True))
            grad_probs = dot(v, g * scale, NT)
            delta = jnp.sum(probs * grad_probs, axis=0, keepdims=True)
            grad_raw = (probs * (grad_probs - delta)).astype(BF)
            acc_v[:, lane] += dot(probs.astype(BF), g, NN)
            acc_k[:, lane] += dot(grad_raw, q, NN)
            grad_joined[here, lane] = dot(grad_raw, k, TN).astype(BF)

        def later(k, fns):
            @pl.when(i == k)
            def _():
                for fn in fns:
                    fn()

        later(1, [gb[2]])
        later(2, [up2])
        later(3, [down1, lambda: upd_near(0)])
        return 0

    lax.fori_loop(0, steps, attend_step, 0)
    grad_joined[:, cols : 2 * cols] = acc_k[...].astype(BF)
    grad_joined[:, 2 * cols :] = acc_v[...].astype(BF)
    load_w.wait()

    def put_ranks(dest):
        def put(lower, value):
            dest[pl.ds(lower * nz, nz)] = value.astype(BF).reshape(nz, part, -1)

        return put

    def back(t):
        here = pl.ds(pl.multiple_of(t * 2 * rows, 2 * rows), 2 * rows)

        def tile(j, _):
            w = pl.ds(pl.multiple_of(j * 512, 512), 512)
            att_p[pl.ds(t * 2, 2), :, w] = dot(grad_joined[here, :], qkv_w[w, :], NT).astype(BF).reshape(2, rows, 512)
            return 0

        lax.fori_loop(0, width // 512, tile, 0)
        att_swap(t).start()

    for i in range(nz):
        back(jnp.where(z < nz // 2, nz - 1 - i, i))
        if i:
            att_begin(i - 1)
    load_a.wait()
    blocks = 256 // part

    def qkv_tile(j, _):
        w = pl.ds(pl.multiple_of(j * 256, 256), 256)
        value = dot(tokens[:, :, w].reshape(tree, 256), grad_joined[...], TN).astype(BF)
        for i in range(blocks):
            r = j * blocks + i
            d, f = r // n, r % n
            p = f // 2 * 2 + d % 2
            qkv_g[d // 2 * 2 + f % 2, pl.ds(pl.multiple_of(p * part, part), part), :] = value[i * part : (i + 1) * part]
        return 0

    col = jnp.sum(grad_joined[...].astype(F32), axis=0, keepdims=True)
    vec[...] = jnp.zeros_like(vec)
    for there, here, size in head_runs(nz, cols)(rank):
        there = pl.multiple_of(there, 128)
        vec[2:3, pl.ds(there, size)] = col[:, here : here + size]
        vec[3:4, pl.ds(there, size)] = col[:, 2 * cols + here : 2 * cols + here + size]
    for i, k in enumerate((2, 0, 1, 3)):
        vec[4 + i : 5 + i, :] = sums[k : k + 1, :]
    vec[9:10, :] = jnp.broadcast_to(jnp.sum(sums[4:5, :], axis=1, keepdims=True), (1, width))
    bias_t[...] = jnp.zeros_like(bias_t)
    per = bias_g.shape[1] // 512
    for g in range(4):
        for i in range(per):
            bias_t[g, i : i + 1, :] = bias_g[:, (g * per + i) * 128 : (g * per + i + 1) * 128]
    for m in (1, 2, 3):
        bias_share(m).start()
    gb[3]()
    lax.fori_loop(0, width // 256, qkv_tile, 0)
    qkv1()
    upd_near(1)
    gb[4]()
    up_total(put_ranks(up_sum))
    ex_up[0]()
    upd_far()
    att_near(0)
    att_near(1)
    qkv2()
    att_far()
    down2()
    for stage in gb[5:]:
        stage()
    load_b.start()
    load_b.wait()
    for copy in lates:
        copy.wait()

    def out_tile(j, _):
        w = pl.ds(pl.multiple_of(j * 512, 512), 512)
        value = dot(mixed[...], tokens[:, :, w].reshape(tree, 512), TN).astype(BF)
        out_g[:, :, w] = value.reshape(4, cols // 4, 512)
        return 0

    lax.fori_loop(0, width // 512, out_tile, 0)
    out1()
    qkv_total(put_ranks(qkv_sum))
    ex_qkv[0]()
    att_total(res)

    def norm(j, _):
        here = pl.ds(pl.multiple_of(j * 32, 32), 32)
        normed, inverse = norm_parts(x_own[here, :].astype(F32))
        value = res[here, :]
        through = grad_middle[here, :] + norm_back(value * whole[0:1, :], normed, inverse)
        grad_low[here, :] = through.astype(BF)
        vec[0:1, :] += jnp.sum(value * normed, axis=0, keepdims=True)
        vec[1:2, :] += jnp.sum(value, axis=0, keepdims=True)
        return 0

    lax.fori_loop(0, rows // 32, norm, 0)
    home_x[0]()
    upd_total(res)
    res[...] += middle[...] + whole[7:8, :]
    res_low[...] = res[...].astype(BF)
    home[0]()
    square = jnp.sum(jnp.sum(res[...] * res[...], axis=0, keepdims=True), axis=1, keepdims=True)
    vec[8:9, :] = jnp.broadcast_to(square, (1, width))
    each(lambda other: share(other).start())
    out2()

    def put_down(lower, value):
        half = value.shape[0]
        down_o[pl.ds(lower * half, half), :] = value

    down_total(put_down)
    def put_out(lower, value):
        half = value.shape[0]
        out_o[pl.ds(lower * half, half), :] = value

    out_total(put_out)
    each(share_come)
    came[me] = vec[:, pl.ds(pl.multiple_of(me // 2 * 128, 128), 128)]
    summed = jnp.sum(came[...], axis=0)
    small_o[...] = jnp.where(y == 1, pltpu.roll(summed, 64, 1), summed)
    for m in (1, 2, 3):
        bias_share(m).wait_recv()
    bias_o[...] = bias_t[group] + jnp.sum(bias_c[...], axis=0)
    ex_up[1]()
    home[1]()
    home_x[1]()
    ex_qkv[1]()
    each(lambda other: share(other).wait_send())
    for m in (1, 2, 3):
        bias_share(m).wait_send()
    for fn in (up_done, down_done, qkv_done, out_done, upd_done, att_done):
        fn()


def tail_call(
    slopes, far_t, grad, joined, a1, mixed, qkv_w, branch, upd, up_g, down_g, middle, x_own, whole, grad_middle, sums, bias_g,
    runs, heads, nz, cid,
):
    tree, cols = mixed.shape
    rows, width = branch.shape
    n = 2 * nz
    part = width // (4 * n)
    unit = down_g.shape[1]
    step = 256
    runs_up, runs_qkv = runs
    shape = jax.ShapeDtypeStruct

    def scatter_refs(own):
        return [
            pltpu.VMEM((own, rows, width), BF),
            pltpu.VMEM((nz, rows, width), BF),
            pltpu.VMEM((nz + 1, rows, width), BF),
            pltpu.SemaphoreType.DMA((5 * nz,)),
            pltpu.SemaphoreType.DMA((5 * nz,)),
        ]

    return pl.pallas_call(
        functools.partial(tail_kernel, heads, nz, runs_up, runs_qkv),
        out_shape=[
            shape((unit, width), F32),
            shape((part, width), F32),
            shape((16, 128), F32),
            shape((8, 128), F32),
            shape((part, 4 * n * unit), BF),
            shape((part, 3 * width), BF),
            shape((n, rows, width), BF),
            shape((rows, width), BF),
            shape((rows, width), BF),
        ],
        in_specs=[pl.BlockSpec(memory_space=pltpu.SMEM), HBM, HBM, VM] + [HBM] * 9 + [VM, HBM, VM, VM],
        out_specs=[VM] * 4 + [HBM] * 5,
        scratch_shapes=[
            pltpu.VMEM((n, rows, cols), BF),
            pltpu.VMEM((2, tree, step), F32),
            pltpu.VMEM((n, rows, width), BF),
            pltpu.VMEM((width, 3 * cols), BF),
            pltpu.VMEM((tree, 3 * cols), BF),
            pltpu.VMEM((tree, cols), F32),
            pltpu.VMEM((tree, cols), F32),
        ]
        + scatter_refs(nz)
        + scatter_refs(n)
        + reduce_scratch(n * part, 4 * unit)
        + reduce_scratch(unit, width)
        + reduce_scratch(n * part, 3 * cols)
        + reduce_scratch(part, width)
        + [
            pltpu.VMEM((n, part, 4 * unit), BF),
            pltpu.VMEM((n, part, 3 * cols), BF),
            pltpu.VMEM((4, n * part, 3 * cols), BF),
            pltpu.VMEM((4, part, width), BF),
            pltpu.VMEM((rows, width), F32),
            pltpu.VMEM((rows, width), BF),
            pltpu.VMEM((rows, width), BF),
            pltpu.VMEM((16, width), F32),
            pltpu.VMEM((4 * n, 16, 128), F32),
            pltpu.VMEM((4, 8, 128), F32),
            pltpu.VMEM((3, 8, 128), F32),
            pltpu.VMEM((tree, cols), BF),
            pltpu.VMEM((rows, width), F32),
            pltpu.VMEM((rows, width), BF),
            pltpu.VMEM((rows, width), F32),
        ]
        + gather_sems(nz)
        + exchange_sems(None, nz)
        + exchange_sems(runs_up, nz)
        + exchange_sems(runs_qkv, nz)
        + trade_sems() * 2
        + [pltpu.SemaphoreType.DMA((4 * n,))] * 2
        + [pltpu.SemaphoreType.DMA((3,))] * 2
        + [pltpu.SemaphoreType.DMA((2,)), pltpu.SemaphoreType.DMA((nz + 7,))],
        compiler_params=params(cid, 63 * MIB),
        name="tail",
    )(
        slopes, far_t, grad, joined, a1, mixed, qkv_w, branch, upd, up_g, down_g,
        middle, x_own, whole, grad_middle, sums, bias_g,
    )


def gelu_and_slope(value):
    normal = 0.5 + 0.5 * lax.erf(value * math.sqrt(0.5))
    density = jnp.exp(-0.5 * value * value) * (1.0 / math.sqrt(2.0 * math.pi))
    return value * normal, normal + value * density


def mlp_kernel(
    nz, mixed, x_own, whole, out_in, cot_in, up_in, down_in, bias,
    middle, grad_middle, grad_branch, grad_mixed, sums, bias_g, upd_out, up_out, down_out,
    mlp, cot, up_w, down_w, p, upd, up_g, down_g, out_w, active, gh, grad, acc, came, gsend, grecv, ssend, srecv, lsem,
):
    pos = place()
    x, c, z, y = pos
    blocks, rows, width = mlp.shape
    units = active.shape[1]
    pair = 2 * rows
    me = z * 2 + c
    sib = at(x, 1 - c, z, y)
    up_dev, dn_dev = at(x, c, z + 1, y), at(x, c, z - 1, y)
    UP, DN, SU, SD = 0, nz, 2 * nz, 3 * nz
    part = out_w.shape[1]

    def f(v):
        return v.astype(F32)

    loads = [
        pltpu.make_async_copy(a, b, lsem.at[i])
        for i, (a, b) in enumerate([(out_in, out_w), (up_in, up_w), (cot_in, cot), (down_in, down_w)])
    ]

    def rank_rows(r):
        d, f = r // blocks, r % blocks
        return up_out.at[d // 2 * 2 + f % 2, pl.ds((f // 2 * 2 + d % 2) * part, part)]

    stores = [
        [pltpu.make_async_copy(upd, upd_out, lsem.at[4])],
        [
            pltpu.make_async_copy(up_g.at[pl.ds(r * part, part)], rank_rows(r), lsem.at[6 + r])
            for r in range(4 * blocks)
        ],
        [pltpu.make_async_copy(down_g, down_out, lsem.at[5])],
    ]

    def store(i):
        for copy in stores[i]:
            copy.start()


    def block(b, sem, target):
        return remote(mlp.at[b], mlp.at[b], gsend.at[sem], grecv.at[sem], target)

    def up(d):
        return block((z - d) * 2 + c, UP + d, up_dev)

    def dn(d):
        return block((z + d) * 2 + c, DN + d, dn_dev)

    def side(d, below):
        return block(jnp.where(below, z - d, z + d) * 2 + c, jnp.where(below, SU, SD) + d, sib)

    def turn(i):
        both = jnp.minimum(z, nz - 1 - z)
        two = i <= 2 * both
        d = jnp.where(two, (i + 1) // 2, i - both)
        below = jnp.where(two, i % 2 == 1, z > nz - 1 - z)
        return d, below

    def arrive(i):
        if i == 0:
            block(z * 2 + 1 - c, SU, sib).wait_recv()
            return z
        d, below = turn(i)
        zi = jnp.where(below, z - d, z + d)
        block(zi * 2 + c, jnp.where(below, UP, DN) + d - 1, sib).wait_recv()
        pl.when(below & (z < nz - 1))(lambda: up(d).start())
        pl.when(jnp.logical_not(below) & (z > 0))(lambda: dn(d).start())
        side(d, below).start()
        block(zi * 2 + 1 - c, jnp.where(below, SU, SD) + d, sib).wait_recv()
        return zi

    swap, slot, _, _, _, total, done = scatter_parts(
        nz, pos, lambda t: p[t * 2 + c], lambda t: p.at[t * 2 + 1 - c], acc, came, ssend, srecv
    )

    def at_rows(ref, zi):
        return ref[pl.ds(zi * 2, 2)].reshape(pair, width)

    def hidden_part(zi):
        here = pl.ds(pl.multiple_of(zi * pair, pair), pair)

        def tile(j, _):
            u = pl.ds(pl.multiple_of(j * 256, 256), 256)
            value = dot(at_rows(mlp, zi), up_w[:, u], NN) + bias[:, u]
            grad_act = dot(at_rows(cot, zi), down_w[u, :], NT)
            act, slope = gelu_and_slope(value)
            low = (grad_act * slope).astype(BF)
            active[here, u] = act.astype(BF)
            gh[here, u] = low
            bias_g[:, u] += jnp.sum(f(low), axis=0, keepdims=True)
            return 0

        lax.fori_loop(0, units // 256, tile, 0)

        def back(j, _):
            w = pl.ds(pl.multiple_of(j * 512, 512), 512)
            p[pl.ds(zi * 2, 2), :, w] = dot(gh[here, :], up_w[w, :], NT).astype(BF).reshape(2, rows, 512)
            return 0

        lax.fori_loop(0, width // 512, back, 0)

    def forward_part(zi):
        here = pl.ds(pl.multiple_of(zi * pair, pair), pair)

        def tile(j, _):
            w = pl.ds(pl.multiple_of(j * 512, 512), 512)
            upd[pl.ds(zi * 2, 2), :, w] = dot(active[here, :], down_w[:, w], NN).astype(BF).reshape(2, rows, 512)
            return 0

        lax.fori_loop(0, width // 512, tile, 0)

    def up_grads(first, count):
        def tile(j, _):
            w = pl.ds(pl.multiple_of(j * 256, 256), 256)
            up_g[w, :] = dot(mlp[:, :, w].reshape(blocks * rows, 256), gh[...], TN).astype(BF)
            return 0

        lax.fori_loop(first, first + count, tile, 0)

    def down_grads():
        def tile(j, _):
            u = pl.ds(pl.multiple_of(j * 256, 256), 256)
            down_g[u, :] = dot(active[:, u], cot[...].reshape(blocks * rows, width), TN).astype(BF)
            return 0

        lax.fori_loop(0, units // 256, tile, 0)

    def project():
        def tile(j, _):
            w = pl.ds(pl.multiple_of(j * 512, 512), 512)
            branch = dot(mixed[...], out_w[:, :, w].reshape(width, 512), NN) + whole[4:5, w]
            sums[4:5, w] = jnp.sum(branch * branch, axis=0, keepdims=True)
            middle[:, w] = f(x_own[:, w]) + branch
            return 0

        lax.fori_loop(0, width // 512, tile, 0)

        def norm(j, _):
            here = pl.ds(pl.multiple_of(j * 32, 32), 32)
            normed, _ = norm_parts(middle[here, :])
            mlp[me, here] = (normed * whole[5:6, :] + whole[6:7, :]).astype(BF)
            return 0

        lax.fori_loop(0, rows // 32, norm, 0)

    def finish_rows():
        def norm(j, _):
            here = pl.ds(pl.multiple_of(j * 32, 32), 32)
            normed, inverse = norm_parts(middle[here, :])
            value, own = grad[here, :], f(cot[me, here])
            through = own + norm_back(value * whole[5:6, :], normed, inverse)
            low = through.astype(BF)
            grad_middle[here, :] = through
            grad_branch[here, :] = low
            for i, v in enumerate((value * normed, value, f(low), own)):
                sums[i : i + 1, :] += jnp.sum(v, axis=0, keepdims=True)
            return 0

        lax.fori_loop(0, rows // 32, norm, 0)
        each = 256 // part

        def tile(j, _):
            value = dot(grad_branch[...], out_w[pl.ds(j * each, each)].reshape(256, width), NT).astype(BF)
            for i in range(2):
                r = j * each + i * (each // 2)
                d, fs = r // blocks, r % blocks
                grad_mixed[fs // 2 * 2 + d % 2, :, pl.ds(pl.multiple_of(d // 2 * 128, 128), 128)] = value[
                    :, i * 128 : (i + 1) * 128
                ]
            return 0

        lax.fori_loop(0, width // 256, tile, 0)

    for copy in loads:
        copy.start()
    bias_g[...] = jnp.zeros_like(bias_g)
    sums[...] = jnp.zeros_like(sums)
    greet(line_partners(nz, pos))
    loads[0].wait()
    project()
    pl.when(z < nz - 1)(up(0).start)
    pl.when(z > 0)(dn(0).start)
    side(0, z >= 0).start()
    for copy in loads[1:]:
        copy.wait()
    slots = 2 * nz - 1
    tiles = width // 256
    for s in range(slots):
        if s < nz:
            zi = arrive(s)
            hidden_part(zi)
            swap(zi).start()
        slot(s)
        if s < nz:
            forward_part(zi)
        if s == nz - 1:
            store(0)
            down_grads()
            store(2)
        elif s == nz:
            up_grads(0, tiles // 2)
        elif s == nz + 1:
            up_grads(tiles // 2, tiles - tiles // 2)
            store(1)
    total(grad)
    finish_rows()
    for copies in stores:
        for copy in copies:
            copy.wait()
    side(0, z >= 0).wait_send()
    pl.when(z < nz - 1)(up(0).wait_send)
    pl.when(z > 0)(dn(0).wait_send)
    for k in range(1, nz):

        @pl.when(z >= k)
        def _():
            pl.when(z < nz - 1)(up(k).wait_send)
            side(k, z >= 0).wait_send()

        @pl.when(z + k < nz)
        def _():
            pl.when(z > 0)(dn(k).wait_send)
            side(k, z < 0).wait_send()

    done()


def mlp_bytes(nz, rows, width, units):
    tree = 2 * nz * rows
    kept = 4 * tree * width + 4 * units * width + 2 * tree * units + 2 * nz * rows * width + width * width
    return 2 * kept + 14 * rows * width


def mlp_call(mixed, x_own, whole, out_w, cot, up_w, down_w, bias, nz, cid):
    rows, width = x_own.shape
    units = down_w.shape[0]
    n = 2 * nz
    shape = jax.ShapeDtypeStruct
    return pl.pallas_call(
        functools.partial(mlp_kernel, nz),
        out_shape=[
            shape((rows, width), F32),
            shape((rows, width), F32),
            shape((rows, width), BF),
            shape((n, rows, width // n), BF),
            shape((8, width), F32),
            shape((1, units), F32),
            shape((n, rows, width), BF),
            shape((4, width // 4, units), BF),
            shape((units, width), BF),
        ],
        in_specs=[VM] * 3 + [HBM] * 4 + [VM],
        out_specs=[VM] * 6 + [HBM] * 3,
        scratch_shapes=[
            pltpu.VMEM((n, rows, width), BF),
            pltpu.VMEM((n, rows, width), BF),
            pltpu.VMEM((width, units), BF),
            pltpu.VMEM((units, width), BF),
            pltpu.VMEM((n, rows, width), BF),
            pltpu.VMEM((n, rows, width), BF),
            pltpu.VMEM((width, units), BF),
            pltpu.VMEM((units, width), BF),
            pltpu.VMEM(out_w.shape, BF),
            pltpu.VMEM((n * rows, units), BF),
            pltpu.VMEM((n * rows, units), BF),
            pltpu.VMEM((rows, width), F32),
            pltpu.VMEM((nz, rows, width), BF),
            pltpu.VMEM((nz + 1, rows, width), BF),
        ]
        + gather_sems(nz)
        + [pltpu.SemaphoreType.DMA((5 * nz,))] * 2
        + [pltpu.SemaphoreType.DMA((6 + 4 * n,))],
        compiler_params=params(cid, 63 * MIB),
        name="mlp",
    )(mixed, x_own, whole, out_w, cot, up_w, down_w, bias)


def attend_kernel(
    heads, nz, unit, slopes, far, joined_q, joined, cot, w_up, w_out, out, cot_all, up_w, out_w, *sems
):
    cols = heads * HD
    step, steps = pl.program_id(0), pl.num_programs(0)
    pos = place()
    n = 2 * nz
    gc = line_gather(cot, cot_all, *sems[:2], nz, True, pos)
    gu = sliced_gather(w_up, up_w, up_runs(nz, unit), sems[2:6], nz, pos)
    go = full_gather(w_out, out_w, *sems[6:8], nz, pos)

    @pl.when(step == 0)
    def _():
        x, c, z, y = pos
        greet(rank_partners(nz, pos) + group_partners(pos) + [(c != y, at(x, y, z, c))])
        gc[0]()
        gu[0]()
        go[0]()

    @pl.when(step == 1)
    def _():
        for stage in go[1:nz]:
            stage()

    @pl.when(step == 2)
    def _():
        for stage in gu[1 : n + 1]:
            stage()
        gc[1]()

    gap = far[...]
    for h in range(heads):
        q = joined_q[:, h * HD : (h + 1) * HD]
        k = joined[:, cols + h * HD : cols + (h + 1) * HD]
        v = joined[:, 2 * cols + h * HD : 2 * cols + (h + 1) * HD]
        logits = dot(q, k, NT) * HD ** (-0.5) + slopes[h] * gap
        weights = jnp.exp(logits - jnp.max(logits, axis=1, keepdims=True))
        probs = weights * (1.0 / jnp.sum(weights, axis=1, keepdims=True))
        out[:, h * HD : (h + 1) * HD] = dot(probs.astype(BF), v, NN).astype(BF)

    @pl.when(step == steps - 1)
    def _():
        for stage in go[nz : 2 * nz]:
            stage()
        ahead, later = gc[2:-1], gu[n + 1 : -1]
        for i, stage in enumerate(ahead):
            stage()
            for other in later[i * n // len(ahead) : (i + 1) * n // len(ahead)]:
                other()
        for stage in go[2 * nz :]:
            stage()
        gc[-1]()
        gu[-1]()


def attend(slopes, far, joined, cot, w_up, w_out, unit, heads, nz, cid):
    tree = far.shape[0]
    cols = heads * HD
    rows = min(256, max(128, 2**18 // tree))
    block, width = cot.shape
    part = w_up.shape[0]
    n = 2 * nz
    shapes = [(tree, cols), (n, block, width), (4 * n, part, 4 * unit), (4 * n, part, width)]
    return pl.pallas_call(
        functools.partial(attend_kernel, heads, nz, unit),
        out_shape=[jax.ShapeDtypeStruct(s, BF) for s in shapes],
        grid=(tree // rows,),
        in_specs=[
            pl.BlockSpec(memory_space=pltpu.SMEM),
            pl.BlockSpec((rows, tree), lambda i: (i, 0)),
            pl.BlockSpec((rows, 3 * cols), lambda i: (i, 0)),
            pl.BlockSpec((tree, 3 * cols), lambda i: (0, 0)),
            HBM,
            HBM,
            HBM,
        ],
        out_specs=[pl.BlockSpec((rows, cols), lambda i: (i, 0)), HBM, HBM, HBM],
        scratch_shapes=gather_sems(nz) + sliced_sems(nz) + full_sems(nz),
        compiler_params=params(cid, 56 * MIB),
        name="attend",
    )(slopes, far, joined, joined, cot, w_up, w_out)


def attend_back_kernel(heads, nz, kinds, slopes, far, joined_q, joined, grad, branch, part_sums, *refs):
    count = len(kinds)
    srcs, refs = refs[:count], refs[count:]
    out_q, out_k, out_v, branch_all, update, refs = *refs[:5], refs[5:]
    dsts, refs = refs[:count], refs[count:]
    acc_k, acc_v, p, refs = *refs[:3], refs[3:]
    scratch, gsems, hsems, psem = refs[:5], refs[5:7], refs[7:9], refs[9]
    cols = heads * HD
    step = pl.program_id(0)
    pos = place()
    gb = line_gather(branch, branch_all, *gsems, nz, False, pos)
    hs = hand_stages(srcs, dsts, kinds, *hsems, nz, pos)
    load = pltpu.make_async_copy(part_sums, p, psem.at[0])

    @pl.when(step == 0)
    def _():
        acc_k[...] = jnp.zeros_like(acc_k)
        acc_v[...] = jnp.zeros_like(acc_v)
        greet(line_partners(nz, pos) + group_partners(pos))
        hs[0]()
        gb[0]()
        gb[1]()
        load.start()

    @pl.when(step == 3)
    def _():
        gb[2]()

    gap = far[...]
    for h in range(heads):
        here = slice(h * HD, (h + 1) * HD)
        q = joined_q[:, here]
        k = joined[:, cols + h * HD : cols + (h + 1) * HD]
        v = joined[:, 2 * cols + h * HD : 2 * cols + (h + 1) * HD]
        g = grad[:, here]
        logits = dot(k, q, NT) * HD ** (-0.5) + slopes[h] * gap
        weights = jnp.exp(logits - jnp.max(logits, axis=0, keepdims=True))
        probs = weights * (1.0 / jnp.sum(weights, axis=0, keepdims=True))
        grad_probs = dot(v, g, NT)
        delta = jnp.sum(probs * grad_probs, axis=0, keepdims=True)
        grad_raw = (probs * (grad_probs - delta) * HD ** (-0.5)).astype(BF)
        acc_v[:, here] += dot(probs.astype(BF), g, NN)
        acc_k[:, here] += dot(grad_raw, q, NN)
        out_q[:, here] = dot(grad_raw, k, TN).astype(BF)

    @pl.when(step == pl.num_programs(0) - 1)
    def _():
        out_k[...] = acc_k[...].astype(BF)
        out_v[...] = acc_v[...].astype(BF)
        for stage in gb[3:]:
            stage()
        load.wait()
        scatter_blocks(nz, pos, p, update, *scratch)
        hs[1]()


def attend_back(slopes, far_t, joined, grad, branch, part_sums, arrays, kinds, heads, nz, cid):
    tree = far_t.shape[0]
    cols = heads * HD
    rows = min(256, max(128, 2**18 // tree))
    block, width = branch.shape
    full = pl.BlockSpec((tree, cols), lambda i: (0, 0))
    part = pl.BlockSpec((rows, cols), lambda i: (i, 0))
    return pl.pallas_call(
        functools.partial(attend_back_kernel, heads, nz, kinds),
        out_shape=[jax.ShapeDtypeStruct((tree, cols), BF)] * 3
        + [jax.ShapeDtypeStruct((2 * nz, block, width), BF), jax.ShapeDtypeStruct((block, width), F32)]
        + hand_shapes(arrays, kinds, nz),
        grid=(tree // rows,),
        in_specs=[
            pl.BlockSpec(memory_space=pltpu.SMEM),
            pl.BlockSpec((tree, rows), lambda i: (0, i)),
            pl.BlockSpec((rows, 3 * cols), lambda i: (i, 0)),
            pl.BlockSpec((tree, 3 * cols), lambda i: (0, 0)),
            part,
            HBM,
            HBM,
        ]
        + [HBM] * len(arrays),
        out_specs=[part, full, full, HBM, pl.BlockSpec((block, width), lambda i: (0, 0))] + [HBM] * len(arrays),
        scratch_shapes=[pltpu.VMEM((tree, cols), F32)] * 2
        + [pltpu.VMEM((2 * nz, block, width), BF)]
        + scatter_scratch(nz, block, width)
        + gather_sems(nz)
        + hand_sems(kinds)
        + [pltpu.SemaphoreType.DMA((1,))],
        compiler_params=params(cid, 62 * MIB),
        name="attend_back",
    )(slopes, far_t, joined, joined, grad, branch, part_sums, *arrays)


def norm_parts(values):
    center = values - jnp.mean(values, axis=-1, keepdims=True)
    inverse = lax.rsqrt(jnp.mean(center * center, axis=-1, keepdims=True) + EPSILON)
    return (center * inverse, inverse)


def norm_back(grad_normed, normed, inverse):
    mean_grad = jnp.mean(grad_normed, axis=-1, keepdims=True)
    mean_cross = jnp.mean(grad_normed * normed, axis=-1, keepdims=True)
    return inverse * (grad_normed - mean_grad - normed * mean_cross)


def tree_tables(parents, seg_blocks, valid):
    segments = parents.shape[0]
    seg_tokens = jnp.broadcast_to(seg_blocks[:, None], (seg_blocks.shape[0], BLK)).reshape(-1)
    labels = jnp.arange(segments, dtype=jnp.int32)
    member = (seg_tokens[:, None] == labels[None, :]).astype(jnp.int32)
    counted = member * valid[:, None]
    before = jnp.cumsum(counted, axis=0) - counted
    rank = jnp.sum(before * member, axis=1)
    seg_len = jnp.sum(counted, axis=0)
    picked = (parents[:, None] == labels[None, :]).astype(jnp.int32)
    grand = jnp.sum(picked * parents[None, :], axis=1)
    ancestor = ((labels[None, :] == parents[:, None]) | (labels[None, :] == grand[:, None])) & (
        labels[None, :] != labels[:, None]
    )
    offset = jnp.sum(ancestor.astype(jnp.int32) * seg_len[None, :], axis=1)
    position = jnp.sum(member * offset[None, :], axis=1) + rank
    return (seg_tokens, position, ancestor.astype(jnp.float32))


def allowed_mask(seg, index, valid, ancestor):
    labels = jnp.arange(ancestor.shape[0], dtype=jnp.int32)
    member = (seg[:, None] == labels[None, :]).astype(jnp.float32)
    reach = jnp.dot(jnp.dot(member, ancestor), member.T) > 0.5
    causal = (seg[:, None] == seg[None, :]) & (index[None, :] <= index[:, None])
    visible = (valid[None, :] == 1) | (index[None, :] == index[:, None])
    return (reach | causal) & visible


def gelu_exact(value):
    return jax.nn.gelu(value, approximate=False)


def mm(spec, a, b):
    return jnp.einsum(spec, a, b, preferred_element_type=F32)


def padded(flat, lanes):
    return jnp.pad(flat, [(0, 0)] * (flat.ndim - 1) + [(0, -flat.shape[-1] % lanes)])


def by_steps(
    layer_in,
    cotangent,
    w_qkv,
    w_out,
    w_up,
    w_down,
    gain_attn,
    shift_attn,
    bias_query,
    bias_value,
    bias_out,
    gain_mlp,
    shift_mlp,
    bias_up,
    bias_down,
    parents,
    seg_blocks,
    token_valid,
):
    rows, width = layer_in.shape
    fsdp = lax.axis_size("fsdp")
    nz = fsdp // 2
    devices = 4 * fsdp
    x, c, z, y = place()
    rank = z * 2 + c
    heads = H // fsdp
    cols = heads * HD
    tree = token_valid.shape[1]
    part = w_up.shape[0]
    unit = w_down.shape[0]

    vec = jnp.concatenate(
        [gain_attn, shift_attn, bias_query, bias_value, bias_out, gain_mlp, shift_mlp, bias_down, bias_up]
    ).astype(F32)
    vec = padded(vec, 1024).reshape(-1, 128)
    tab = jnp.concatenate([token_valid[0], seg_blocks[0], parents[0]])
    tab = padded(tab, 1024).reshape(-1, 128)
    aligned = part == HD and cols % 256 == 0
    if not aligned:
        w_qkv = w_qkv.reshape(part, 3, fsdp, cols).transpose(2, 0, 1, 3).reshape(fsdp, part, 3 * cols)
    x_all, qkv_w, down_w, vecs, tab = fetch(nz, layer_in, w_qkv, w_down, part, vec, tab, 1)
    down_w = down_w.reshape(4 * unit, width)
    x_all = x_all.reshape(tree, width)
    qkv_w = qkv_w.reshape(width, 3 * cols)
    vecs = vecs.reshape(devices, -1)
    (gain_one, shift_one, query_bias, value_bias, out_bias, gain_two, shift_two, down_bias) = [
        vecs[:, i * part : (i + 1) * part].reshape(-1) for i in range(8)
    ]
    up_bias = vecs[:, 8 * part : 8 * part + unit].reshape(2, 2, nz, 2, unit)
    up_bias = lax.dynamic_slice(up_bias, (0, c, z, 0, 0), (2, 1, 1, 2, unit)).reshape(-1)

    def own_rows(v):
        return lax.dynamic_slice_in_dim(v, rank * rows, rows, 0)

    normed_all, _ = norm_parts(x_all.astype(F32))
    attn_in = (normed_all * gain_one + shift_one).astype(BF)
    inputs = own_rows(x_all).astype(F32)
    normed_one, inverse_one = norm_parts(inputs)

    if aligned:

        def own_cols(v):
            v = v.reshape(2, 2, nz, 2, HD)
            return lax.dynamic_slice(v, (0, c, z, 0, 0), (2, 1, 1, 2, HD)).reshape(-1)

        def spread(v):
            v = v.reshape(2, 1, 1, 2, HD)
            return lax.dynamic_update_slice(jnp.zeros((2, 2, nz, 2, HD), F32), v, (0, c, z, 0, 0))

        numbers = block_of(jnp.arange(2)[:, None], c, z, jnp.arange(2)[None, :], nz).reshape(-1)
    else:

        def own_cols(v):
            return lax.dynamic_slice_in_dim(v, rank * cols, cols, 0)

        def spread(v):
            return lax.dynamic_update_slice_in_dim(jnp.zeros((width,), F32), v, rank * cols, 0)

        numbers = rank * heads + jnp.arange(heads)

    joined_bias = jnp.concatenate([own_cols(query_bias), jnp.zeros((cols,), F32), own_cols(value_bias)])
    joined = (jnp.dot(attn_in, qkv_w, preferred_element_type=F32) + joined_bias).astype(BF)

    tab = tab.reshape(-1)
    blocks = seg_blocks.shape[1]
    valid = tab[:tree]
    seg, position, ancestor = tree_tables(
        tab[tree + blocks : tree + blocks + parents.shape[1]], tab[tree : tree + blocks], valid
    )
    index = jnp.arange(tree, dtype=jnp.int32)
    mask = allowed_mask(seg, index, valid, ancestor)
    far = jnp.where(mask, (position[None, :] - position[:, None]).astype(F32), MASKED)
    slopes = jnp.exp2(-8.0 * (numbers.astype(F32) + 1.0) / H)
    mixed, cot, up_w, out_w = attend(slopes, far, joined, cotangent, w_up, w_out, unit, heads, nz, 9)
    out_w = out_w.reshape(width, width)
    cot = cot.reshape(tree, width)
    up_w = up_w.reshape(width, 4 * unit)

    mixed_own = exchange(mixed.reshape(fsdp, rows, cols), nz, 2, "mixed_to_tokens")
    if aligned:
        mixed_own = mixed_own.reshape(nz, 2, rows, 2, 2 * HD).transpose(2, 3, 1, 0, 4).reshape(rows, width)
    else:
        mixed_own = mixed_own.transpose(1, 0, 2).reshape(rows, width)
    branch = jnp.dot(mixed_own, out_w, preferred_element_type=F32) + out_bias
    middle = inputs + branch
    normed_two, inverse_two = norm_parts(middle)
    mlp_own = (normed_two * gain_two + shift_two).astype(BF)
    cot_blocks = cot.reshape(fsdp, rows, width)
    mlp_in = gather_tokens(mlp_own, nz, 3).reshape(tree, width)
    hidden = jnp.dot(mlp_in, up_w, preferred_element_type=F32) + up_bias
    active_float, gelu_pull = jax.vjp(gelu_exact, hidden)
    active = active_float.astype(BF)
    grad_active = mm("td,fd->tf", cot, down_w)
    grad_hidden = gelu_pull(grad_active)[0].astype(BF)
    grad_mlp_in = mm("tf,df->td", grad_hidden, up_w).astype(BF).reshape(fsdp, rows, width)
    grad_mlp_in = scatter_tokens(grad_mlp_in, nz, 4)
    update = jnp.dot(active, down_w, preferred_element_type=F32).astype(BF).reshape(fsdp, rows, width)
    down_g = mm("tf,td->fd", active, cot).astype(BF)
    up_g = mm("td,tf->df", mlp_in, grad_hidden).astype(BF)
    grad_bias_up = jnp.sum(grad_hidden.astype(F32), axis=0)
    down_g = down_g.reshape(4, unit, width)
    cot_own = own_rows(cot).astype(F32)
    grad_middle = cot_own + norm_back(grad_mlp_in * gain_two, normed_two, inverse_two)
    grad_branch = grad_middle.astype(BF)
    grad_mixed = mm("te,de->td", grad_branch, out_w).astype(BF)
    if not aligned:
        grad_out_w = lax.psum_scatter(
            mm("td,te->de", mixed_own, grad_branch).astype(BF), BOTH, scatter_dimension=0, tiled=True
        ).astype(F32)
    if aligned:
        grad_mixed = grad_mixed.reshape(rows, 2, 2, nz, 2 * HD).transpose(3, 2, 0, 1, 4).reshape(fsdp, rows, cols)
    else:
        grad_mixed = grad_mixed.reshape(rows, fsdp, cols).transpose(1, 0, 2)
    up_g = up_g.reshape(devices, part, 4 * unit)
    grad_heads = exchange(grad_mixed, nz, 5, "grad_to_heads")
    grad_heads = grad_heads.reshape(tree, cols)
    grad_q, grad_k, grad_v, branch_all, update, down_c, up_c = attend_back(
        slopes, far.T, joined, grad_heads, grad_branch, update, [down_g, up_g], (False, True), heads, nz, 6
    )
    result = middle + update + down_bias
    grad_joined = jnp.concatenate([grad_q, grad_k, grad_v], axis=1)

    def mine(g, came):
        g = g.reshape((2, 2, nz, 2) + g.shape[1:])
        g = lax.dynamic_slice(g, (x, 0, 0, y, 0, 0), (1, 2, nz, 1) + g.shape[4:])
        g = g.reshape((2, nz) + g.shape[4:]).swapaxes(0, 1)
        return (g.reshape(came.shape[1:]).astype(F32) + jnp.sum(came.astype(F32), axis=0)).astype(BF)

    def mine_flat(g, came):
        return lax.dynamic_index_in_dim(g, x * 2 + y, 0, keepdims=False).astype(F32) + jnp.sum(came.astype(F32), axis=0)

    grad_down_w = mine_flat(down_g, down_c)
    qkv_g = mm("td,te->de", attn_in, grad_joined).astype(BF).reshape(devices, part, 3 * cols)
    flat = []
    if aligned:
        flat = [mm("td,te->de", mixed, branch_all.reshape(tree, width)).astype(BF).reshape(4, part, width)]
    kinds = (True,) + (False,) * len(flat)
    grad_attn_in = mm("te,de->td", grad_joined, qkv_w).astype(BF).reshape(fsdp, rows, width)
    grad_attn_in, grad_up_w, layer_out, qkv_c, *out_c = scatter_and_hand(
        grad_attn_in, mine(up_g, up_c), up_runs(nz, unit), result.astype(BF), [qkv_g] + flat, kinds, nz, 10
    )
    if aligned:
        grad_out_w = mine_flat(flat[0], out_c[0])
    col, square = jnp.sum(grad_joined.astype(F32), axis=0), jnp.sum(result * result)
    grad_up_w = grad_up_w.astype(F32)
    grad_inputs = grad_middle + norm_back(grad_attn_in * gain_one, normed_one, inverse_one)

    smalls = [
        jnp.sum(grad_attn_in * normed_one, axis=0),
        jnp.sum(grad_attn_in, axis=0),
        spread(col[:cols]),
        spread(col[2 * cols :]),
        jnp.sum(grad_branch.astype(F32), axis=0),
        jnp.sum(grad_mlp_in * normed_two, axis=0),
        jnp.sum(grad_mlp_in, axis=0),
        jnp.sum(cot_own, axis=0),
    ]
    grad_bias_up = grad_bias_up.reshape(2, 1, 1, 2, unit)
    grad_bias_up = lax.dynamic_update_slice(jnp.zeros((2, 2, nz, 2, unit), F32), grad_bias_up, (0, c, z, 0, 0))
    squares = jnp.stack([square, jnp.sum(branch * branch)])
    packed = jnp.concatenate(
        [v.reshape(devices, part) for v in smalls]
        + [grad_bias_up.reshape(devices, unit), jnp.broadcast_to(squares, (devices, 2))],
        axis=1,
    )
    packed = padded(packed, 1024).reshape(devices, -1, 128)
    runs = qkv_runs(nz, width, cols) if aligned else None
    grad_x, packed, grad_qkv_w = finish(grad_inputs.astype(BF), packed, mine(qkv_g, qkv_c), runs, nz, 8)
    if not aligned:
        grad_qkv_w = grad_qkv_w.reshape(fsdp, part, 3, cols).transpose(1, 2, 0, 3).reshape(part, -1)
    grad_qkv_w = grad_qkv_w.astype(F32)
    packed = packed.reshape(-1)
    small = [packed[i * part : (i + 1) * part] for i in range(8)]
    up_at = 8 * part
    root_squares = jnp.sqrt(packed[up_at + unit : up_at + unit + 2] / (devices * rows * width))
    return (
        layer_out,
        grad_x,
        grad_qkv_w,
        grad_out_w,
        grad_up_w,
        grad_down_w,
        small[0],
        small[1],
        small[2],
        small[3],
        small[4],
        small[5],
        small[6],
        packed[up_at : up_at + unit],
        small[7],
        root_squares,
    )


def by_kernels(
    layer_in,
    cotangent,
    w_qkv,
    w_out,
    w_up,
    w_down,
    gain_attn,
    shift_attn,
    bias_query,
    bias_value,
    bias_out,
    gain_mlp,
    shift_mlp,
    bias_up,
    bias_down,
    parents,
    seg_blocks,
    token_valid,
):
    rows, width = layer_in.shape
    fsdp = lax.axis_size("fsdp")
    nz = fsdp // 2
    devices = 4 * fsdp
    heads = H // fsdp
    cols = heads * HD
    tree = token_valid.shape[1]
    part = w_up.shape[0]
    unit = w_down.shape[0]

    slopes = jnp.asarray(np.exp2(-8.0 * (np.arange(H) + 1.0) / H).astype(np.float32))
    vectors = (gain_attn, shift_attn, bias_query, bias_value, bias_out, gain_mlp, shift_mlp, bias_down)
    joined, mixed, mixed_own, own, whole, up_bias, attn_in, far, cot, qkv_w, up_w, out_w, down_w = head_call(
        slopes, (token_valid, seg_blocks, parents), vectors, bias_up, layer_in, cotangent, w_qkv, w_up, w_out, w_down,
        heads, nz, 1,
    )
    qkv_w = qkv_w.reshape(width, 3 * cols)
    up_w = up_w.reshape(width, 4 * unit)
    down_w = down_w.reshape(4 * unit, width)
    middle, grad_middle, grad_branch, grad_mixed, sums, grad_bias_up, update, up_g, down_g = mlp_call(
        mixed_own, own, whole, out_w, cot, up_w, down_w, up_bias, nz, 3
    )
    down_g = down_g.reshape(4, unit, width)
    runs = up_runs(nz, unit), qkv_runs(nz, width, cols)
    grad_down_w, grad_out_w, small, bias, grad_up_w, grad_qkv_w, _, layer_out, grad_x = tail_call(
        slopes, far, grad_mixed, joined, attn_in, mixed.reshape(tree, cols), qkv_w, grad_branch, update, up_g, down_g,
        middle, own, whole, grad_middle, sums, grad_bias_up, runs, heads, nz, 6,
    )
    root_squares = jnp.sqrt(small[8:10, 0] / (devices * rows * width))
    vectors = [small[i, :part] for i in range(8)]
    return (
        layer_out,
        grad_x,
        grad_qkv_w.astype(F32),
        grad_out_w,
        grad_up_w.astype(F32),
        grad_down_w,
        *vectors[:7],
        bias.reshape(-1)[:unit],
        vectors[7],
        root_squares,
    )


def per_device(*args):
    layer_in, w_down, token_valid = args[0], args[5], args[17]
    fsdp = lax.axis_size("fsdp")
    rows, width = layer_in.shape
    unit = w_down.shape[0]
    fits = mlp_bytes(fsdp // 2, rows, width, 4 * unit) < 60 * MIB
    whole_heads = args[2].shape[0] == HD and H // fsdp == 4 and width == H * HD
    if fsdp == 8 and fits and whole_heads and unit % 128 == 0 and token_valid.shape[1] % 256 == 0 and rows == 128:
        return by_kernels(*args)
    return by_steps(*args)


def solution(mesh):
    matrix, vector, table = P(BOTH, None), P(BOTH), P("dp", None)
    return jax.shard_map(
        per_device,
        mesh=mesh,
        in_specs=(matrix,) * 6 + (vector,) * 9 + (table,) * 3,
        out_specs=(matrix,) * 6 + (vector,) * 9 + (P(),),
        check_vma=False,
    )
```

```python
import functools
import math

import jax
import jax.numpy as jnp
import numpy as np
from jax import lax
from jax.experimental import pallas as pl
from jax.experimental.pallas import tpu as pltpu
from jax.sharding import PartitionSpec as P

H = 32
HD = 64
BLK = 32

EPSILON = 1e-05
MASKED = -1e30
BF = jnp.bfloat16
F32 = jnp.float32
BOTH = ("dp", "fsdp")
MESH = pl.DeviceIdType.MESH
HBM = pl.BlockSpec(memory_space=pl.ANY)
VM = pl.BlockSpec(memory_space=pltpu.VMEM)
MIB = 2**20


def place():
    d, f = lax.axis_index("dp"), lax.axis_index("fsdp")
    return d // 2, d % 2, f // 2, f % 2


def at(x, c, z, y):
    return (x * 2 + c, z * 2 + y)


def remote(src, dst, send, recv, target):
    return pltpu.make_async_remote_copy(
        src_ref=src, dst_ref=dst, send_sem=send, recv_sem=recv, device_id=target, device_id_type=MESH
    )


def greet(partners):
    barrier = pltpu.get_barrier_semaphore()
    count = 0
    for condition, device in partners:

        @pl.when(condition)
        def _():
            pl.semaphore_signal(barrier, inc=1, device_id=device, device_id_type=MESH)

        count = count + jnp.asarray(condition).astype(jnp.int32)
    pl.semaphore_wait(barrier, count)


def greet_all(devices, fsdp, me):
    barrier = pltpu.get_barrier_semaphore()

    def one(k, _):
        other = (me + k) % devices
        pl.semaphore_signal(barrier, inc=1, device_id=(other // fsdp, other % fsdp), device_id_type=MESH)
        return 0

    lax.fori_loop(1, devices, one, 0)
    pl.semaphore_wait(barrier, devices - 1)


def line_partners(nz, pos):
    x, c, z, y = pos
    return [(z >= 0, at(x, 1 - c, z, y)), (z > 0, at(x, c, z - 1, y)), (z < nz - 1, at(x, c, z + 1, y))]


def rank_partners(nz, pos):
    x, c, z, y = pos
    n = 2 * nz
    others = [(z * 2 + c + k) % n for k in range(1, n)]
    return [(z >= 0, at(x, p % 2, p // 2, y)) for p in others]


def group_partners(pos):
    x, c, z, y = pos
    return [(z >= 0, at(x ^ (m // 2), c, z, y ^ (m % 2))) for m in (1, 2, 3)]


def line_gather(src, dst, send, recv, nz, swap, pos):
    x, c, z, y = pos
    own = z * 2 + c
    sib = at(x, 1 - c, z, y)
    up_dev, dn_dev = at(x, c, z + 1, y), at(x, c, z - 1, y)
    UP, DN, SU, SD = 0, nz, 2 * nz, 3 * nz
    OWN = 4 * nz

    def block(b, moved):
        return dst.at[b] if moved else src

    def up(k):
        b = (z - k) * 2 + c
        return remote(block(b, k or swap), dst.at[b], send.at[UP + k], recv.at[UP + k], up_dev)

    def dn(k):
        b = (z + k) * 2 + c
        return remote(block(b, k or swap), dst.at[b], send.at[DN + k], recv.at[DN + k], dn_dev)

    def side(k, base, sign):
        b = (z + sign * k) * 2 + c
        return remote(block(b, k or swap), dst.at[b], send.at[base + k], recv.at[base + k], sib)

    def got(b, sem):
        return remote(dst.at[b], dst.at[b], send.at[OWN], recv.at[sem], sib)

    local = pltpu.make_async_copy(src, dst.at[own], recv.at[OWN])
    trade = remote(src, dst.at[z * 2 + y], send.at[OWN], recv.at[OWN], at(x, y, z, c))

    def first():
        if swap:
            pl.when(c == y)(local.start)
            pl.when(c != y)(trade.start)
        else:
            local.start()

    def spread():
        if swap:
            local.wait()
        pl.when(z < nz - 1)(up(0).start)
        pl.when(z > 0)(dn(0).start)
        side(0, SU, 1).start()

    def step(k):
        @pl.when(z >= k)
        def _():
            got((z - k) * 2 + c, UP + k - 1).wait_recv()
            pl.when(z < nz - 1)(up(k).start)
            side(k, SU, -1).start()

        @pl.when(z + k < nz)
        def _():
            got((z + k) * 2 + c, DN + k - 1).wait_recv()
            pl.when(z > 0)(dn(k).start)
            side(k, SD, 1).start()

    def last():
        if swap:
            pl.when(c != y)(trade.wait_send)
        else:
            local.wait()
        got(z * 2 + 1 - c, SU).wait_recv()
        pl.when(z < nz - 1)(up(0).wait_send)
        pl.when(z > 0)(dn(0).wait_send)
        side(0, SU, 1).wait_send()
        for k in range(1, nz):

            @pl.when(z >= k)
            def _():
                got((z - k) * 2 + 1 - c, SU + k).wait_recv()
                pl.when(z < nz - 1)(up(k).wait_send)
                side(k, SU, -1).wait_send()

            @pl.when(z + k < nz)
            def _():
                got((z + k) * 2 + 1 - c, SD + k).wait_recv()
                pl.when(z > 0)(dn(k).wait_send)
                side(k, SD, 1).wait_send()

    return [first, spread] + [functools.partial(step, k) for k in range(1, nz)] + [last]


def gather_sems(nz):
    return [pltpu.SemaphoreType.DMA((4 * nz + 1,))] * 2


def gather_kernel(nz, src, dst, send, recv):
    pos = place()
    greet(line_partners(nz, pos))
    for stage in line_gather(src, dst, send, recv, nz, False, pos):
        stage()


def params(cid, vmem=None):
    return pltpu.CompilerParams(collective_id=cid, has_side_effects=True, vmem_limit_bytes=vmem)


def gather_tokens(a, nz, cid):
    return pl.pallas_call(
        functools.partial(gather_kernel, nz),
        out_shape=jax.ShapeDtypeStruct((2 * nz,) + a.shape, a.dtype),
        in_specs=[HBM],
        out_specs=HBM,
        scratch_shapes=gather_sems(nz),
        compiler_params=params(cid),
        name="gather_tokens",
    )(a)


def scatter_blocks(nz, pos, p, out, acc, ups, dns, send, recv):
    x, c, z, y = pos
    sib = at(x, 1 - c, z, y)
    S, U, D = 0, nz, 2 * nz

    def f(v):
        return v.astype(F32)

    def swap(t):
        return remote(p.at[t * 2 + 1 - c], acc.at[t], send.at[S + t], recv.at[S + t], sib)

    def up(t):
        return remote(acc.at[t], ups.at[t], send.at[U + t], recv.at[U + t], at(x, c, z + 1, y))

    def dn(t):
        return remote(acc.at[t], dns.at[t], send.at[D + t], recv.at[D + t], at(x, c, z - 1, y))

    order = []
    for i in range(nz - 1):
        order += [(True, nz - 1 - i), (False, i)]
    for upward, t in order:
        pl.when(z < t if upward else z > t)(swap(t).start)
    swap(z).start()
    for upward, t in order:

        @pl.when(z < t if upward else z > t)
        def _():
            swap(t).wait_recv()
            acc[t] = (f(acc[t]) + f(p[t * 2 + c])).astype(BF)
            move, came = (up, ups) if upward else (dn, dns)

            @pl.when(z > 0 if upward else z < nz - 1)
            def _():
                move(t).wait_recv()
                acc[t] = (f(acc[t]) + f(came[t])).astype(BF)

            move(t).start()

    swap(z).wait_recv()
    out[...] = f(acc[z]) + f(p[z * 2 + c])

    @pl.when(z > 0)
    def _():
        up(z).wait_recv()
        out[...] += f(ups[z])

    @pl.when(z < nz - 1)
    def _():
        dn(z).wait_recv()
        out[...] += f(dns[z])

    for t in range(nz):
        swap(t).wait_send()
        pl.when(z < t)(up(t).wait_send)
        pl.when(z > t)(dn(t).wait_send)


def scatter_scratch(nz, rows, width):
    return [pltpu.VMEM((nz, rows, width), BF)] * 3 + [pltpu.SemaphoreType.DMA((3 * nz,))] * 2


def scatter_kernel(nz, p, out, *scratch):
    pos = place()
    greet(line_partners(nz, pos))
    scatter_blocks(nz, pos, p, out, *scratch)


def scatter_tokens(p, nz, cid):
    blocks, rows, width = p.shape
    return pl.pallas_call(
        functools.partial(scatter_kernel, nz),
        out_shape=jax.ShapeDtypeStruct((rows, width), F32),
        in_specs=[VM],
        out_specs=VM,
        scratch_shapes=scatter_scratch(nz, rows, width),
        compiler_params=params(cid, 60 * MIB),
        name="scatter_tokens",
    )(p)


def scatter_and_hand_kernel(nz, kinds, runs, p, up_s, res, *refs):
    count = len(kinds)
    srcs, refs = refs[:count], refs[count:]
    out, up_o, res_o, refs = *refs[:3], refs[3:]
    dsts, refs = refs[:count], refs[count:]
    scratch, hsems, esems, tsems = refs[:5], refs[5:7], refs[7:9], refs[9:11]
    pos = place()
    x, c, z, y = pos
    greet(rank_partners(nz, pos) + group_partners(pos) + [(c != y, at(x, y, z, c))])
    hs = hand_stages(srcs, dsts, kinds, *hsems, nz, pos)
    es = exchange_stages(up_s, up_o, runs, *esems, nz, pos)
    ts = trade_stages(res, res_o, *tsems, pos)
    hs[0]()
    es[0]()
    ts[0]()
    scatter_blocks(nz, pos, p, out, *scratch)
    hs[1]()
    es[1]()
    ts[1]()


def scatter_and_hand(p, up_s, runs, res, arrays, kinds, nz, cid):
    blocks, rows, width = p.shape
    n, part, share = up_s.shape
    return pl.pallas_call(
        functools.partial(scatter_and_hand_kernel, nz, kinds, runs),
        out_shape=[
            jax.ShapeDtypeStruct((rows, width), F32),
            jax.ShapeDtypeStruct((part, n * share), BF),
            jax.ShapeDtypeStruct(res.shape, BF),
        ]
        + hand_shapes(arrays, kinds, nz),
        in_specs=[VM] + [HBM] * (2 + len(arrays)),
        out_specs=[VM] + [HBM] * (2 + len(arrays)),
        scratch_shapes=scatter_scratch(nz, rows, width) + hand_sems(kinds) + exchange_sems(runs, nz) + trade_sems(),
        compiler_params=params(cid, 60 * MIB),
        name="scatter_and_hand",
    )(p, up_s, res, *arrays)


def block_of(x, c, z, y, nz):
    return (x * 2 + c) * 2 * nz + z * 2 + y


def halves(ref, rows, cut=2):
    half = rows // cut
    if half % 16:
        return {1: None, 2: ref}
    return {1: ref.at[pl.ds(half, rows - half)], 2: ref.at[pl.ds(0, half)]}


def sliced_gather(src, dst, runs, sems, nz, pos):
    x, c, z, y = pos
    n = 2 * nz
    me = z * 2 + c
    part = dst.shape[1]
    send1, recv1, send2, recv2 = sems

    def pieces(p):
        if runs is None:
            return [(src.at[p], slice(None))]
        return [(src.at[:, pl.ds(there, size)], pl.ds(here, size)) for there, here, size in runs(p)]

    def row(p, gx, gy):
        return dst.at[block_of(gx, p % 2, p // 2, gy, nz)]

    mine = block_of(x, c, z, y, nz)

    def out(k):
        p = (me + k) % n
        return [
            remote(a, dst.at[mine, :, b], send1.at[p], recv1.at[me], at(x, p % 2, p // 2, y))
            for a, b in pieces(p)
        ]

    local = [pltpu.make_async_copy(a, dst.at[mine, :, b], recv1.at[me]) for a, b in pieces(me)]

    def came(k):
        return (me - k + n) % n

    def arrival(b, sem):
        return remote(b, b, send1.at[me], sem, at(x, 1 - c, z, y))

    def neighbour(m):
        return at(x ^ (m // 2), c, z, y ^ (m % 2))

    def forward(k, m):
        p = came(k)
        b = row(p, x, y)
        slot = (m - 1) * n + p
        return remote(b, b, send2.at[slot], recv2.at[slot], neighbour(m))

    def relay(k, m):
        p = came(k)
        b = halves(row(p, x ^ (m // 2), y ^ (m % 2)), part)[m]
        slot = (1 + m) * n + p
        return b is not None and remote(b, b, send2.at[slot], recv2.at[slot], neighbour(3 - m))

    def first():
        for copy in local:
            copy.start()
        for k in range(1, n):
            for copy in out(k):
                copy.start()

    def step(k):
        p = came(k)
        arrival(row(p, x, y), recv1.at[p]).wait_recv()
        for m in (1, 2):
            forward(k, m).start()

    def pass_on(k):
        p = came(k)
        for m in (1, 2):
            arrival(row(p, x ^ (m // 2), y ^ (m % 2)), recv2.at[(m - 1) * n + p]).wait_recv()
            if relay(k, m):
                relay(k, m).start()

    def last():
        for k in range(n):
            p = came(k)
            parts = halves(row(p, 1 - x, 1 - y), part)
            for m in (1, 2):
                if parts[m] is not None:
                    arrival(parts[m], recv2.at[(1 + m) * n + p]).wait_recv()
        for k in range(n):
            if k:
                p = (me + k) % n
                b = dst.at[mine]
                remote(b, b, send1.at[p], recv1.at[me], at(x, p % 2, p // 2, y)).wait_send()
            for m in (1, 2):
                forward(k, m).wait_send()
                if relay(k, m):
                    relay(k, m).wait_send()

    stages = [functools.partial(step, k) for k in range(n)] + [functools.partial(pass_on, k) for k in range(n)]
    return [first] + stages + [last]


def sliced_sems(nz):
    n = 2 * nz
    return [pltpu.SemaphoreType.DMA((n,))] * 2 + [pltpu.SemaphoreType.DMA((4 * n,))] * 2


def group_gather(src, dst, send, recv, pos):
    x, c, z, y = pos
    rows = src.shape[0]
    local = pltpu.make_async_copy(src, dst.at[x * 2 + y], recv.at[0])

    def there(m):
        return dst.at[(x ^ (m // 2)) * 2 + (y ^ (m % 2))]

    def neighbour(m):
        return at(x ^ (m // 2), c, z, y ^ (m % 2))

    def out(m):
        return remote(src, dst.at[x * 2 + y], send.at[m], recv.at[m], neighbour(m))

    def relay(m):
        b = halves(there(m), rows, 4)[m]
        return b is not None and remote(b, b, send.at[2 + m], recv.at[2 + m], neighbour(3 - m))

    def arrival(b, sem):
        return remote(b, b, send.at[0], sem, at(x, 1 - c, z, y))

    def first():
        local.start()
        for m in (1, 2):
            out(m).start()

    def pass_on():
        for m in (1, 2):
            arrival(there(m), recv.at[m]).wait_recv()
            if relay(m):
                relay(m).start()

    def last():
        local.wait()
        parts = halves(there(3), rows, 4)
        for m in (1, 2):
            if parts[m] is not None:
                arrival(parts[m], recv.at[2 + m]).wait_recv()
            out(m).wait_send()
            if relay(m):
                relay(m).wait_send()

    return [first, pass_on, last]


def full_gather(src, dst, send, recv, nz, pos):
    x, c, z, y = pos
    rows = src.shape[0]
    sib = at(x, 1 - c, z, y)
    mine = dst.at[block_of(x, c, z, y, nz)]

    def row(core, k, m):
        return dst.at[block_of(x ^ (m // 2), core, z + k, y ^ (m % 2), nz)]

    def neighbour(m):
        return at(x ^ (m // 2), c, z, y ^ (m % 2))

    def arrival(b, sem):
        return remote(b, b, send.at[0], recv.at[sem], sib)

    def along(k, sign):
        b = row(c, k, 0)
        return remote(
            b if k else src, b, send.at[(0 if sign > 0 else nz) + z + k], recv.at[z + k], at(x, c, z + sign, y)
        )

    def forward(k, m):
        b = row(c, k, 0)
        return remote(b if k else src, b, send.at[(1 + m) * nz + z + k], recv.at[m * nz + z + k], neighbour(m))

    def relay(k, m):
        b = halves(row(c, k, m), rows)[m]
        if b is None:
            return None
        return remote(b, b, send.at[(3 + m) * nz + z + k], recv.at[(2 + m) * nz + z + k], neighbour(3 - m))

    def side(k, m):
        b = row(c, k, m)
        return remote(b if k or m else src, b, send.at[(6 + m) * nz + z + k], recv.at[(5 + m) * nz + z + k], sib)

    local = pltpu.make_async_copy(src, mine, recv.at[z])

    def first():
        local.start()
        pl.when(z < nz - 1)(along(0, 1).start)
        pl.when(z > 0)(along(0, -1).start)
        for m in (1, 2):
            forward(0, m).start()
        side(0, 0).start()

    def both(k, fn):
        @pl.when(z >= k)
        def _():
            fn(-k)

        if k:

            @pl.when(z + k < nz)
            def _():
                fn(k)

    def step(k):
        def one(k):
            arrival(row(c, k, 0), z + k).wait_recv()
            if k > 0:
                pl.when(z > 0)(along(k, -1).start)
            else:
                pl.when(z < nz - 1)(along(k, 1).start)
            for m in (1, 2):
                forward(k, m).start()
            side(k, 0).start()

        both(k, one)

    def pass_on(k):
        def one(k):
            for m in (1, 2):
                arrival(row(c, k, m), m * nz + z + k).wait_recv()
                if relay(k, m) is not None:
                    relay(k, m).start()
                side(k, m).start()

        both(k, one)

    def diagonal(k):
        def one(k):
            parts = halves(row(c, k, 3), rows)
            for m in (1, 2):
                if parts[m] is not None:
                    arrival(parts[m], (2 + m) * nz + z + k).wait_recv()
            side(k, 3).start()

        both(k, one)

    def last():
        local.wait()

        def one(k):
            for m in range(4):
                arrival(row(1 - c, k, m), (5 + m) * nz + z + k).wait_recv()
                side(k, m).wait_send()
            if k >= 0:
                pl.when(z > 0)(along(k, -1).wait_send)
            if k <= 0:
                pl.when(z < nz - 1)(along(k, 1).wait_send)
            for m in (1, 2):
                forward(k, m).wait_send()
                if relay(k, m) is not None:
                    relay(k, m).wait_send()

        for k in range(nz):
            both(k, one)

    return (
        [first]
        + [functools.partial(step, k) for k in range(1, nz)]
        + [functools.partial(pass_on, k) for k in range(nz)]
        + [functools.partial(diagonal, k) for k in range(nz)]
        + [last]
    )


def full_sems(nz):
    return [pltpu.SemaphoreType.DMA((10 * nz,)), pltpu.SemaphoreType.DMA((9 * nz,))]


def head_runs(nz, cols):
    return lambda p: [
        (block_of(x, p % 2, p // 2, 0, nz) * HD, x * cols // 2, cols // 2) for x in range(2)
    ]


def up_runs(nz, unit):
    return lambda p: [(block_of(x, p % 2, p // 2, 0, nz) * unit, x * 2 * unit, 2 * unit) for x in range(2)]


def qkv_runs(nz, width, cols):
    runs = head_runs(nz, cols)
    return lambda p: [(j * width + there, j * cols + here, size) for j in range(3) for there, here, size in runs(p)]


def fetch_kernel(
    nz, width, cols, x_in, w_qkv, w_down, vec, tab, x_all, qkv_w, down_w, vecs, tab_out, *sems
):
    pos = place()
    x, c, z, y = pos
    fsdp = 2 * nz
    devices = 4 * fsdp
    me = (x * 2 + c) * fsdp + z * 2 + y
    x_sems, qkv_sems, vec_sems, tab_sems, down_sems = sems[:2], sems[2:6], sems[6:8], sems[8:10], sems[10:]
    greet_all(devices, fsdp, me)

    def vec_copy(other):
        return remote(vec, vecs.at[me], vec_sems[0].at[other], vec_sems[1].at[me], (other // fsdp, other % fsdp))

    def each(fn):
        def body(k, _):
            fn((me + k) % devices)
            return 0

        lax.fori_loop(1, devices, body, 0)

    vec_local = pltpu.make_async_copy(vec, vecs.at[me], vec_sems[1].at[me])
    tab_local = pltpu.make_async_copy(tab, tab_out, tab_sems[1].at[0])
    tab_trade = remote(tab, tab_out, tab_sems[0].at[0], tab_sems[1].at[0], at(x, y, z, c))

    gx = line_gather(x_in, x_all, *x_sems, nz, True, pos)
    runs = qkv_runs(nz, width, cols) if len(w_qkv.shape) == 2 else None
    gq = sliced_gather(w_qkv, qkv_w, runs, qkv_sems, nz, pos)
    gx[0]()
    gq[0]()
    gx[1]()
    vec_local.start()
    each(lambda other: vec_copy(other).start())
    pl.when(c == y)(tab_local.start)
    pl.when(c != y)(tab_trade.start)
    gd = group_gather(w_down, down_w, *down_sems, pos)
    for stage in gq[1 : fsdp + 1]:
        stage()
    gx[2]()
    gd[0]()
    for stage in gx[3:-1]:
        stage()
    for stage in gq[fsdp + 1 :]:
        stage()
    gx[-1]()
    for stage in gd[1:]:
        stage()

    def vec_done(other):
        remote(vec, vecs.at[other], vec_sems[0].at[other], vec_sems[1].at[other], at(x, 1 - c, z, y)).wait_recv()
        vec_copy(other).wait_send()

    vec_local.wait()
    each(vec_done)
    tab_local.wait()
    pl.when(c != y)(tab_trade.wait_send)


def fetch(nz, x_in, w_qkv, w_down, part, vec, tab, cid):
    rows, width = x_in.shape
    n = 2 * nz
    devices = 4 * n
    cols = width // n
    shapes = [
        ((n, rows, width), BF),
        ((devices, part, 3 * cols), BF),
        ((4,) + w_down.shape, BF),
        ((devices,) + vec.shape, F32),
        (tab.shape, jnp.int32),
    ]
    return pl.pallas_call(
        functools.partial(fetch_kernel, nz, width, cols),
        out_shape=[jax.ShapeDtypeStruct(s, t) for s, t in shapes],
        in_specs=[HBM] * 5,
        out_specs=[HBM] * 5,
        scratch_shapes=gather_sems(nz)
        + sliced_sems(nz)
        + [pltpu.SemaphoreType.DMA((devices,))] * 2
        + [pltpu.SemaphoreType.DMA((1,))] * 2
        + [pltpu.SemaphoreType.DMA((5,))] * 2,
        compiler_params=params(cid),
        name="fetch",
    )(x_in, w_qkv, w_down, vec, tab)


def hand_stages(srcs, dsts, kinds, send, recv, nz, pos):
    x, c, z, y = pos
    n = 2 * nz
    count = len(kinds)

    def copies(i, m):
        gx, gy = x ^ (m // 2), y ^ (m % 2)
        sem = i * 3 + m - 1
        target = at(gx, c, z, gy)
        if not kinds[i]:
            return [remote(srcs[i].at[gx * 2 + gy], dsts[i].at[m - 1], send.at[sem], recv.at[sem], target)]
        return [
            remote(
                srcs[i].at[block_of(gx, p % 2, p // 2, gy, nz)],
                dsts[i].at[m - 1, p],
                send.at[sem],
                recv.at[sem],
                target,
            )
            for p in range(n)
        ]

    def first():
        for i in range(count):
            for m in (3, 1, 2):
                for copy in copies(i, m):
                    copy.start()

    def last():
        for i in range(count):
            for m in (1, 2, 3):
                sem = i * 3 + m - 1
                there = dsts[i].at[m - 1]
                whole = remote(there, there, send.at[sem], recv.at[sem], at(x, 1 - c, z, y))
                whole.wait_recv()
                whole.wait_send()

    return [first, last]


def hand_shapes(arrays, kinds, nz):
    return [
        jax.ShapeDtypeStruct((3, 2 * nz) + a.shape[1:] if k else (3,) + a.shape[1:], a.dtype)
        for a, k in zip(arrays, kinds)
    ]


def hand_sems(kinds):
    return [pltpu.SemaphoreType.DMA((3 * len(kinds),))] * 2


def exchange_stages(src, dst, runs, send, recv, nz, pos, single=False):
    x, c, z, y = pos
    n = 2 * nz
    me = z * 2 + c

    def give(to, p):
        if runs is None:
            return [(src.at[to], dst.at[p])]
        return [(src.at[to, :, pl.ds(here, size)], dst.at[:, pl.ds(there, size)]) for there, here, size in runs(p)]

    width = len(give(0, 0))

    def move(p):
        return [
            remote(a, b, send.at[p * width + i], recv.at[me * width + i], at(x, p % 2, p // 2, y))
            for i, (a, b) in enumerate(give(p, me))
        ]

    def come(p):
        return [
            remote(b, b, send.at[me * width + i], recv.at[p * width + i], at(x, 1 - c, z, y))
            for i, (_, b) in enumerate(give(me, p))
        ]

    local = [pltpu.make_async_copy(a, b, recv.at[me * width + i]) for i, (a, b) in enumerate(give(me, me))]

    def first():
        for copy in local:
            copy.start()
        for k in range(1, n):
            for copy in move((me + k) % n):
                copy.start()

    def one(p):
        @pl.when(me == p)
        def _():
            for copy in local:
                copy.start()

        @pl.when(me != p)
        def _():
            for copy in move(p):
                copy.start()

    def last():
        for copy in local:
            copy.wait()
        for k in range(1, n):
            for copy in come((me - k + n) % n):
                copy.wait_recv()
            for copy in move((me + k) % n):
                copy.wait_send()

    return [one if single else first, last]


def exchange_sems(runs, nz):
    width = 1 if runs is None else len(runs(0))
    return [pltpu.SemaphoreType.DMA((width * 2 * nz,))] * 2


def exchange_kernel(nz, src, dst, send, recv):
    pos = place()
    greet(rank_partners(nz, pos))
    for stage in exchange_stages(src, dst, None, send, recv, nz, pos):
        stage()


def exchange(a, nz, cid, name):
    return pl.pallas_call(
        functools.partial(exchange_kernel, nz),
        out_shape=jax.ShapeDtypeStruct(a.shape, a.dtype),
        in_specs=[HBM],
        out_specs=HBM,
        scratch_shapes=exchange_sems(None, nz),
        compiler_params=params(cid),
        name=name,
    )(a)


def trade_stages(src, dst, send, recv, pos):
    x, c, z, y = pos
    local = pltpu.make_async_copy(src, dst, recv.at[0])
    trade = remote(src, dst, send.at[0], recv.at[0], at(x, y, z, c))

    def first():
        pl.when(c == y)(local.start)
        pl.when(c != y)(trade.start)

    def last():
        local.wait()
        pl.when(c != y)(trade.wait_send)

    return [first, last]


def trade_sems():
    return [pltpu.SemaphoreType.DMA((1,))] * 2


def finish_kernel(nz, runs, has, *refs):
    grad, small, *refs = refs
    qkv_s = refs.pop(0) if has else None
    grad_out, small_out, *refs = refs
    qkv_o = refs.pop(0) if has else None
    came, send, recv, *sems = refs
    pos = place()
    x, c, z, y = pos
    fsdp = 2 * nz
    devices = 4 * fsdp
    me = (x * 2 + c) * fsdp + z * 2 + y
    es = exchange_stages(qkv_s, qkv_o, runs, *sems[2:], nz, pos) if has else [lambda: None] * 2
    ts = trade_stages(grad, grad_out, *sems[:2], pos)
    greet_all(devices, fsdp, me)

    def each(fn):
        def body(k, _):
            fn((me + k) % devices)
            return 0

        lax.fori_loop(1, devices, body, 0)

    def share(other):
        return remote(small.at[other], came.at[me], send.at[other], recv.at[me], (other // fsdp, other % fsdp))

    es[0]()
    ts[0]()
    each(lambda other: share(other).start())

    def done(other):
        remote(small.at[me], came.at[other], send.at[other], recv.at[other], at(x, 1 - c, z, y)).wait_recv()
        share(other).wait_send()

    each(done)
    came[me] = small[me]
    small_out[...] = jnp.sum(came[...], axis=0)
    ts[1]()
    es[1]()


def finish(grad, small, qkv_s, runs, nz, cid):
    devices = small.shape[0]
    has = qkv_s is not None
    shapes = [jax.ShapeDtypeStruct(grad.shape, grad.dtype), jax.ShapeDtypeStruct(small.shape[1:], F32)]
    if has:
        out_shape = qkv_s.shape if runs is None else (qkv_s.shape[1], qkv_s.shape[0] * qkv_s.shape[2])
        shapes.append(jax.ShapeDtypeStruct(out_shape, BF))
    return pl.pallas_call(
        functools.partial(finish_kernel, nz, runs, has),
        out_shape=shapes,
        in_specs=[HBM, VM] + [HBM] * has,
        out_specs=[HBM, VM] + [HBM] * has,
        scratch_shapes=[pltpu.VMEM(small.shape, F32)]
        + [pltpu.SemaphoreType.DMA((devices,))] * 2
        + trade_sems()
        + (exchange_sems(runs, nz) if has else []),
        compiler_params=params(cid, 32 * MIB),
        name="finish",
    )(*((grad, small, qkv_s) if has else (grad, small)))


def dot(a, b, dims):
    return lax.dot_general(a, b, (dims, ((), ())), preferred_element_type=F32)


NN = ((1,), (0,))
NT = ((1,), (1,))
TN = ((0,), (0,))


def head_number(h, heads, nz, pos):
    x, c, z, y = pos
    return block_of(h // (heads // 2), c, z, h % (heads // 2), nz)


def head_kernel(heads, nz, runs_qkv, runs_up, runs_out, *refs):
    refs = list(refs)

    def take(n):
        got = refs[:n]
        del refs[:n]
        return got

    slopes, valid_in, blocks_in, parents_in = take(4)
    vectors, bias_up = take(8), take(1)[0]
    x_in, cot, w_qkv, w_up, w_out, w_down = take(6)
    joined, mixed, mixed_own, x_own, rows_o, up_bias = take(6)
    a1_o, far_o, cot_all, qkv_o, up_w, out_w, down_w = take(7)
    pack, vecs, tab, tab_in, table, columns, member_s, reach_s, far_s, x_all, a1, qkv_w, bias_s = take(13)
    x_sems, cot_sems, qkv_sems, up_sems, out_sems, down_sems = take(2), take(2), take(4), take(4), take(2), take(2)
    vec_sems, tab_sems, mix_sems, (local_sem, far_sem) = take(2), take(2), take(2), take(2)

    pos = place()
    x, c, z, y = pos
    n = 2 * nz
    devices = 4 * n
    me = block_of(x, c, z, y, nz)
    rank = z * 2 + c
    tree, cols = joined.shape[0], joined.shape[1] // 3
    rows, width = x_own.shape
    part = w_out.shape[0]

    gx = line_gather(x_in, x_all, *x_sems, nz, True, pos)
    gc = line_gather(cot, cot_all, *cot_sems, nz, True, pos)
    gq = sliced_gather(w_qkv, qkv_w, runs_qkv, qkv_sems, nz, pos)
    gu = sliced_gather(w_up, up_w, runs_up, up_sems, nz, pos)
    go = full_gather(w_out, out_w, *out_sems, nz, pos)
    gd = group_gather(w_down, down_w, *down_sems, pos)
    ex = exchange_stages(mixed, mixed_own, runs_out, *mix_sems, nz, pos, single=True)
    ts = trade_stages(tab, tab_in, *tab_sems, pos)
    store_a = pltpu.make_async_copy(a1, a1_o, local_sem.at[0])
    store_q = pltpu.make_async_copy(qkv_w, qkv_o, local_sem.at[1])

    def each(fn):
        def body(k, _):
            fn((me + k) % devices)
            return 0

        lax.fori_loop(1, devices, body, 0)

    def vec_copy(other):
        return remote(pack, vecs.at[me], vec_sems[0].at[other], vec_sems[1].at[me], (other // n, other % n))

    def vec_come(other):
        remote(vecs.at[other], vecs.at[other], vec_sems[0].at[me], vec_sems[1].at[other], at(x, 1 - c, z, y)).wait_recv()

    pack[...] = jnp.zeros_like(pack)
    for i, v in enumerate(vectors):
        pack[i : i + 1, 0:part] = v[...].astype(F32).reshape(1, part)
    lined = pack[...]
    pack[...] = jnp.where(y == 1, pltpu.roll(lined, part, 1), lined)
    for i in range(bias_up.shape[0] // 128):
        pack[8 + i : 9 + i, :] = bias_up[i * 128 : (i + 1) * 128].astype(F32).reshape(1, 128)
    tab[...] = jnp.full_like(tab, -1)
    tab[0:1, :] = valid_in[...]
    tab[1:2, 0 : blocks_in.shape[1]] = blocks_in[...]
    tab[2:3, 0 : parents_in.shape[1]] = parents_in[...]

    greet_all(devices, n, me)
    gx[0]()
    gq[0]()
    ts[0]()
    go[0]()
    gd[0]()
    each(lambda other: vec_copy(other).start())
    vecs[me] = pack[...]
    gx[1]()

    ts[1]()
    seg = lax.broadcasted_iota(jnp.int32, (128, 128), 0)
    lane = lax.broadcasted_iota(jnp.int32, (128, 128), 1)

    def low(v):
        return v.astype(F32).astype(BF)

    parent = low(seg == tab_in[2:3, 0:128])
    above = (parent.astype(F32) + dot(parent, parent, NN)) > 0.5
    ancestor = low(above & (seg != lane))
    owner = low(seg == tab_in[1:2, 0:128])
    spread = low(
        lax.shift_right_logical(lax.broadcasted_iota(jnp.int32, (128, tree), 1), BLK.bit_length() - 1)
        == lax.broadcasted_iota(jnp.int32, (128, tree), 0)
    )
    member = dot(owner, spread, NN)
    valid = tab_in[0:1, :].astype(F32)
    counted = member * valid
    member_s[...] = member.astype(BF)
    reach_s[...] = (2.0 * dot(ancestor, member_s[...], NN) + member).astype(BF)
    lens = jnp.broadcast_to(jnp.sum(counted, axis=1, keepdims=True), (128, 128))
    offset = lax.dot_general(
        ancestor.astype(F32), lens, (TN, ((), ())), precision=lax.Precision.HIGHEST, preferred_element_type=F32
    )
    table[...] = jnp.zeros_like(table)
    table[1:2, :] = valid
    for j in range(tree // 256):
        here = slice(j * 256, (j + 1) * 256)
        earlier = low(
            lax.broadcasted_iota(jnp.int32, (tree, 256), 0) < lax.broadcasted_iota(jnp.int32, (tree, 256), 1) + j * 256
        )
        before = dot(counted.astype(BF), earlier, NN) + offset[:, 0:1]
        table[0:1, here] = jnp.sum(before * member[:, here], axis=0, keepdims=True)
    columns[...] = table[...].T

    step = far_s.shape[2]
    steps = tree // step
    far_store = [
        pltpu.make_async_copy(far_s.at[i % 2], far_o.at[:, pl.ds(i * step, step)], far_sem.at[i % 2]) for i in range(steps)
    ]

    def allow(value, key, query, key_valid):
        return ((value > 1.5) | ((value > 0.5) & (key <= query))) & ((key_valid > 0.5) | (key == query))

    def far_blocks():
        for i in range(steps):
            here = slice(i * step, (i + 1) * step)
            key = lax.broadcasted_iota(jnp.int32, (tree, step), 0)
            query = lax.broadcasted_iota(jnp.int32, (tree, step), 1) + i * step
            allowed = allow(dot(member_s[...], reach_s[:, here], TN), key, query, columns[:, 1:2])
            if i >= 2:
                far_store[i - 2].wait()
            far_s[i % 2] = jnp.where(allowed, columns[:, 0:1], MASKED)
            far_store[i].start()

    def whole_vectors():
        each(vec_come)
        for i in range(devices // 2):
            rows_o[:, i * 128 : (i + 1) * 128] = vecs[2 * i, 0:8] + vecs[2 * i + 1, 0:8]
        per = bias_up.shape[0] // 128
        for g in range(4):
            r = block_of(g // 2, c, z, g % 2, nz)
            for i in range(per):
                up_bias[:, (g * per + i) * 128 : (g * per + i + 1) * 128] = vecs[r, 8 + i : 9 + i]
        bias_s[...] = jnp.zeros_like(bias_s)
        for there, here, size in runs_out(rank):
            there = pl.multiple_of(there, 128)
            bias_s[:, here : here + size] = rows_o[2:3, pl.ds(there, size)]
            bias_s[:, 2 * cols + here : 2 * cols + here + size] = rows_o[3:4, pl.ds(there, size)]

    def norm(b):
        def tile(j, _):
            here = pl.ds(pl.multiple_of(j * 32, 32), 32)
            normed, _ = norm_parts(x_all[b, here].astype(F32))
            a1[b, here] = (normed * rows_o[0:1, :] + rows_o[1:2, :]).astype(BF)
            return 0

        lax.fori_loop(0, rows // 32, tile, 0)

    def norm_at(k, core):
        pl.when(z >= k)(lambda: norm((z - k) * 2 + core))
        if k:
            pl.when(z + k < nz)(lambda: norm((z + k) * 2 + core))

    for stage in gq[1 : n + 1]:
        stage()
    gx[2]()
    go[1]()
    gd[1]()
    far_blocks()
    whole_vectors()
    norm_at(0, c)
    norm_at(1, c)
    gx[3]()
    gu[0]()
    gc[0]()
    norm_at(2, c)
    go[2]()
    for stage in gq[n + 1 : 2 * n + 1]:
        stage()
    gx[4]()
    gc[1]()
    norm_at(3, c)
    go[3]()
    gx[-1]()
    x_own[...] = x_all[rank]
    for k in range(nz):
        norm_at(k, 1 - c)
    store_a.start()
    gq[-1]()
    store_q.start()
    for stage in gu[1 : n + 1]:
        stage()

    def project(i, _):
        here = pl.ds(pl.multiple_of(i * 2 * rows, 2 * rows), 2 * rows)
        tokens = a1[pl.ds(2 * i, 2)].reshape(2 * rows, width)

        def tile(j, _):
            u = pl.ds(pl.multiple_of(j * 256, 256), 256)
            value = dot(tokens, qkv_w[:, :, u].reshape(width, 256), NN) + bias_s[:, u]
            joined[here, u] = value.astype(BF)
            return 0

        lax.fori_loop(0, 3 * cols // 256, tile, 0)
        return 0

    lax.fori_loop(0, nz, project, 0)
    slope = [slopes[head_number(h, heads, nz, pos)] for h in range(heads)]

    gc[2]()
    def attend_step(i, _):
        here = pl.ds(pl.multiple_of(i * step, step), step)
        per = step // rows
        key = lax.broadcasted_iota(jnp.int32, (step, tree), 1)
        query = lax.broadcasted_iota(jnp.int32, (step, tree), 0) + i * step
        allowed = allow(dot(reach_s[:, here], member_s[...], TN), key, query, table[1:2, :])
        gap = jnp.where(allowed, table[0:1, :], MASKED)
        for h in range(heads):
            lanes = slice(h * HD, (h + 1) * HD)
            q = joined[here, lanes] * BF(HD ** (-0.5))
            k = joined[:, cols + h * HD : cols + (h + 1) * HD]
            v = joined[:, 2 * cols + h * HD : 2 * cols + (h + 1) * HD]
            logits = dot(q, k, NT) + slope[h] * gap
            weights = jnp.exp(logits - jnp.max(logits, axis=1, keepdims=True))
            probs = weights * (1.0 / jnp.sum(weights, axis=1, keepdims=True))
            mixed[pl.ds(i * per, per), :, lanes] = dot(probs.astype(BF), v, NN).astype(BF).reshape(per, rows, HD)

        def later(k, fns):
            @pl.when(i == k)
            def _():
                for fn in fns:
                    fn()

        for k in range(steps):
            later(k, [functools.partial(ex[0], p) for p in range(k * per, (k + 1) * per)])
        later(0, go[nz : 2 * nz])
        later(1, gc[3:4] + gu[n + 1 : n + 1 + n // 2])
        later(2, gc[4:5] + gu[n + 1 + n // 2 : 2 * n + 1])
        return 0

    lax.fori_loop(0, steps, attend_step, 0)
    for stage in go[2 * nz : 3 * nz]:
        stage()
    ex[1]()
    for stage in (go[-1], gc[-1], gu[-1], gd[-1]):
        stage()
    each(lambda other: vec_copy(other).wait_send())
    for i in range(max(0, steps - 2), steps):
        far_store[i].wait()
    store_a.wait()
    store_q.wait()


def head_call(slopes, tables, vectors, bias_up, layer_in, cot, w_qkv, w_up, w_out, w_down, heads, nz, cid):
    rows, width = layer_in.shape
    n = 2 * nz
    devices = 4 * n
    tree = n * rows
    cols = heads * HD
    part, unit = w_out.shape[0], w_down.shape[0]
    step = 256
    runs_qkv, runs_up, runs_out = qkv_runs(nz, width, cols), up_runs(nz, unit), head_runs(nz, cols)
    shape = jax.ShapeDtypeStruct
    return pl.pallas_call(
        functools.partial(head_kernel, heads, nz, runs_qkv, runs_up, runs_out),
        out_shape=[
            shape((tree, 3 * cols), BF),
            shape((n, rows, cols), BF),
            shape((rows, width), BF),
            shape((rows, width), BF),
            shape((8, width), F32),
            shape((1, 4 * unit), F32),
            shape((n, rows, width), BF),
            shape((tree, tree), F32),
            shape((n, rows, width), BF),
            shape((devices, part, 3 * cols), BF),
            shape((devices, part, 4 * unit), BF),
            shape((devices, part, width), BF),
            shape((4, unit, width), BF),
        ],
        in_specs=[pl.BlockSpec(memory_space=pltpu.SMEM)] + [VM] * 12 + [HBM] * 6,
        out_specs=[VM] * 6 + [HBM] * 7,
        scratch_shapes=[
            pltpu.VMEM((16, 128), F32),
            pltpu.VMEM((devices, 16, 128), F32),
            pltpu.VMEM((8, tree), jnp.int32),
            pltpu.VMEM((8, tree), jnp.int32),
            pltpu.VMEM((128, tree), F32),
            pltpu.VMEM((tree, 128), F32),
            pltpu.VMEM((128, tree), BF),
            pltpu.VMEM((128, tree), BF),
            pltpu.VMEM((2, tree, step), F32),
            pltpu.VMEM((n, rows, width), BF),
            pltpu.VMEM((n, rows, width), BF),
            pltpu.VMEM((devices, part, 3 * cols), BF),
            pltpu.VMEM((1, 3 * cols), F32),
        ]
        + gather_sems(nz) * 2
        + sliced_sems(nz) * 2
        + full_sems(nz)
        + [pltpu.SemaphoreType.DMA((5,))] * 2
        + [pltpu.SemaphoreType.DMA((devices,))] * 2
        + trade_sems()
        + exchange_sems(runs_out, nz)
        + [pltpu.SemaphoreType.DMA((2,))] * 2,
        compiler_params=params(cid, 60 * MIB),
        name="head",
    )(slopes, *tables, *vectors, bias_up, layer_in, cot, w_qkv, w_up, w_out, w_down)


def scatter_parts(nz, pos, own, other, acc, came, send, recv):
    x, c, z, y = pos
    S, U, D = 0, nz, 3 * nz
    sib = at(x, 1 - c, z, y)
    half = acc.shape[1] // 2

    def f(v):
        return v.astype(F32)

    def swap(t):
        return remote(other(t), acc.at[t], send.at[S + t], recv.at[S + t], sib)

    def piece(ref, t, h):
        return ref.at[t, pl.ds(h * half, half)]

    def rise(t, h):
        sem = U + t * 2 + h
        return remote(piece(acc, t, h), piece(came, t, h), send.at[sem], recv.at[sem], at(x, c, z + 1, y))

    def fall(t, h):
        slot = jnp.where(z - 1 == t, nz, t)
        sem = D + t * 2 + h
        return remote(piece(acc, t, h), piece(came, slot, h), send.at[sem], recv.at[sem], at(x, c, z - 1, y))

    def arrival(slot, h, sem):
        there = piece(came, slot, h)
        return remote(there, there, send.at[S], recv.at[sem], sib)

    def event(t, upward):
        swap(t).wait_recv()
        acc[t] = (f(acc[t]) + f(own(t))).astype(BF)
        for h in range(2):

            @pl.when(z > 0 if upward else z < nz - 1)
            def _():
                arrival(t, h, (U if upward else D) + t * 2 + h).wait_recv()
                here = slice(h * half, (h + 1) * half)
                acc[t, here] = (f(acc[t, here]) + f(came[t, here])).astype(BF)

            (rise if upward else fall)(t, h).start()

    def slot(k):
        for t in range(nz):
            zz = k - t
            if 0 <= zz < t:
                pl.when(z == zz)(functools.partial(event, t, True))
            zz = 2 * (nz - 1) - k - t
            if t < zz < nz:
                pl.when(z == zz)(functools.partial(event, t, False))

    def begin(i):
        pl.when(z == 0)(functools.partial(event, nz - 1 - i, True))
        pl.when(z == nz - 1)(functools.partial(event, i, False))

    def near(i):
        t = nz - 1 - i
        pl.when((z > 0) & (z < nz // 2) & (z < t))(functools.partial(event, t, True))
        pl.when((z >= nz // 2) & (z < nz - 1) & (z > i))(functools.partial(event, i, False))

    def far():
        for i in range(nz - 1):
            t = nz - 1 - i
            pl.when((z >= nz // 2) & (z < t))(functools.partial(event, t, True))
            pl.when((z < nz // 2) & (z > i))(functools.partial(event, i, False))

    def total(out):
        swap(z).wait_recv()
        out[...] = f(acc[z]) + f(own(z))
        for upward, slot, base in ((True, z, U), (False, nz, D)):

            @pl.when(z > 0 if upward else z < nz - 1)
            def _():
                for h in range(2):
                    here = slice(h * half, (h + 1) * half)
                    arrival(slot, h, base + z * 2 + h).wait_recv()
                    out[here, :] += f(came[slot, here])

    def done():
        for t in range(nz):
            swap(t).wait_send()
            for h in range(2):
                pl.when(z < t)(lambda: rise(t, h).wait_send())
                pl.when(z > t)(lambda: fall(t, h).wait_send())

    return swap, slot, begin, near, far, total, done


def reduce_parts(src, mine, near, far, send, recv, lsem, pos):
    x, c, z, y = pos
    half = src.shape[1] // 2

    def f(v):
        return v.astype(F32)

    def share(gx, gy, lower):
        return src.at[gx * 2 + gy, pl.ds(lower * half, half)]

    parts = [(x, y, 0), (x, y, 1), (x, 1 - y, 0), (1 - x, y, 1)]
    loads = [pltpu.make_async_copy(share(*p), mine.at[i], lsem.at[i]) for i, p in enumerate(parts)]
    along_x, along_y = at(1 - x, c, z, y), at(x, c, z, 1 - y)

    def out(i):
        a, b, target = [
            (share(1 - x, y, 0), near.at[0, 0], along_x),
            (share(1 - x, 1 - y, 0), near.at[0, 1], along_x),
            (share(x, 1 - y, 1), near.at[1, 0], along_y),
            (share(1 - x, 1 - y, 1), near.at[1, 1], along_y),
        ][i]
        return remote(a, b, send.at[i], recv.at[i], target)

    def on(i):
        return remote(near.at[i, 1], far.at[i], send.at[4 + i], recv.at[4 + i], [along_y, along_x][i])

    def first():
        for i in (1, 3, 0, 2):
            out(i).start()
        for copy in loads:
            copy.start()

    def second():
        for copy in loads:
            copy.wait()
        for i in range(2):
            out(2 * i + 1).wait_recv()
            near[i, 1] = (f(near[i, 1]) + f(mine[2 + i])).astype(BF)
            on(i).start()

    def total(put):
        for i in range(2):
            out(2 * i).wait_recv()
            on(i).wait_recv()
            put(i, f(mine[i]) + f(near[i, 0]) + f(far[i]))

    def done():
        for i in range(4):
            out(i).wait_send()
        for i in range(2):
            on(i).wait_send()

    return first, second, total, done


def reduce_scratch(rows, width):
    half = rows // 2
    return [
        pltpu.VMEM((4, half, width), BF),
        pltpu.VMEM((2, 2, half, width), BF),
        pltpu.VMEM((2, half, width), BF),
        pltpu.SemaphoreType.DMA((6,)),
        pltpu.SemaphoreType.DMA((6,)),
        pltpu.SemaphoreType.DMA((4,)),
    ]


def tail_kernel(
    heads, nz, runs_up, runs_qkv, slopes, far_in, grad_in, joined, a1_in, mixed_in, qkv_in, branch, upd_in, up_src, down_src,
    middle_in, x_in, whole, grad_in_middle, sums, bias_g,
    down_o, out_o, small_o, bias_o, up_o, qkv_o, branch_all, layer_o, grad_o, grad_s, *refs,
):
    refs = list(refs)

    def take(n):
        got = refs[:n]
        del refs[:n]
        return got

    gap_s, tokens, qkv_w, grad_joined, acc_k, acc_v = take(6)
    upd_own, upd_acc, upd_came, upd_send, upd_recv = take(5)
    att_p, att_acc, att_came, att_send, att_recv = take(5)
    up_refs, down_refs, qkv_refs, out_refs = take(6), take(6), take(6), take(6)
    up_sum, qkv_sum, qkv_g, out_g, res, res_low = take(6)
    grad_low, vec, came, bias_t, bias_c, mixed, middle, x_own, grad_middle = take(9)
    gsems, esems, esems_up, esems_qkv, tsems, tsems_x = take(2), take(2), take(2), take(2), take(2), take(2)
    vsems, bsems = take(2), take(2)
    gap_sem, load_sem = take(2)

    pos = place()
    x, c, z, y = pos
    n = 2 * nz
    tree, cols = mixed_in.shape
    rows, width = branch.shape
    part = up_sum.shape[1]
    rank = z * 2 + c
    step = gap_s.shape[2]

    es = exchange_stages(grad_in, grad_s, None, *esems, nz, pos)
    gb = line_gather(branch, branch_all, *gsems, nz, False, pos)
    up1, up2, up_total, up_done = reduce_parts(up_src, *up_refs, pos)
    down1, down2, down_total, down_done = reduce_parts(down_src, *down_refs, pos)
    qkv1, qkv2, qkv_total, qkv_done = reduce_parts(qkv_g, *qkv_refs, pos)
    out1, out2, out_total, out_done = reduce_parts(out_g, *out_refs, pos)
    upd_swap, _, upd_begin, upd_near, upd_far, upd_total, upd_done = scatter_parts(
        nz, pos, lambda t: upd_own[t], lambda t: upd_in.at[t * 2 + 1 - c], upd_acc, upd_came, upd_send, upd_recv
    )
    att_swap, _, att_begin, att_near, att_far, att_total, att_done = scatter_parts(
        nz, pos, lambda t: att_p[t * 2 + c], lambda t: att_p.at[t * 2 + 1 - c], att_acc, att_came, att_send, att_recv
    )
    ex_up = exchange_stages(up_sum, up_o, runs_up, *esems_up, nz, pos)
    ex_qkv = exchange_stages(qkv_sum, qkv_o, runs_qkv, *esems_qkv, nz, pos)
    home = trade_stages(res_low, layer_o, *tsems, pos)
    home_x = trade_stages(grad_low, grad_o, *tsems_x, pos)
    devices = 4 * n
    me = block_of(x, c, z, y, nz)
    group = x * 2 + y

    def each(fn):
        def body(k, _):
            fn((me + k) % devices)
            return 0

        lax.fori_loop(1, devices, body, 0)

    def share(other):
        tile = vec.at[:, pl.ds(pl.multiple_of(other // 2 * 128, 128), 128)]
        return remote(tile, came.at[me], vsems[0].at[other], vsems[1].at[me], (other // n, other % n))

    def share_come(other):
        there = came.at[other]
        remote(there, there, vsems[0].at[me], vsems[1].at[other], at(x, 1 - c, z, y)).wait_recv()

    def bias_share(m):
        target = at(x ^ (m // 2), c, z, y ^ (m % 2))
        return remote(bias_t.at[group ^ m], bias_c.at[m - 1], bsems[0].at[m - 1], bsems[1].at[m - 1], target)
    loads = [pltpu.make_async_copy(upd_in.at[t * 2 + c], upd_own.at[t], load_sem.at[t]) for t in range(nz)]
    load_w = pltpu.make_async_copy(qkv_in, qkv_w, load_sem.at[nz])
    load_a = pltpu.make_async_copy(a1_in, tokens, load_sem.at[nz + 1])
    load_b = pltpu.make_async_copy(branch_all, tokens, load_sem.at[nz + 2])

    def gap_load(i, slot):
        return pltpu.make_async_copy(
            far_in.at[:, pl.ds(pl.multiple_of(i * step, step), step)], gap_s.at[slot], gap_sem.at[slot]
        )

    greet_all(devices, n, me)
    es[0]()
    up1()
    for t in range(nz):
        upd_swap(t).start()
    gap_load(0, 0).start()
    lates = [
        pltpu.make_async_copy(a, b, load_sem.at[nz + 3 + i])
        for i, (a, b) in enumerate([(mixed_in, mixed), (middle_in, middle), (x_in, x_own), (grad_in_middle, grad_middle)])
    ]
    for copy in loads + [load_w, load_a] + lates:
        copy.start()
    acc_k[...] = jnp.zeros_like(acc_k)
    acc_v[...] = jnp.zeros_like(acc_v)
    for copy in loads:
        copy.wait()
    es[1]()
    gb[0]()
    gb[1]()
    for i in range(nz - 1):
        upd_begin(i)

    steps = tree // step
    slope = [slopes[head_number(h, heads, nz, pos)] for h in range(heads)]

    def attend_step(i, _):
        slot = i % 2
        gap_load(i, slot).wait()
        pl.when(i + 1 < steps)(lambda: gap_load(i + 1, 1 - slot).start())
        gap = gap_s[slot]
        here = pl.ds(pl.multiple_of(i * step, step), step)
        per = step // rows
        grads = grad_s[pl.ds(i * per, per)].reshape(step, cols)
        for h in range(heads):
            lane = slice(h * HD, (h + 1) * HD)
            q = joined[here, lane]
            scale = BF(HD ** (-0.5))
            k = joined[:, cols + h * HD : cols + (h + 1) * HD]
            v = joined[:, 2 * cols + h * HD : 2 * cols + (h + 1) * HD]
            g = grads[:, lane]
            logits = dot(k, q * scale, NT) + slope[h] * gap
            weights = jnp.exp(logits - jnp.max(logits, axis=0, keepdims=True))
            probs = weights * (1.0 / jnp.sum(weights, axis=0, keepdims=True))
            grad_probs = dot(v, g * scale, NT)
            delta = jnp.sum(probs * grad_probs, axis=0, keepdims=True)
            grad_raw = (probs * (grad_probs - delta)).astype(BF)
            acc_v[:, lane] += dot(probs.astype(BF), g, NN)
            acc_k[:, lane] += dot(grad_raw, q, NN)
            grad_joined[here, lane] = dot(grad_raw, k, TN).astype(BF)

        def later(k, fns):
            @pl.when(i == k)
            def _():
                for fn in fns:
                    fn()

        later(1, [gb[2]])
        later(2, [up2])
        later(3, [down1, lambda: upd_near(0)])
        return 0

    lax.fori_loop(0, steps, attend_step, 0)
    grad_joined[:, cols : 2 * cols] = acc_k[...].astype(BF)
    grad_joined[:, 2 * cols :] = acc_v[...].astype(BF)
    load_w.wait()

    def put_ranks(dest):
        def put(lower, value):
            dest[pl.ds(lower * nz, nz)] = value.astype(BF).reshape(nz, part, -1)

        return put

    def back(t):
        here = pl.ds(pl.multiple_of(t * 2 * rows, 2 * rows), 2 * rows)

        def tile(j, _):
            w = pl.ds(pl.multiple_of(j * 512, 512), 512)
            att_p[pl.ds(t * 2, 2), :, w] = dot(grad_joined[here, :], qkv_w[w, :], NT).astype(BF).reshape(2, rows, 512)
            return 0

        lax.fori_loop(0, width // 512, tile, 0)
        att_swap(t).start()

    for i in range(nz):
        back(jnp.where(z < nz // 2, nz - 1 - i, i))
        if i:
            att_begin(i - 1)
    load_a.wait()
    blocks = 256 // part

    def qkv_tile(j, _):
        w = pl.ds(pl.multiple_of(j * 256, 256), 256)
        value = dot(tokens[:, :, w].reshape(tree, 256), grad_joined[...], TN).astype(BF)
        for i in range(blocks):
            r = j * blocks + i
            d, f = r // n, r % n
            p = f // 2 * 2 + d % 2
            qkv_g[d // 2 * 2 + f % 2, pl.ds(pl.multiple_of(p * part, part), part), :] = value[i * part : (i + 1) * part]
        return 0

    col = jnp.sum(grad_joined[...].astype(F32), axis=0, keepdims=True)
    vec[...] = jnp.zeros_like(vec)
    for there, here, size in head_runs(nz, cols)(rank):
        there = pl.multiple_of(there, 128)
        vec[2:3, pl.ds(there, size)] = col[:, here : here + size]
        vec[3:4, pl.ds(there, size)] = col[:, 2 * cols + here : 2 * cols + here + size]
    for i, k in enumerate((2, 0, 1, 3)):
        vec[4 + i : 5 + i, :] = sums[k : k + 1, :]
    vec[9:10, :] = jnp.broadcast_to(jnp.sum(sums[4:5, :], axis=1, keepdims=True), (1, width))
    bias_t[...] = jnp.zeros_like(bias_t)
    per = bias_g.shape[1] // 512
    for g in range(4):
        for i in range(per):
            bias_t[g, i : i + 1, :] = bias_g[:, (g * per + i) * 128 : (g * per + i + 1) * 128]
    for m in (1, 2, 3):
        bias_share(m).start()
    gb[3]()
    lax.fori_loop(0, width // 256, qkv_tile, 0)
    qkv1()
    upd_near(1)
    gb[4]()
    up_total(put_ranks(up_sum))
    ex_up[0]()
    upd_far()
    att_near(0)
    att_near(1)
    qkv2()
    att_far()
    down2()
    for stage in gb[5:]:
        stage()
    load_b.start()
    load_b.wait()
    for copy in lates:
        copy.wait()

    def out_tile(j, _):
        w = pl.ds(pl.multiple_of(j * 512, 512), 512)
        value = dot(mixed[...], tokens[:, :, w].reshape(tree, 512), TN).astype(BF)
        out_g[:, :, w] = value.reshape(4, cols // 4, 512)
        return 0

    lax.fori_loop(0, width // 512, out_tile, 0)
    out1()
    qkv_total(put_ranks(qkv_sum))
    ex_qkv[0]()
    att_total(res)

    def norm(j, _):
        here = pl.ds(pl.multiple_of(j * 32, 32), 32)
        normed, inverse = norm_parts(x_own[here, :].astype(F32))
        value = res[here, :]
        through = grad_middle[here, :] + norm_back(value * whole[0:1, :], normed, inverse)
        grad_low[here, :] = through.astype(BF)
        vec[0:1, :] += jnp.sum(value * normed, axis=0, keepdims=True)
        vec[1:2, :] += jnp.sum(value, axis=0, keepdims=True)
        return 0

    lax.fori_loop(0, rows // 32, norm, 0)
    home_x[0]()
    upd_total(res)
    res[...] += middle[...] + whole[7:8, :]
    res_low[...] = res[...].astype(BF)
    home[0]()
    square = jnp.sum(jnp.sum(res[...] * res[...], axis=0, keepdims=True), axis=1, keepdims=True)
    vec[8:9, :] = jnp.broadcast_to(square, (1, width))
    each(lambda other: share(other).start())
    out2()

    def put_down(lower, value):
        half = value.shape[0]
        down_o[pl.ds(lower * half, half), :] = value

    down_total(put_down)
    def put_out(lower, value):
        half = value.shape[0]
        out_o[pl.ds(lower * half, half), :] = value

    out_total(put_out)
    each(share_come)
    came[me] = vec[:, pl.ds(pl.multiple_of(me // 2 * 128, 128), 128)]
    summed = jnp.sum(came[...], axis=0)
    small_o[...] = jnp.where(y == 1, pltpu.roll(summed, 64, 1), summed)
    for m in (1, 2, 3):
        bias_share(m).wait_recv()
    bias_o[...] = bias_t[group] + jnp.sum(bias_c[...], axis=0)
    ex_up[1]()
    home[1]()
    home_x[1]()
    ex_qkv[1]()
    each(lambda other: share(other).wait_send())
    for m in (1, 2, 3):
        bias_share(m).wait_send()
    for fn in (up_done, down_done, qkv_done, out_done, upd_done, att_done):
        fn()


def tail_call(
    slopes, far_t, grad, joined, a1, mixed, qkv_w, branch, upd, up_g, down_g, middle, x_own, whole, grad_middle, sums, bias_g,
    runs, heads, nz, cid,
):
    tree, cols = mixed.shape
    rows, width = branch.shape
    n = 2 * nz
    part = width // (4 * n)
    unit = down_g.shape[1]
    step = 256
    runs_up, runs_qkv = runs
    shape = jax.ShapeDtypeStruct

    def scatter_refs(own):
        return [
            pltpu.VMEM((own, rows, width), BF),
            pltpu.VMEM((nz, rows, width), BF),
            pltpu.VMEM((nz + 1, rows, width), BF),
            pltpu.SemaphoreType.DMA((5 * nz,)),
            pltpu.SemaphoreType.DMA((5 * nz,)),
        ]

    return pl.pallas_call(
        functools.partial(tail_kernel, heads, nz, runs_up, runs_qkv),
        out_shape=[
            shape((unit, width), F32),
            shape((part, width), F32),
            shape((16, 128), F32),
            shape((8, 128), F32),
            shape((part, 4 * n * unit), BF),
            shape((part, 3 * width), BF),
            shape((n, rows, width), BF),
            shape((rows, width), BF),
            shape((rows, width), BF),
        ],
        in_specs=[pl.BlockSpec(memory_space=pltpu.SMEM), HBM, HBM, VM] + [HBM] * 9 + [VM, HBM, VM, VM],
        out_specs=[VM] * 4 + [HBM] * 5,
        scratch_shapes=[
            pltpu.VMEM((n, rows, cols), BF),
            pltpu.VMEM((2, tree, step), F32),
            pltpu.VMEM((n, rows, width), BF),
            pltpu.VMEM((width, 3 * cols), BF),
            pltpu.VMEM((tree, 3 * cols), BF),
            pltpu.VMEM((tree, cols), F32),
            pltpu.VMEM((tree, cols), F32),
        ]
        + scatter_refs(nz)
        + scatter_refs(n)
        + reduce_scratch(n * part, 4 * unit)
        + reduce_scratch(unit, width)
        + reduce_scratch(n * part, 3 * cols)
        + reduce_scratch(part, width)
        + [
            pltpu.VMEM((n, part, 4 * unit), BF),
            pltpu.VMEM((n, part, 3 * cols), BF),
            pltpu.VMEM((4, n * part, 3 * cols), BF),
            pltpu.VMEM((4, part, width), BF),
            pltpu.VMEM((rows, width), F32),
            pltpu.VMEM((rows, width), BF),
            pltpu.VMEM((rows, width), BF),
            pltpu.VMEM((16, width), F32),
            pltpu.VMEM((4 * n, 16, 128), F32),
            pltpu.VMEM((4, 8, 128), F32),
            pltpu.VMEM((3, 8, 128), F32),
            pltpu.VMEM((tree, cols), BF),
            pltpu.VMEM((rows, width), F32),
            pltpu.VMEM((rows, width), BF),
            pltpu.VMEM((rows, width), F32),
        ]
        + gather_sems(nz)
        + exchange_sems(None, nz)
        + exchange_sems(runs_up, nz)
        + exchange_sems(runs_qkv, nz)
        + trade_sems() * 2
        + [pltpu.SemaphoreType.DMA((4 * n,))] * 2
        + [pltpu.SemaphoreType.DMA((3,))] * 2
        + [pltpu.SemaphoreType.DMA((2,)), pltpu.SemaphoreType.DMA((nz + 7,))],
        compiler_params=params(cid, 63 * MIB),
        name="tail",
    )(
        slopes, far_t, grad, joined, a1, mixed, qkv_w, branch, upd, up_g, down_g,
        middle, x_own, whole, grad_middle, sums, bias_g,
    )


def gelu_and_slope(value):
    normal = 0.5 + 0.5 * lax.erf(value * math.sqrt(0.5))
    density = jnp.exp(-0.5 * value * value) * (1.0 / math.sqrt(2.0 * math.pi))
    return value * normal, normal + value * density


def mlp_kernel(
    nz, mixed, x_own, whole, out_in, cot_in, up_in, down_in, bias,
    middle, grad_middle, grad_branch, grad_mixed, sums, bias_g, upd_out, up_out, down_out,
    mlp, cot, up_w, down_w, p, upd, up_g, down_g, out_w, active, gh, grad, acc, came, gsend, grecv, ssend, srecv, lsem,
):
    pos = place()
    x, c, z, y = pos
    blocks, rows, width = mlp.shape
    units = active.shape[1]
    pair = 2 * rows
    me = z * 2 + c
    sib = at(x, 1 - c, z, y)
    up_dev, dn_dev = at(x, c, z + 1, y), at(x, c, z - 1, y)
    UP, DN, SU, SD = 0, nz, 2 * nz, 3 * nz
    part = out_w.shape[1]

    def f(v):
        return v.astype(F32)

    loads = [
        pltpu.make_async_copy(a, b, lsem.at[i])
        for i, (a, b) in enumerate([(out_in, out_w), (up_in, up_w), (cot_in, cot), (down_in, down_w)])
    ]

    def rank_rows(r):
        d, f = r // blocks, r % blocks
        return up_out.at[d // 2 * 2 + f % 2, pl.ds((f // 2 * 2 + d % 2) * part, part)]

    stores = [
        [pltpu.make_async_copy(upd, upd_out, lsem.at[4])],
        [
            pltpu.make_async_copy(up_g.at[pl.ds(r * part, part)], rank_rows(r), lsem.at[6 + r])
            for r in range(4 * blocks)
        ],
        [pltpu.make_async_copy(down_g, down_out, lsem.at[5])],
    ]

    def store(i):
        for copy in stores[i]:
            copy.start()


    def block(b, sem, target):
        return remote(mlp.at[b], mlp.at[b], gsend.at[sem], grecv.at[sem], target)

    def up(d):
        return block((z - d) * 2 + c, UP + d, up_dev)

    def dn(d):
        return block((z + d) * 2 + c, DN + d, dn_dev)

    def side(d, below):
        return block(jnp.where(below, z - d, z + d) * 2 + c, jnp.where(below, SU, SD) + d, sib)

    def turn(i):
        both = jnp.minimum(z, nz - 1 - z)
        two = i <= 2 * both
        d = jnp.where(two, (i + 1) // 2, i - both)
        below = jnp.where(two, i % 2 == 1, z > nz - 1 - z)
        return d, below

    def arrive(i):
        if i == 0:
            block(z * 2 + 1 - c, SU, sib).wait_recv()
            return z
        d, below = turn(i)
        zi = jnp.where(below, z - d, z + d)
        block(zi * 2 + c, jnp.where(below, UP, DN) + d - 1, sib).wait_recv()
        pl.when(below & (z < nz - 1))(lambda: up(d).start())
        pl.when(jnp.logical_not(below) & (z > 0))(lambda: dn(d).start())
        side(d, below).start()
        block(zi * 2 + 1 - c, jnp.where(below, SU, SD) + d, sib).wait_recv()
        return zi

    swap, slot, _, _, _, total, done = scatter_parts(
        nz, pos, lambda t: p[t * 2 + c], lambda t: p.at[t * 2 + 1 - c], acc, came, ssend, srecv
    )

    def at_rows(ref, zi):
        return ref[pl.ds(zi * 2, 2)].reshape(pair, width)

    def hidden_part(zi):
        here = pl.ds(pl.multiple_of(zi * pair, pair), pair)

        def tile(j, _):
            u = pl.ds(pl.multiple_of(j * 256, 256), 256)
            value = dot(at_rows(mlp, zi), up_w[:, u], NN) + bias[:, u]
            grad_act = dot(at_rows(cot, zi), down_w[u, :], NT)
            act, slope = gelu_and_slope(value)
            low = (grad_act * slope).astype(BF)
            active[here, u] = act.astype(BF)
            gh[here, u] = low
            bias_g[:, u] += jnp.sum(f(low), axis=0, keepdims=True)
            return 0

        lax.fori_loop(0, units // 256, tile, 0)

        def back(j, _):
            w = pl.ds(pl.multiple_of(j * 512, 512), 512)
            p[pl.ds(zi * 2, 2), :, w] = dot(gh[here, :], up_w[w, :], NT).astype(BF).reshape(2, rows, 512)
            return 0

        lax.fori_loop(0, width // 512, back, 0)

    def forward_part(zi):
        here = pl.ds(pl.multiple_of(zi * pair, pair), pair)

        def tile(j, _):
            w = pl.ds(pl.multiple_of(j * 512, 512), 512)
            upd[pl.ds(zi * 2, 2), :, w] = dot(active[here, :], down_w[:, w], NN).astype(BF).reshape(2, rows, 512)
            return 0

        lax.fori_loop(0, width // 512, tile, 0)

    def up_grads(first, count):
        def tile(j, _):
            w = pl.ds(pl.multiple_of(j * 256, 256), 256)
            up_g[w, :] = dot(mlp[:, :, w].reshape(blocks * rows, 256), gh[...], TN).astype(BF)
            return 0

        lax.fori_loop(first, first + count, tile, 0)

    def down_grads():
        def tile(j, _):
            u = pl.ds(pl.multiple_of(j * 256, 256), 256)
            down_g[u, :] = dot(active[:, u], cot[...].reshape(blocks * rows, width), TN).astype(BF)
            return 0

        lax.fori_loop(0, units // 256, tile, 0)

    def project():
        def tile(j, _):
            w = pl.ds(pl.multiple_of(j * 512, 512), 512)
            branch = dot(mixed[...], out_w[:, :, w].reshape(width, 512), NN) + whole[4:5, w]
            sums[4:5, w] = jnp.sum(branch * branch, axis=0, keepdims=True)
            middle[:, w] = f(x_own[:, w]) + branch
            return 0

        lax.fori_loop(0, width // 512, tile, 0)

        def norm(j, _):
            here = pl.ds(pl.multiple_of(j * 32, 32), 32)
            normed, _ = norm_parts(middle[here, :])
            mlp[me, here] = (normed * whole[5:6, :] + whole[6:7, :]).astype(BF)
            return 0

        lax.fori_loop(0, rows // 32, norm, 0)

    def finish_rows():
        def norm(j, _):
            here = pl.ds(pl.multiple_of(j * 32, 32), 32)
            normed, inverse = norm_parts(middle[here, :])
            value, own = grad[here, :], f(cot[me, here])
            through = own + norm_back(value * whole[5:6, :], normed, inverse)
            low = through.astype(BF)
            grad_middle[here, :] = through
            grad_branch[here, :] = low
            for i, v in enumerate((value * normed, value, f(low), own)):
                sums[i : i + 1, :] += jnp.sum(v, axis=0, keepdims=True)
            return 0

        lax.fori_loop(0, rows // 32, norm, 0)
        each = 256 // part

        def tile(j, _):
            value = dot(grad_branch[...], out_w[pl.ds(j * each, each)].reshape(256, width), NT).astype(BF)
            for i in range(2):
                r = j * each + i * (each // 2)
                d, fs = r // blocks, r % blocks
                grad_mixed[fs // 2 * 2 + d % 2, :, pl.ds(pl.multiple_of(d // 2 * 128, 128), 128)] = value[
                    :, i * 128 : (i + 1) * 128
                ]
            return 0

        lax.fori_loop(0, width // 256, tile, 0)

    for copy in loads:
        copy.start()
    bias_g[...] = jnp.zeros_like(bias_g)
    sums[...] = jnp.zeros_like(sums)
    greet(line_partners(nz, pos))
    loads[0].wait()
    project()
    pl.when(z < nz - 1)(up(0).start)
    pl.when(z > 0)(dn(0).start)
    side(0, z >= 0).start()
    for copy in loads[1:]:
        copy.wait()
    slots = 2 * nz - 1
    tiles = width // 256
    for s in range(slots):
        if s < nz:
            zi = arrive(s)
            hidden_part(zi)
            swap(zi).start()
        slot(s)
        if s < nz:
            forward_part(zi)
        if s == nz - 1:
            store(0)
            down_grads()
            store(2)
        elif s == nz:
            up_grads(0, tiles // 2)
        elif s == nz + 1:
            up_grads(tiles // 2, tiles - tiles // 2)
            store(1)
    total(grad)
    finish_rows()
    for copies in stores:
        for copy in copies:
            copy.wait()
    side(0, z >= 0).wait_send()
    pl.when(z < nz - 1)(up(0).wait_send)
    pl.when(z > 0)(dn(0).wait_send)
    for k in range(1, nz):

        @pl.when(z >= k)
        def _():
            pl.when(z < nz - 1)(up(k).wait_send)
            side(k, z >= 0).wait_send()

        @pl.when(z + k < nz)
        def _():
            pl.when(z > 0)(dn(k).wait_send)
            side(k, z < 0).wait_send()

    done()


def mlp_bytes(nz, rows, width, units):
    tree = 2 * nz * rows
    kept = 4 * tree * width + 4 * units * width + 2 * tree * units + 2 * nz * rows * width + width * width
    return 2 * kept + 14 * rows * width


def mlp_call(mixed, x_own, whole, out_w, cot, up_w, down_w, bias, nz, cid):
    rows, width = x_own.shape
    units = down_w.shape[0]
    n = 2 * nz
    shape = jax.ShapeDtypeStruct
    return pl.pallas_call(
        functools.partial(mlp_kernel, nz),
        out_shape=[
            shape((rows, width), F32),
            shape((rows, width), F32),
            shape((rows, width), BF),
            shape((n, rows, width // n), BF),
            shape((8, width), F32),
            shape((1, units), F32),
            shape((n, rows, width), BF),
            shape((4, width // 4, units), BF),
            shape((units, width), BF),
        ],
        in_specs=[VM] * 3 + [HBM] * 4 + [VM],
        out_specs=[VM] * 6 + [HBM] * 3,
        scratch_shapes=[
            pltpu.VMEM((n, rows, width), BF),
            pltpu.VMEM((n, rows, width), BF),
            pltpu.VMEM((width, units), BF),
            pltpu.VMEM((units, width), BF),
            pltpu.VMEM((n, rows, width), BF),
            pltpu.VMEM((n, rows, width), BF),
            pltpu.VMEM((width, units), BF),
            pltpu.VMEM((units, width), BF),
            pltpu.VMEM(out_w.shape, BF),
            pltpu.VMEM((n * rows, units), BF),
            pltpu.VMEM((n * rows, units), BF),
            pltpu.VMEM((rows, width), F32),
            pltpu.VMEM((nz, rows, width), BF),
            pltpu.VMEM((nz + 1, rows, width), BF),
        ]
        + gather_sems(nz)
        + [pltpu.SemaphoreType.DMA((5 * nz,))] * 2
        + [pltpu.SemaphoreType.DMA((6 + 4 * n,))],
        compiler_params=params(cid, 63 * MIB),
        name="mlp",
    )(mixed, x_own, whole, out_w, cot, up_w, down_w, bias)


def attend_kernel(
    heads, nz, unit, slopes, far, joined_q, joined, cot, w_up, w_out, out, cot_all, up_w, out_w, *sems
):
    cols = heads * HD
    step, steps = pl.program_id(0), pl.num_programs(0)
    pos = place()
    n = 2 * nz
    gc = line_gather(cot, cot_all, *sems[:2], nz, True, pos)
    gu = sliced_gather(w_up, up_w, up_runs(nz, unit), sems[2:6], nz, pos)
    go = full_gather(w_out, out_w, *sems[6:8], nz, pos)

    @pl.when(step == 0)
    def _():
        x, c, z, y = pos
        greet(rank_partners(nz, pos) + group_partners(pos) + [(c != y, at(x, y, z, c))])
        gc[0]()
        gu[0]()
        go[0]()

    @pl.when(step == 1)
    def _():
        for stage in go[1:nz]:
            stage()

    @pl.when(step == 2)
    def _():
        for stage in gu[1 : n + 1]:
            stage()
        gc[1]()

    gap = far[...]
    for h in range(heads):
        q = joined_q[:, h * HD : (h + 1) * HD]
        k = joined[:, cols + h * HD : cols + (h + 1) * HD]
        v = joined[:, 2 * cols + h * HD : 2 * cols + (h + 1) * HD]
        logits = dot(q, k, NT) * HD ** (-0.5) + slopes[h] * gap
        weights = jnp.exp(logits - jnp.max(logits, axis=1, keepdims=True))
        probs = weights * (1.0 / jnp.sum(weights, axis=1, keepdims=True))
        out[:, h * HD : (h + 1) * HD] = dot(probs.astype(BF), v, NN).astype(BF)

    @pl.when(step == steps - 1)
    def _():
        for stage in go[nz : 2 * nz]:
            stage()
        ahead, later = gc[2:-1], gu[n + 1 : -1]
        for i, stage in enumerate(ahead):
            stage()
            for other in later[i * n // len(ahead) : (i + 1) * n // len(ahead)]:
                other()
        for stage in go[2 * nz :]:
            stage()
        gc[-1]()
        gu[-1]()


def attend(slopes, far, joined, cot, w_up, w_out, unit, heads, nz, cid):
    tree = far.shape[0]
    cols = heads * HD
    rows = min(256, max(128, 2**18 // tree))
    block, width = cot.shape
    part = w_up.shape[0]
    n = 2 * nz
    shapes = [(tree, cols), (n, block, width), (4 * n, part, 4 * unit), (4 * n, part, width)]
    return pl.pallas_call(
        functools.partial(attend_kernel, heads, nz, unit),
        out_shape=[jax.ShapeDtypeStruct(s, BF) for s in shapes],
        grid=(tree // rows,),
        in_specs=[
            pl.BlockSpec(memory_space=pltpu.SMEM),
            pl.BlockSpec((rows, tree), lambda i: (i, 0)),
            pl.BlockSpec((rows, 3 * cols), lambda i: (i, 0)),
            pl.BlockSpec((tree, 3 * cols), lambda i: (0, 0)),
            HBM,
            HBM,
            HBM,
        ],
        out_specs=[pl.BlockSpec((rows, cols), lambda i: (i, 0)), HBM, HBM, HBM],
        scratch_shapes=gather_sems(nz) + sliced_sems(nz) + full_sems(nz),
        compiler_params=params(cid, 56 * MIB),
        name="attend",
    )(slopes, far, joined, joined, cot, w_up, w_out)


def attend_back_kernel(heads, nz, kinds, slopes, far, joined_q, joined, grad, branch, part_sums, *refs):
    count = len(kinds)
    srcs, refs = refs[:count], refs[count:]
    out_q, out_k, out_v, branch_all, update, refs = *refs[:5], refs[5:]
    dsts, refs = refs[:count], refs[count:]
    acc_k, acc_v, p, refs = *refs[:3], refs[3:]
    scratch, gsems, hsems, psem = refs[:5], refs[5:7], refs[7:9], refs[9]
    cols = heads * HD
    step = pl.program_id(0)
    pos = place()
    gb = line_gather(branch, branch_all, *gsems, nz, False, pos)
    hs = hand_stages(srcs, dsts, kinds, *hsems, nz, pos)
    load = pltpu.make_async_copy(part_sums, p, psem.at[0])

    @pl.when(step == 0)
    def _():
        acc_k[...] = jnp.zeros_like(acc_k)
        acc_v[...] = jnp.zeros_like(acc_v)
        greet(line_partners(nz, pos) + group_partners(pos))
        hs[0]()
        gb[0]()
        gb[1]()
        load.start()

    @pl.when(step == 3)
    def _():
        gb[2]()

    gap = far[...]
    for h in range(heads):
        here = slice(h * HD, (h + 1) * HD)
        q = joined_q[:, here]
        k = joined[:, cols + h * HD : cols + (h + 1) * HD]
        v = joined[:, 2 * cols + h * HD : 2 * cols + (h + 1) * HD]
        g = grad[:, here]
        logits = dot(k, q, NT) * HD ** (-0.5) + slopes[h] * gap
        weights = jnp.exp(logits - jnp.max(logits, axis=0, keepdims=True))
        probs = weights * (1.0 / jnp.sum(weights, axis=0, keepdims=True))
        grad_probs = dot(v, g, NT)
        delta = jnp.sum(probs * grad_probs, axis=0, keepdims=True)
        grad_raw = (probs * (grad_probs - delta) * HD ** (-0.5)).astype(BF)
        acc_v[:, here] += dot(probs.astype(BF), g, NN)
        acc_k[:, here] += dot(grad_raw, q, NN)
        out_q[:, here] = dot(grad_raw, k, TN).astype(BF)

    @pl.when(step == pl.num_programs(0) - 1)
    def _():
        out_k[...] = acc_k[...].astype(BF)
        out_v[...] = acc_v[...].astype(BF)
        for stage in gb[3:]:
            stage()
        load.wait()
        scatter_blocks(nz, pos, p, update, *scratch)
        hs[1]()


def attend_back(slopes, far_t, joined, grad, branch, part_sums, arrays, kinds, heads, nz, cid):
    tree = far_t.shape[0]
    cols = heads * HD
    rows = min(256, max(128, 2**18 // tree))
    block, width = branch.shape
    full = pl.BlockSpec((tree, cols), lambda i: (0, 0))
    part = pl.BlockSpec((rows, cols), lambda i: (i, 0))
    return pl.pallas_call(
        functools.partial(attend_back_kernel, heads, nz, kinds),
        out_shape=[jax.ShapeDtypeStruct((tree, cols), BF)] * 3
        + [jax.ShapeDtypeStruct((2 * nz, block, width), BF), jax.ShapeDtypeStruct((block, width), F32)]
        + hand_shapes(arrays, kinds, nz),
        grid=(tree // rows,),
        in_specs=[
            pl.BlockSpec(memory_space=pltpu.SMEM),
            pl.BlockSpec((tree, rows), lambda i: (0, i)),
            pl.BlockSpec((rows, 3 * cols), lambda i: (i, 0)),
            pl.BlockSpec((tree, 3 * cols), lambda i: (0, 0)),
            part,
            HBM,
            HBM,
        ]
        + [HBM] * len(arrays),
        out_specs=[part, full, full, HBM, pl.BlockSpec((block, width), lambda i: (0, 0))] + [HBM] * len(arrays),
        scratch_shapes=[pltpu.VMEM((tree, cols), F32)] * 2
        + [pltpu.VMEM((2 * nz, block, width), BF)]
        + scatter_scratch(nz, block, width)
        + gather_sems(nz)
        + hand_sems(kinds)
        + [pltpu.SemaphoreType.DMA((1,))],
        compiler_params=params(cid, 62 * MIB),
        name="attend_back",
    )(slopes, far_t, joined, joined, grad, branch, part_sums, *arrays)


def norm_parts(values):
    center = values - jnp.mean(values, axis=-1, keepdims=True)
    inverse = lax.rsqrt(jnp.mean(center * center, axis=-1, keepdims=True) + EPSILON)
    return (center * inverse, inverse)


def norm_back(grad_normed, normed, inverse):
    mean_grad = jnp.mean(grad_normed, axis=-1, keepdims=True)
    mean_cross = jnp.mean(grad_normed * normed, axis=-1, keepdims=True)
    return inverse * (grad_normed - mean_grad - normed * mean_cross)


def tree_tables(parents, seg_blocks, valid):
    segments = parents.shape[0]
    seg_tokens = jnp.broadcast_to(seg_blocks[:, None], (seg_blocks.shape[0], BLK)).reshape(-1)
    labels = jnp.arange(segments, dtype=jnp.int32)
    member = (seg_tokens[:, None] == labels[None, :]).astype(jnp.int32)
    counted = member * valid[:, None]
    before = jnp.cumsum(counted, axis=0) - counted
    rank = jnp.sum(before * member, axis=1)
    seg_len = jnp.sum(counted, axis=0)
    picked = (parents[:, None] == labels[None, :]).astype(jnp.int32)
    grand = jnp.sum(picked * parents[None, :], axis=1)
    ancestor = ((labels[None, :] == parents[:, None]) | (labels[None, :] == grand[:, None])) & (
        labels[None, :] != labels[:, None]
    )
    offset = jnp.sum(ancestor.astype(jnp.int32) * seg_len[None, :], axis=1)
    position = jnp.sum(member * offset[None, :], axis=1) + rank
    return (seg_tokens, position, ancestor.astype(jnp.float32))


def allowed_mask(seg, index, valid, ancestor):
    labels = jnp.arange(ancestor.shape[0], dtype=jnp.int32)
    member = (seg[:, None] == labels[None, :]).astype(jnp.float32)
    reach = jnp.dot(jnp.dot(member, ancestor), member.T) > 0.5
    causal = (seg[:, None] == seg[None, :]) & (index[None, :] <= index[:, None])
    visible = (valid[None, :] == 1) | (index[None, :] == index[:, None])
    return (reach | causal) & visible


def gelu_exact(value):
    return jax.nn.gelu(value, approximate=False)


def mm(spec, a, b):
    return jnp.einsum(spec, a, b, preferred_element_type=F32)


def padded(flat, lanes):
    return jnp.pad(flat, [(0, 0)] * (flat.ndim - 1) + [(0, -flat.shape[-1] % lanes)])


def by_steps(
    layer_in,
    cotangent,
    w_qkv,
    w_out,
    w_up,
    w_down,
    gain_attn,
    shift_attn,
    bias_query,
    bias_value,
    bias_out,
    gain_mlp,
    shift_mlp,
    bias_up,
    bias_down,
    parents,
    seg_blocks,
    token_valid,
):
    rows, width = layer_in.shape
    fsdp = lax.axis_size("fsdp")
    nz = fsdp // 2
    devices = 4 * fsdp
    x, c, z, y = place()
    rank = z * 2 + c
    heads = H // fsdp
    cols = heads * HD
    tree = token_valid.shape[1]
    part = w_up.shape[0]
    unit = w_down.shape[0]

    vec = jnp.concatenate(
        [gain_attn, shift_attn, bias_query, bias_value, bias_out, gain_mlp, shift_mlp, bias_down, bias_up]
    ).astype(F32)
    vec = padded(vec, 1024).reshape(-1, 128)
    tab = jnp.concatenate([token_valid[0], seg_blocks[0], parents[0]])
    tab = padded(tab, 1024).reshape(-1, 128)
    aligned = part == HD and cols % 256 == 0
    if not aligned:
        w_qkv = w_qkv.reshape(part, 3, fsdp, cols).transpose(2, 0, 1, 3).reshape(fsdp, part, 3 * cols)
    x_all, qkv_w, down_w, vecs, tab = fetch(nz, layer_in, w_qkv, w_down, part, vec, tab, 1)
    down_w = down_w.reshape(4 * unit, width)
    x_all = x_all.reshape(tree, width)
    qkv_w = qkv_w.reshape(width, 3 * cols)
    vecs = vecs.reshape(devices, -1)
    (gain_one, shift_one, query_bias, value_bias, out_bias, gain_two, shift_two, down_bias) = [
        vecs[:, i * part : (i + 1) * part].reshape(-1) for i in range(8)
    ]
    up_bias = vecs[:, 8 * part : 8 * part + unit].reshape(2, 2, nz, 2, unit)
    up_bias = lax.dynamic_slice(up_bias, (0, c, z, 0, 0), (2, 1, 1, 2, unit)).reshape(-1)

    def own_rows(v):
        return lax.dynamic_slice_in_dim(v, rank * rows, rows, 0)

    normed_all, _ = norm_parts(x_all.astype(F32))
    attn_in = (normed_all * gain_one + shift_one).astype(BF)
    inputs = own_rows(x_all).astype(F32)
    normed_one, inverse_one = norm_parts(inputs)

    if aligned:

        def own_cols(v):
            v = v.reshape(2, 2, nz, 2, HD)
            return lax.dynamic_slice(v, (0, c, z, 0, 0), (2, 1, 1, 2, HD)).reshape(-1)

        def spread(v):
            v = v.reshape(2, 1, 1, 2, HD)
            return lax.dynamic_update_slice(jnp.zeros((2, 2, nz, 2, HD), F32), v, (0, c, z, 0, 0))

        numbers = block_of(jnp.arange(2)[:, None], c, z, jnp.arange(2)[None, :], nz).reshape(-1)
    else:

        def own_cols(v):
            return lax.dynamic_slice_in_dim(v, rank * cols, cols, 0)

        def spread(v):
            return lax.dynamic_update_slice_in_dim(jnp.zeros((width,), F32), v, rank * cols, 0)

        numbers = rank * heads + jnp.arange(heads)

    joined_bias = jnp.concatenate([own_cols(query_bias), jnp.zeros((cols,), F32), own_cols(value_bias)])
    joined = (jnp.dot(attn_in, qkv_w, preferred_element_type=F32) + joined_bias).astype(BF)

    tab = tab.reshape(-1)
    blocks = seg_blocks.shape[1]
    valid = tab[:tree]
    seg, position, ancestor = tree_tables(
        tab[tree + blocks : tree + blocks + parents.shape[1]], tab[tree : tree + blocks], valid
    )
    index = jnp.arange(tree, dtype=jnp.int32)
    mask = allowed_mask(seg, index, valid, ancestor)
    far = jnp.where(mask, (position[None, :] - position[:, None]).astype(F32), MASKED)
    slopes = jnp.exp2(-8.0 * (numbers.astype(F32) + 1.0) / H)
    mixed, cot, up_w, out_w = attend(slopes, far, joined, cotangent, w_up, w_out, unit, heads, nz, 9)
    out_w = out_w.reshape(width, width)
    cot = cot.reshape(tree, width)
    up_w = up_w.reshape(width, 4 * unit)

    mixed_own = exchange(mixed.reshape(fsdp, rows, cols), nz, 2, "mixed_to_tokens")
    if aligned:
        mixed_own = mixed_own.reshape(nz, 2, rows, 2, 2 * HD).transpose(2, 3, 1, 0, 4).reshape(rows, width)
    else:
        mixed_own = mixed_own.transpose(1, 0, 2).reshape(rows, width)
    branch = jnp.dot(mixed_own, out_w, preferred_element_type=F32) + out_bias
    middle = inputs + branch
    normed_two, inverse_two = norm_parts(middle)
    mlp_own = (normed_two * gain_two + shift_two).astype(BF)
    cot_blocks = cot.reshape(fsdp, rows, width)
    mlp_in = gather_tokens(mlp_own, nz, 3).reshape(tree, width)
    hidden = jnp.dot(mlp_in, up_w, preferred_element_type=F32) + up_bias
    active_float, gelu_pull = jax.vjp(gelu_exact, hidden)
    active = active_float.astype(BF)
    grad_active = mm("td,fd->tf", cot, down_w)
    grad_hidden = gelu_pull(grad_active)[0].astype(BF)
    grad_mlp_in = mm("tf,df->td", grad_hidden, up_w).astype(BF).reshape(fsdp, rows, width)
    grad_mlp_in = scatter_tokens(grad_mlp_in, nz, 4)
    update = jnp.dot(active, down_w, preferred_element_type=F32).astype(BF).reshape(fsdp, rows, width)
    down_g = mm("tf,td->fd", active, cot).astype(BF)
    up_g = mm("td,tf->df", mlp_in, grad_hidden).astype(BF)
    grad_bias_up = jnp.sum(grad_hidden.astype(F32), axis=0)
    down_g = down_g.reshape(4, unit, width)
    cot_own = own_rows(cot).astype(F32)
    grad_middle = cot_own + norm_back(grad_mlp_in * gain_two, normed_two, inverse_two)
    grad_branch = grad_middle.astype(BF)
    grad_mixed = mm("te,de->td", grad_branch, out_w).astype(BF)
    if not aligned:
        grad_out_w = lax.psum_scatter(
            mm("td,te->de", mixed_own, grad_branch).astype(BF), BOTH, scatter_dimension=0, tiled=True
        ).astype(F32)
    if aligned:
        grad_mixed = grad_mixed.reshape(rows, 2, 2, nz, 2 * HD).transpose(3, 2, 0, 1, 4).reshape(fsdp, rows, cols)
    else:
        grad_mixed = grad_mixed.reshape(rows, fsdp, cols).transpose(1, 0, 2)
    up_g = up_g.reshape(devices, part, 4 * unit)
    grad_heads = exchange(grad_mixed, nz, 5, "grad_to_heads")
    grad_heads = grad_heads.reshape(tree, cols)
    grad_q, grad_k, grad_v, branch_all, update, down_c, up_c = attend_back(
        slopes, far.T, joined, grad_heads, grad_branch, update, [down_g, up_g], (False, True), heads, nz, 6
    )
    result = middle + update + down_bias
    grad_joined = jnp.concatenate([grad_q, grad_k, grad_v], axis=1)

    def mine(g, came):
        g = g.reshape((2, 2, nz, 2) + g.shape[1:])
        g = lax.dynamic_slice(g, (x, 0, 0, y, 0, 0), (1, 2, nz, 1) + g.shape[4:])
        g = g.reshape((2, nz) + g.shape[4:]).swapaxes(0, 1)
        return (g.reshape(came.shape[1:]).astype(F32) + jnp.sum(came.astype(F32), axis=0)).astype(BF)

    def mine_flat(g, came):
        return lax.dynamic_index_in_dim(g, x * 2 + y, 0, keepdims=False).astype(F32) + jnp.sum(came.astype(F32), axis=0)

    grad_down_w = mine_flat(down_g, down_c)
    qkv_g = mm("td,te->de", attn_in, grad_joined).astype(BF).reshape(devices, part, 3 * cols)
    flat = []
    if aligned:
        flat = [mm("td,te->de", mixed, branch_all.reshape(tree, width)).astype(BF).reshape(4, part, width)]
    kinds = (True,) + (False,) * len(flat)
    grad_attn_in = mm("te,de->td", grad_joined, qkv_w).astype(BF).reshape(fsdp, rows, width)
    grad_attn_in, grad_up_w, layer_out, qkv_c, *out_c = scatter_and_hand(
        grad_attn_in, mine(up_g, up_c), up_runs(nz, unit), result.astype(BF), [qkv_g] + flat, kinds, nz, 10
    )
    if aligned:
        grad_out_w = mine_flat(flat[0], out_c[0])
    col, square = jnp.sum(grad_joined.astype(F32), axis=0), jnp.sum(result * result)
    grad_up_w = grad_up_w.astype(F32)
    grad_inputs = grad_middle + norm_back(grad_attn_in * gain_one, normed_one, inverse_one)

    smalls = [
        jnp.sum(grad_attn_in * normed_one, axis=0),
        jnp.sum(grad_attn_in, axis=0),
        spread(col[:cols]),
        spread(col[2 * cols :]),
        jnp.sum(grad_branch.astype(F32), axis=0),
        jnp.sum(grad_mlp_in * normed_two, axis=0),
        jnp.sum(grad_mlp_in, axis=0),
        jnp.sum(cot_own, axis=0),
    ]
    grad_bias_up = grad_bias_up.reshape(2, 1, 1, 2, unit)
    grad_bias_up = lax.dynamic_update_slice(jnp.zeros((2, 2, nz, 2, unit), F32), grad_bias_up, (0, c, z, 0, 0))
    squares = jnp.stack([square, jnp.sum(branch * branch)])
    packed = jnp.concatenate(
        [v.reshape(devices, part) for v in smalls]
        + [grad_bias_up.reshape(devices, unit), jnp.broadcast_to(squares, (devices, 2))],
        axis=1,
    )
    packed = padded(packed, 1024).reshape(devices, -1, 128)
    runs = qkv_runs(nz, width, cols) if aligned else None
    grad_x, packed, grad_qkv_w = finish(grad_inputs.astype(BF), packed, mine(qkv_g, qkv_c), runs, nz, 8)
    if not aligned:
        grad_qkv_w = grad_qkv_w.reshape(fsdp, part, 3, cols).transpose(1, 2, 0, 3).reshape(part, -1)
    grad_qkv_w = grad_qkv_w.astype(F32)
    packed = packed.reshape(-1)
    small = [packed[i * part : (i + 1) * part] for i in range(8)]
    up_at = 8 * part
    root_squares = jnp.sqrt(packed[up_at + unit : up_at + unit + 2] / (devices * rows * width))
    return (
        layer_out,
        grad_x,
        grad_qkv_w,
        grad_out_w,
        grad_up_w,
        grad_down_w,
        small[0],
        small[1],
        small[2],
        small[3],
        small[4],
        small[5],
        small[6],
        packed[up_at : up_at + unit],
        small[7],
        root_squares,
    )


def by_kernels(
    layer_in,
    cotangent,
    w_qkv,
    w_out,
    w_up,
    w_down,
    gain_attn,
    shift_attn,
    bias_query,
    bias_value,
    bias_out,
    gain_mlp,
    shift_mlp,
    bias_up,
    bias_down,
    parents,
    seg_blocks,
    token_valid,
):
    rows, width = layer_in.shape
    fsdp = lax.axis_size("fsdp")
    nz = fsdp // 2
    devices = 4 * fsdp
    heads = H // fsdp
    cols = heads * HD
    tree = token_valid.shape[1]
    part = w_up.shape[0]
    unit = w_down.shape[0]

    slopes = jnp.asarray(np.exp2(-8.0 * (np.arange(H) + 1.0) / H).astype(np.float32))
    vectors = (gain_attn, shift_attn, bias_query, bias_value, bias_out, gain_mlp, shift_mlp, bias_down)
    joined, mixed, mixed_own, own, whole, up_bias, attn_in, far, cot, qkv_w, up_w, out_w, down_w = head_call(
        slopes, (token_valid, seg_blocks, parents), vectors, bias_up, layer_in, cotangent, w_qkv, w_up, w_out, w_down,
        heads, nz, 1,
    )
    qkv_w = qkv_w.reshape(width, 3 * cols)
    up_w = up_w.reshape(width, 4 * unit)
    down_w = down_w.reshape(4 * unit, width)
    middle, grad_middle, grad_branch, grad_mixed, sums, grad_bias_up, update, up_g, down_g = mlp_call(
        mixed_own, own, whole, out_w, cot, up_w, down_w, up_bias, nz, 3
    )
    down_g = down_g.reshape(4, unit, width)
    runs = up_runs(nz, unit), qkv_runs(nz, width, cols)
    grad_down_w, grad_out_w, small, bias, grad_up_w, grad_qkv_w, _, layer_out, grad_x = tail_call(
        slopes, far, grad_mixed, joined, attn_in, mixed.reshape(tree, cols), qkv_w, grad_branch, update, up_g, down_g,
        middle, own, whole, grad_middle, sums, grad_bias_up, runs, heads, nz, 6,
    )
    root_squares = jnp.sqrt(small[8:10, 0] / (devices * rows * width))
    vectors = [small[i, :part] for i in range(8)]
    return (
        layer_out,
        grad_x,
        grad_qkv_w.astype(F32),
        grad_out_w,
        grad_up_w.astype(F32),
        grad_down_w,
        *vectors[:7],
        bias.reshape(-1)[:unit],
        vectors[7],
        root_squares,
    )


def per_device(*args):
    layer_in, w_down, token_valid = args[0], args[5], args[17]
    fsdp = lax.axis_size("fsdp")
    rows, width = layer_in.shape
    unit = w_down.shape[0]
    fits = mlp_bytes(fsdp // 2, rows, width, 4 * unit) < 60 * MIB
    whole_heads = args[2].shape[0] == HD and H // fsdp == 4 and width == H * HD
    if fsdp == 8 and fits and whole_heads and unit % 128 == 0 and token_valid.shape[1] % 256 == 0 and rows == 128:
        return by_kernels(*args)
    return by_steps(*args)


def solution(mesh):
    matrix, vector, table = P(BOTH, None), P(BOTH), P("dp", None)
    return jax.shard_map(
        per_device,
        mesh=mesh,
        in_specs=(matrix,) * 6 + (vector,) * 9 + (table,) * 3,
        out_specs=(matrix,) * 6 + (vector,) * 9 + (P(),),
        check_vma=False,
    )
```
